32 devices in a mesh: dp: 16 (over z, y, core), tensor: 2 (over x).
Axes of the slice: x: 2, y: 2, z: 4, core: 2. Of those that a mesh axis runs over, the one named last changes fastest.
Arguments:
- tokens: bfloat16 [32768, 768], P('dp'), may hold values from -6 to 6
- lengths: int32 [16, 8], P('dp'), may hold values from 1 to 1344, 1792 in all within a row
- qkv_weight: bfloat16 [3, 768, 768], P(None, None, 'tensor'), may hold values from -0.21875 to 0.21875
- qkv_bias: bfloat16 [2, 768], P(None, 'tensor'), may hold values from -3 to 3
- out_weight: bfloat16 [768, 768], P('tensor'), may hold values from -1.75 to 1.75
- out_bias: bfloat16 [768], replicated, may hold values from -3 to 3
- up_weight: bfloat16 [768, 3072], P(None, 'tensor'), may hold values from -0.21875 to 0.21875
- up_bias: bfloat16 [3072], P('tensor'), may hold values from -3 to 3
- down_weight: bfloat16 [3072, 768], P('tensor'), may hold values from -0.109375 to 0.109375
- down_bias: bfloat16 [768], replicated, may hold values from -3 to 3
- norm_gains: float32 [2, 768], replicated, may hold values from 0.5 to 1.5
- norm_biases: float32 [2, 768], replicated, may hold values from -2 to 2
- cotangent: bfloat16 [32768, 768], P('dp'), may hold values from -6 to 6
Outputs:
- output: bfloat16 [32768, 768], P('dp')
- input_grad: bfloat16 [32768, 768], P('dp')
- grad_qkv_weight: float32 [3, 768, 768], P(None, None, 'tensor')
- grad_qkv_bias: float32 [2, 768], P(None, 'tensor')
- grad_out_weight: float32 [768, 768], P('tensor')
- grad_out_bias: float32 [768], replicated
- grad_up_weight: float32 [768, 3072], P(None, 'tensor')
- grad_up_bias: float32 [3072], P('tensor')
- grad_down_weight: float32 [3072, 768], P('tensor')
- grad_down_bias: float32 [768], replicated
- grad_norm_gains: float32 [2, 768], replicated
- grad_norm_biases: float32 [2, 768], replicated
The draws below stay inside these ranges and needn't reach their ends.
Inputs may be any that keep to these rules, and one draw needn't show every extreme that they name: Each row's lengths sum to 1792, one of them is exactly 1344; the last 256 tokens of each row are padding.
All inputs are finite; a program needn't handle non-finite values.
Results may differ from the reference program's by a relative error of at most 0.0072.
Values sent between devices are 32-bit elements; how exact they have to be, the bound alone decides.
A program may use at most 256 MiB of HBM per device.

```python
import math
import jax
import jax.numpy as jnp
import numpy as np
from jax import lax

D = 768
FF = 3072
HEADS = 12
HEAD = 64
ROT = 16
ROW_LEN = 2048
SLOTS = 8
FILLED = 1792
LONGEST = 1344
TOKENS = 32768
N_DP = 16


def steps_of(stream_key, extent, shards, smallest, largest):
    level = 1.0
    for dim, parts in shards:
        draws = jax.random.uniform(jax.random.fold_in(jax.random.fold_in(stream_key, 6), dim), (parts,), jnp.float32, smallest / len(shards), largest / len(shards))
        level = level * jnp.repeat(jnp.exp(draws), extent[dim] // parts).reshape((-1,) + (1,) * (len(extent) - 1 - dim))
    return level


def split_up(number_of, total, most, skew):
    loads = [(1 << 20) // math.isqrt(standing ** skew) + 1 for standing in range(2, number_of + 1)]
    rest, given = total - most - (number_of - 1), [1] * (number_of - 1)
    while rest > 0:
        movable = [i for i in range(number_of - 1) if given[i] < most]
        pool, remaining = sum([loads[i] for i in movable]), rest
        for i in movable:
            extra = min(most - given[i], max(1, remaining * loads[i] // pool), rest)
            given[i] = given[i] + extra
            rest = rest - extra
    return np.array([most] + given)


def ragged_sizes(key, count, total, bound, slope):
    if count == 2:
        one = jax.random.randint(key, (), max(1, total - bound), min(bound, total - 1) + 1)
        return jnp.stack([one, total - one])
    sizes = jnp.asarray(split_up(count, total, bound, slope), jnp.int32)
    twos = (count - 1) // 2
    source_of, sink = sizes[1:1 + 2 * twos:2], sizes[2:2 + 2 * twos:2]
    margin = jnp.minimum(source_of - 1, bound - sink)
    moved = jax.random.randint(jax.random.fold_in(key, 1), (twos,), 0, 1 << 20) % (margin + 1)
    sizes = sizes.at[1:1 + 2 * twos:2].set(source_of - moved).at[2:2 + 2 * twos:2].set(sink + moved)
    return sizes[jax.random.permutation(jax.random.fold_in(key, 2), count)]


def gaussian(rng, extent, deviation, bound, split=(), kind=jnp.bfloat16):
    array = deviation * jax.random.normal(rng, extent, jnp.float32)
    if split:
        array = array * steps_of(rng, extent, split, -0.22, 0.18)
    return jnp.clip(array, -bound, bound).astype(kind)


def setup_inputs(seed: int = 0) -> dict:
    keys = jax.random.split(jax.random.key(seed), 14)
    tokens = gaussian(keys[0], (TOKENS, D), 1.0, 6.0, ((0, 16),))
    lengths = jax.vmap(lambda own: ragged_sizes(own, SLOTS, FILLED, LONGEST, 2))(jax.random.split(keys[1], N_DP)).reshape((N_DP, SLOTS)).astype(jnp.int32)
    qkv_weight = gaussian(keys[2], (3, D, D), D ** -0.5, 0.21875, ((2, 2),))
    qkv_bias = gaussian(keys[3], (2, D), 0.5, 3.0, ((1, 2),))
    out_weight = gaussian(keys[4], (D, D), (D // 64) ** -0.5, 1.75, ((0, 2),))
    out_bias = gaussian(keys[5], (D,), 0.5, 3.0)
    up_weight = gaussian(keys[6], (D, FF), D ** -0.5, 0.21875, ((1, 2),))
    up_bias = gaussian(keys[7], (FF,), 0.5, 3.0, ((0, 2),))
    down_weight = gaussian(keys[8], (FF, D), FF ** -0.5, 0.109375, ((0, 2),))
    down_bias = gaussian(keys[9], (D,), 0.5, 3.0)
    norm_gains = jnp.clip(1.0 + 0.1 * jax.random.normal(keys[10], (2, D), jnp.float32), 0.5, 1.5)
    norm_biases = gaussian(keys[11], (2, D), 0.3, 2.0, (), jnp.float32)
    cotangent = gaussian(keys[12], (TOKENS, D), 1.0, 6.0, ((0, 16),))
    return {"tokens": tokens, "lengths": lengths, "qkv_weight": qkv_weight, "qkv_bias": qkv_bias, "out_weight": out_weight, "out_bias": out_bias, "up_weight": up_weight, "up_bias": up_bias, "down_weight": down_weight, "down_bias": down_bias, "norm_gains": norm_gains, "norm_biases": norm_biases, "cotangent": cotangent}


epsilon = 1e-05
rot_base = 10000.0
highest = lax.Precision.HIGHEST

@jax.custom_vjp
def low(v):
    return lax.optimization_barrier(v.astype(jnp.bfloat16)).astype(jnp.float32)

@jax.custom_vjp
def low_back(v):
    return v

def low_keep(v):
    return (low(v), None)

def low_pass(kept, grad):
    return (grad,)

def back_keep(v):
    return (v, None)

def back_low(kept, grad):
    return (low(grad),)
low.defvjp(low_keep, low_pass)
low_back.defvjp(back_keep, back_low)

def layout(lengths_row, length):
    slots = lengths_row.shape[0]
    seg_ends = jnp.cumsum(lengths_row, dtype=jnp.int32)
    seg_starts = seg_ends - lengths_row
    places = jnp.arange(length, dtype=jnp.int32)
    segment = lax.optimization_barrier(jnp.sum((places[:, None] >= seg_ends[None, :]).astype(jnp.int32), axis=1, dtype=jnp.int32))
    member = segment[:, None] == jnp.arange(slots, dtype=jnp.int32)[None, :]
    first = lax.optimization_barrier(jnp.sum(jnp.where(member, seg_starts[None, :], 0), axis=1, dtype=jnp.int32))
    padded = segment >= slots
    position = jnp.where(padded, 0, places - first)
    segment = jnp.where(padded, slots + places, segment)
    return (segment, position)

def angles(position):
    half = ROT // 2
    frequency = rot_base ** (-(2.0 * jnp.arange(half, dtype=jnp.float32)) / ROT)
    theta = position.astype(jnp.float32)[:, None] * frequency[None, :]
    return (jnp.cos(theta), jnp.sin(theta))

def rotate(values, cosine, sine):
    half = ROT // 2
    first_half = values[..., :half]
    second_half = values[..., half:ROT]
    cosine = cosine[:, None, :]
    sine = sine[:, None, :]
    return jnp.concatenate([first_half * cosine - second_half * sine, second_half * cosine + first_half * sine, values[..., ROT:]], axis=-1)

def layer_norm(values, gain, shift):
    average = lax.optimization_barrier(jnp.mean(values, axis=-1, keepdims=True))
    centered = values - average
    inverse = lax.rsqrt(lax.optimization_barrier(jnp.mean(centered * centered, axis=-1, keepdims=True)) + epsilon)
    return centered * inverse * gain + shift

def attention(query, key, value, segment):
    length = query.shape[0]
    block = min(512, length)
    steps = length // block
    places = jnp.arange(length, dtype=jnp.int32)
    scale = HEAD ** (-0.5)

    @jax.checkpoint
    def one_block(items):
        query_block, seg_block, place_block = items
        raw = jnp.einsum('qhd,khd->hqk', query_block, key, precision=highest)
        scores = low_back(raw * scale)
        allowed = (seg_block[:, None] == segment[None, :]) & (places[None, :] <= place_block[:, None])
        scores = jnp.where(allowed[None], scores, -1e+30)
        probabilities = low(jax.nn.softmax(scores, axis=-1))
        return jnp.einsum('hqk,khd->qhd', probabilities, value, precision=highest)
    result = lax.map(one_block, (query.reshape(steps, block, HEADS, HEAD), segment.reshape(steps, block), places.reshape(steps, block)))
    return result.reshape(length, HEADS, HEAD)

def forward(inputs, weights, segment, cosine, sine):
    qkv_w, qkv_b, out_w, out_b, up_w, up_b, down_w, down_b, gains, shifts = weights
    length = inputs.shape[0]
    first_norm = low(layer_norm(inputs, gains[0], shifts[0]))
    query_pre = low_back(jnp.dot(first_norm, qkv_w[0], precision=highest) + qkv_b[0])
    key_pre = low_back(jnp.dot(first_norm, qkv_w[1], precision=highest))
    value = low(low_back(jnp.dot(first_norm, qkv_w[2], precision=highest) + qkv_b[1]))
    query = low(rotate(query_pre.reshape(length, HEADS, HEAD), cosine, sine))
    key = low(rotate(key_pre.reshape(length, HEADS, HEAD), cosine, sine))
    attended = attention(query, key, value.reshape(length, HEADS, HEAD), segment)
    attended = low(low_back(attended.reshape(length, D)))
    branch_attn = jnp.dot(attended, out_w, precision=highest) + out_b
    second_norm = low(layer_norm(inputs, gains[1], shifts[1]))
    hidden = low_back(jnp.dot(second_norm, up_w, precision=highest) + up_b)
    active = low(jax.nn.gelu(hidden, approximate=False))
    branch_mlp = jnp.dot(active, down_w, precision=highest) + down_b
    return inputs + branch_attn + branch_mlp

def reference(tokens, lengths, qkv_weight, qkv_bias, out_weight, out_bias, up_weight, up_bias, down_weight, down_bias, norm_gains, norm_biases, cotangent):
    weights = tuple((arr.astype(jnp.float32) for arr in (qkv_weight, qkv_bias, out_weight, out_bias, up_weight, up_bias, down_weight, down_bias, norm_gains, norm_biases)))
    rows_in = tokens.astype(jnp.float32).reshape(N_DP, ROW_LEN, D)
    rows_grad = cotangent.astype(jnp.float32).reshape(N_DP, ROW_LEN, D)
    totals = tuple((jnp.zeros_like(arr) for arr in weights))

    def one_row(carry, items):
        row_in, row_grad, row_lengths = items
        segment, position = layout(row_lengths, ROW_LEN)
        cosine, sine = angles(position)

        def apply(inputs, params):
            return forward(inputs, params, segment, cosine, sine)
        result, pullback = jax.vjp(apply, row_in, weights)
        input_part, weight_parts = pullback(row_grad)
        carry = jax.tree.map(lambda a, b: a + b, carry, weight_parts)
        return (carry, (result.astype(jnp.bfloat16), input_part.astype(jnp.bfloat16)))
    totals, (outputs, input_grads) = lax.scan(one_row, totals, (rows_in, rows_grad, lengths))
    return (outputs.reshape(TOKENS, D), input_grads.reshape(TOKENS, D), totals[0], totals[1], totals[2], totals[3], totals[4], totals[5], totals[6], totals[7], totals[8], totals[9])
```

```python
import functools
import math

import jax
import jax.numpy as jnp
import numpy as np
from jax import lax
from jax.experimental import pallas as pl
from jax.experimental.pallas import tpu as pltpu
from jax.sharding import PartitionSpec as P

HEAD = 64
ROT = 16
HALF = ROT // 2
epsilon = 1e-05
rot_base = 10000.0
f32 = jnp.float32
bf16 = jnp.bfloat16
NN = (((1,), (0,)), ((), ()))
NT = (((1,), (1,)), ((), ()))
TN = (((0,), (0,)), ((), ()))
TT = (((0,), (1,)), ((), ()))
VMEM_LIMIT = 60 * 2**20


def dot(a, b, dims=NN):
    return lax.dot_general(a, b, dims, preferred_element_type=f32)


def whole(shape):
    zeros = (0,) * len(shape)
    return pl.BlockSpec(shape, lambda *_: zeros, pipeline_mode=pl.Buffered(1))


def once(shape):
    zeros = (0,) * len(shape)
    return pl.BlockSpec(shape, lambda *_: zeros)


def hat_of(values):
    average = jnp.mean(values, axis=-1, keepdims=True)
    centered = values - average
    inverse = lax.rsqrt(jnp.mean(centered * centered, axis=-1, keepdims=True) + epsilon)
    return centered * inverse, inverse


def gelu_pair(h):
    a = jnp.abs(h) * np.float32(math.sqrt(0.5))
    t = 1.0 / (1.0 + np.float32(0.3275911) * a)
    bell = jnp.exp(-0.5 * (h * h))
    poly = np.float32(0.5 * 1.061405429) * t + np.float32(0.5 * -1.453152027)
    poly = poly * t + np.float32(0.5 * 1.421413741)
    poly = poly * t + np.float32(0.5 * -0.284496736)
    poly = poly * t + np.float32(0.5 * 0.254829592)
    tail = poly * t * bell
    phi = jnp.where(h >= 0, 1.0 - tail, tail)
    return h * phi, phi + h * bell * np.float32(1.0 / math.sqrt(2.0 * math.pi))


def add_to(ref, first, value):
    @pl.when(first)
    def _():
        ref[...] = value

    @pl.when(jnp.logical_not(first))
    def _():
        ref[...] += value


def mlp_kernel(chunk, tok, g, up, upb, down, gains, biases, part, share, dup, ddown, small, upb_sum):
    i = pl.program_id(0)
    hat, _ = hat_of(tok[...].astype(f32))
    gain = gains[1:2, :]
    normed = (hat * gain + biases[1:2, :]).astype(bf16)
    gt = g[...]
    total = None
    back = None
    wide = up.shape[1]

    @pl.when(i == 0)
    def _():
        dup[...] = jnp.zeros_like(dup)
        ddown[...] = jnp.zeros_like(ddown)
        small[...] = jnp.zeros_like(small)
        upb_sum[...] = jnp.zeros_like(upb_sum)

    for c in range(wide // chunk):
        sl = slice(c * chunk, (c + 1) * chunk)
        hidden = dot(normed, up[:, sl]) + upb[:, sl]
        act_grad = dot(gt, down[sl, :], NT)
        act, slope = gelu_pair(hidden)
        act = act.astype(bf16)
        hid_grad = (act_grad * slope).astype(bf16)
        p = dot(act, down[sl, :])
        e = dot(hid_grad, up[:, sl], NT)
        total = p if total is None else total + p
        back = e if back is None else back + e
        dup[:, sl] += dot(normed, hid_grad, TN)
        ddown[sl, :] += dot(act, gt, TN)
        upb_sum[:, sl] += jnp.sum(hid_grad.astype(f32), axis=0, keepdims=True)
    part[...] = total
    share[...] = back * gain
    small[0:1, :] += jnp.sum(gt.astype(f32), axis=0, keepdims=True)
    small[1:2, :] += jnp.sum(back * hat, axis=0, keepdims=True)
    small[2:3, :] += jnp.sum(back, axis=0, keepdims=True)


def mlp(tok, g, up, upb, down, gains, biases, tile=256, chunk=512):
    length, d = tok.shape
    wide = up.shape[1]
    rows = pl.BlockSpec((tile, d), lambda i: (i, 0))
    return pl.pallas_call(
        functools.partial(mlp_kernel, chunk),
        grid=(length // tile,),
        in_specs=[rows, rows, whole((d, wide)), whole((1, wide)), whole((wide, d)), whole((2, d)), whole((2, d))],
        out_specs=[rows, rows, once((d, wide)), once((wide, d)), once((8, d)), once((1, wide))],
        out_shape=[
            jax.ShapeDtypeStruct((length, d), f32),
            jax.ShapeDtypeStruct((length, d), f32),
            jax.ShapeDtypeStruct((d, wide), f32),
            jax.ShapeDtypeStruct((wide, d), f32),
            jax.ShapeDtypeStruct((8, d), f32),
            jax.ShapeDtypeStruct((1, wide), f32),
        ],
        compiler_params=pltpu.CompilerParams(vmem_limit_bytes=VMEM_LIMIT),
        cost_estimate=pl.CostEstimate(flops=12 * length * d * wide, bytes_accessed=4 * length * d * 4, transcendentals=0),
        name="mlp",
    )(tok, g, up, upb, down, gains, biases)


def first_tokens(lens, places):
    first = jnp.zeros_like(places)
    end = lens[0, 0]
    for j in range(1, lens.shape[1]):
        first = jnp.where(places >= end, end, first)
        end = end + lens[0, j]
    return jnp.where(places >= end, places, first)


def turn(block, cosine, sine, sign):
    parts = []
    for h in range(block.shape[0] // HEAD):
        r = h * HEAD
        a = block[r : r + HALF, :]
        b = block[r + HALF : r + ROT, :]
        if sign > 0:
            parts += [a * cosine - b * sine, b * cosine + a * sine]
        else:
            parts += [a * cosine + b * sine, b * cosine - a * sine]
        parts.append(block[r + ROT : r + HEAD, :])
    return jnp.concatenate(parts, axis=0)


def proj_kernel(lens, tok, g, w, bias, ow, gains, biases, freq, qt, q, kt, k, vt, dot_t, do, cosine, sine):
    tile = tok.shape[0]
    i = pl.program_id(0)
    hat, _ = hat_of(tok[...].astype(f32))
    normed = (hat * gains[0:1, :] + biases[0:1, :]).astype(bf16)
    places = i * tile + lax.broadcasted_iota(jnp.int32, (1, tile), 1)
    position = (places - first_tokens(lens, places)).astype(f32)
    theta = freq[:, 0:1] * position
    c = jnp.cos(theta)
    s = jnp.sin(theta)
    cosine[...] = c
    sine[...] = s
    scale = HEAD ** (-0.5)
    query = turn(dot(w[0], normed, TT) + bias[:, 0:1], c, s, 1).astype(bf16) * scale
    qt[...] = query
    q[...] = query.T
    key = turn(dot(w[1], normed, TT), c, s, 1).astype(bf16)
    kt[...] = key
    k[...] = key.T
    vt[...] = (dot(w[2], normed, TT) + bias[:, 1:2]).astype(bf16)
    grad = dot(ow[...], g[...], NT).astype(bf16)
    dot_t[...] = grad
    do[...] = grad.T


def project(lens, tok, g, w, bias, ow, gains, biases, freq, tile=512):
    length, d = tok.shape
    e = w.shape[2]
    rows = pl.BlockSpec((tile, d), lambda i, *_: (i, 0))
    tr = pl.BlockSpec((e, tile), lambda i, *_: (0, i))
    nat = pl.BlockSpec((tile, e), lambda i, *_: (i, 0))
    ang = pl.BlockSpec((HALF, tile), lambda i, *_: (0, i))
    t_shape = jax.ShapeDtypeStruct((e, length), bf16)
    n_shape = jax.ShapeDtypeStruct((length, e), bf16)
    a_shape = jax.ShapeDtypeStruct((HALF, length), f32)
    return pl.pallas_call(
        proj_kernel,
        grid_spec=pltpu.PrefetchScalarGridSpec(
            num_scalar_prefetch=1,
            grid=(length // tile,),
            in_specs=[rows, rows, whole((3, d, e)), whole((e, 2)), whole((e, d)), whole((2, d)), whole((2, d)), whole((HALF, 128))],
            out_specs=[tr, nat, tr, nat, tr, tr, nat, ang, ang],
        ),
        out_shape=[t_shape, n_shape, t_shape, n_shape, t_shape, t_shape, n_shape, a_shape, a_shape],
        compiler_params=pltpu.CompilerParams(vmem_limit_bytes=VMEM_LIMIT),
        cost_estimate=pl.CostEstimate(flops=8 * length * d * e, bytes_accessed=20 * length * e, transcendentals=0),
        name="project",
    )(lens, tok, g, w, bias, ow, gains, biases, freq)


def tile_range(lens, start):
    first = jnp.int32(0)
    end = lens[0, 0]
    for j in range(1, lens.shape[1]):
        first = jnp.where(start >= end, end, first)
        end = end + lens[0, j]
    return jnp.where(start >= end, start, first)


def attend_kernel(tk, lens, qt, k, vt, dot_t, ot, lse, delta, qpad, m_s, l_s, acc):
    i = pl.program_id(0)
    tq = qt.shape[1]
    heads = qt.shape[0] // HEAD
    q0 = i * tq
    places = q0 + lax.broadcasted_iota(jnp.int32, (1, tq), 1)
    first = first_tokens(lens, places)
    zero = jnp.zeros((HEAD, tq), bf16)
    for h in range(heads):
        qh = qt[h * HEAD : (h + 1) * HEAD, :]
        qpad[h] = jnp.concatenate([qh, zero] if h % 2 == 0 else [zero, qh], axis=0)
    m_s[...] = jnp.full_like(m_s, -1e30)
    l_s[...] = jnp.zeros_like(l_s)
    acc[...] = jnp.zeros_like(acc)
    low = lax.div(tile_range(lens, q0), tk)
    high = lax.div(q0 + tq + tk - 1, tk)

    def step(j, carry):
        k0 = pl.multiple_of(j * tk, tk)
        rows = k0 + lax.broadcasted_iota(jnp.int32, (tk, tq), 0)
        allowed = (rows >= first) & (rows <= places)
        for h in range(heads):
            pair = (h // 2) * 128
            s = dot(k[pl.ds(k0, tk), pair : pair + 128], qpad[h])
            s = jnp.where(allowed, s, -1e30)
            m_old = m_s[h : h + 1, :]
            m_new = jnp.maximum(m_old, jnp.max(s, axis=0, keepdims=True))
            p = jnp.exp(s - m_new)
            alpha = jnp.exp(m_old - m_new)
            m_s[h : h + 1, :] = m_new
            l_s[h : h + 1, :] = l_s[h : h + 1, :] * alpha + jnp.sum(p, axis=0, keepdims=True)
            o = dot(vt[h * HEAD : (h + 1) * HEAD, pl.ds(k0, tk)], p.astype(bf16))
            acc[h * HEAD : (h + 1) * HEAD, :] = acc[h * HEAD : (h + 1) * HEAD, :] * alpha + o
        return carry

    lax.fori_loop(low, high, step, 0)
    lse[...] = m_s[...] + jnp.log(l_s[...])
    for h in range(heads):
        sl = slice(h * HEAD, (h + 1) * HEAD)
        o = acc[sl, :] / l_s[h : h + 1, :]
        ot[sl, :] = o.astype(bf16)
        delta[h : h + 1, :] = jnp.sum(o * dot_t[sl, :].astype(f32), axis=0, keepdims=True)


def attend(lens, qt, k, vt, dot_t, tq=256, tk=256):
    e, length = qt.shape
    heads = e // HEAD
    cols = pl.BlockSpec((e, tq), lambda i, *_: (0, i))
    stat = pl.BlockSpec((8, tq), lambda i, *_: (0, i))
    return pl.pallas_call(
        functools.partial(attend_kernel, tk),
        grid_spec=pltpu.PrefetchScalarGridSpec(
            num_scalar_prefetch=1,
            grid=(length // tq,),
            in_specs=[cols, whole((length, e)), whole((e, length)), cols],
            out_specs=[cols, stat, stat],
            scratch_shapes=[
                pltpu.VMEM((heads, 128, tq), bf16),
                pltpu.VMEM((8, tq), f32),
                pltpu.VMEM((8, tq), f32),
                pltpu.VMEM((e, tq), f32),
            ],
        ),
        out_shape=[
            jax.ShapeDtypeStruct((e, length), bf16),
            jax.ShapeDtypeStruct((8, length), f32),
            jax.ShapeDtypeStruct((8, length), f32),
        ],
        compiler_params=pltpu.CompilerParams(vmem_limit_bytes=VMEM_LIMIT),
        cost_estimate=pl.CostEstimate(flops=2 * length * length * e, bytes_accessed=8 * length * e, transcendentals=0),
        name="attend",
    )(lens, qt, k, vt, dot_t)


def attend_back_kernel(tk, lens, q, qt, k, kt, vt, do, dot_t, lse, delta, cosine, sine, grads_q, grads_k, grads_v, kpad, vpad, dk, dv, dq, lse_b, del_b):
    i = pl.program_id(0)
    tq = q.shape[0]
    length = k.shape[0]
    heads = q.shape[1] // HEAD
    q0 = i * tq

    @pl.when(i == 0)
    def _():
        dk[...] = jnp.zeros_like(dk)
        dv[...] = jnp.zeros_like(dv)
        zero = jnp.zeros((HEAD, length), bf16)
        for h in range(heads):
            sl = slice(h * HEAD, (h + 1) * HEAD)
            own, other = (0, HEAD) if h % 2 == 0 else (HEAD, 0)
            kpad[h, own : own + HEAD, :] = kt[sl, :]
            kpad[h, other : other + HEAD, :] = zero
            vpad[h, own : own + HEAD, :] = vt[sl, :]
            vpad[h, other : other + HEAD, :] = zero

    places = q0 + lax.broadcasted_iota(jnp.int32, (tq, 1), 0)
    first = first_tokens(lens, places)
    lse_cols = lse[...].T
    del_cols = delta[...].T
    for h in range(heads):
        lse_b[h] = jnp.broadcast_to(lse_cols[:, h : h + 1], (tq, 128))
        del_b[h] = jnp.broadcast_to(del_cols[:, h : h + 1], (tq, 128))
    dq[...] = jnp.zeros_like(dq)
    low = lax.div(tile_range(lens, q0), tk)
    high = lax.div(q0 + tq + tk - 1, tk)

    def step(j, carry):
        k0 = pl.multiple_of(j * tk, tk)
        ks = pl.ds(k0, tk)
        cols = k0 + lax.broadcasted_iota(jnp.int32, (tq, tk), 1)
        allowed = (cols >= first) & (cols <= places)
        for h in range(heads):
            sl = slice(h * HEAD, (h + 1) * HEAD)
            pair = slice((h // 2) * 128, (h // 2) * 128 + 128)
            s = dot(q[:, pair], kpad[h, :, ks])
            s = s - jnp.concatenate([lse_b[h]] * (tk // 128), axis=1)
            p = jnp.where(allowed, jnp.exp(s), 0.0)
            dp = dot(do[:, pair], vpad[h, :, ks])
            ds = p * (dp - jnp.concatenate([del_b[h]] * (tk // 128), axis=1))
            ds = ds.astype(bf16)
            dv[sl, ks] += dot(dot_t[sl, :], p.astype(bf16))
            dk[sl, ks] += dot(qt[sl, :], ds)
            dq[h] += dot(ds, k[ks, pair])
        return carry

    lax.fori_loop(low, high, step, 0)
    scale = HEAD ** (-0.5)
    lane = lax.broadcasted_iota(jnp.int32, (tq, 128), 1)
    q_parts = [
        jnp.where(lane < HEAD, dq[2 * h], dq[2 * h + 1]).T * scale for h in range(heads // 2)
    ]
    angle = pl.ds(pl.multiple_of(q0, tq), tq)
    grads_q[...] = turn(jnp.concatenate(q_parts, axis=0), cosine[:, angle], sine[:, angle], -1).astype(bf16)

    @pl.when(i == pl.num_programs(0) - 1)
    def _():
        grads_k[...] = turn(dk[...], cosine[...], sine[...], -1).astype(bf16)
        grads_v[...] = dv[...].astype(bf16)


def attend_back(lens, q, qt, k, kt, vt, do, dot_t, lse, delta, cosine, sine, tq=256, tk=256):
    e, length = qt.shape
    heads = e // HEAD
    cols = pl.BlockSpec((e, tq), lambda i, *_: (0, i))
    rows = pl.BlockSpec((tq, e), lambda i, *_: (i, 0))
    stat = pl.BlockSpec((8, tq), lambda i, *_: (0, i))
    nat, tr, ang = whole((length, e)), whole((e, length)), whole((HALF, length))
    out = jax.ShapeDtypeStruct((e, length), bf16)
    return pl.pallas_call(
        functools.partial(attend_back_kernel, tk),
        grid_spec=pltpu.PrefetchScalarGridSpec(
            num_scalar_prefetch=1,
            grid=(length // tq,),
            in_specs=[rows, cols, nat, tr, tr, rows, cols, stat, stat, ang, ang],
            out_specs=[cols, once((e, length)), once((e, length))],
            scratch_shapes=[
                pltpu.VMEM((heads, 128, length), bf16),
                pltpu.VMEM((heads, 128, length), bf16),
                pltpu.VMEM((e, length), f32),
                pltpu.VMEM((e, length), f32),
                pltpu.VMEM((heads, tq, 128), f32),
                pltpu.VMEM((heads, tq, 128), f32),
                pltpu.VMEM((heads, tq, 128), f32),
            ],
        ),
        out_shape=[out, out, out],
        compiler_params=pltpu.CompilerParams(vmem_limit_bytes=VMEM_LIMIT),
        cost_estimate=pl.CostEstimate(flops=5 * length * length * e, bytes_accessed=20 * length * e, transcendentals=0),
        name="attend_back",
    )(lens, q, qt, k, kt, vt, do, dot_t, lse, delta, cosine, sine)


def merge_kernel(tok, g, gq, gk, gv, ot, w, ow, gains, biases, part_in, share_in, part, share, dw, dow, small, bias_sum):
    i = pl.program_id(0)
    tile = tok.shape[0]

    @pl.when(i == 0)
    def _():
        dw[...] = jnp.zeros_like(dw)
        dow[...] = jnp.zeros_like(dow)
        small[...] = jnp.zeros_like(small)
        bias_sum[...] = jnp.zeros_like(bias_sum)

    hat, _ = hat_of(tok[...].astype(f32))
    gain = gains[0:1, :]
    normed = (hat * gain + biases[0:1, :]).astype(bf16)
    back = dot(gq[...], w[0], TT) + dot(gk[...], w[1], TT) + dot(gv[...], w[2], TT)
    share[...] = share_in[...] + back * gain
    part[...] = part_in[...] + dot(ot[...], ow[...], TN)
    dw[0] += dot(normed, gq[...], TT)
    dw[1] += dot(normed, gk[...], TT)
    dw[2] += dot(normed, gv[...], TT)
    dow[...] += dot(ot[...], g[...])
    small[0:1, :] += jnp.sum(back * hat, axis=0, keepdims=True)
    small[1:2, :] += jnp.sum(back, axis=0, keepdims=True)
    ones = jnp.ones((8, tile), bf16)
    bias_sum[0] += dot(ones, gq[...], NT)
    bias_sum[1] += dot(ones, gv[...], NT)


def merge(tok, g, gq, gk, gv, ot, w, ow, gains, biases, part, share, tile=512):
    length, d = tok.shape
    e = w.shape[2]
    rows = pl.BlockSpec((tile, d), lambda i: (i, 0))
    cols = pl.BlockSpec((e, tile), lambda i: (0, i))
    full = jax.ShapeDtypeStruct((length, d), f32)
    return pl.pallas_call(
        merge_kernel,
        grid=(length // tile,),
        in_specs=[rows, rows, cols, cols, cols, cols, whole((3, d, e)), whole((e, d)), whole((2, d)), whole((2, d)), rows, rows],
        out_specs=[rows, rows, once((3, d, e)), once((e, d)), once((8, d)), once((2, 8, e))],
        out_shape=[
            full,
            full,
            jax.ShapeDtypeStruct((3, d, e), f32),
            jax.ShapeDtypeStruct((e, d), f32),
            jax.ShapeDtypeStruct((8, d), f32),
            jax.ShapeDtypeStruct((2, 8, e), f32),
        ],
        compiler_params=pltpu.CompilerParams(vmem_limit_bytes=VMEM_LIMIT),
        cost_estimate=pl.CostEstimate(flops=16 * length * d * e, bytes_accessed=24 * length * d, transcendentals=0),
        name="merge",
    )(tok, g, gq, gk, gv, ot, w, ow, gains, biases, part, share)


def per_device(
    tokens, lengths, qkv_weight, qkv_bias, out_weight, out_bias, up_weight, up_bias, down_weight, down_bias, norm_gains, norm_biases, cotangent
):
    freq = jnp.broadcast_to(
        (rot_base ** (-(2.0 * jnp.arange(HALF, dtype=f32)) / ROT))[:, None], (HALF, 128)
    )
    bias_cols = qkv_bias.astype(f32).T
    part, share, d_up, d_down, small_a, d_upb = mlp(
        tokens, cotangent, up_weight, up_bias.astype(f32)[None], down_weight, norm_gains, norm_biases
    )
    qt, q, kt, k, vt, dot_t, do, cosine, sine = project(
        lengths, tokens, cotangent, qkv_weight, bias_cols, out_weight, norm_gains, norm_biases, freq
    )
    ot, lse, delta = attend(lengths, qt, k, vt, dot_t)
    gq, gk, gv = attend_back(lengths, q, qt, k, kt, vt, do, dot_t, lse, delta, cosine, sine)
    part, share, d_qkv, d_out, small_b, bias_sum = merge(
        tokens, cotangent, gq, gk, gv, ot, qkv_weight, out_weight, norm_gains, norm_biases, part, share
    )
    summed, shares = lax.psum((part, share), "tensor")
    inputs = tokens.astype(f32)
    output = (inputs + summed + out_bias.astype(f32) + down_bias.astype(f32)).astype(bf16)
    hat, inverse = hat_of(inputs)
    input_share = inverse * (
        shares
        - jnp.mean(shares, axis=-1, keepdims=True)
        - hat * jnp.mean(shares * hat, axis=-1, keepdims=True)
    )
    input_grad = (cotangent.astype(f32) + input_share).astype(bf16)
    d_qkvb = bias_sum[:, 0, :]
    gain_shift = jnp.stack([small_b[0], small_a[1], small_b[1], small_a[2]])
    bias_grad = small_a[0]
    gain_shift = lax.psum(gain_shift, ("dp", "tensor"))
    d_qkv, d_qkvb, d_out, d_up, d_upb, d_down, bias_grad = lax.psum(
        (d_qkv, d_qkvb, d_out, d_up, d_upb, d_down, bias_grad), "dp"
    )
    return (
        output, input_grad, d_qkv, d_qkvb, d_out, bias_grad, d_up, d_upb[0], d_down, bias_grad, gain_shift[:2], gain_shift[2:],
    )


def solution(mesh):
    in_specs = (
        P("dp", None), P("dp", None), P(None, None, "tensor"), P(None, "tensor"), P("tensor", None), P(), P(None, "tensor"),
        P("tensor"), P("tensor", None), P(), P(), P(), P("dp", None),
    )
    out_specs = (
        P("dp", None), P("dp", None), P(None, None, "tensor"), P(None, "tensor"), P("tensor", None), P(), P(None, "tensor"),
        P("tensor"), P("tensor", None), P(), P(), P(),
    )
    return jax.shard_map(per_device, mesh=mesh, in_specs=in_specs, out_specs=out_specs, check_vma=False)
```

```python
import functools
import math

import jax
import jax.numpy as jnp
import numpy as np
from jax import lax
from jax.experimental import pallas as pl
from jax.experimental.pallas import tpu as pltpu
from jax.sharding import PartitionSpec as P

HEAD = 64
ROT = 16
HALF = ROT // 2
epsilon = 1e-05
rot_base = 10000.0
f32 = jnp.float32
bf16 = jnp.bfloat16
NN = (((1,), (0,)), ((), ()))
NT = (((1,), (1,)), ((), ()))
TN = (((0,), (0,)), ((), ()))
TT = (((0,), (1,)), ((), ()))
VMEM_LIMIT = 60 * 2**20


def dot(a, b, dims=NN):
    return lax.dot_general(a, b, dims, preferred_element_type=f32)


def whole(shape):
    zeros = (0,) * len(shape)
    return pl.BlockSpec(shape, lambda *_: zeros, pipeline_mode=pl.Buffered(1))


def once(shape):
    zeros = (0,) * len(shape)
    return pl.BlockSpec(shape, lambda *_: zeros)


def hat_of(values):
    average = jnp.mean(values, axis=-1, keepdims=True)
    centered = values - average
    inverse = lax.rsqrt(jnp.mean(centered * centered, axis=-1, keepdims=True) + epsilon)
    return centered * inverse, inverse


def gelu_pair(h):
    a = jnp.abs(h) * np.float32(math.sqrt(0.5))
    t = 1.0 / (1.0 + np.float32(0.3275911) * a)
    bell = jnp.exp(-0.5 * (h * h))
    poly = np.float32(0.5 * 1.061405429) * t + np.float32(0.5 * -1.453152027)
    poly = poly * t + np.float32(0.5 * 1.421413741)
    poly = poly * t + np.float32(0.5 * -0.284496736)
    poly = poly * t + np.float32(0.5 * 0.254829592)
    tail = poly * t * bell
    phi = jnp.where(h >= 0, 1.0 - tail, tail)
    return h * phi, phi + h * bell * np.float32(1.0 / math.sqrt(2.0 * math.pi))


def add_to(ref, first, value):
    @pl.when(first)
    def _():
        ref[...] = value

    @pl.when(jnp.logical_not(first))
    def _():
        ref[...] += value


def mlp_tile(chunk, tok, g, up, upb, down, gains, biases, visit):
    hat, _ = hat_of(tok[...].astype(f32))
    gain = gains[1:2, :]
    normed = (hat * gain + biases[1:2, :]).astype(bf16)
    gt = g[...]
    total = None
    back = None
    for c in range(up.shape[1] // chunk):
        sl = slice(c * chunk, (c + 1) * chunk)
        hidden = dot(normed, up[:, sl]) + upb[:, sl]
        act_grad = dot(gt, down[sl, :], NT)
        act, slope = gelu_pair(hidden)
        act = act.astype(bf16)
        hid_grad = (act_grad * slope).astype(bf16)
        p = dot(act, down[sl, :])
        e = dot(hid_grad, up[:, sl], NT)
        total = p if total is None else total + p
        back = e if back is None else back + e
        visit(sl, normed, gt, act, hid_grad)
    return hat, gt, total, back, gain


def mlp_own_kernel(chunk, meta, tok, g, up, upb, down, gains, biases, part, share, keep_d, send_d, keep_u, send_u, small, upb_sum, dup, ddown):
    i = pl.program_id(0)

    @pl.when(i == 0)
    def _():
        dup[...] = jnp.zeros_like(dup)
        ddown[...] = jnp.zeros_like(ddown)
        small[...] = jnp.zeros_like(small)
        upb_sum[...] = jnp.zeros_like(upb_sum)

    def visit(sl, normed, gt, act, hid_grad):
        dup[:, sl] += dot(normed, hid_grad, TN)
        ddown[sl, :] += dot(act, gt, TN)
        upb_sum[:, sl] += jnp.sum(hid_grad.astype(f32), axis=0, keepdims=True)

    hat, gt, total, back, gain = mlp_tile(chunk, tok, g, up, upb, down, gains, biases, visit)
    part[...] = total
    share[...] = back * gain
    small[0:1, :] += jnp.sum(gt.astype(f32), axis=0, keepdims=True)
    small[1:2, :] += jnp.sum(back * hat, axis=0, keepdims=True)
    small[2:3, :] += jnp.sum(back, axis=0, keepdims=True)

    @pl.when(i == pl.num_programs(0) - 1)
    def _():
        d, wide = dup.shape
        core = meta[0]
        for down_out, up_out, half in ((keep_d, keep_u, core), (send_d, send_u, 1 - core)):
            rows = pl.multiple_of(half * (wide // 2), wide // 2)
            down_out[...] = ddown[pl.ds(rows, wide // 2), :]
            rows = pl.multiple_of(half * (d // 2), d // 2)
            for c in range(wide // d):
                up_out[c * (d // 2) : (c + 1) * (d // 2), :] = dup[pl.ds(rows, d // 2), c * d : (c + 1) * d]


def mlp_own(meta, tok, g, up, upb, down, gains, biases, tile=512, chunk=768):
    length, d = tok.shape
    wide = up.shape[1]
    rows = pl.BlockSpec((tile, d), lambda i, *_: (i, 0))
    half = (wide // 2, d)
    shape = jax.ShapeDtypeStruct(half, f32)
    return pl.pallas_call(
        functools.partial(mlp_own_kernel, chunk),
        grid_spec=pltpu.PrefetchScalarGridSpec(
            num_scalar_prefetch=1,
            grid=(length // tile,),
            in_specs=[rows, rows, whole((d, wide)), whole((1, wide)), whole((wide, d)), whole((2, d)), whole((2, d))],
            out_specs=[rows, rows, once(half), once(half), once(half), once(half), once((8, d)), once((1, wide))],
            scratch_shapes=[pltpu.VMEM((d, wide), f32), pltpu.VMEM((wide, d), f32)],
        ),
        out_shape=[
            jax.ShapeDtypeStruct((length, d), f32),
            jax.ShapeDtypeStruct((length, d), f32),
            shape,
            shape,
            shape,
            shape,
            jax.ShapeDtypeStruct((8, d), f32),
            jax.ShapeDtypeStruct((1, wide), f32),
        ],
        compiler_params=pltpu.CompilerParams(vmem_limit_bytes=VMEM_LIMIT),
        cost_estimate=pl.CostEstimate(flops=12 * length * d * wide, bytes_accessed=4 * length * d * 4, transcendentals=0),
        name="mlp_own",
    )(meta, tok, g, up, upb, down, gains, biases)


def mlp_other_kernel(chunk, tok, g, up, upb, down, gains, biases, part_in, share_in, part, share):
    nothing = lambda *_: None
    _, _, total, back, gain = mlp_tile(chunk, tok, g, up, upb, down, gains, biases, nothing)
    part[...] = part_in[...] + total
    share[...] = share_in[...] + back * gain


def mlp_other(tok, g, up, upb, down, gains, biases, part, share, tile=512, chunk=768):
    length, d = tok.shape
    wide = up.shape[1]
    rows = pl.BlockSpec((tile, d), lambda i: (i, 0))
    full = jax.ShapeDtypeStruct((length, d), f32)
    return pl.pallas_call(
        functools.partial(mlp_other_kernel, chunk),
        grid=(length // tile,),
        in_specs=[rows, rows, whole((d, wide)), whole((1, wide)), whole((wide, d)), whole((2, d)), whole((2, d)), rows, rows],
        out_specs=[rows, rows],
        out_shape=[full, full],
        compiler_params=pltpu.CompilerParams(vmem_limit_bytes=VMEM_LIMIT),
        cost_estimate=pl.CostEstimate(flops=8 * length * d * wide, bytes_accessed=4 * length * d * 4, transcendentals=0),
        name="mlp_other",
    )(tok, g, up, upb, down, gains, biases, part, share)


def first_tokens(lens, places):
    first = jnp.zeros_like(places)
    end = lens[0, 0]
    for j in range(1, lens.shape[1]):
        first = jnp.where(places >= end, end, first)
        end = end + lens[0, j]
    return jnp.where(places >= end, places, first)


def turn(block, cosine, sine, sign):
    parts = []
    for h in range(block.shape[0] // HEAD):
        r = h * HEAD
        a = block[r : r + HALF, :]
        b = block[r + HALF : r + ROT, :]
        if sign > 0:
            parts += [a * cosine - b * sine, b * cosine + a * sine]
        else:
            parts += [a * cosine + b * sine, b * cosine - a * sine]
        parts.append(block[r + ROT : r + HEAD, :])
    return jnp.concatenate(parts, axis=0)


def proj_kernel(lens, tok, g, w, bias, ow, gains, biases, freq, qt, q, kt, k, vt, dot_t, do, cosine, sine):
    tile = tok.shape[0]
    i = pl.program_id(0)
    hat, _ = hat_of(tok[...].astype(f32))
    normed = (hat * gains[0:1, :] + biases[0:1, :]).astype(bf16)
    places = i * tile + lax.broadcasted_iota(jnp.int32, (1, tile), 1)
    position = (places - first_tokens(lens, places)).astype(f32)
    theta = freq[:, 0:1] * position
    c = jnp.cos(theta)
    s = jnp.sin(theta)
    cosine[...] = c
    sine[...] = s
    scale = HEAD ** (-0.5)
    query = turn(dot(w[0], normed, TT) + bias[:, 0:1], c, s, 1).astype(bf16) * scale
    qt[...] = query
    q[...] = query.T
    key = turn(dot(w[1], normed, TT), c, s, 1).astype(bf16)
    kt[...] = key
    k[...] = key.T
    vt[...] = (dot(w[2], normed, TT) + bias[:, 1:2]).astype(bf16)
    grad = dot(ow[...], g[...], NT).astype(bf16)
    dot_t[...] = grad
    do[...] = grad.T


def project(lens, tok, g, w, bias, ow, gains, biases, freq, tile=512):
    length, d = tok.shape
    e = w.shape[2]
    rows = pl.BlockSpec((tile, d), lambda i, *_: (i, 0))
    tr = pl.BlockSpec((e, tile), lambda i, *_: (0, i))
    nat = pl.BlockSpec((tile, e), lambda i, *_: (i, 0))
    ang = pl.BlockSpec((HALF, tile), lambda i, *_: (0, i))
    t_shape = jax.ShapeDtypeStruct((e, length), bf16)
    n_shape = jax.ShapeDtypeStruct((length, e), bf16)
    a_shape = jax.ShapeDtypeStruct((HALF, length), f32)
    return pl.pallas_call(
        proj_kernel,
        grid_spec=pltpu.PrefetchScalarGridSpec(
            num_scalar_prefetch=1,
            grid=(length // tile,),
            in_specs=[rows, rows, whole((3, d, e)), whole((e, 2)), whole((e, d)), whole((2, d)), whole((2, d)), whole((HALF, 128))],
            out_specs=[tr, nat, tr, nat, tr, tr, nat, ang, ang],
        ),
        out_shape=[t_shape, n_shape, t_shape, n_shape, t_shape, t_shape, n_shape, a_shape, a_shape],
        compiler_params=pltpu.CompilerParams(vmem_limit_bytes=VMEM_LIMIT),
        cost_estimate=pl.CostEstimate(flops=8 * length * d * e, bytes_accessed=20 * length * e, transcendentals=0),
        name="project",
    )(lens, tok, g, w, bias, ow, gains, biases, freq)


def tile_range(lens, start):
    first = jnp.int32(0)
    end = lens[0, 0]
    for j in range(1, lens.shape[1]):
        first = jnp.where(start >= end, end, first)
        end = end + lens[0, j]
    return jnp.where(start >= end, start, first)


def low_parts(x):
    high = x.astype(bf16)
    rest = x - high.astype(f32)
    mid = rest.astype(bf16)
    return [high, mid, (rest - mid.astype(f32)).astype(bf16)]


def tile_plan(lens, q0, tq, tk):
    low = lax.div(tile_range(lens, q0), tk)
    diagonal = lax.div(q0, tk)
    high = lax.div(q0 + tq + tk - 1, tk)
    inner = jnp.minimum(lax.div(tile_range(lens, q0 + tq - 1) + tk - 1, tk), diagonal)
    return low, jnp.maximum(inner, low), diagonal, high


def over_tiles(lens, q0, tq, tk, step, carry):
    low, inner, diagonal, high = tile_plan(lens, q0, tq, tk)
    edges = inner - low
    masked = lambda t, c: step(jnp.where(t < edges, low + t, diagonal + t - edges), c, True)
    carry = lax.fori_loop(0, edges + high - diagonal, masked, carry)
    return lax.fori_loop(inner, diagonal, lambda j, c: step(j, c, False), carry)


VROWS = 80


def attend_kernel(tk, lens, qt, k, vt, ot, qpad, vpad, acc):
    i = pl.program_id(0)
    tq = qt.shape[1]
    heads = qt.shape[0] // HEAD
    q0 = i * tq

    @pl.when(i == 0)
    def _():
        row = lax.broadcasted_iota(jnp.int32, (VROWS - HEAD, vt.shape[1]), 0)
        ones = jnp.where(row == 0, 1.0, 0.0).astype(bf16)
        for h in range(heads):
            vpad[h, :HEAD, :] = vt[h * HEAD : (h + 1) * HEAD, :]
            vpad[h, HEAD:, :] = ones

    places = q0 + lax.broadcasted_iota(jnp.int32, (1, tq), 1)
    first = first_tokens(lens, places)
    zero = jnp.zeros((HEAD, tq), bf16)
    for h in range(heads):
        qh = qt[h * HEAD : (h + 1) * HEAD, :]
        qpad[h] = jnp.concatenate([qh, zero] if h % 2 == 0 else [zero, qh], axis=0)
    acc[...] = jnp.zeros_like(acc)

    def step(j, peaks, masked):
        k0 = pl.multiple_of(j * tk, tk)
        if masked:
            rows = k0 + lax.broadcasted_iota(jnp.int32, (tk, tq), 0)
            allowed = (rows >= first) & (rows <= places)
        scores, new, raised = [], [], []
        for h in range(heads):
            pair = (h // 2) * 128
            s = dot(k[pl.ds(k0, tk), pair : pair + 128], qpad[h])
            scores.append(jnp.where(allowed, s, -1e30) if masked else s)
        for h in range(heads):
            new.append(jnp.maximum(peaks[h], jnp.max(scores[h], axis=0, keepdims=True)))
            raised.append(jnp.exp(scores[h] - new[h]).astype(bf16))
        for h in range(heads):
            o = dot(vpad[h, :, pl.ds(k0, tk)], raised[h])
            acc[h] = acc[h] * jnp.exp(peaks[h] - new[h]) + o
        return tuple(new)

    start = tuple(jnp.full((1, tq), -1e30, f32) for _ in range(heads))
    peaks = over_tiles(lens, q0, tq, tk, step, start)
    logs = []
    for h in range(heads):
        total = acc[h, HEAD : HEAD + 1, :]
        ot[h * HEAD : (h + 1) * HEAD, :] = acc[h, :HEAD, :] / total
        logs.append(peaks[h] + jnp.log(total))
    logs.append(jnp.zeros((8 - heads, tq), f32))
    ot[heads * HEAD :, :] = jnp.concatenate(logs, axis=0)


def attend(lens, qt, k, vt, tq=256, tk=256):
    e, length = qt.shape
    heads = e // HEAD
    cols = pl.BlockSpec((e, tq), lambda i, *_: (0, i))
    return pl.pallas_call(
        functools.partial(attend_kernel, tk),
        grid_spec=pltpu.PrefetchScalarGridSpec(
            num_scalar_prefetch=1,
            grid=(length // tq,),
            in_specs=[cols, whole((length, e)), whole((e, length))],
            out_specs=pl.BlockSpec((e + 8, tq), lambda i, *_: (0, i)),
            scratch_shapes=[
                pltpu.VMEM((heads, 128, tq), bf16),
                pltpu.VMEM((heads, VROWS, length), bf16),
                pltpu.VMEM((heads, VROWS, tq), f32),
            ],
        ),
        out_shape=jax.ShapeDtypeStruct((e + 8, length), f32),
        compiler_params=pltpu.CompilerParams(vmem_limit_bytes=VMEM_LIMIT),
        cost_estimate=pl.CostEstimate(flops=2 * length * length * e, bytes_accessed=8 * length * e, transcendentals=0),
        name="attend",
    )(lens, qt, k, vt)


def attend_back_kernel(tk, lens, q, qt, k, kt, vt, do, dot_t, ot, cosine, sine, grads_q, grads_k, grads_v, kpad, vpad, dk, dv, dq, qa, da, cs, cd):
    i = pl.program_id(0)
    tq = q.shape[0]
    length = k.shape[0]
    heads = q.shape[1] // HEAD
    q0 = i * tq

    @pl.when(i == 0)
    def _():
        dk[...] = jnp.zeros_like(dk)
        dv[...] = jnp.zeros_like(dv)
        zero = jnp.zeros((HEAD, length), bf16)
        row = lax.broadcasted_iota(jnp.int32, (128, tk), 0)
        for h in range(heads):
            sl = slice(h * HEAD, (h + 1) * HEAD)
            own, other = (0, HEAD) if h % 2 == 0 else (HEAD, 0)
            kpad[h, own : own + HEAD, :] = kt[sl, :]
            kpad[h, other : other + HEAD, :] = zero
            vpad[h, own : own + HEAD, :] = vt[sl, :]
            vpad[h, other : other + HEAD, :] = zero
            cs[h] = jnp.where((row < 24) & (row % 8 == h), -1.0, 0.0).astype(bf16)
            cd[h] = jnp.where((row >= 24) & (row < 48) & (row % 8 == h), -1.0, 0.0).astype(bf16)

    places = q0 + lax.broadcasted_iota(jnp.int32, (tq, 1), 0)
    first = first_tokens(lens, places)
    deltas = [
        jnp.sum(ot[h * HEAD : (h + 1) * HEAD, :] * dot_t[h * HEAD : (h + 1) * HEAD, :].astype(f32), axis=0, keepdims=True)
        for h in range(heads)
    ]
    deltas.append(jnp.zeros((8 - heads, tq), f32))
    stats = low_parts(ot[heads * HEAD :, :]) + low_parts(jnp.concatenate(deltas, axis=0))
    stats.append(jnp.zeros((128 - 48, tq), bf16))
    stat_cols = jnp.concatenate(stats, axis=0).T
    for r in range(heads // 2):
        pair = slice(r * 128, r * 128 + 128)
        qa[r, :, :128] = q[:, pair]
        qa[r, :, 128:] = stat_cols
        da[r, :, :128] = do[:, pair]
        da[r, :, 128:] = stat_cols
    dq[...] = jnp.zeros_like(dq)

    def step(j, carry, masked):
        k0 = pl.multiple_of(j * tk, tk)
        ks = pl.ds(k0, tk)
        if masked:
            cols = k0 + lax.broadcasted_iota(jnp.int32, (tq, tk), 1)
            allowed = (cols >= first) & (cols <= places)
        probs, grads = [], []
        for h in range(heads):
            s = dot(qa[h // 2], jnp.concatenate([kpad[h, :, ks], cs[h]], axis=0))
            dp = dot(da[h // 2], jnp.concatenate([vpad[h, :, ks], cd[h]], axis=0))
            p = jnp.exp(s)
            if masked:
                p = jnp.where(allowed, p, 0.0)
            probs.append(p.astype(bf16))
            grads.append((p * dp).astype(bf16))
        for h in range(heads):
            sl = slice(h * HEAD, (h + 1) * HEAD)
            pair = slice((h // 2) * 128, (h // 2) * 128 + 128)
            dv[sl, ks] += dot(dot_t[sl, :], probs[h])
            dk[sl, ks] += dot(qt[sl, :], grads[h])
            dq[h] += dot(grads[h], k[ks, pair])
        return carry

    over_tiles(lens, q0, tq, tk, step, 0)
    scale = HEAD ** (-0.5)
    lane = lax.broadcasted_iota(jnp.int32, (tq, 128), 1)
    q_parts = [
        jnp.where(lane < HEAD, dq[2 * h], dq[2 * h + 1]).T * scale for h in range(heads // 2)
    ]
    angle = pl.ds(pl.multiple_of(q0, tq), tq)
    grads_q[...] = turn(jnp.concatenate(q_parts, axis=0), cosine[:, angle], sine[:, angle], -1).astype(bf16)

    @pl.when(i == pl.num_programs(0) - 1)
    def _():
        grads_k[...] = turn(dk[...], cosine[...], sine[...], -1).astype(bf16)
        grads_v[...] = dv[...].astype(bf16)


def attend_back(lens, q, qt, k, kt, vt, do, dot_t, ot, cosine, sine, tq=256, tk=256):
    e, length = qt.shape
    heads = e // HEAD
    cols = pl.BlockSpec((e, tq), lambda i, *_: (0, i))
    rows = pl.BlockSpec((tq, e), lambda i, *_: (i, 0))
    stat = pl.BlockSpec((e + 8, tq), lambda i, *_: (0, i))
    nat, tr, ang = whole((length, e)), whole((e, length)), whole((HALF, length))
    out = jax.ShapeDtypeStruct((e, length), bf16)
    return pl.pallas_call(
        functools.partial(attend_back_kernel, tk),
        grid_spec=pltpu.PrefetchScalarGridSpec(
            num_scalar_prefetch=1,
            grid=(length // tq,),
            in_specs=[rows, cols, nat, tr, tr, rows, cols, stat, ang, ang],
            out_specs=[cols, once((e, length)), once((e, length))],
            scratch_shapes=[
                pltpu.VMEM((heads, 128, length), bf16),
                pltpu.VMEM((heads, 128, length), bf16),
                pltpu.VMEM((e, length), f32),
                pltpu.VMEM((e, length), f32),
                pltpu.VMEM((heads, tq, 128), f32),
                pltpu.VMEM((heads // 2, tq, 256), bf16),
                pltpu.VMEM((heads // 2, tq, 256), bf16),
                pltpu.VMEM((heads, 128, tk), bf16),
                pltpu.VMEM((heads, 128, tk), bf16),
            ],
        ),
        out_shape=[out, out, out],
        compiler_params=pltpu.CompilerParams(vmem_limit_bytes=VMEM_LIMIT),
        cost_estimate=pl.CostEstimate(flops=5 * length * length * e, bytes_accessed=20 * length * e, transcendentals=0),
        name="attend_back",
    )(lens, q, qt, k, kt, vt, do, dot_t, ot, cosine, sine)


def merge_tile(tok, gq, gk, gv, ot, w, ow, gains, biases):
    hat, inverse = hat_of(tok[...].astype(f32))
    gain = gains[0:1, :]
    back = dot(gq[...], w[0], TT) + dot(gk[...], w[1], TT) + dot(gv[...], w[2], TT)
    low = ot[...].astype(bf16)
    return hat, inverse, gain, back, low, dot(low, ow[...], TN)


def merge_own_kernel(meta, tok, g, gq, gk, gv, ot, w, ow, gains, biases, part_in, share_in, part, share, keep, send, small, bias_sum, dw, dow):
    i = pl.program_id(0)
    tile = tok.shape[0]

    @pl.when(i == 0)
    def _():
        dw[...] = jnp.zeros_like(dw)
        dow[...] = jnp.zeros_like(dow)
        small[...] = jnp.zeros_like(small)
        bias_sum[...] = jnp.zeros_like(bias_sum)

    hat, _, gain, back, low, out = merge_tile(tok, gq, gk, gv, ot, w, ow, gains, biases)
    normed = (hat * gain + biases[0:1, :]).astype(bf16)
    share[...] = share_in[...] + back * gain
    part[...] = part_in[...] + out
    dw[0] += dot(normed, gq[...], TT)
    dw[1] += dot(normed, gk[...], TT)
    dw[2] += dot(normed, gv[...], TT)
    dow[...] += dot(low, g[...])
    small[0:1, :] += jnp.sum(back * hat, axis=0, keepdims=True)
    small[1:2, :] += jnp.sum(back, axis=0, keepdims=True)
    ones = jnp.ones((8, tile), bf16)
    bias_sum[0] += dot(ones, gq[...], NT)
    bias_sum[1] += dot(ones, gv[...], NT)

    @pl.when(i == pl.num_programs(0) - 1)
    def _():
        _, d, e = dw.shape
        core = meta[0]
        quarter = d // 4
        for ref, half in ((keep, core), (send, 1 - core)):
            for c in range(3):
                for s in range(2):
                    rows = pl.multiple_of(half * (2 * quarter) + s * quarter, quarter)
                    ref[c * quarter : (c + 1) * quarter, s * e : (s + 1) * e] = dw[c, pl.ds(rows, quarter), :]
            rows = pl.multiple_of(half * (e // 2), e // 2)
            ref[3 * quarter :, :] = dow[pl.ds(rows, e // 2), :]


def merge_own(meta, tok, g, gq, gk, gv, ot, w, ow, gains, biases, part, share, tile=512):
    length, d = tok.shape
    e = w.shape[2]
    rows = pl.BlockSpec((tile, d), lambda i, *_: (i, 0))
    cols = pl.BlockSpec((e, tile), lambda i, *_: (0, i))
    full = jax.ShapeDtypeStruct((length, d), f32)
    half = (3 * d // 4 + e // 2, d)
    return pl.pallas_call(
        merge_own_kernel,
        grid_spec=pltpu.PrefetchScalarGridSpec(
            num_scalar_prefetch=1,
            grid=(length // tile,),
            in_specs=[rows, rows, cols, cols, cols, cols, whole((3, d, e)), whole((e, d)), whole((2, d)), whole((2, d)), rows, rows],
            out_specs=[rows, rows, once(half), once(half), once((8, d)), once((2, 8, e))],
            scratch_shapes=[pltpu.VMEM((3, d, e), f32), pltpu.VMEM((e, d), f32)],
        ),
        out_shape=[
            full,
            full,
            jax.ShapeDtypeStruct(half, f32),
            jax.ShapeDtypeStruct(half, f32),
            jax.ShapeDtypeStruct((8, d), f32),
            jax.ShapeDtypeStruct((2, 8, e), f32),
        ],
        compiler_params=pltpu.CompilerParams(vmem_limit_bytes=VMEM_LIMIT),
        cost_estimate=pl.CostEstimate(flops=16 * length * d * e, bytes_accessed=24 * length * d, transcendentals=0),
        name="merge_own",
    )(meta, tok, g, gq, gk, gv, ot, w, ow, gains, biases, part, share)


def merge_other_kernel(tok, g, gq, gk, gv, ot, w, ow, gains, biases, out_bias, part_in, share_in, output, input_grad):
    hat, inverse, gain, back, _, out = merge_tile(tok, gq, gk, gv, ot, w, ow, gains, biases)
    shares = share_in[...] + back * gain
    inputs = tok[...].astype(f32)
    output[...] = (inputs + (part_in[...] + out) + out_bias[0:1, :] + out_bias[1:2, :]).astype(bf16)
    input_share = inverse * (
        shares
        - jnp.mean(shares, axis=-1, keepdims=True)
        - hat * jnp.mean(shares * hat, axis=-1, keepdims=True)
    )
    input_grad[...] = (g[...].astype(f32) + input_share).astype(bf16)


def merge_other(tok, g, gq, gk, gv, ot, w, ow, gains, biases, out_bias, part, share, tile=512):
    length, d = tok.shape
    e = w.shape[2]
    rows = pl.BlockSpec((tile, d), lambda i: (i, 0))
    cols = pl.BlockSpec((e, tile), lambda i: (0, i))
    full = jax.ShapeDtypeStruct((length, d), bf16)
    return pl.pallas_call(
        merge_other_kernel,
        grid=(length // tile,),
        in_specs=[rows, rows, cols, cols, cols, cols, whole((3, d, e)), whole((e, d)), whole((2, d)), whole((2, d)), whole((2, d)), rows, rows],
        out_specs=[rows, rows],
        out_shape=[full, full],
        compiler_params=pltpu.CompilerParams(vmem_limit_bytes=VMEM_LIMIT),
        cost_estimate=pl.CostEstimate(flops=8 * length * d * e, bytes_accessed=24 * length * d, transcendentals=0),
        name="merge_other",
    )(tok, g, gq, gk, gv, ot, w, ow, gains, biases, out_bias, part, share)


def pack_kernel(meta, w, ow, up, down, first, second):
    d = ow.shape[1]
    e = w.shape[2]
    for n, ref in enumerate((first, second)):
        at = 0
        r = down.shape[0] // 2
        ref[at : at + r, :] = down[n * r : (n + 1) * r, :].astype(f32)
        at += r
        r = up.shape[0] // 2
        for c in range(up.shape[1] // d):
            ref[at : at + r, :] = up[n * r : (n + 1) * r, c * d : (c + 1) * d].astype(f32)
            at += r
        r = w.shape[1] // 4
        for c in range(3):
            for s in range(2):
                ref[at : at + r, s * e : (s + 1) * e] = w[c, (2 * n + s) * r : (2 * n + s + 1) * r, :].astype(f32)
            at += r
        r = ow.shape[0] // 2
        ref[at : at + r, :] = ow[n * r : (n + 1) * r, :].astype(f32)


def pack(meta, w, ow, up, down):
    _, d, e = w.shape
    wide = up.shape[1]
    rows = (wide + (wide // d) * d + 3 * d // 2 + e) // 8
    piece = jax.ShapeDtypeStruct((rows, d), f32)
    return pl.pallas_call(
        pack_kernel,
        grid_spec=pltpu.PrefetchScalarGridSpec(
            num_scalar_prefetch=1,
            grid=(1,),
            in_specs=[
                pl.BlockSpec((3, d // 4, e), lambda i, m: (0, m[1], 0)),
                pl.BlockSpec((e // 4, d), lambda i, m: (m[1], 0)),
                pl.BlockSpec((d // 4, wide), lambda i, m: (m[1], 0)),
                pl.BlockSpec((wide // 4, d), lambda i, m: (m[1], 0)),
            ],
            out_specs=[once((rows, d)), once((rows, d))],
        ),
        out_shape=[piece, piece],
        compiler_params=pltpu.CompilerParams(vmem_limit_bytes=VMEM_LIMIT),
        name="pack",
    )(meta, w, ow, up, down)


def unpack_kernel(meta, *refs):
    pieces, (w, ow, up, down) = refs[:8], refs[8:]
    d = ow.shape[1]
    e = w.shape[2]
    for n, ref in enumerate(pieces):
        core = meta[0] ^ (n // 4)
        parity = meta[2] ^ ((n // 2) % 2)
        at_piece = (parity * 2 + core) * 2 + n % 2
        at = 0
        r = down.shape[0] // 8
        down[pl.ds(pl.multiple_of(at_piece * r, r), r), :] = ref[at : at + r, :].astype(bf16)
        at += r
        r = up.shape[0] // 8
        for c in range(up.shape[1] // d):
            up[pl.ds(pl.multiple_of(at_piece * r, r), r), c * d : (c + 1) * d] = ref[at : at + r, :].astype(bf16)
            at += r
        r = w.shape[1] // 16
        for c in range(3):
            for s in range(2):
                w[c, pl.ds(pl.multiple_of((at_piece * 2 + s) * r, r), r), :] = ref[at : at + r, s * e : (s + 1) * e].astype(bf16)
            at += r
        r = ow.shape[0] // 8
        ow[pl.ds(pl.multiple_of(at_piece * r, r), r), :] = ref[at : at + r, :].astype(bf16)


def unpack(meta, pieces, w, ow, up, down):
    shapes = [jax.ShapeDtypeStruct(x.shape, bf16) for x in (w, ow, up, down)]
    return pl.pallas_call(
        unpack_kernel,
        grid_spec=pltpu.PrefetchScalarGridSpec(
            num_scalar_prefetch=1,
            grid=(1,),
            in_specs=[once(p.shape) for p in pieces],
            out_specs=[once(s.shape) for s in shapes],
        ),
        out_shape=shapes,
        compiler_params=pltpu.CompilerParams(vmem_limit_bytes=VMEM_LIMIT),
        name="unpack",
    )(meta, *pieces)


def swap(x, bit):
    n = lax.axis_size("dp")
    return lax.ppermute(x, "dp", [(i, i ^ (1 << bit)) for i in range(n)])


def across(x):
    return lax.ppermute(x, "tensor", [(0, 1), (1, 0)])


def total_over_dp(keep, send, order, me):
    got = swap(send, 0)
    for b in order:
        v = (me >> b) & 1
        r = keep.shape[0] // 2
        part = lambda x, at: lax.dynamic_slice_in_dim(x, at * r, r, 0)
        send = part(keep, 1 - v) + part(got, 1 - v)
        keep = part(keep, v) + part(got, v)
        got = swap(send, b)
    full = keep + got
    for b in reversed(order):
        got = swap(full, b)
        full = in_order((me >> b) & 1, full, got, 0)
    return full


def in_order(v, mine, got, axis):
    return jnp.concatenate([jnp.where(v == 0, mine, got), jnp.where(v == 0, got, mine)], axis=axis)


def small_total(x, bits):
    for b in range(bits):
        x = x + swap(x, b)
    return x


def per_device(
    tokens, lengths, qkv_weight, qkv_bias, out_weight, out_bias, up_weight, up_bias, down_weight, down_bias, norm_gains, norm_biases, cotangent
):
    length, d = tokens.shape
    e = qkv_weight.shape[2]
    wide = up_weight.shape[1]
    size = lax.axis_size("dp")
    bits = size.bit_length() - 1
    me = lax.axis_index("dp")
    core = me & 1
    parity = ((me >> 1) ^ (me >> 2)) & 1
    meta = jnp.stack([core, parity * 2 + core, parity] + [jnp.int32(0)] * 5)
    freq = jnp.broadcast_to(
        (rot_base ** (-(2.0 * jnp.arange(HALF, dtype=f32)) / ROT))[:, None], (HALF, 128)
    )
    first, second = pack(meta, qkv_weight, out_weight, up_weight, down_weight)
    own_biases = jnp.concatenate([up_bias.astype(f32), qkv_bias.astype(f32).reshape(-1)]).reshape(-1, d)
    other_biases = across(own_biases)
    first, second = across(first), across(second)
    near = [first, second, swap(first, 1), swap(second, 2)]
    pieces = near + [swap(x, 0) for x in near]
    other_w, other_ow, other_up, other_down = unpack(meta, pieces, qkv_weight, out_weight, up_weight, down_weight)

    def half_biases(rows):
        flat = rows.reshape(-1)
        return flat[None, :wide], flat[wide:].reshape(2, e).T

    own_upb, own_qkvb = half_biases(own_biases)
    other_upb, other_qkvb = half_biases(other_biases)
    part, share, keep_d, send_d, keep_u, send_u, small_a, d_upb = mlp_own(
        meta, tokens, cotangent, up_weight, own_upb, down_weight, norm_gains, norm_biases
    )
    order = list(range(1, bits))
    turned = order[1:] + order[:1]
    half_d = total_over_dp(keep_d, send_d, order, me)
    half_u = total_over_dp(keep_u, send_u, turned, me)
    part, share, lengths_b = lax.optimization_barrier((part, share, lengths))
    qt, q, kt, k, vt, dot_t, do, cosine, sine = project(
        lengths_b, tokens, cotangent, qkv_weight, own_qkvb, out_weight, norm_gains, norm_biases, freq
    )
    ot = attend(lengths, qt, k, vt)
    other_ot = across(ot)
    gq, gk, gv = attend_back(lengths, q, qt, k, kt, vt, do, dot_t, ot, cosine, sine)
    part, share, keep_a, send_a, small_b, bias_sum = merge_own(
        meta, tokens, cotangent, gq, gk, gv, ot, qkv_weight, out_weight, norm_gains, norm_biases, part, share
    )
    half_a = total_over_dp(keep_a, send_a, order, me)
    norm_sums = jnp.stack([small_b[0], small_a[1], small_b[1], small_a[2]])
    norm_sums = norm_sums + across(norm_sums)
    smalls = jnp.concatenate([norm_sums, small_a[:1], d_upb.reshape(-1, d), bias_sum[:, 0, :].reshape(-1, d)])
    smalls = small_total(smalls, bits)
    part, share, lengths_c = lax.optimization_barrier((part, share, lengths))
    qt, q, kt, k, vt, dot_t, do, cosine, sine = project(
        lengths_c, tokens, cotangent, other_w, other_qkvb, other_ow, norm_gains, norm_biases, freq
    )
    gq, gk, gv = attend_back(lengths, q, qt, k, kt, vt, do, dot_t, other_ot, cosine, sine)
    part, share = mlp_other(tokens, cotangent, other_up, other_upb, other_down, norm_gains, norm_biases, part, share)
    out_biases = jnp.stack([out_bias, down_bias]).astype(f32)
    output, input_grad = merge_other(
        tokens, cotangent, gq, gk, gv, other_ot, other_w, other_ow, norm_gains, norm_biases, out_biases, part, share
    )
    d_down = in_order(core, half_d, swap(half_d, 0), 0)
    d_up = in_order(core, half_u, swap(half_u, 0), 0)
    d_up = d_up.reshape(2, wide // d, d // 2, d).transpose(0, 2, 1, 3).reshape(d, wide)
    d_a = in_order(core, half_a, swap(half_a, 0), 0).reshape(2, -1, d)
    d_qkv = d_a[:, : 3 * d // 4].reshape(2, 3, d // 4, 2, e).transpose(1, 0, 3, 2, 4).reshape(3, d, e)
    d_out = d_a[:, 3 * d // 4 :].reshape(e, d)
    rest = smalls[5:].reshape(-1)
    return (
        output, input_grad, d_qkv, rest[wide:].reshape(2, e), d_out, smalls[4], d_up, rest[:wide], d_down, smalls[4], smalls[:2], smalls[2:4],
    )


def solution(mesh):
    in_specs = (
        P("dp", None), P("dp", None), P(None, None, "tensor"), P(None, "tensor"), P("tensor", None), P(), P(None, "tensor"),
        P("tensor"), P("tensor", None), P(), P(), P(), P("dp", None),
    )
    out_specs = (
        P("dp", None), P("dp", None), P(None, None, "tensor"), P(None, "tensor"), P("tensor", None), P(), P(None, "tensor"),
        P("tensor"), P("tensor", None), P(), P(), P(),
    )
    return jax.shard_map(per_device, mesh=mesh, in_specs=in_specs, out_specs=out_specs, check_vma=False)
```

```python
import functools
import math

import jax
import jax.numpy as jnp
import numpy as np
from jax import lax
from jax.experimental import pallas as pl
from jax.experimental.pallas import tpu as pltpu
from jax.sharding import PartitionSpec as P

HEAD = 64
ROT = 16
HALF = ROT // 2
epsilon = 1e-05
rot_base = 10000.0
f32 = jnp.float32
bf16 = jnp.bfloat16
NN = (((1,), (0,)), ((), ()))
NT = (((1,), (1,)), ((), ()))
TN = (((0,), (0,)), ((), ()))
TT = (((0,), (1,)), ((), ()))
VMEM_LIMIT = 60 * 2**20


def dot(a, b, dims=NN):
    return lax.dot_general(a, b, dims, preferred_element_type=f32)


def call(kernel, *, grid, in_specs, out_specs, out_shape, scalars=0, scratch=(), deps=(), flops=0, nbytes=0, name=None, aliases=None):
    first, last = scalars + len(in_specs), scalars + len(in_specs) + len(deps)

    def body(*refs):
        kernel(*refs[:first], *refs[last:])

    return lambda *args: pl.pallas_call(
        body,
        grid_spec=pltpu.PrefetchScalarGridSpec(
            num_scalar_prefetch=scalars,
            grid=grid,
            in_specs=list(in_specs) + [pl.BlockSpec(memory_space=pl.ANY)] * len(deps),
            out_specs=out_specs,
            scratch_shapes=scratch,
        ),
        out_shape=out_shape,
        compiler_params=pltpu.CompilerParams(vmem_limit_bytes=VMEM_LIMIT),
        cost_estimate=pl.CostEstimate(flops=20 * flops, bytes_accessed=nbytes, transcendentals=0),
        input_output_aliases=aliases or {},
        name=name,
    )(*args, *deps)


def whole(shape):
    zeros = (0,) * len(shape)
    return pl.BlockSpec(shape, lambda *_: zeros, pipeline_mode=pl.Buffered(1))


def once(shape):
    zeros = (0,) * len(shape)
    return pl.BlockSpec(shape, lambda *_: zeros)


def hat_of(values):
    average = jnp.mean(values, axis=-1, keepdims=True)
    centered = values - average
    inverse = lax.rsqrt(jnp.mean(centered * centered, axis=-1, keepdims=True) + epsilon)
    return centered * inverse, inverse


def gelu_pair(h):
    a = jnp.abs(h) * np.float32(math.sqrt(0.5))
    t = 1.0 / (1.0 + np.float32(0.3275911) * a)
    bell = jnp.exp(-0.5 * (h * h))
    poly = np.float32(0.5 * 1.061405429) * t + np.float32(0.5 * -1.453152027)
    poly = poly * t + np.float32(0.5 * 1.421413741)
    poly = poly * t + np.float32(0.5 * -0.284496736)
    poly = poly * t + np.float32(0.5 * 0.254829592)
    tail = poly * t * bell
    phi = jnp.where(h >= 0, 1.0 - tail, tail)
    return h * phi, phi + h * bell * np.float32(1.0 / math.sqrt(2.0 * math.pi))


def add_to(ref, first, value):
    @pl.when(first)
    def _():
        ref[...] = value

    @pl.when(jnp.logical_not(first))
    def _():
        ref[...] += value


def mlp_tile(chunk, tok, g, up, upb, down, gains, biases, visit):
    hat, _ = hat_of(tok[...].astype(f32))
    gain = gains[1:2, :]
    normed = (hat * gain + biases[1:2, :]).astype(bf16)
    gt = g[...]
    total = None
    back = None
    for c in range(up.shape[1] // chunk):
        sl = slice(c * chunk, (c + 1) * chunk)
        hidden = dot(normed, up[:, sl]) + upb[:, sl]
        act_grad = dot(gt, down[sl, :], NT)
        act, slope = gelu_pair(hidden)
        act = act.astype(bf16)
        hid_grad = (act_grad * slope).astype(bf16)
        p = dot(act, down[sl, :])
        e = dot(hid_grad, up[:, sl], NT)
        total = p if total is None else total + p
        back = e if back is None else back + e
        visit(sl, normed, gt, act, hid_grad)
    return hat, gt, total, back, gain


def mlp_own_kernel(chunk, meta, tok, g, up, upb, down, gains, biases, part, share, keep, send, ddown, small, upb_sum, dup):
    i = pl.program_id(0)

    @pl.when(i == 0)
    def _():
        dup[...] = jnp.zeros_like(dup)
        ddown[...] = jnp.zeros_like(ddown)
        small[...] = jnp.zeros_like(small)
        upb_sum[...] = jnp.zeros_like(upb_sum)

    def visit(sl, normed, gt, act, hid_grad):
        dup[:, sl] += dot(normed, hid_grad, TN)
        ddown[sl, :] += dot(act, gt, TN)
        upb_sum[:, sl] += jnp.sum(hid_grad.astype(f32), axis=0, keepdims=True)

    hat, gt, total, back, gain = mlp_tile(chunk, tok, g, up, upb, down, gains, biases, visit)
    part[...] = total
    share[...] = back * gain
    small[0:1, :] += jnp.sum(gt.astype(f32), axis=0, keepdims=True)
    small[1:2, :] += jnp.sum(back * hat, axis=0, keepdims=True)
    small[2:3, :] += jnp.sum(back, axis=0, keepdims=True)

    @pl.when(i == pl.num_programs(0) - 1)
    def _():
        d, wide = dup.shape
        for out, half in ((keep, meta[0]), (send, 1 - meta[0])):
            rows = pl.multiple_of(half * (d // 2), d // 2)
            for c in range(wide // d):
                out[c * (d // 2) : (c + 1) * (d // 2), :] = dup[pl.ds(rows, d // 2), c * d : (c + 1) * d]


def mlp_own(meta, tok, g, up, upb, down, gains, biases, tile=512, chunk=768, deps=()):
    length, d = tok.shape
    wide = up.shape[1]
    rows = pl.BlockSpec((tile, d), lambda i, *_: (i, 0))
    return call(
        functools.partial(mlp_own_kernel, chunk),
        grid=(length // tile,),
        scalars=1,
        in_specs=[rows, rows, whole((d, wide)), whole((1, wide)), whole((wide, d)), whole((2, d)), whole((2, d))],
        out_specs=[rows, rows, once((wide // 2, d)), once((wide // 2, d)), once((wide, d)), once((8, d)), once((1, wide))],
        out_shape=[
            jax.ShapeDtypeStruct((length, d), f32),
            jax.ShapeDtypeStruct((length, d), f32),
            jax.ShapeDtypeStruct((wide // 2, d), f32),
            jax.ShapeDtypeStruct((wide // 2, d), f32),
            jax.ShapeDtypeStruct((wide, d), f32),
            jax.ShapeDtypeStruct((8, d), f32),
            jax.ShapeDtypeStruct((1, wide), f32),
        ],
        scratch=[pltpu.VMEM((d, wide), f32)],
        flops=12 * length * d * wide,
        nbytes=4 * length * d * 4,
        deps=deps,
        name="mlp_own",
    )(meta, tok, g, up, upb, down, gains, biases)


def mlp_other_kernel(chunk, tok, g, up, upb, down, gains, biases, part_in, share_in, part, share):
    nothing = lambda *_: None
    _, _, total, back, gain = mlp_tile(chunk, tok, g, up, upb, down, gains, biases, nothing)
    part[...] = part_in[...] + total
    share[...] = share_in[...] + back * gain


def mlp_other(tok, g, up, upb, down, gains, biases, part, share, tile=512, chunk=768, deps=()):
    length, d = tok.shape
    wide = up.shape[1]
    rows = pl.BlockSpec((tile, d), lambda i: (i, 0))
    full = jax.ShapeDtypeStruct((length, d), f32)
    return call(
        functools.partial(mlp_other_kernel, chunk),
        grid=(length // tile,),
        in_specs=[rows, rows, whole((d, wide)), whole((1, wide)), whole((wide, d)), whole((2, d)), whole((2, d)), rows, rows],
        out_specs=[rows, rows],
        out_shape=[full, full],
        flops=8 * length * d * wide,
        nbytes=4 * length * d * 4,
        deps=deps,
        name="mlp_other",
    )(tok, g, up, upb, down, gains, biases, part, share)


def first_tokens(lens, places):
    first = jnp.zeros_like(places)
    end = lens[0, 0]
    for j in range(1, lens.shape[1]):
        first = jnp.where(places >= end, end, first)
        end = end + lens[0, j]
    return jnp.where(places >= end, places, first)


def turn(block, cosine, sine, sign):
    parts = []
    for h in range(block.shape[0] // HEAD):
        r = h * HEAD
        a = block[r : r + HALF, :]
        b = block[r + HALF : r + ROT, :]
        if sign > 0:
            parts += [a * cosine - b * sine, b * cosine + a * sine]
        else:
            parts += [a * cosine + b * sine, b * cosine - a * sine]
        parts.append(block[r + ROT : r + HEAD, :])
    return jnp.concatenate(parts, axis=0)


def proj_kernel(lens, tok, g, w, bias, ow, gains, biases, freq, qt, q, kt, k, vt, dot_t, do, cosine, sine):
    tile = tok.shape[0]
    i = pl.program_id(0)
    hat, _ = hat_of(tok[...].astype(f32))
    normed = (hat * gains[0:1, :] + biases[0:1, :]).astype(bf16)
    places = i * tile + lax.broadcasted_iota(jnp.int32, (1, tile), 1)
    position = (places - first_tokens(lens, places)).astype(f32)
    theta = freq[:, 0:1] * position
    c = jnp.cos(theta)
    s = jnp.sin(theta)
    cosine[...] = c
    sine[...] = s
    scale = HEAD ** (-0.5)
    query = turn(dot(w[0], normed, TT) + bias[:, 0:1], c, s, 1).astype(bf16) * scale
    qt[...] = query
    q[...] = query.T
    key = turn(dot(w[1], normed, TT), c, s, 1).astype(bf16)
    kt[...] = key
    k[...] = key.T
    vt[...] = (dot(w[2], normed, TT) + bias[:, 1:2]).astype(bf16)
    grad = dot(ow[...], g[...], NT).astype(bf16)
    dot_t[...] = grad
    do[...] = grad.T


def project(lens, tok, g, w, bias, ow, gains, biases, freq, tile=512, deps=()):
    length, d = tok.shape
    e = w.shape[2]
    rows = pl.BlockSpec((tile, d), lambda i, *_: (i, 0))
    tr = pl.BlockSpec((e, tile), lambda i, *_: (0, i))
    nat = pl.BlockSpec((tile, e), lambda i, *_: (i, 0))
    ang = pl.BlockSpec((HALF, tile), lambda i, *_: (0, i))
    t_shape = jax.ShapeDtypeStruct((e, length), bf16)
    n_shape = jax.ShapeDtypeStruct((length, e), bf16)
    a_shape = jax.ShapeDtypeStruct((HALF, length), f32)
    return call(
        proj_kernel,
        grid=(length // tile,),
        in_specs=[rows, rows, whole((3, d, e)), whole((e, 2)), whole((e, d)), whole((2, d)), whole((2, d)), whole((HALF, 128))],
        out_specs=[tr, nat, tr, nat, tr, tr, nat, ang, ang],
        scalars=1,
        out_shape=[t_shape, n_shape, t_shape, n_shape, t_shape, t_shape, n_shape, a_shape, a_shape],
        flops=8 * length * d * e,
        nbytes=20 * length * e,
        deps=deps,
        name="project",
    )(lens, tok, g, w, bias, ow, gains, biases, freq)


def tile_range(lens, start):
    first = jnp.int32(0)
    end = lens[0, 0]
    for j in range(1, lens.shape[1]):
        first = jnp.where(start >= end, end, first)
        end = end + lens[0, j]
    return jnp.where(start >= end, start, first)


def low_parts(x):
    high = x.astype(bf16)
    rest = x - high.astype(f32)
    mid = rest.astype(bf16)
    return [high, mid, (rest - mid.astype(f32)).astype(bf16)]


def tile_plan(lens, q0, tq, tk):
    low = lax.div(tile_range(lens, q0), tk)
    diagonal = lax.div(q0, tk)
    high = lax.div(q0 + tq + tk - 1, tk)
    inner = jnp.minimum(lax.div(tile_range(lens, q0 + tq - 1) + tk - 1, tk), diagonal)
    return low, jnp.maximum(inner, low), diagonal, high


def over_tiles(lens, q0, tq, tk, step, carry):
    low, inner, diagonal, high = tile_plan(lens, q0, tq, tk)
    edges = inner - low
    masked = lambda t, c: step(jnp.where(t < edges, low + t, diagonal + t - edges), c, True)
    carry = lax.fori_loop(0, edges + high - diagonal, masked, carry)
    return lax.fori_loop(inner, diagonal, lambda j, c: step(j, c, False), carry)


VROWS = 80


def attend_kernel(tk, lens, qt, k, vt, ot, qpad, vpad, acc):
    i = pl.program_id(0)
    tq = qt.shape[1]
    heads = qt.shape[0] // HEAD
    q0 = i * tq

    @pl.when(i == 0)
    def _():
        row = lax.broadcasted_iota(jnp.int32, (VROWS - HEAD, vt.shape[1]), 0)
        ones = jnp.where(row == 0, 1.0, 0.0).astype(bf16)
        for h in range(heads):
            vpad[h, :HEAD, :] = vt[h * HEAD : (h + 1) * HEAD, :]
            vpad[h, HEAD:, :] = ones

    places = q0 + lax.broadcasted_iota(jnp.int32, (1, tq), 1)
    first = first_tokens(lens, places)
    zero = jnp.zeros((HEAD, tq), bf16)
    for h in range(heads):
        qh = qt[h * HEAD : (h + 1) * HEAD, :]
        qpad[h] = jnp.concatenate([qh, zero] if h % 2 == 0 else [zero, qh], axis=0)
    acc[...] = jnp.zeros_like(acc)

    def step(j, peaks, masked):
        k0 = pl.multiple_of(j * tk, tk)
        if masked:
            rows = k0 + lax.broadcasted_iota(jnp.int32, (tk, tq), 0)
            allowed = (rows >= first) & (rows <= places)
        scores, new, raised = [], [], []
        for h in range(heads):
            pair = (h // 2) * 128
            s = dot(k[pl.ds(k0, tk), pair : pair + 128], qpad[h])
            scores.append(jnp.where(allowed, s, -1e30) if masked else s)
        for h in range(heads):
            new.append(jnp.maximum(peaks[h], jnp.max(scores[h], axis=0, keepdims=True)))
            raised.append(jnp.exp(scores[h] - new[h]).astype(bf16))
        for h in range(heads):
            o = dot(vpad[h, :, pl.ds(k0, tk)], raised[h])
            acc[h] = acc[h] * jnp.exp(peaks[h] - new[h]) + o
        return tuple(new)

    start = tuple(jnp.full((1, tq), -1e30, f32) for _ in range(heads))
    peaks = over_tiles(lens, q0, tq, tk, step, start)
    logs = []
    for h in range(heads):
        total = acc[h, HEAD : HEAD + 1, :]
        ot[h * HEAD : (h + 1) * HEAD, :] = acc[h, :HEAD, :] / total
        logs.append(peaks[h] + jnp.log(total))
    logs.append(jnp.zeros((8 - heads, tq), f32))
    ot[heads * HEAD :, :] = jnp.concatenate(logs, axis=0)


def attend(lens, qt, k, vt, tq=256, tk=256, deps=()):
    e, length = qt.shape
    heads = e // HEAD
    cols = pl.BlockSpec((e, tq), lambda i, *_: (0, i))
    return call(
        functools.partial(attend_kernel, tk),
        grid=(length // tq,),
        in_specs=[cols, whole((length, e)), whole((e, length))],
        out_specs=pl.BlockSpec((e + 8, tq), lambda i, *_: (0, i)),
        scratch=[
            pltpu.VMEM((heads, 128, tq), bf16),
            pltpu.VMEM((heads, VROWS, length), bf16),
            pltpu.VMEM((heads, VROWS, tq), f32),
        ],
        scalars=1,
        out_shape=jax.ShapeDtypeStruct((e + 8, length), f32),
        flops=2 * length * length * e,
        nbytes=8 * length * e,
        deps=deps,
        name="attend",
    )(lens, qt, k, vt)


def attend_back_kernel(tk, lens, q, qt, k, kt, vt, do, dot_t, ot, cosine, sine, grads_q, grads_k, grads_v, kpad, vpad, dk, dv, dq, qa, da, cs, cd):
    i = pl.program_id(0)
    tq = q.shape[0]
    length = k.shape[0]
    heads = q.shape[1] // HEAD
    q0 = i * tq

    @pl.when(i == 0)
    def _():
        dk[...] = jnp.zeros_like(dk)
        dv[...] = jnp.zeros_like(dv)
        zero = jnp.zeros((HEAD, length), bf16)
        row = lax.broadcasted_iota(jnp.int32, (128, tk), 0)
        for h in range(heads):
            sl = slice(h * HEAD, (h + 1) * HEAD)
            own, other = (0, HEAD) if h % 2 == 0 else (HEAD, 0)
            kpad[h, own : own + HEAD, :] = kt[sl, :]
            kpad[h, other : other + HEAD, :] = zero
            vpad[h, own : own + HEAD, :] = vt[sl, :]
            vpad[h, other : other + HEAD, :] = zero
            cs[h] = jnp.where((row < 24) & (row % 8 == h), -1.0, 0.0).astype(bf16)
            cd[h] = jnp.where((row >= 24) & (row < 48) & (row % 8 == h), -1.0, 0.0).astype(bf16)

    places = q0 + lax.broadcasted_iota(jnp.int32, (tq, 1), 0)
    first = first_tokens(lens, places)
    deltas = [
        jnp.sum(ot[h * HEAD : (h + 1) * HEAD, :] * dot_t[h * HEAD : (h + 1) * HEAD, :].astype(f32), axis=0, keepdims=True)
        for h in range(heads)
    ]
    deltas.append(jnp.zeros((8 - heads, tq), f32))
    stats = low_parts(ot[heads * HEAD :, :]) + low_parts(jnp.concatenate(deltas, axis=0))
    stats.append(jnp.zeros((128 - 48, tq), bf16))
    stat_cols = jnp.concatenate(stats, axis=0).T
    for r in range(heads // 2):
        pair = slice(r * 128, r * 128 + 128)
        qa[r, :, :128] = q[:, pair]
        qa[r, :, 128:] = stat_cols
        da[r, :, :128] = do[:, pair]
        da[r, :, 128:] = stat_cols
    dq[...] = jnp.zeros_like(dq)

    def step(j, carry, masked):
        k0 = pl.multiple_of(j * tk, tk)
        ks = pl.ds(k0, tk)
        if masked:
            cols = k0 + lax.broadcasted_iota(jnp.int32, (tq, tk), 1)
            allowed = (cols >= first) & (cols <= places)
        probs, grads = [], []
        for h in range(heads):
            s = dot(qa[h // 2], jnp.concatenate([kpad[h, :, ks], cs[h]], axis=0))
            dp = dot(da[h // 2], jnp.concatenate([vpad[h, :, ks], cd[h]], axis=0))
            p = jnp.exp(s)
            if masked:
                p = jnp.where(allowed, p, 0.0)
            probs.append(p.astype(bf16))
            grads.append((p * dp).astype(bf16))
        for h in range(heads):
            sl = slice(h * HEAD, (h + 1) * HEAD)
            pair = slice((h // 2) * 128, (h // 2) * 128 + 128)
            dv[sl, ks] += dot(dot_t[sl, :], probs[h])
            dk[sl, ks] += dot(qt[sl, :], grads[h])
            dq[h] += dot(grads[h], k[ks, pair])
        return carry

    over_tiles(lens, q0, tq, tk, step, 0)
    scale = HEAD ** (-0.5)
    lane = lax.broadcasted_iota(jnp.int32, (tq, 128), 1)
    q_parts = [
        jnp.where(lane < HEAD, dq[2 * h], dq[2 * h + 1]).T * scale for h in range(heads // 2)
    ]
    angle = pl.ds(pl.multiple_of(q0, tq), tq)
    grads_q[...] = turn(jnp.concatenate(q_parts, axis=0), cosine[:, angle], sine[:, angle], -1).astype(bf16)

    @pl.when(i == pl.num_programs(0) - 1)
    def _():
        grads_k[...] = turn(dk[...], cosine[...], sine[...], -1).astype(bf16)
        grads_v[...] = dv[...].astype(bf16)


def attend_back(lens, q, qt, k, kt, vt, do, dot_t, ot, cosine, sine, tq=256, tk=256, deps=()):
    e, length = qt.shape
    heads = e // HEAD
    cols = pl.BlockSpec((e, tq), lambda i, *_: (0, i))
    rows = pl.BlockSpec((tq, e), lambda i, *_: (i, 0))
    stat = pl.BlockSpec((e + 8, tq), lambda i, *_: (0, i))
    nat, tr, ang = whole((length, e)), whole((e, length)), whole((HALF, length))
    out = jax.ShapeDtypeStruct((e, length), bf16)
    return call(
        functools.partial(attend_back_kernel, tk),
        grid=(length // tq,),
        in_specs=[rows, cols, nat, tr, tr, rows, cols, stat, ang, ang],
        out_specs=[cols, once((e, length)), once((e, length))],
        scratch=[
            pltpu.VMEM((heads, 128, length), bf16),
            pltpu.VMEM((heads, 128, length), bf16),
            pltpu.VMEM((e, length), f32),
            pltpu.VMEM((e, length), f32),
            pltpu.VMEM((heads, tq, 128), f32),
            pltpu.VMEM((heads // 2, tq, 256), bf16),
            pltpu.VMEM((heads // 2, tq, 256), bf16),
            pltpu.VMEM((heads, 128, tk), bf16),
            pltpu.VMEM((heads, 128, tk), bf16),
        ],
        scalars=1,
        out_shape=[out, out, out],
        flops=5 * length * length * e,
        nbytes=20 * length * e,
        deps=deps,
        name="attend_back",
    )(lens, q, qt, k, kt, vt, do, dot_t, ot, cosine, sine)


def merge_tile(tok, gq, gk, gv, ot, w, ow, gains, biases):
    hat, inverse = hat_of(tok[...].astype(f32))
    gain = gains[0:1, :]
    back = dot(gq[...], w[0], TT) + dot(gk[...], w[1], TT) + dot(gv[...], w[2], TT)
    low = ot[...].astype(bf16)
    return hat, inverse, gain, back, low, dot(low, ow[...], TN)


def merge_own_kernel(tok, g, gq, gk, gv, ot, w, ow, gains, biases, part_in, share_in, small_in, upb_in, part, share, dw, dow):
    i = pl.program_id(0)
    tile = tok.shape[0]
    e, d = ow.shape
    wide = upb_in.shape[1]

    @pl.when(i == 0)
    def _():
        dw[...] = jnp.zeros_like(dw)
        dow[...] = jnp.zeros_like(dow)
        dow[e + 1 : e + 2, :] = small_in[1:2, :]
        dow[e + 3 : e + 4, :] = small_in[2:3, :]
        dow[e + 4 : e + 5, :] = small_in[0:1, :]
        for c in range(wide // d):
            dow[e + 5 + c : e + 6 + c, :] = upb_in[:, c * d : (c + 1) * d]

    hat, _, gain, back, low, out = merge_tile(tok, gq, gk, gv, ot, w, ow, gains, biases)
    normed = (hat * gain + biases[0:1, :]).astype(bf16)
    share[...] = share_in[...] + back * gain
    part[...] = part_in[...] + out
    dw[0] += dot(normed, gq[...], TT)
    dw[1] += dot(normed, gk[...], TT)
    dw[2] += dot(normed, gv[...], TT)
    dow[:e, :] += dot(low, g[...])
    dow[e : e + 1, :] += jnp.sum(back * hat, axis=0, keepdims=True)
    dow[e + 2 : e + 3, :] += jnp.sum(back, axis=0, keepdims=True)
    ones = jnp.ones((8, tile), bf16)
    at = e + 5 + wide // d
    dow[at : at + 1, :e] += dot(ones, gq[...], NT)[0:1]
    dow[at : at + 1, e : 2 * e] += dot(ones, gv[...], NT)[0:1]


def merge_own(tok, g, gq, gk, gv, ot, w, ow, gains, biases, part, share, small, upb, tile=512, deps=()):
    length, d = tok.shape
    e = w.shape[2]
    wide = upb.shape[1]
    rows = pl.BlockSpec((tile, d), lambda i: (i, 0))
    cols = pl.BlockSpec((e, tile), lambda i: (0, i))
    full = jax.ShapeDtypeStruct((length, d), f32)
    return call(
        merge_own_kernel,
        grid=(length // tile,),
        in_specs=[rows, rows, cols, cols, cols, cols, whole((3, d, e)), whole((e, d)), whole((2, d)), whole((2, d)), rows, rows, whole((8, d)), whole((1, wide))],
        out_specs=[rows, rows, once((3, d, e)), once((e + 8, d))],
        out_shape=[full, full, jax.ShapeDtypeStruct((3, d, e), f32), jax.ShapeDtypeStruct((e + 8, d), f32)],
        flops=16 * length * d * e,
        nbytes=24 * length * d,
        deps=deps,
        name="merge_own",
    )(tok, g, gq, gk, gv, ot, w, ow, gains, biases, part, share, small, upb)


def merge_other_kernel(tok, g, gq, gk, gv, ot, w, ow, gains, biases, out_bias, part_in, share_in, output, input_grad):
    hat, inverse, gain, back, _, out = merge_tile(tok, gq, gk, gv, ot, w, ow, gains, biases)
    shares = share_in[...] + back * gain
    inputs = tok[...].astype(f32)
    output[...] = (inputs + (part_in[...] + out) + out_bias[0:1, :] + out_bias[1:2, :]).astype(bf16)
    input_share = inverse * (
        shares
        - jnp.mean(shares, axis=-1, keepdims=True)
        - hat * jnp.mean(shares * hat, axis=-1, keepdims=True)
    )
    input_grad[...] = (g[...].astype(f32) + input_share).astype(bf16)


def merge_other(tok, g, gq, gk, gv, ot, w, ow, gains, biases, out_bias, part, share, tile=512, deps=()):
    length, d = tok.shape
    e = w.shape[2]
    rows = pl.BlockSpec((tile, d), lambda i: (i, 0))
    cols = pl.BlockSpec((e, tile), lambda i: (0, i))
    full = jax.ShapeDtypeStruct((length, d), bf16)
    return call(
        merge_other_kernel,
        grid=(length // tile,),
        in_specs=[rows, rows, cols, cols, cols, cols, whole((3, d, e)), whole((e, d)), whole((2, d)), whole((2, d)), whole((2, d)), rows, rows],
        out_specs=[rows, rows],
        out_shape=[full, full],
        flops=8 * length * d * e,
        nbytes=24 * length * d,
        deps=deps,
        name="merge_other",
    )(tok, g, gq, gk, gv, ot, w, ow, gains, biases, out_bias, part, share)


def pack_kernel(meta, w, ow, up, down, first, second):
    d = ow.shape[1]
    e = w.shape[2]
    for n, ref in enumerate((first, second)):
        at = 0
        r = down.shape[0] // 2
        ref[at : at + r, :] = down[n * r : (n + 1) * r, :].astype(f32)
        at += r
        r = up.shape[0] // 2
        for c in range(up.shape[1] // d):
            ref[at : at + r, :] = up[n * r : (n + 1) * r, c * d : (c + 1) * d].astype(f32)
            at += r
        r = w.shape[1] // 4
        for c in range(3):
            for s in range(2):
                ref[at : at + r, s * e : (s + 1) * e] = w[c, (2 * n + s) * r : (2 * n + s + 1) * r, :].astype(f32)
            at += r
        r = ow.shape[0] // 2
        ref[at : at + r, :] = ow[n * r : (n + 1) * r, :].astype(f32)


def pack(meta, w, ow, up, down, deps=()):
    _, d, e = w.shape
    wide = up.shape[1]
    rows = (wide + (wide // d) * d + 3 * d // 2 + e) // 8
    piece = jax.ShapeDtypeStruct((rows, d), f32)
    return call(
        pack_kernel,
        grid=(1,),
        in_specs=[
            pl.BlockSpec((3, d // 4, e), lambda i, m: (0, m[1], 0)),
            pl.BlockSpec((e // 4, d), lambda i, m: (m[1], 0)),
            pl.BlockSpec((d // 4, wide), lambda i, m: (m[1], 0)),
            pl.BlockSpec((wide // 4, d), lambda i, m: (m[1], 0)),
        ],
        out_specs=[once((rows, d)), once((rows, d))],
        scalars=1,
        out_shape=[piece, piece],
        deps=deps,
        name="pack",
    )(meta, w, ow, up, down)


def unpack_kernel(meta, *refs):
    pieces, (w, ow, up, down) = refs[:8], refs[8:]
    d = ow.shape[1]
    e = w.shape[2]
    for n, ref in enumerate(pieces):
        core = meta[0] ^ (n // 4)
        parity = meta[2] ^ ((n // 2) % 2)
        at_piece = (parity * 2 + core) * 2 + n % 2
        at = 0
        r = down.shape[0] // 8
        down[pl.ds(pl.multiple_of(at_piece * r, r), r), :] = ref[at : at + r, :].astype(bf16)
        at += r
        r = up.shape[0] // 8
        for c in range(up.shape[1] // d):
            up[pl.ds(pl.multiple_of(at_piece * r, r), r), c * d : (c + 1) * d] = ref[at : at + r, :].astype(bf16)
            at += r
        r = w.shape[1] // 16
        for c in range(3):
            for s in range(2):
                w[c, pl.ds(pl.multiple_of((at_piece * 2 + s) * r, r), r), :] = ref[at : at + r, s * e : (s + 1) * e].astype(bf16)
            at += r
        r = ow.shape[0] // 8
        ow[pl.ds(pl.multiple_of(at_piece * r, r), r), :] = ref[at : at + r, :].astype(bf16)


def unpack(meta, pieces, w, ow, up, down, deps=()):
    shapes = [jax.ShapeDtypeStruct(x.shape, bf16) for x in (w, ow, up, down)]
    return call(
        unpack_kernel,
        grid=(1,),
        in_specs=[once(p.shape) for p in pieces],
        out_specs=[once(s.shape) for s in shapes],
        scalars=1,
        out_shape=shapes,
        deps=deps,
        name="unpack",
    )(meta, *pieces)


def swap(x, bit):
    n = lax.axis_size("dp")
    return lax.ppermute(x, "dp", [(i, i ^ (1 << bit)) for i in range(n)])


def across(x):
    return lax.ppermute(x, "tensor", [(0, 1), (1, 0)])


def tie(arrays, deps):
    n = len(arrays)
    anywhere = [pl.BlockSpec(memory_space=pl.ANY)] * n
    return call(
        lambda *refs: None,
        grid=(1,),
        in_specs=anywhere,
        out_specs=anywhere,
        out_shape=[jax.ShapeDtypeStruct(x.shape, x.dtype) for x in arrays],
        aliases={i: i for i in range(n)},
        deps=deps,
        name="tie",
    )(*arrays)


BITS_AT = 4


def exchange(meta, ops, deps=()):
    small = min(op[1].shape[0] // (2 if op[0] == "halve" else 1) for op in ops if op[0] != "norm" and op[1].shape[0] > 8)
    grid = next(g for g in (4, 2, 1) if small % (8 * g) == 0)
    args, in_specs, out_specs, out_shape, plan = [], [], [], [], []
    for op in ops:
        kind, mine, got = op[:3]
        rows, d = mine.shape
        if kind == "halve":
            r = rows // 2
            spec = lambda keep, r=r, bit=op[3]: pl.BlockSpec(
                (1, r // grid, d), lambda i, m: ((m[BITS_AT + bit] if keep else 1 - m[BITS_AT + bit]), i, 0)
            )
            a, b = mine.reshape(2, r, d), got.reshape(2, r, d)
            args += [a, b, a, b]
            in_specs += [spec(False), spec(False), spec(True), spec(True)]
            out_specs += [pl.BlockSpec((r // grid, d), lambda i, m: (i, 0))] * 2
            out_shape += [jax.ShapeDtypeStruct((r, d), f32)] * 2
            plan.append((kind, 4, 2, None))
        elif kind == "join":
            block = pl.BlockSpec((rows // grid, d), lambda i, m: (i, 0))
            args += [mine, got]
            in_specs += [block, block]
            out_specs.append(pl.BlockSpec((2, rows // grid, d), lambda i, m: (0, i, 0)))
            out_shape.append(jax.ShapeDtypeStruct((2, rows, d), f32))
            plan.append((kind, 2, 1, op[3]))
        else:
            r = rows // grid if rows > 8 else rows
            block = pl.BlockSpec((r, d), (lambda i, m: (i, 0)) if rows > 8 else (lambda i, m: (0, 0)))
            args += [mine, got]
            in_specs += [block, block]
            out_specs.append(block)
            out_shape.append(jax.ShapeDtypeStruct((rows, d), f32))
            plan.append((kind, 2, 1, None))

    def kernel(m, *refs):
        ins, outs = refs[: len(args)], refs[len(args) :]
        at, to = 0, 0
        for kind, n_in, n_out, bit in plan:
            x, y = ins[at : at + n_in], outs[to : to + n_out]
            if kind == "halve":
                y[0][...] = x[0][0] + x[1][0]
                y[1][...] = x[2][0] + x[3][0]
            elif kind == "join":
                v = m[BITS_AT + bit]
                y[0][v] = x[0][...]
                y[0][1 - v] = x[1][...]
            elif kind == "norm":
                row = lax.broadcasted_iota(jnp.int32, x[0].shape, 0)
                y[0][...] = x[0][...] + jnp.where(row < 4, x[1][...], 0.0)
            else:
                y[0][...] = x[0][...] + x[1][...]
            at += n_in
            to += n_out

    outs = call(
        kernel, grid=(grid,), scalars=1, in_specs=in_specs, out_specs=out_specs, out_shape=out_shape, deps=deps, name="exchange"
    )(meta, *args)
    return [x.reshape(-1, x.shape[-1]) if x.ndim == 3 else x for x in outs]


def assemble_up(meta, up, got, deps=()):
    d = up.shape[1]
    lanes = 2
    r = up.shape[0] // lanes
    grid = 4

    def kernel(m, a, b, out):
        for x, half in ((a, m[0]), (b, 1 - m[0])):
            for s in range(lanes):
                out[half, :, s * d : (s + 1) * d] = x[s]

    pair = pl.BlockSpec((lanes, r // grid, d), lambda i, m: (0, i, 0))
    return call(
        kernel,
        grid=(grid,),
        scalars=1,
        in_specs=[pair, pair],
        out_specs=pl.BlockSpec((2, r // grid, lanes * d), lambda i, m: (0, i, 0)),
        out_shape=jax.ShapeDtypeStruct((2, r, lanes * d), f32),
        deps=deps,
        name="assemble_up",
    )(meta, up.reshape(lanes, r, d), got.reshape(lanes, r, d)).reshape(2 * r, lanes * d)


class Sum:
    def __init__(self, keep, send, order):
        self.mine, self.got = keep, swap(send, 0)
        self.todo = [("halve", b) for b in order] + [("add", None)] + [("join", b) for b in reversed(order)]
        self.order = order

    @property
    def done(self):
        return not self.todo

    def op(self):
        kind, bit = self.todo[0]
        return (kind, self.mine, self.got) + (() if bit is None else (bit,))

    def take(self, outs):
        kind, _ = self.todo.pop(0)
        if kind == "halve":
            send, self.mine = outs.pop(0), outs.pop(0)
        else:
            send = self.mine = outs.pop(0)
        if not self.todo:
            self.got = swap(send, 0)
            return [send]
        following, bit = self.todo[0]
        if kind == "halve":
            bit = self.order[len(self.order) - 1 - sum(1 for k, _ in self.todo if k == "halve")]
        self.got = swap(send, bit)
        return [send, self.mine]


def advance(meta, sums, deps):
    sums = [s for s in sums if not s.done]
    if not sums:
        return []
    outs = exchange(meta, [s.op() for s in sums], deps)
    return [x for s in sums for x in s.take(outs)]


def per_device(
    tokens, lengths, qkv_weight, qkv_bias, out_weight, out_bias, up_weight, up_bias, down_weight, down_bias, norm_gains, norm_biases, cotangent
):
    length, d = tokens.shape
    e = qkv_weight.shape[2]
    wide = up_weight.shape[1]
    bits = lax.axis_size("dp").bit_length() - 1
    me = lax.axis_index("dp")
    core = me & 1
    parity = ((me >> 1) ^ (me >> 2)) & 1
    meta = jnp.stack([core, parity * 2 + core, parity, parity] + [(me >> b) & 1 for b in range(12)])
    freq = jnp.broadcast_to(
        (rot_base ** (-(2.0 * jnp.arange(HALF, dtype=f32)) / ROT))[:, None], (HALF, 128)
    )
    first, second = pack(meta, qkv_weight, out_weight, up_weight, down_weight)
    own_biases = jnp.concatenate([up_bias.astype(f32), qkv_bias.astype(f32).reshape(-1)]).reshape(-1, d)
    other_biases = across(own_biases)

    def half_biases(rows):
        flat = rows.reshape(-1)
        return flat[None, :wide], flat[wide:].reshape(2, e).T

    own_upb, own_qkvb = half_biases(own_biases)
    other_upb, other_qkvb = half_biases(other_biases)
    got_first = across(first)
    part, share, keep_u, send_u, d_down, small, d_upb = mlp_own(
        meta, tokens, cotangent, up_weight, own_upb, down_weight, norm_gains, norm_biases, deps=[first]
    )
    d_down = lax.psum(d_down, "dp")
    order = list(range(1, bits))
    sum_u = Sum(keep_u, send_u, order)
    got_first, second = tie([got_first, second], [part])
    got_second = across(second)
    near_first = swap(got_first, 1)
    qt, q, kt, k, vt, dot_t, do, cosine, sine = project(
        lengths, tokens, cotangent, qkv_weight, own_qkvb, out_weight, norm_gains, norm_biases, freq, deps=[got_first, send_u]
    )
    wait = advance(meta, [sum_u], [qt])
    ot = attend(lengths, qt, k, vt, deps=wait)
    (got_second,) = tie([got_second], [ot])
    near_second = swap(got_second, 2)
    other_ot = across(ot)
    gq, gk, gv = attend_back(lengths, q, qt, k, kt, vt, do, dot_t, ot, cosine, sine, deps=[got_second])
    quarter = list(tie([got_first, got_second, near_first], [gq]))
    pieces = [swap(x, 0) for x in quarter]
    wait = advance(meta, [sum_u], [gq])
    part, share, d_qkv, d_out = merge_own(
        tokens, cotangent, gq, gk, gv, ot, qkv_weight, out_weight, norm_gains, norm_biases, part, share, small, d_upb, deps=quarter + wait
    )
    d_qkv, d_out = tie([d_qkv, d_out], [d_down])
    turned = [list(range(lax.axis_size("dp")))[::-1]]
    d_qkv, d_out = lax.psum((d_qkv, d_out), "dp", axis_index_groups=turned)
    near_second, other_ot = tie([near_second, other_ot], [part])
    quarter.append(near_second)
    pieces.append(swap(near_second, 0))
    wait = advance(meta, [sum_u], [part])
    other_w, other_ow, other_up, other_down = unpack(
        meta, quarter + pieces, qkv_weight, out_weight, up_weight, down_weight, deps=wait + [other_ot]
    )
    wait = advance(meta, [sum_u], [other_w])
    qt, q, kt, k, vt, dot_t, do, cosine, sine = project(
        lengths, tokens, cotangent, other_w, other_qkvb, other_ow, norm_gains, norm_biases, freq, deps=wait
    )
    wait = advance(meta, [sum_u], [qt])
    gq, gk, gv = attend_back(lengths, q, qt, k, kt, vt, do, dot_t, other_ot, cosine, sine, deps=wait)
    wait = advance(meta, [sum_u], [gq])
    part, share = mlp_other(tokens, cotangent, other_up, other_upb, other_down, norm_gains, norm_biases, part, share, deps=wait)
    wait = advance(meta, [sum_u], [part])
    out_biases = jnp.stack([out_bias, down_bias]).astype(f32)
    output, input_grad = merge_other(
        tokens, cotangent, gq, gk, gv, other_ot, other_w, other_ow, norm_gains, norm_biases, out_biases, part, share, deps=wait
    )
    wait = [output]
    while not sum_u.done:
        wait = advance(meta, [sum_u], wait)
    d_qkv, d_out = tie([d_qkv, d_out], [output])
    d_up = assemble_up(meta, sum_u.mine, sum_u.got)
    smalls = d_out[e:]
    norm_sums = smalls[:4] + across(smalls[:4])
    rest = smalls[5:].reshape(-1)
    return (
        output, input_grad, d_qkv, rest[wide:].reshape(2, e), d_out[:e], smalls[4], d_up, rest[:wide], d_down, smalls[4], norm_sums[:2], norm_sums[2:],
    )


def solution(mesh):
    in_specs = (
        P("dp", None), P("dp", None), P(None, None, "tensor"), P(None, "tensor"), P("tensor", None), P(), P(None, "tensor"),
        P("tensor"), P("tensor", None), P(), P(), P(), P("dp", None),
    )
    out_specs = (
        P("dp", None), P("dp", None), P(None, None, "tensor"), P(None, "tensor"), P("tensor", None), P(), P(None, "tensor"),
        P("tensor"), P("tensor", None), P(), P(), P(),
    )
    return jax.shard_map(per_device, mesh=mesh, in_specs=in_specs, out_specs=out_specs, check_vma=False)
```

```python
import functools
import math

import jax
import jax.numpy as jnp
import numpy as np
from jax import lax
from jax.experimental import pallas as pl
from jax.experimental.pallas import tpu as pltpu
from jax.sharding import PartitionSpec as P

HEAD = 64
ROT = 16
HALF = ROT // 2
epsilon = 1e-05
rot_base = 10000.0
f32 = jnp.float32
bf16 = jnp.bfloat16
NN = (((1,), (0,)), ((), ()))
NT = (((1,), (1,)), ((), ()))
TN = (((0,), (0,)), ((), ()))
TT = (((0,), (1,)), ((), ()))
VMEM_LIMIT = 60 * 2**20


def dot(a, b, dims=NN):
    return lax.dot_general(a, b, dims, preferred_element_type=f32)


MESH = pl.DeviceIdType.MESH


class Move:
    def __init__(self, x, axis, flip):
        self.x, self.axis, self.flip = x, axis, flip

    @property
    def shape(self):
        return jax.ShapeDtypeStruct(self.x.shape, self.x.dtype)

    def partner(self):
        return {self.axis: lax.axis_index(self.axis) ^ self.flip}


def call(
    kernel, *, grid, in_specs, out_specs, out_shape, scalars=0, scratch=(), deps=(), moves=(), collective=None, flops=0, nbytes=0, name=None, aliases=None
):
    n_move = len(moves)
    first, last = scalars + len(in_specs), scalars + len(in_specs) + len(deps)
    single = not isinstance(out_shape, (list, tuple))
    out_specs = [out_specs] if single else list(out_specs)
    out_shape = [out_shape] if single else list(out_shape)
    n_out = len(out_shape)
    anywhere = pl.BlockSpec(memory_space=pl.ANY)

    def body(*refs):
        ins, sources = refs[:first], refs[last : last + n_move]
        rest = refs[last + n_move :]
        outs, targets, held = rest[:n_out], rest[n_out : n_out + n_move], rest[n_out + n_move :]
        if n_move:
            sent, came = held[-2:]
            held = held[:-2]
            copies = [
                pltpu.make_async_remote_copy(
                    src_ref=sources[j], dst_ref=targets[j], send_sem=sent.at[j], recv_sem=came.at[j], device_id=m.partner(), device_id_type=MESH
                )
                for j, m in enumerate(moves)
            ]

            @pl.when(pl.program_id(0) == 0)
            def _():
                barrier = pltpu.get_barrier_semaphore()
                seen = {(m.axis, m.flip): m for m in moves}
                for m in seen.values():
                    pl.semaphore_signal(barrier, inc=1, device_id=m.partner(), device_id_type=MESH)
                pl.semaphore_wait(barrier, len(seen))
                for c in copies:
                    c.start()

        kernel(*ins, *outs, *held)
        if n_move:

            @pl.when(pl.program_id(0) == pl.num_programs(0) - 1)
            def _():
                for c in copies:
                    c.wait()

    params = dict(vmem_limit_bytes=VMEM_LIMIT)
    scratch = list(scratch)
    if n_move:
        params.update(collective_id=collective, has_side_effects=True)
        scratch += [pltpu.SemaphoreType.DMA((n_move,)), pltpu.SemaphoreType.DMA((n_move,))]

    def run(*args):
        outs = pl.pallas_call(
            body,
            grid_spec=pltpu.PrefetchScalarGridSpec(
                num_scalar_prefetch=scalars,
                grid=grid,
                in_specs=list(in_specs) + [anywhere] * (len(deps) + n_move),
                out_specs=out_specs + [anywhere] * n_move,
                scratch_shapes=scratch,
            ),
            out_shape=out_shape + [m.shape for m in moves],
            compiler_params=pltpu.CompilerParams(**params),
            cost_estimate=pl.CostEstimate(flops=20 * flops, bytes_accessed=nbytes, transcendentals=0),
            input_output_aliases=aliases or {},
            name=name,
        )(*args, *deps, *[m.x for m in moves])
        outs = list(outs)
        own = outs[0] if single else outs[:n_out]
        return (own, outs[n_out:]) if n_move else own

    return run


def whole(shape):
    zeros = (0,) * len(shape)
    return pl.BlockSpec(shape, lambda *_: zeros, pipeline_mode=pl.Buffered(1))


def once(shape):
    zeros = (0,) * len(shape)
    return pl.BlockSpec(shape, lambda *_: zeros)


def hat_of(values):
    average = jnp.mean(values, axis=-1, keepdims=True)
    centered = values - average
    inverse = lax.rsqrt(jnp.mean(centered * centered, axis=-1, keepdims=True) + epsilon)
    return centered * inverse, inverse


def gelu_pair(h):
    a = jnp.abs(h) * np.float32(math.sqrt(0.5))
    t = 1.0 / (1.0 + np.float32(0.3275911) * a)
    bell = jnp.exp(-0.5 * (h * h))
    poly = np.float32(0.5 * 1.061405429) * t + np.float32(0.5 * -1.453152027)
    poly = poly * t + np.float32(0.5 * 1.421413741)
    poly = poly * t + np.float32(0.5 * -0.284496736)
    poly = poly * t + np.float32(0.5 * 0.254829592)
    tail = poly * t * bell
    phi = jnp.where(h >= 0, 1.0 - tail, tail)
    return h * phi, phi + h * bell * np.float32(1.0 / math.sqrt(2.0 * math.pi))


def add_to(ref, first, value):
    @pl.when(first)
    def _():
        ref[...] = value

    @pl.when(jnp.logical_not(first))
    def _():
        ref[...] += value


def mlp_tile(chunk, tok, g, up, upb, down, gains, biases, visit):
    hat, _ = hat_of(tok[...].astype(f32))
    gain = gains[1:2, :]
    normed = (hat * gain + biases[1:2, :]).astype(bf16)
    gt = g[...]
    total = None
    back = None
    for c in range(up.shape[1] // chunk):
        sl = slice(c * chunk, (c + 1) * chunk)
        hidden = dot(normed, up[:, sl]) + upb[:, sl]
        act_grad = dot(gt, down[sl, :], NT)
        act, slope = gelu_pair(hidden)
        act = act.astype(bf16)
        hid_grad = (act_grad * slope).astype(bf16)
        p = dot(act, down[sl, :])
        e = dot(hid_grad, up[:, sl], NT)
        total = p if total is None else total + p
        back = e if back is None else back + e
        visit(sl, normed, gt, act, hid_grad)
    return hat, gt, total, back, gain


def mlp_own_kernel(chunk, meta, tok, g, up, upb, down, gains, biases, part, share, keep, send, ddown, small, upb_sum, dup):
    i = pl.program_id(0)

    @pl.when(i == 0)
    def _():
        dup[...] = jnp.zeros_like(dup)
        ddown[...] = jnp.zeros_like(ddown)
        small[...] = jnp.zeros_like(small)
        upb_sum[...] = jnp.zeros_like(upb_sum)

    def visit(sl, normed, gt, act, hid_grad):
        dup[:, sl] += dot(normed, hid_grad, TN)
        ddown[sl, :] += dot(act, gt, TN)
        upb_sum[:, sl] += jnp.sum(hid_grad.astype(f32), axis=0, keepdims=True)

    hat, gt, total, back, gain = mlp_tile(chunk, tok, g, up, upb, down, gains, biases, visit)
    part[...] = total
    share[...] = back * gain
    small[0:1, :] += jnp.sum(gt.astype(f32), axis=0, keepdims=True)
    small[1:2, :] += jnp.sum(back * hat, axis=0, keepdims=True)
    small[2:3, :] += jnp.sum(back, axis=0, keepdims=True)

    @pl.when(i == pl.num_programs(0) - 1)
    def _():
        d, wide = dup.shape
        for out, half in ((keep, meta[0]), (send, 1 - meta[0])):
            rows = pl.multiple_of(half * (d // 2), d // 2)
            for c in range(wide // d):
                out[c * (d // 2) : (c + 1) * (d // 2), :] = dup[pl.ds(rows, d // 2), c * d : (c + 1) * d]


def mlp_own(meta, tok, g, up, upb, down, gains, biases, tile=512, chunk=768, deps=()):
    length, d = tok.shape
    wide = up.shape[1]
    rows = pl.BlockSpec((tile, d), lambda i, *_: (i, 0))
    return call(
        functools.partial(mlp_own_kernel, chunk),
        grid=(length // tile,),
        scalars=1,
        in_specs=[rows, rows, whole((d, wide)), whole((1, wide)), whole((wide, d)), whole((2, d)), whole((2, d))],
        out_specs=[rows, rows, once((wide // 2, d)), once((wide // 2, d)), once((wide, d)), once((8, d)), once((1, wide))],
        out_shape=[
            jax.ShapeDtypeStruct((length, d), f32),
            jax.ShapeDtypeStruct((length, d), f32),
            jax.ShapeDtypeStruct((wide // 2, d), f32),
            jax.ShapeDtypeStruct((wide // 2, d), f32),
            jax.ShapeDtypeStruct((wide, d), f32),
            jax.ShapeDtypeStruct((8, d), f32),
            jax.ShapeDtypeStruct((1, wide), f32),
        ],
        scratch=[pltpu.VMEM((d, wide), f32)],
        flops=12 * length * d * wide,
        nbytes=4 * length * d * 4,
        deps=deps,
        name="mlp_own",
    )(meta, tok, g, up, upb, down, gains, biases)


def mlp_other_kernel(chunk, tok, g, up, upb, down, gains, biases, part_in, share_in, part, share):
    nothing = lambda *_: None
    _, _, total, back, gain = mlp_tile(chunk, tok, g, up, upb, down, gains, biases, nothing)
    part[...] = part_in[...] + total
    share[...] = share_in[...] + back * gain


def mlp_other(tok, g, up, upb, down, gains, biases, part, share, tile=512, chunk=768, deps=()):
    length, d = tok.shape
    wide = up.shape[1]
    rows = pl.BlockSpec((tile, d), lambda i: (i, 0))
    full = jax.ShapeDtypeStruct((length, d), f32)
    return call(
        functools.partial(mlp_other_kernel, chunk),
        grid=(length // tile,),
        in_specs=[rows, rows, whole((d, wide)), whole((1, wide)), whole((wide, d)), whole((2, d)), whole((2, d)), rows, rows],
        out_specs=[rows, rows],
        out_shape=[full, full],
        flops=8 * length * d * wide,
        nbytes=4 * length * d * 4,
        deps=deps,
        name="mlp_other",
    )(tok, g, up, upb, down, gains, biases, part, share)


def first_tokens(lens, places):
    first = jnp.zeros_like(places)
    end = lens[0, 0]
    for j in range(1, lens.shape[1]):
        first = jnp.where(places >= end, end, first)
        end = end + lens[0, j]
    return jnp.where(places >= end, places, first)


def turn(block, cosine, sine, sign):
    parts = []
    for h in range(block.shape[0] // HEAD):
        r = h * HEAD
        a = block[r : r + HALF, :]
        b = block[r + HALF : r + ROT, :]
        if sign > 0:
            parts += [a * cosine - b * sine, b * cosine + a * sine]
        else:
            parts += [a * cosine + b * sine, b * cosine - a * sine]
        parts.append(block[r + ROT : r + HEAD, :])
    return jnp.concatenate(parts, axis=0)


def proj_kernel(lens, tok, g, w, bias, ow, gains, biases, freq, qt, q, kt, k, vt, dot_t, do, cosine, sine):
    tile = tok.shape[0]
    i = pl.program_id(0)
    hat, _ = hat_of(tok[...].astype(f32))
    normed = (hat * gains[0:1, :] + biases[0:1, :]).astype(bf16)
    places = i * tile + lax.broadcasted_iota(jnp.int32, (1, tile), 1)
    position = (places - first_tokens(lens, places)).astype(f32)
    theta = freq[:, 0:1] * position
    c = jnp.cos(theta)
    s = jnp.sin(theta)
    cosine[...] = c
    sine[...] = s
    scale = HEAD ** (-0.5)
    query = turn(dot(w[0], normed, TT) + bias[:, 0:1], c, s, 1).astype(bf16) * scale
    qt[...] = query
    q[...] = query.T
    key = turn(dot(w[1], normed, TT), c, s, 1).astype(bf16)
    kt[...] = key
    k[...] = key.T
    vt[...] = (dot(w[2], normed, TT) + bias[:, 1:2]).astype(bf16)
    grad = dot(ow[...], g[...], NT).astype(bf16)
    dot_t[...] = grad
    do[...] = grad.T


def project(lens, tok, g, w, bias, ow, gains, biases, freq, tile=512, deps=()):
    length, d = tok.shape
    e = w.shape[2]
    rows = pl.BlockSpec((tile, d), lambda i, *_: (i, 0))
    tr = pl.BlockSpec((e, tile), lambda i, *_: (0, i))
    nat = pl.BlockSpec((tile, e), lambda i, *_: (i, 0))
    ang = pl.BlockSpec((HALF, tile), lambda i, *_: (0, i))
    t_shape = jax.ShapeDtypeStruct((e, length), bf16)
    n_shape = jax.ShapeDtypeStruct((length, e), bf16)
    a_shape = jax.ShapeDtypeStruct((HALF, length), f32)
    return call(
        proj_kernel,
        grid=(length // tile,),
        in_specs=[rows, rows, whole((3, d, e)), whole((e, 2)), whole((e, d)), whole((2, d)), whole((2, d)), whole((HALF, 128))],
        out_specs=[tr, nat, tr, nat, tr, tr, nat, ang, ang],
        scalars=1,
        out_shape=[t_shape, n_shape, t_shape, n_shape, t_shape, t_shape, n_shape, a_shape, a_shape],
        flops=8 * length * d * e,
        nbytes=20 * length * e,
        deps=deps,
        name="project",
    )(lens, tok, g, w, bias, ow, gains, biases, freq)


def tile_range(lens, start):
    first = jnp.int32(0)
    end = lens[0, 0]
    for j in range(1, lens.shape[1]):
        first = jnp.where(start >= end, end, first)
        end = end + lens[0, j]
    return jnp.where(start >= end, start, first)


def low_parts(x):
    high = x.astype(bf16)
    rest = x - high.astype(f32)
    mid = rest.astype(bf16)
    return [high, mid, (rest - mid.astype(f32)).astype(bf16)]


def tile_plan(lens, q0, tq, tk):
    low = lax.div(tile_range(lens, q0), tk)
    diagonal = lax.div(q0, tk)
    high = lax.div(q0 + tq + tk - 1, tk)
    inner = jnp.minimum(lax.div(tile_range(lens, q0 + tq - 1) + tk - 1, tk), diagonal)
    return low, jnp.maximum(inner, low), diagonal, high


def over_tiles(lens, q0, tq, tk, step, carry):
    low, inner, diagonal, high = tile_plan(lens, q0, tq, tk)
    edges = inner - low
    masked = lambda t, c: step(jnp.where(t < edges, low + t, diagonal + t - edges), c, True)
    carry = lax.fori_loop(0, edges + high - diagonal, masked, carry)
    return lax.fori_loop(inner, diagonal, lambda j, c: step(j, c, False), carry)


VROWS = 80


def attend_kernel(tk, lens, qt, k, vt, ot, qpad, vpad, acc):
    i = pl.program_id(0)
    tq = qt.shape[1]
    heads = qt.shape[0] // HEAD
    q0 = i * tq

    @pl.when(i == 0)
    def _():
        row = lax.broadcasted_iota(jnp.int32, (VROWS - HEAD, vt.shape[1]), 0)
        ones = jnp.where(row == 0, 1.0, 0.0).astype(bf16)
        for h in range(heads):
            vpad[h, :HEAD, :] = vt[h * HEAD : (h + 1) * HEAD, :]
            vpad[h, HEAD:, :] = ones

    places = q0 + lax.broadcasted_iota(jnp.int32, (1, tq), 1)
    first = first_tokens(lens, places)
    zero = jnp.zeros((HEAD, tq), bf16)
    for h in range(heads):
        qh = qt[h * HEAD : (h + 1) * HEAD, :]
        qpad[h] = jnp.concatenate([qh, zero] if h % 2 == 0 else [zero, qh], axis=0)
    acc[...] = jnp.zeros_like(acc)

    def step(j, peaks, masked):
        k0 = pl.multiple_of(j * tk, tk)
        if masked:
            rows = k0 + lax.broadcasted_iota(jnp.int32, (tk, tq), 0)
            allowed = (rows >= first) & (rows <= places)
        scores, new, raised = [], [], []
        for h in range(heads):
            pair = (h // 2) * 128
            s = dot(k[pl.ds(k0, tk), pair : pair + 128], qpad[h])
            scores.append(jnp.where(allowed, s, -1e30) if masked else s)
        for h in range(heads):
            new.append(jnp.maximum(peaks[h], jnp.max(scores[h], axis=0, keepdims=True)))
            raised.append(jnp.exp(scores[h] - new[h]).astype(bf16))
        for h in range(heads):
            o = dot(vpad[h, :, pl.ds(k0, tk)], raised[h])
            acc[h] = acc[h] * jnp.exp(peaks[h] - new[h]) + o
        return tuple(new)

    start = tuple(jnp.full((1, tq), -1e30, f32) for _ in range(heads))
    peaks = over_tiles(lens, q0, tq, tk, step, start)
    logs = []
    for h in range(heads):
        total = acc[h, HEAD : HEAD + 1, :]
        ot[h * HEAD : (h + 1) * HEAD, :] = acc[h, :HEAD, :] / total
        logs.append(peaks[h] + jnp.log(total))
    logs.append(jnp.zeros((8 - heads, tq), f32))
    ot[heads * HEAD :, :] = jnp.concatenate(logs, axis=0)


def attend(lens, qt, k, vt, tq=256, tk=256, deps=()):
    e, length = qt.shape
    heads = e // HEAD
    cols = pl.BlockSpec((e, tq), lambda i, *_: (0, i))
    return call(
        functools.partial(attend_kernel, tk),
        grid=(length // tq,),
        in_specs=[cols, whole((length, e)), whole((e, length))],
        out_specs=pl.BlockSpec((e + 8, tq), lambda i, *_: (0, i)),
        scratch=[
            pltpu.VMEM((heads, 128, tq), bf16),
            pltpu.VMEM((heads, VROWS, length), bf16),
            pltpu.VMEM((heads, VROWS, tq), f32),
        ],
        scalars=1,
        out_shape=jax.ShapeDtypeStruct((e + 8, length), f32),
        flops=2 * length * length * e,
        nbytes=8 * length * e,
        deps=deps,
        name="attend",
    )(lens, qt, k, vt)


def attend_back_kernel(tk, lens, q, qt, k, kt, vt, do, dot_t, ot, cosine, sine, grads_q, grads_k, grads_v, kpad, vpad, dk, dv, dq, qa, da, cs, cd):
    i = pl.program_id(0)
    tq = q.shape[0]
    length = k.shape[0]
    heads = q.shape[1] // HEAD
    q0 = i * tq

    @pl.when(i == 0)
    def _():
        dk[...] = jnp.zeros_like(dk)
        dv[...] = jnp.zeros_like(dv)
        zero = jnp.zeros((HEAD, length), bf16)
        row = lax.broadcasted_iota(jnp.int32, (128, tk), 0)
        for h in range(heads):
            sl = slice(h * HEAD, (h + 1) * HEAD)
            own, other = (0, HEAD) if h % 2 == 0 else (HEAD, 0)
            kpad[h, own : own + HEAD, :] = kt[sl, :]
            kpad[h, other : other + HEAD, :] = zero
            vpad[h, own : own + HEAD, :] = vt[sl, :]
            vpad[h, other : other + HEAD, :] = zero
            cs[h] = jnp.where((row < 24) & (row % 8 == h), -1.0, 0.0).astype(bf16)
            cd[h] = jnp.where((row >= 24) & (row < 48) & (row % 8 == h), -1.0, 0.0).astype(bf16)

    places = q0 + lax.broadcasted_iota(jnp.int32, (tq, 1), 0)
    first = first_tokens(lens, places)
    deltas = [
        jnp.sum(ot[h * HEAD : (h + 1) * HEAD, :] * dot_t[h * HEAD : (h + 1) * HEAD, :].astype(f32), axis=0, keepdims=True)
        for h in range(heads)
    ]
    deltas.append(jnp.zeros((8 - heads, tq), f32))
    stats = low_parts(ot[heads * HEAD :, :]) + low_parts(jnp.concatenate(deltas, axis=0))
    stats.append(jnp.zeros((128 - 48, tq), bf16))
    stat_cols = jnp.concatenate(stats, axis=0).T
    for r in range(heads // 2):
        pair = slice(r * 128, r * 128 + 128)
        qa[r, :, :128] = q[:, pair]
        qa[r, :, 128:] = stat_cols
        da[r, :, :128] = do[:, pair]
        da[r, :, 128:] = stat_cols
    dq[...] = jnp.zeros_like(dq)

    def step(j, carry, masked):
        k0 = pl.multiple_of(j * tk, tk)
        ks = pl.ds(k0, tk)
        if masked:
            cols = k0 + lax.broadcasted_iota(jnp.int32, (tq, tk), 1)
            allowed = (cols >= first) & (cols <= places)
        probs, grads = [], []
        for h in range(heads):
            s = dot(qa[h // 2], jnp.concatenate([kpad[h, :, ks], cs[h]], axis=0))
            dp = dot(da[h // 2], jnp.concatenate([vpad[h, :, ks], cd[h]], axis=0))
            p = jnp.exp(s)
            if masked:
                p = jnp.where(allowed, p, 0.0)
            probs.append(p.astype(bf16))
            grads.append((p * dp).astype(bf16))
        for h in range(heads):
            sl = slice(h * HEAD, (h + 1) * HEAD)
            pair = slice((h // 2) * 128, (h // 2) * 128 + 128)
            dv[sl, ks] += dot(dot_t[sl, :], probs[h])
            dk[sl, ks] += dot(qt[sl, :], grads[h])
            dq[h] += dot(grads[h], k[ks, pair])
        return carry

    last = lax.div(q0, tk)
    lax.fori_loop(jnp.where(q0 >= 1792, last, 0), last + 1, lambda j, c: step(j, c, True), 0)
    scale = HEAD ** (-0.5)
    lane = lax.broadcasted_iota(jnp.int32, (tq, 128), 1)
    q_parts = [
        jnp.where(lane < HEAD, dq[2 * h], dq[2 * h + 1]).T * scale for h in range(heads // 2)
    ]
    angle = pl.ds(pl.multiple_of(q0, tq), tq)
    grads_q[...] = turn(jnp.concatenate(q_parts, axis=0), cosine[:, angle], sine[:, angle], -1).astype(bf16)

    @pl.when(i == pl.num_programs(0) - 1)
    def _():
        grads_k[...] = turn(dk[...], cosine[...], sine[...], -1).astype(bf16)
        grads_v[...] = dv[...].astype(bf16)


def attend_back(lens, q, qt, k, kt, vt, do, dot_t, ot, cosine, sine, tq=256, tk=256, deps=(), moves=(), collective=None):
    e, length = qt.shape
    heads = e // HEAD
    cols = pl.BlockSpec((e, tq), lambda i, *_: (0, i))
    rows = pl.BlockSpec((tq, e), lambda i, *_: (i, 0))
    stat = pl.BlockSpec((e + 8, tq), lambda i, *_: (0, i))
    nat, tr, ang = whole((length, e)), whole((e, length)), whole((HALF, length))
    out = jax.ShapeDtypeStruct((e, length), bf16)
    return call(
        functools.partial(attend_back_kernel, tk),
        grid=(length // tq,),
        in_specs=[rows, cols, nat, tr, tr, rows, cols, stat, ang, ang],
        out_specs=[cols, once((e, length)), once((e, length))],
        scratch=[
            pltpu.VMEM((heads, 128, length), bf16),
            pltpu.VMEM((heads, 128, length), bf16),
            pltpu.VMEM((e, length), f32),
            pltpu.VMEM((e, length), f32),
            pltpu.VMEM((heads, tq, 128), f32),
            pltpu.VMEM((heads // 2, tq, 256), bf16),
            pltpu.VMEM((heads // 2, tq, 256), bf16),
            pltpu.VMEM((heads, 128, tk), bf16),
            pltpu.VMEM((heads, 128, tk), bf16),
        ],
        scalars=1,
        out_shape=[out, out, out],
        flops=5 * length * length * e,
        nbytes=20 * length * e,
        deps=deps,
        moves=moves,
        collective=collective,
        name="attend_back",
    )(lens, q, qt, k, kt, vt, do, dot_t, ot, cosine, sine)


def merge_tile(tok, gq, gk, gv, ot, w, ow, gains, biases):
    hat, inverse = hat_of(tok[...].astype(f32))
    gain = gains[0:1, :]
    back = dot(gq[...], w[0], TT) + dot(gk[...], w[1], TT) + dot(gv[...], w[2], TT)
    low = ot[...].astype(bf16)
    return hat, inverse, gain, back, low, dot(low, ow[...], TN)


def merge_own_kernel(tok, g, gq, gk, gv, ot, w, ow, gains, biases, part_in, share_in, small_in, upb_in, part, share, dw, dow):
    i = pl.program_id(0)
    tile = tok.shape[0]
    e, d = ow.shape
    wide = upb_in.shape[1]

    @pl.when(i == 0)
    def _():
        dw[...] = jnp.zeros_like(dw)
        dow[...] = jnp.zeros_like(dow)
        dow[e + 1 : e + 2, :] = small_in[1:2, :]
        dow[e + 3 : e + 4, :] = small_in[2:3, :]
        dow[e + 4 : e + 5, :] = small_in[0:1, :]
        for c in range(wide // d):
            dow[e + 5 + c : e + 6 + c, :] = upb_in[:, c * d : (c + 1) * d]

    hat, _, gain, back, low, out = merge_tile(tok, gq, gk, gv, ot, w, ow, gains, biases)
    normed = (hat * gain + biases[0:1, :]).astype(bf16)
    share[...] = share_in[...] + back * gain
    part[...] = part_in[...] + out
    dw[0] += dot(normed, gq[...], TT)
    dw[1] += dot(normed, gk[...], TT)
    dw[2] += dot(normed, gv[...], TT)
    dow[:e, :] += dot(low, g[...])
    dow[e : e + 1, :] += jnp.sum(back * hat, axis=0, keepdims=True)
    dow[e + 2 : e + 3, :] += jnp.sum(back, axis=0, keepdims=True)
    ones = jnp.ones((8, tile), bf16)
    at = e + 5 + wide // d
    dow[at : at + 1, :e] += dot(ones, gq[...], NT)[0:1]
    dow[at : at + 1, e : 2 * e] += dot(ones, gv[...], NT)[0:1]


def merge_own(tok, g, gq, gk, gv, ot, w, ow, gains, biases, part, share, small, upb, tile=512, deps=()):
    length, d = tok.shape
    e = w.shape[2]
    wide = upb.shape[1]
    rows = pl.BlockSpec((tile, d), lambda i: (i, 0))
    cols = pl.BlockSpec((e, tile), lambda i: (0, i))
    full = jax.ShapeDtypeStruct((length, d), f32)
    return call(
        merge_own_kernel,
        grid=(length // tile,),
        in_specs=[rows, rows, cols, cols, cols, cols, whole((3, d, e)), whole((e, d)), whole((2, d)), whole((2, d)), rows, rows, whole((8, d)), whole((1, wide))],
        out_specs=[rows, rows, once((3, d, e)), once((e + 8, d))],
        out_shape=[full, full, jax.ShapeDtypeStruct((3, d, e), f32), jax.ShapeDtypeStruct((e + 8, d), f32)],
        flops=16 * length * d * e,
        nbytes=24 * length * d,
        deps=deps,
        name="merge_own",
    )(tok, g, gq, gk, gv, ot, w, ow, gains, biases, part, share, small, upb)


def merge_other_kernel(tok, g, gq, gk, gv, ot, w, ow, gains, biases, out_bias, part_in, share_in, output, input_grad):
    hat, inverse, gain, back, _, out = merge_tile(tok, gq, gk, gv, ot, w, ow, gains, biases)
    shares = share_in[...] + back * gain
    inputs = tok[...].astype(f32)
    output[...] = (inputs + (part_in[...] + out) + out_bias[0:1, :] + out_bias[1:2, :]).astype(bf16)
    input_share = inverse * (
        shares
        - jnp.mean(shares, axis=-1, keepdims=True)
        - hat * jnp.mean(shares * hat, axis=-1, keepdims=True)
    )
    input_grad[...] = (g[...].astype(f32) + input_share).astype(bf16)


def merge_other(tok, g, gq, gk, gv, ot, w, ow, gains, biases, out_bias, part, share, tile=512, deps=()):
    length, d = tok.shape
    e = w.shape[2]
    rows = pl.BlockSpec((tile, d), lambda i: (i, 0))
    cols = pl.BlockSpec((e, tile), lambda i: (0, i))
    full = jax.ShapeDtypeStruct((length, d), bf16)
    return call(
        merge_other_kernel,
        grid=(length // tile,),
        in_specs=[rows, rows, cols, cols, cols, cols, whole((3, d, e)), whole((e, d)), whole((2, d)), whole((2, d)), whole((2, d)), rows, rows],
        out_specs=[rows, rows],
        out_shape=[full, full],
        flops=8 * length * d * e,
        nbytes=24 * length * d,
        deps=deps,
        name="merge_other",
    )(tok, g, gq, gk, gv, ot, w, ow, gains, biases, out_bias, part, share)


def pack_kernel(meta, w, ow, up, down, first, second):
    d = ow.shape[1]
    e = w.shape[2]
    for n, ref in enumerate((first, second)):
        at = 0
        r = down.shape[0] // 2
        ref[at : at + r, :] = down[n * r : (n + 1) * r, :].astype(f32)
        at += r
        r = up.shape[0] // 2
        for c in range(up.shape[1] // d):
            ref[at : at + r, :] = up[n * r : (n + 1) * r, c * d : (c + 1) * d].astype(f32)
            at += r
        r = w.shape[1] // 4
        for c in range(3):
            for s in range(2):
                ref[at : at + r, s * e : (s + 1) * e] = w[c, (2 * n + s) * r : (2 * n + s + 1) * r, :].astype(f32)
            at += r
        r = ow.shape[0] // 2
        ref[at : at + r, :] = ow[n * r : (n + 1) * r, :].astype(f32)


def pack(meta, w, ow, up, down, deps=()):
    _, d, e = w.shape
    wide = up.shape[1]
    rows = (wide + (wide // d) * d + 3 * d // 2 + e) // 8
    piece = jax.ShapeDtypeStruct((rows, d), f32)
    return call(
        pack_kernel,
        grid=(1,),
        in_specs=[
            pl.BlockSpec((3, d // 4, e), lambda i, m: (0, m[1], 0)),
            pl.BlockSpec((e // 4, d), lambda i, m: (m[1], 0)),
            pl.BlockSpec((d // 4, wide), lambda i, m: (m[1], 0)),
            pl.BlockSpec((wide // 4, d), lambda i, m: (m[1], 0)),
        ],
        out_specs=[once((rows, d)), once((rows, d))],
        scalars=1,
        out_shape=[piece, piece],
        deps=deps,
        name="pack",
    )(meta, w, ow, up, down)


def unpack_kernel(meta, *refs):
    pieces, (w, ow, up, down) = refs[:8], refs[8:]
    d = ow.shape[1]
    e = w.shape[2]
    for n, ref in enumerate(pieces):
        core = meta[0] ^ (n // 4)
        parity = meta[2] ^ ((n // 2) % 2)
        at_piece = (parity * 2 + core) * 2 + n % 2
        at = 0
        r = down.shape[0] // 8
        down[pl.ds(pl.multiple_of(at_piece * r, r), r), :] = ref[at : at + r, :].astype(bf16)
        at += r
        r = up.shape[0] // 8
        for c in range(up.shape[1] // d):
            up[pl.ds(pl.multiple_of(at_piece * r, r), r), c * d : (c + 1) * d] = ref[at : at + r, :].astype(bf16)
            at += r
        r = w.shape[1] // 16
        for c in range(3):
            for s in range(2):
                w[c, pl.ds(pl.multiple_of((at_piece * 2 + s) * r, r), r), :] = ref[at : at + r, s * e : (s + 1) * e].astype(bf16)
            at += r
        r = ow.shape[0] // 8
        ow[pl.ds(pl.multiple_of(at_piece * r, r), r), :] = ref[at : at + r, :].astype(bf16)


def unpack(meta, pieces, w, ow, up, down, deps=()):
    shapes = [jax.ShapeDtypeStruct(x.shape, bf16) for x in (w, ow, up, down)]
    return call(
        unpack_kernel,
        grid=(1,),
        in_specs=[once(p.shape) for p in pieces],
        out_specs=[once(s.shape) for s in shapes],
        scalars=1,
        out_shape=shapes,
        deps=deps,
        name="unpack",
    )(meta, *pieces)


def swap(x, bit):
    n = lax.axis_size("dp")
    return lax.ppermute(x, "dp", [(i, i ^ (1 << bit)) for i in range(n)])


def across(x):
    return lax.ppermute(x, "tensor", [(0, 1), (1, 0)])


def tie(arrays, deps):
    n = len(arrays)
    anywhere = [pl.BlockSpec(memory_space=pl.ANY)] * n
    return call(
        lambda *refs: None,
        grid=(1,),
        in_specs=anywhere,
        out_specs=anywhere,
        out_shape=[jax.ShapeDtypeStruct(x.shape, x.dtype) for x in arrays],
        aliases={i: i for i in range(n)},
        deps=deps,
        name="tie",
    )(*arrays)


BITS_AT = 4


def exchange(meta, ops, deps=()):
    small = min(op[1].shape[0] // (2 if op[0] == "halve" else 1) for op in ops if op[0] != "norm" and op[1].shape[0] > 8)
    grid = next(g for g in (4, 2, 1) if small % (8 * g) == 0)
    args, in_specs, out_specs, out_shape, plan = [], [], [], [], []
    for op in ops:
        kind, mine, got = op[:3]
        rows, d = mine.shape
        if kind == "halve":
            r = rows // 2
            spec = lambda keep, r=r, bit=op[3]: pl.BlockSpec(
                (1, r // grid, d), lambda i, m: ((m[BITS_AT + bit] if keep else 1 - m[BITS_AT + bit]), i, 0)
            )
            a, b = mine.reshape(2, r, d), got.reshape(2, r, d)
            args += [a, b, a, b]
            in_specs += [spec(False), spec(False), spec(True), spec(True)]
            out_specs += [pl.BlockSpec((r // grid, d), lambda i, m: (i, 0))] * 2
            out_shape += [jax.ShapeDtypeStruct((r, d), f32)] * 2
            plan.append((kind, 4, 2, None))
        elif kind == "join":
            block = pl.BlockSpec((rows // grid, d), lambda i, m: (i, 0))
            args += [mine, got]
            in_specs += [block, block]
            out_specs.append(pl.BlockSpec((2, rows // grid, d), lambda i, m: (0, i, 0)))
            out_shape.append(jax.ShapeDtypeStruct((2, rows, d), f32))
            plan.append((kind, 2, 1, op[3]))
        else:
            r = rows // grid if rows > 8 else rows
            block = pl.BlockSpec((r, d), (lambda i, m: (i, 0)) if rows > 8 else (lambda i, m: (0, 0)))
            args += [mine, got]
            in_specs += [block, block]
            out_specs.append(block)
            out_shape.append(jax.ShapeDtypeStruct((rows, d), f32))
            plan.append((kind, 2, 1, None))

    def kernel(m, *refs):
        ins, outs = refs[: len(args)], refs[len(args) :]
        at, to = 0, 0
        for kind, n_in, n_out, bit in plan:
            x, y = ins[at : at + n_in], outs[to : to + n_out]
            if kind == "halve":
                y[0][...] = x[0][0] + x[1][0]
                y[1][...] = x[2][0] + x[3][0]
            elif kind == "join":
                v = m[BITS_AT + bit]
                y[0][v] = x[0][...]
                y[0][1 - v] = x[1][...]
            elif kind == "norm":
                row = lax.broadcasted_iota(jnp.int32, x[0].shape, 0)
                y[0][...] = x[0][...] + jnp.where(row < 4, x[1][...], 0.0)
            else:
                y[0][...] = x[0][...] + x[1][...]
            at += n_in
            to += n_out

    outs = call(
        kernel, grid=(grid,), scalars=1, in_specs=in_specs, out_specs=out_specs, out_shape=out_shape, deps=deps, name="exchange"
    )(meta, *args)
    return [x.reshape(-1, x.shape[-1]) if x.ndim == 3 else x for x in outs]


def assemble_up(meta, up, got, deps=()):
    d = up.shape[1]
    lanes = 2
    r = up.shape[0] // lanes
    grid = 4

    def kernel(m, a, b, out):
        for x, half in ((a, m[0]), (b, 1 - m[0])):
            for s in range(lanes):
                out[half, :, s * d : (s + 1) * d] = x[s]

    pair = pl.BlockSpec((lanes, r // grid, d), lambda i, m: (0, i, 0))
    return call(
        kernel,
        grid=(grid,),
        scalars=1,
        in_specs=[pair, pair],
        out_specs=pl.BlockSpec((2, r // grid, lanes * d), lambda i, m: (0, i, 0)),
        out_shape=jax.ShapeDtypeStruct((2, r, lanes * d), f32),
        deps=deps,
        name="assemble_up",
    )(meta, up.reshape(lanes, r, d), got.reshape(lanes, r, d)).reshape(2 * r, lanes * d)


class Sum:
    def __init__(self, keep, send, order):
        self.mine, self.got = keep, swap(send, 0)
        self.todo = [("halve", b) for b in order] + [("add", None)] + [("join", b) for b in reversed(order)]
        self.order = order

    @property
    def done(self):
        return not self.todo

    def op(self):
        kind, bit = self.todo[0]
        return (kind, self.mine, self.got) + (() if bit is None else (bit,))

    def take(self, outs):
        kind, _ = self.todo.pop(0)
        if kind == "halve":
            send, self.mine = outs.pop(0), outs.pop(0)
        else:
            send = self.mine = outs.pop(0)
        if not self.todo:
            self.got = swap(send, 0)
            return [send]
        following, bit = self.todo[0]
        if kind == "halve":
            bit = self.order[len(self.order) - 1 - sum(1 for k, _ in self.todo if k == "halve")]
        self.got = swap(send, bit)
        return [send, self.mine]


def advance(meta, sums, deps):
    sums = [s for s in sums if not s.done]
    if not sums:
        return []
    outs = exchange(meta, [s.op() for s in sums], deps)
    return [x for s in sums for x in s.take(outs)]


def per_device(
    tokens, lengths, qkv_weight, qkv_bias, out_weight, out_bias, up_weight, up_bias, down_weight, down_bias, norm_gains, norm_biases, cotangent
):
    length, d = tokens.shape
    e = qkv_weight.shape[2]
    wide = up_weight.shape[1]
    bits = lax.axis_size("dp").bit_length() - 1
    me = lax.axis_index("dp")
    core = me & 1
    parity = ((me >> 1) ^ (me >> 2)) & 1
    meta = jnp.stack([core, parity * 2 + core, parity, parity] + [(me >> b) & 1 for b in range(12)])
    freq = jnp.broadcast_to(
        (rot_base ** (-(2.0 * jnp.arange(HALF, dtype=f32)) / ROT))[:, None], (HALF, 128)
    )
    first, second = pack(meta, qkv_weight, out_weight, up_weight, down_weight)
    own_biases = jnp.concatenate([up_bias.astype(f32), qkv_bias.astype(f32).reshape(-1)]).reshape(-1, d)
    other_biases = across(own_biases)

    def half_biases(rows):
        flat = rows.reshape(-1)
        return flat[None, :wide], flat[wide:].reshape(2, e).T

    own_upb, own_qkvb = half_biases(own_biases)
    other_upb, other_qkvb = half_biases(other_biases)
    got_first = across(first)
    part, share, keep_u, send_u, d_down, small, d_upb = mlp_own(
        meta, tokens, cotangent, up_weight, own_upb, down_weight, norm_gains, norm_biases, deps=[first]
    )
    d_down = lax.psum(d_down, "dp")
    order = list(range(1, bits))
    sum_u = Sum(keep_u, send_u, order)
    got_first, second = tie([got_first, second], [part])
    got_second = across(second)
    near_first = swap(got_first, 1)
    qt, q, kt, k, vt, dot_t, do, cosine, sine = project(
        lengths, tokens, cotangent, qkv_weight, own_qkvb, out_weight, norm_gains, norm_biases, freq, deps=[got_first, send_u]
    )
    wait = advance(meta, [sum_u], [qt])
    ot = attend(lengths, qt, k, vt, deps=wait)
    (got_second,) = tie([got_second], [ot])
    near_second = swap(got_second, 2)
    (gq, gk, gv), (other_ot,) = attend_back(
        lengths, q, qt, k, kt, vt, do, dot_t, ot, cosine, sine, deps=[got_second], moves=[Move(ot, "tensor", 1)], collective=1
    )
    quarter = list(tie([got_first, got_second, near_first], [gq]))
    pieces = [swap(x, 0) for x in quarter]
    wait = advance(meta, [sum_u], [gq])
    part, share, d_qkv, d_out = merge_own(
        tokens, cotangent, gq, gk, gv, ot, qkv_weight, out_weight, norm_gains, norm_biases, part, share, small, d_upb, deps=quarter + wait
    )
    d_qkv, d_out = tie([d_qkv, d_out], [d_down])
    turned = [list(range(lax.axis_size("dp")))[::-1]]
    d_qkv, d_out = lax.psum((d_qkv, d_out), "dp", axis_index_groups=turned)
    near_second, other_ot = tie([near_second, other_ot], [part])
    quarter.append(near_second)
    pieces.append(swap(near_second, 0))
    wait = advance(meta, [sum_u], [part])
    other_w, other_ow, other_up, other_down = unpack(
        meta, quarter + pieces, qkv_weight, out_weight, up_weight, down_weight, deps=wait + [other_ot]
    )
    wait = advance(meta, [sum_u], [other_w])
    qt, q, kt, k, vt, dot_t, do, cosine, sine = project(
        lengths, tokens, cotangent, other_w, other_qkvb, other_ow, norm_gains, norm_biases, freq, deps=wait
    )
    wait = advance(meta, [sum_u], [qt])
    gq, gk, gv = attend_back(lengths, q, qt, k, kt, vt, do, dot_t, other_ot, cosine, sine, deps=wait)
    wait = advance(meta, [sum_u], [gq])
    part, share = mlp_other(tokens, cotangent, other_up, other_upb, other_down, norm_gains, norm_biases, part, share, deps=wait)
    wait = advance(meta, [sum_u], [part])
    out_biases = jnp.stack([out_bias, down_bias]).astype(f32)
    output, input_grad = merge_other(
        tokens, cotangent, gq, gk, gv, other_ot, other_w, other_ow, norm_gains, norm_biases, out_biases, part, share, deps=wait
    )
    wait = [output]
    while not sum_u.done:
        wait = advance(meta, [sum_u], wait)
    d_qkv, d_out = tie([d_qkv, d_out], [output])
    d_up = assemble_up(meta, sum_u.mine, sum_u.got)
    smalls = d_out[e:]
    norm_sums = smalls[:4] + across(smalls[:4])
    rest = smalls[5:].reshape(-1)
    return (
        output, input_grad, d_qkv, rest[wide:].reshape(2, e), d_out[:e], smalls[4], d_up, rest[:wide], d_down, smalls[4], norm_sums[:2], norm_sums[2:],
    )


def solution(mesh):
    in_specs = (
        P("dp", None), P("dp", None), P(None, None, "tensor"), P(None, "tensor"), P("tensor", None), P(), P(None, "tensor"),
        P("tensor"), P("tensor", None), P(), P(), P(), P("dp", None),
    )
    out_specs = (
        P("dp", None), P("dp", None), P(None, None, "tensor"), P(None, "tensor"), P("tensor", None), P(), P(None, "tensor"),
        P("tensor"), P("tensor", None), P(), P(), P(),
    )
    return jax.shard_map(per_device, mesh=mesh, in_specs=in_specs, out_specs=out_specs, check_vma=False)
```

```python
import functools
import math

import jax
import jax.numpy as jnp
import numpy as np
from jax import lax
from jax.experimental import pallas as pl
from jax.experimental.pallas import tpu as pltpu
from jax.sharding import PartitionSpec as P

HEAD = 64
ROT = 16
HALF = ROT // 2
epsilon = 1e-05
rot_base = 10000.0
f32 = jnp.float32
bf16 = jnp.bfloat16
NN = (((1,), (0,)), ((), ()))
NT = (((1,), (1,)), ((), ()))
TN = (((0,), (0,)), ((), ()))
TT = (((0,), (1,)), ((), ()))
VMEM_LIMIT = 60 * 2**20


def dot(a, b, dims=NN):
    return lax.dot_general(a, b, dims, preferred_element_type=f32)


MESH = pl.DeviceIdType.MESH


def bit_of(b):
    return lax.rem(lax.div(lax.axis_index("dp"), 1 << b), 2)


def partner(flip):
    if flip == "tensor":
        return {"tensor": 1 - lax.axis_index("tensor")}
    return {"dp": lax.axis_index("dp") + (1 - 2 * bit_of(flip)) * (1 << flip)}


def by_rows(rows, step):
    size = next(c for c in (96, 48, 24, 8, rows) if rows % c == 0)
    if rows == size:
        step(0, size)
    else:
        lax.fori_loop(0, rows // size, lambda j, c: (step(pl.multiple_of(j * size, 8), size), c)[1], 0)


class Sends:
    def __init__(self, *phases, at=(0,)):
        self.at = at
        self.phases = phases if isinstance(phases[0], list) else [list(phases)]
        moves = [m for phase in self.phases for m in phase]
        self.flips = [flip for _, flip in moves]
        self.inputs = [x for x, _ in moves if not isinstance(x, int)]
        shapes = []
        for x, _ in moves:
            shapes.append(shapes[x] if isinstance(x, int) else jax.ShapeDtypeStruct(x.shape, x.dtype))
        self.outputs = [(s, True) for s in shapes]
        self.scratch = [pltpu.SemaphoreType.DMA((2, len(moves)))]

    def build(self, ins, outs, scratch):
        sems, ins, events, j = scratch[0], list(ins), [], 0
        for phase in self.phases:
            copies = []
            for x, flip in phase:
                source = outs[x] if isinstance(x, int) else ins.pop(0)
                copies.append(
                    pltpu.make_async_remote_copy(
                        src_ref=source, dst_ref=outs[j], send_sem=sems.at[0, j], recv_sem=sems.at[1, j], device_id=partner(flip), device_id_type=MESH
                    )
                )
                j += 1

            def begin(copies=copies):
                for c in copies:
                    c.start()

            def finish(copies=copies):
                for c in copies:
                    c.wait()

            events.append((begin, finish))
        return events

    def receive(self, outs):
        self.got = list(outs)


class Sum:
    def __init__(self, keep, send, order):
        self.mine, self.send = keep, send
        halved = [b for j, b in enumerate(order) if keep.shape[0] % (16 << j) == 0]
        way = [0] + halved
        self.steps = [(way[j], "halve", b) for j, b in enumerate(halved)] + [(way[-1], "add", None)]
        self.steps += [(b, "add", None) for b in order if b not in halved]
        self.steps += [(b, "join", b) for b in reversed(halved)]

    @property
    def done(self):
        return not self.steps

    def take(self, *at):
        steps, self.steps = self.steps[: len(at)], self.steps[len(at) :]
        return Steps(self, steps, at)


class SmallSum(Sum):
    def __init__(self, x, bits):
        self.mine = self.send = x
        self.steps = [(b, "add", None) for b in range(bits)] + [("tensor", "norm", None)]


class Final:
    def __init__(self, sums, shapes, count, places):
        self.sums, self.shapes, self.count, self.places = sums, shapes, count, places
        self.at, self.flips = (0,), [0]

    @property
    def inputs(self):
        return [s.mine for s in self.sums]

    @property
    def outputs(self):
        return [(jax.ShapeDtypeStruct(s, f32), True) for s in self.shapes]

    @property
    def scratch(self):
        stage = [pltpu.VMEM(s.mine.shape, f32) for s in self.sums]
        return [pltpu.SemaphoreType.DMA((3, self.count)), pltpu.SemaphoreType.DMA((len(stage),))] + stage

    def build(self, ins, outs, scratch):
        put = lambda sources: self.places(sources, outs, bit_of(0))
        return [place_copies(put, ins, scratch[2:], 0, scratch[0], scratch[1])]

    def receive(self, outs):
        self.results = list(outs)


def place_copies(put, sources, held, flip, sems, load_sems):
    at = (lambda k, j: sems.at[k]) if load_sems is None else (lambda k, j: sems.at[k, j])
    there = [
        pltpu.make_async_remote_copy(
            src_ref=s, dst_ref=t, send_sem=at(0, j), recv_sem=at(1, j), device_id=partner(flip), device_id_type=MESH
        )
        for j, (s, t) in enumerate(put(sources))
    ]
    loads = [] if held is None else [
        pltpu.make_async_copy(s, h, sems.at[2] if load_sems is None else load_sems.at[j]) for j, (s, h) in enumerate(zip(sources, held))
    ]
    here = [pltpu.make_async_copy(s, t, at(2, j)) for j, (s, t) in enumerate(put(sources if held is None else held))]

    def begin():
        for c in there + (here if held is None else loads):
            c.start()

    def finish():
        for c in loads:
            c.wait()
        if held is not None:
            for c in here:
                c.start()
        for c in here + there:
            c.wait()

    return begin, finish


class Steps:
    def __init__(self, owner, steps, at):
        self.owner, self.steps, self.at = owner, steps, at
        self.flips = [s[0] for s in steps]
        self.same = owner.mine is owner.send
        reads = [k for _, k, _ in steps][0] in ("halve", "add", "norm")
        self.inputs = [owner.send] + ([owner.mine] if reads and not self.same else [])
        self.outputs, self.scratch = [], []
        rows, d = owner.send.shape
        local = True
        for n, (_, kind, _) in enumerate(steps):
            last = n == len(steps) - 1
            self.scratch.append(pltpu.SemaphoreType.DMA((3,)))
            if kind in ("halve", "add", "norm"):
                self.scratch += [pltpu.VMEM((rows, d), f32)] * (2 if local else 1)
                rows = rows // 2 if kind == "halve" else rows
                shapes = [(rows, d)] * (2 if kind == "halve" else 1)
                if last:
                    self.outputs += [(jax.ShapeDtypeStruct(s, f32), False) for s in shapes]
                else:
                    self.scratch += [pltpu.VMEM(s, f32) for s in shapes]
                local = False
            elif kind == "join":
                if local:
                    self.scratch.append(pltpu.VMEM((rows, d), f32))
                local = True
                rows *= 2
                self.outputs.append((jax.ShapeDtypeStruct((rows, d), f32), True))

    def build(self, ins, outs, scratch):
        outs, scratch = list(outs), list(scratch)
        send = ins[0]
        mine = ins[-1]
        events = []
        in_hbm = True
        for n, (flip, kind, bit) in enumerate(self.steps):
            last = n == len(self.steps) - 1
            sems = scratch.pop(0)
            rows = send.shape[0]
            if kind in ("halve", "add", "norm"):
                got = scratch.pop(0)
                held = scratch.pop(0) if in_hbm else mine
                fresh = (outs if last else scratch).pop(0)
                kept = (outs if last else scratch).pop(0) if kind == "halve" else None
                events.append(self.reduce(kind, bit, flip, send, mine, in_hbm, got, held, fresh, kept, sems))
                send, mine, in_hbm = fresh, (fresh if kept is None else kept), False
            elif kind == "join":
                target = outs.pop(0)
                held = scratch.pop(0) if in_hbm else None
                put = lambda xs, target=target, bit=bit, rows=rows: [
                    (xs[0], target.at[pl.ds(pl.multiple_of(bit_of(bit) * rows, 8), rows)])
                ]
                events.append(self.copies(put, send, held, flip, sems))
                send = mine = target
                in_hbm = True
        return events

    @staticmethod
    def copies(put, send, held, flip, sems, load_sems=None):
        return place_copies(put, [send], None if held is None else [held], flip, sems, load_sems)

    @staticmethod
    def reduce(kind, bit, flip, send, mine, in_hbm, got, held, fresh, kept, sems):
        there = pltpu.make_async_remote_copy(
            src_ref=send, dst_ref=got, send_sem=sems.at[0], recv_sem=sems.at[1], device_id=partner(flip), device_id_type=MESH
        )
        load = pltpu.make_async_copy(mine, held, sems.at[2]) if in_hbm else None

        def begin():
            there.start()
            if load is not None:
                load.start()

        def finish():
            if load is not None:
                load.wait()
            there.wait()
            if kind == "halve":
                r = held.shape[0] // 2
                v = bit_of(bit)
                for out, half in ((fresh, 1 - v), (kept, v)):
                    base = half * r

                    def step(j, size, out=out, base=base):
                        rows = pl.ds(pl.multiple_of(base + j, 8), size)
                        out[pl.ds(j, size), :] = held[rows, :] + got[rows, :]

                    by_rows(r, step)
            elif kind == "norm":
                row = lax.broadcasted_iota(jnp.int32, held.shape, 0)
                fresh[...] = held[...] + jnp.where(row < 4, got[...], 0.0)
            else:

                def step(j, size):
                    rows = pl.ds(j, size)
                    fresh[rows, :] = held[rows, :] + got[rows, :]

                by_rows(held.shape[0], step)

        return begin, finish

    def receive(self, outs):
        outs = list(outs)
        owner = self.owner
        for n, (_, kind, _) in enumerate(self.steps):
            last = n == len(self.steps) - 1
            if kind == "join":
                owner.mine = owner.send = outs.pop(0)
            elif last:
                owner.send = outs.pop(0)
                owner.mine = outs.pop(0) if kind == "halve" else owner.send


def call(
    kernel, *, grid, in_specs, out_specs, out_shape, scalars=0, scratch=(), deps=(), rides=(), collective=None, flops=0, nbytes=0, name=None, aliases=None
):
    single = not isinstance(out_shape, (list, tuple))
    out_specs = [out_specs] if single else list(out_specs)
    out_shape = [out_shape] if single else list(out_shape)
    n_in, n_out, n_scratch = scalars + len(in_specs), len(out_shape), len(scratch)
    anywhere = pl.BlockSpec(memory_space=pl.ANY)
    ride_in = [x for r in rides for x in r.inputs]
    ride_out = [o for r in rides for o in r.outputs]
    flips = list(dict.fromkeys(f for r in rides for f in r.flips))

    def body(*refs):
        refs = list(refs)
        cut = lambda n: [refs.pop(0) for _ in range(n)]
        ins, _, sources = cut(n_in), cut(len(deps)), cut(len(ride_in))
        outs, targets, held = cut(n_out), cut(len(ride_out)), cut(n_scratch)
        at_step, at_end = {}, []
        for r in rides:
            take = lambda refs, n: [refs.pop(0) for _ in range(n)]
            events = r.build(take(sources, len(r.inputs)), take(targets, len(r.outputs)), take(refs, len(r.scratch)))
            for n, (begin, finish) in enumerate(events):
                at_step.setdefault(r.at[n], []).append(begin)
                if n + 1 < len(events):
                    at_step.setdefault(r.at[n + 1], []).append(finish)
                else:
                    at_end.append(finish)
        if rides:

            @pl.when(pl.program_id(0) == 0)
            def _():
                barrier = pltpu.get_barrier_semaphore()
                for f in flips:
                    pl.semaphore_signal(barrier, inc=1, device_id=partner(f), device_id_type=MESH)
                pl.semaphore_wait(barrier, len(flips))

        for g, acts in at_step.items():

            @pl.when(pl.program_id(0) == g)
            def _(acts=acts):
                for act in acts:
                    act()

        kernel(*ins, *outs, *held)
        if at_end:

            @pl.when(pl.program_id(0) == pl.num_programs(0) - 1)
            def _():
                for act in at_end:
                    act()

    params = dict(vmem_limit_bytes=VMEM_LIMIT)
    if rides:
        params.update(collective_id=collective, has_side_effects=True)

    def run(*args):
        outs = pl.pallas_call(
            body,
            grid_spec=pltpu.PrefetchScalarGridSpec(
                num_scalar_prefetch=scalars,
                grid=grid,
                in_specs=list(in_specs) + [anywhere] * (len(deps) + len(ride_in)),
                out_specs=out_specs + [anywhere if hbm else once(s.shape) for s, hbm in ride_out],
                scratch_shapes=list(scratch) + [s for r in rides for s in r.scratch],
            ),
            out_shape=out_shape + [s for s, _ in ride_out],
            compiler_params=pltpu.CompilerParams(**params),
            cost_estimate=pl.CostEstimate(flops=20 * flops, bytes_accessed=nbytes, transcendentals=0),
            input_output_aliases=aliases or {},
            name=name,
        )(*args, *deps, *ride_in)
        outs = list(outs)
        own, rest = outs[:n_out], outs[n_out:]
        for r in rides:
            r.receive(rest[: len(r.outputs)])
            rest = rest[len(r.outputs) :]
        return own[0] if single else own

    return run


def whole(shape):
    zeros = (0,) * len(shape)
    return pl.BlockSpec(shape, lambda *_: zeros, pipeline_mode=pl.Buffered(1))


def once(shape):
    zeros = (0,) * len(shape)
    return pl.BlockSpec(shape, lambda *_: zeros)


def hat_of(values):
    average = jnp.mean(values, axis=-1, keepdims=True)
    centered = values - average
    inverse = lax.rsqrt(jnp.mean(centered * centered, axis=-1, keepdims=True) + epsilon)
    return centered * inverse, inverse


def gelu_pair(h):
    a = jnp.abs(h) * np.float32(math.sqrt(0.5))
    t = 1.0 / (1.0 + np.float32(0.3275911) * a)
    bell = jnp.exp(-0.5 * (h * h))
    poly = np.float32(0.5 * 1.061405429) * t + np.float32(0.5 * -1.453152027)
    poly = poly * t + np.float32(0.5 * 1.421413741)
    poly = poly * t + np.float32(0.5 * -0.284496736)
    poly = poly * t + np.float32(0.5 * 0.254829592)
    tail = poly * t * bell
    phi = jnp.where(h >= 0, 1.0 - tail, tail)
    return h * phi, phi + h * bell * np.float32(1.0 / math.sqrt(2.0 * math.pi))


def add_to(ref, first, value):
    @pl.when(first)
    def _():
        ref[...] = value

    @pl.when(jnp.logical_not(first))
    def _():
        ref[...] += value


def mlp_tile(chunk, tok, g, up, upb, down, gains, biases, visit):
    hat, _ = hat_of(tok[...].astype(f32))
    gain = gains[1:2, :]
    normed = (hat * gain + biases[1:2, :]).astype(bf16)
    gt = g[...]
    total = None
    back = None
    for c in range(up.shape[1] // chunk):
        sl = slice(c * chunk, (c + 1) * chunk)
        hidden = dot(normed, up[:, sl]) + upb[:, sl]
        act_grad = dot(gt, down[sl, :], NT)
        act, slope = gelu_pair(hidden)
        act = act.astype(bf16)
        hid_grad = (act_grad * slope).astype(bf16)
        p = dot(act, down[sl, :])
        e = dot(hid_grad, up[:, sl], NT)
        total = p if total is None else total + p
        back = e if back is None else back + e
        visit(sl, normed, gt, act, hid_grad)
    return hat, gt, total, back, gain


def mlp_own_kernel(chunk, tok, g, up, upb, down, gains, biases, part, share, keep_d, send_d, keep_u, send_u, small, upb_sum, ddown, dup):
    i = pl.program_id(0)

    @pl.when(i == 0)
    def _():
        dup[...] = jnp.zeros_like(dup)
        ddown[...] = jnp.zeros_like(ddown)
        small[...] = jnp.zeros_like(small)
        upb_sum[...] = jnp.zeros_like(upb_sum)

    def visit(sl, normed, gt, act, hid_grad):
        dup[:, sl] += dot(normed, hid_grad, TN)
        ddown[sl, :] += dot(act, gt, TN)
        upb_sum[:, sl] += jnp.sum(hid_grad.astype(f32), axis=0, keepdims=True)

    hat, gt, total, back, gain = mlp_tile(chunk, tok, g, up, upb, down, gains, biases, visit)
    part[...] = total
    share[...] = back * gain
    small[0:1, :] += jnp.sum(gt.astype(f32), axis=0, keepdims=True)
    small[1:2, :] += jnp.sum(back * hat, axis=0, keepdims=True)
    small[2:3, :] += jnp.sum(back, axis=0, keepdims=True)

    @pl.when(i == pl.num_programs(0) - 1)
    def _():
        d, wide = dup.shape
        core = bit_of(0)
        for down_out, up_out, half in ((keep_d, keep_u, core), (send_d, send_u, 1 - core)):
            rows = pl.multiple_of(half * (wide // 2), wide // 2)
            down_out[...] = ddown[pl.ds(rows, wide // 2), :]
            rows = pl.multiple_of(half * (d // 2), d // 2)
            for c in range(wide // d):
                up_out[c * (d // 2) : (c + 1) * (d // 2), :] = dup[pl.ds(rows, d // 2), c * d : (c + 1) * d]


def mlp_own(tok, g, up, upb, down, gains, biases, tile=512, chunk=768, deps=(), rides=(), collective=None):
    length, d = tok.shape
    wide = up.shape[1]
    rows = pl.BlockSpec((tile, d), lambda i, *_: (i, 0))
    return call(
        functools.partial(mlp_own_kernel, chunk),
        grid=(length // tile,),
        in_specs=[rows, rows, whole((d, wide)), whole((1, wide)), whole((wide, d)), whole((2, d)), whole((2, d))],
        out_specs=[rows, rows, *[once((wide // 2, d))] * 4, once((8, d)), once((1, wide))],
        out_shape=[
            jax.ShapeDtypeStruct((length, d), f32),
            jax.ShapeDtypeStruct((length, d), f32),
            *[jax.ShapeDtypeStruct((wide // 2, d), f32)] * 4,
            jax.ShapeDtypeStruct((8, d), f32),
            jax.ShapeDtypeStruct((1, wide), f32),
        ],
        scratch=[pltpu.VMEM((wide, d), f32), pltpu.VMEM((d, wide), f32)],
        flops=12 * length * d * wide,
        nbytes=4 * length * d * 4,
        deps=deps,
        rides=rides,
        collective=collective,
        name="mlp_own",
    )(tok, g, up, upb, down, gains, biases)


def mlp_other_kernel(chunk, tok, g, up, upb, down, gains, biases, part_in, share_in, part, share):
    nothing = lambda *_: None
    _, _, total, back, gain = mlp_tile(chunk, tok, g, up, upb, down, gains, biases, nothing)
    part[...] = part_in[...] + total
    share[...] = share_in[...] + back * gain


def mlp_other(tok, g, up, upb, down, gains, biases, part, share, tile=512, chunk=768, deps=(), rides=(), collective=None):
    length, d = tok.shape
    wide = up.shape[1]
    rows = pl.BlockSpec((tile, d), lambda i: (i, 0))
    full = jax.ShapeDtypeStruct((length, d), f32)
    return call(
        functools.partial(mlp_other_kernel, chunk),
        grid=(length // tile,),
        in_specs=[rows, rows, whole((d, wide)), whole((1, wide)), whole((wide, d)), whole((2, d)), whole((2, d)), rows, rows],
        out_specs=[rows, rows],
        out_shape=[full, full],
        flops=8 * length * d * wide,
        nbytes=4 * length * d * 4,
        deps=deps,
        rides=rides,
        collective=collective,
        name="mlp_other",
    )(tok, g, up, upb, down, gains, biases, part, share)


def first_tokens(lens, places):
    first = jnp.zeros_like(places)
    end = lens[0, 0]
    for j in range(1, lens.shape[1]):
        first = jnp.where(places >= end, end, first)
        end = end + lens[0, j]
    return jnp.where(places >= end, places, first)


def turn(block, cosine, sine, sign):
    parts = []
    for h in range(block.shape[0] // HEAD):
        r = h * HEAD
        a = block[r : r + HALF, :]
        b = block[r + HALF : r + ROT, :]
        if sign > 0:
            parts += [a * cosine - b * sine, b * cosine + a * sine]
        else:
            parts += [a * cosine + b * sine, b * cosine - a * sine]
        parts.append(block[r + ROT : r + HEAD, :])
    return jnp.concatenate(parts, axis=0)


def proj_kernel(lens, tok, g, w, bias, ow, gains, biases, freq, qt, q, kt, k, vt, dot_t, do, cosine, sine):
    tile = tok.shape[0]
    i = pl.program_id(0)
    hat, _ = hat_of(tok[...].astype(f32))
    normed = (hat * gains[0:1, :] + biases[0:1, :]).astype(bf16)
    places = i * tile + lax.broadcasted_iota(jnp.int32, (1, tile), 1)
    position = (places - first_tokens(lens, places)).astype(f32)
    theta = freq[:, 0:1] * position
    c = jnp.cos(theta)
    s = jnp.sin(theta)
    cosine[...] = c
    sine[...] = s
    scale = HEAD ** (-0.5)
    query = turn(dot(w[0], normed, TT) + bias[:, 0:1], c, s, 1).astype(bf16) * scale
    qt[...] = query
    q[...] = query.T
    key = turn(dot(w[1], normed, TT), c, s, 1).astype(bf16)
    kt[...] = key
    k[...] = key.T
    vt[...] = (dot(w[2], normed, TT) + bias[:, 1:2]).astype(bf16)
    grad = dot(ow[...], g[...], NT).astype(bf16)
    dot_t[...] = grad
    do[...] = grad.T


def project(lens, tok, g, w, bias, ow, gains, biases, freq, tile=512, deps=(), rides=(), collective=None):
    length, d = tok.shape
    e = w.shape[2]
    rows = pl.BlockSpec((tile, d), lambda i, *_: (i, 0))
    tr = pl.BlockSpec((e, tile), lambda i, *_: (0, i))
    nat = pl.BlockSpec((tile, e), lambda i, *_: (i, 0))
    ang = pl.BlockSpec((HALF, tile), lambda i, *_: (0, i))
    t_shape = jax.ShapeDtypeStruct((e, length), bf16)
    n_shape = jax.ShapeDtypeStruct((length, e), bf16)
    a_shape = jax.ShapeDtypeStruct((HALF, length), f32)
    return call(
        proj_kernel,
        grid=(length // tile,),
        in_specs=[rows, rows, whole((3, d, e)), whole((e, 2)), whole((e, d)), whole((2, d)), whole((2, d)), whole((HALF, 128))],
        out_specs=[tr, nat, tr, nat, tr, tr, nat, ang, ang],
        scalars=1,
        out_shape=[t_shape, n_shape, t_shape, n_shape, t_shape, t_shape, n_shape, a_shape, a_shape],
        flops=8 * length * d * e,
        nbytes=20 * length * e,
        deps=deps,
        rides=rides,
        collective=collective,
        name="project",
    )(lens, tok, g, w, bias, ow, gains, biases, freq)


def low_parts(x):
    high = x.astype(bf16)
    rest = x - high.astype(f32)
    mid = rest.astype(bf16)
    return [high, mid, (rest - mid.astype(f32)).astype(bf16)]


FILLED = 1792


def fixed_tiles(q0, tk, step, carry):
    last = lax.div(q0, tk)
    first = jnp.where(q0 >= FILLED, last, 0)
    return lax.fori_loop(first, last + 1, lambda j, c: step(j, c, True), carry)


def tile_range(lens, start):
    first = jnp.int32(0)
    end = lens[0, 0]
    for j in range(1, lens.shape[1]):
        first = jnp.where(start >= end, end, first)
        end = end + lens[0, j]
    return jnp.where(start >= end, start, first)


def tile_plan(lens, q0, tq, tk):
    low = lax.div(tile_range(lens, q0), tk)
    diagonal = lax.div(q0, tk)
    high = lax.div(q0 + tq + tk - 1, tk)
    inner = jnp.minimum(lax.div(tile_range(lens, q0 + tq - 1) + tk - 1, tk), diagonal)
    return low, jnp.maximum(inner, low), diagonal, high


def over_tiles(fixed, lens, q0, tq, tk, step, carry):
    if fixed:
        return fixed_tiles(q0, tk, step, carry)
    low, inner, diagonal, high = tile_plan(lens, q0, tq, tk)
    edges = inner - low
    masked = lambda t, c: step(jnp.where(t < edges, low + t, diagonal + t - edges), c, True)
    carry = lax.fori_loop(0, edges + high - diagonal, masked, carry)
    return lax.fori_loop(inner, diagonal, lambda j, c: step(j, c, False), carry)


VROWS = 80


def attend_kernel(tk, fixed, lens, qt, k, vt, ot, ot_send, qpad, vpad, acc):
    i = pl.program_id(0)
    tq = qt.shape[1]
    heads = qt.shape[0] // HEAD
    q0 = i * tq

    @pl.when(i == 0)
    def _():
        row = lax.broadcasted_iota(jnp.int32, (VROWS - HEAD, vt.shape[1]), 0)
        ones = jnp.where(row == 0, 1.0, 0.0).astype(bf16)
        for h in range(heads):
            vpad[h, :HEAD, :] = vt[h * HEAD : (h + 1) * HEAD, :]
            vpad[h, HEAD:, :] = ones

    places = q0 + lax.broadcasted_iota(jnp.int32, (1, tq), 1)
    first = first_tokens(lens, places)
    zero = jnp.zeros((HEAD, tq), bf16)
    for h in range(heads):
        qh = qt[h * HEAD : (h + 1) * HEAD, :]
        qpad[h] = jnp.concatenate([qh, zero] if h % 2 == 0 else [zero, qh], axis=0)
    acc[...] = jnp.zeros_like(acc)

    def step(j, peaks, masked):
        k0 = pl.multiple_of(j * tk, tk)
        if masked:
            rows = k0 + lax.broadcasted_iota(jnp.int32, (tk, tq), 0)
            allowed = (rows >= first) & (rows <= places)
        scores, new, raised = [], [], []
        for h in range(heads):
            pair = (h // 2) * 128
            s = dot(k[pl.ds(k0, tk), pair : pair + 128], qpad[h])
            scores.append(jnp.where(allowed, s, -1e30) if masked else s)
        for h in range(heads):
            new.append(jnp.maximum(peaks[h], jnp.max(scores[h], axis=0, keepdims=True)))
            raised.append(jnp.exp(scores[h] - new[h]).astype(bf16))
        for h in range(heads):
            o = dot(vpad[h, :, pl.ds(k0, tk)], raised[h])
            acc[h] = acc[h] * jnp.exp(peaks[h] - new[h]) + o
        return tuple(new)

    start = tuple(jnp.full((1, tq), -1e30, f32) for _ in range(heads))
    peaks = over_tiles(fixed, lens, q0, tq, tk, step, start)
    logs = []
    for h in range(heads):
        total = acc[h, HEAD : HEAD + 1, :]
        ot[h * HEAD : (h + 1) * HEAD, :] = acc[h, :HEAD, :] / total
        logs.append(peaks[h] + jnp.log(total))
    logs.append(jnp.zeros((8 - heads, tq), f32))
    ot[heads * HEAD :, :] = jnp.concatenate(logs, axis=0)
    ot_send[...] = ot[...]


def attend(lens, qt, k, vt, tq=256, tk=256, deps=(), rides=(), collective=None):
    e, length = qt.shape
    heads = e // HEAD
    cols = pl.BlockSpec((e, tq), lambda i, *_: (0, i))
    return call(
        functools.partial(attend_kernel, tk, len(rides) > 0),
        grid=(length // tq,),
        in_specs=[cols, whole((length, e)), whole((e, length))],
        out_specs=[pl.BlockSpec((e + 8, tq), lambda i, *_: (0, i))] * 2,
        scratch=[
            pltpu.VMEM((heads, 128, tq), bf16),
            pltpu.VMEM((heads, VROWS, length), bf16),
            pltpu.VMEM((heads, VROWS, tq), f32),
        ],
        scalars=1,
        out_shape=[jax.ShapeDtypeStruct((e + 8, length), f32)] * 2,
        flops=2 * length * length * e,
        nbytes=8 * length * e,
        deps=deps,
        rides=rides,
        collective=collective,
        name="attend",
    )(lens, qt, k, vt)


def attend_back_kernel(tk, fixed, lens, q, qt, k, kt, vt, do, dot_t, ot, cosine, sine, grads_q, grads_k, grads_v, kpad, vpad, dk, dv, dq, qa, da, cs, cd):
    i = pl.program_id(0)
    tq = q.shape[0]
    length = k.shape[0]
    heads = q.shape[1] // HEAD
    q0 = i * tq

    @pl.when(i == 0)
    def _():
        dk[...] = jnp.zeros_like(dk)
        dv[...] = jnp.zeros_like(dv)
        zero = jnp.zeros((HEAD, length), bf16)
        row = lax.broadcasted_iota(jnp.int32, (128, tk), 0)
        for h in range(heads):
            sl = slice(h * HEAD, (h + 1) * HEAD)
            own, other = (0, HEAD) if h % 2 == 0 else (HEAD, 0)
            kpad[h, own : own + HEAD, :] = kt[sl, :]
            kpad[h, other : other + HEAD, :] = zero
            vpad[h, own : own + HEAD, :] = vt[sl, :]
            vpad[h, other : other + HEAD, :] = zero
            cs[h] = jnp.where((row < 24) & (row % 8 == h), -1.0, 0.0).astype(bf16)
            cd[h] = jnp.where((row >= 24) & (row < 48) & (row % 8 == h), -1.0, 0.0).astype(bf16)

    places = q0 + lax.broadcasted_iota(jnp.int32, (tq, 1), 0)
    first = first_tokens(lens, places)
    deltas = [
        jnp.sum(ot[h * HEAD : (h + 1) * HEAD, :] * dot_t[h * HEAD : (h + 1) * HEAD, :].astype(f32), axis=0, keepdims=True)
        for h in range(heads)
    ]
    deltas.append(jnp.zeros((8 - heads, tq), f32))
    stats = low_parts(ot[heads * HEAD :, :]) + low_parts(jnp.concatenate(deltas, axis=0))
    stats.append(jnp.zeros((128 - 48, tq), bf16))
    stat_cols = jnp.concatenate(stats, axis=0).T
    for r in range(heads // 2):
        pair = slice(r * 128, r * 128 + 128)
        qa[r, :, :128] = q[:, pair]
        qa[r, :, 128:] = stat_cols
        da[r, :, :128] = do[:, pair]
        da[r, :, 128:] = stat_cols
    dq[...] = jnp.zeros_like(dq)

    def step(j, carry, masked):
        k0 = pl.multiple_of(j * tk, tk)
        ks = pl.ds(k0, tk)
        if masked:
            cols = k0 + lax.broadcasted_iota(jnp.int32, (tq, tk), 1)
            allowed = (cols >= first) & (cols <= places)
        probs, grads = [], []
        for h in range(heads):
            s = dot(qa[h // 2], jnp.concatenate([kpad[h, :, ks], cs[h]], axis=0))
            dp = dot(da[h // 2], jnp.concatenate([vpad[h, :, ks], cd[h]], axis=0))
            p = jnp.exp(s)
            if masked:
                p = jnp.where(allowed, p, 0.0)
            probs.append(p.astype(bf16))
            grads.append((p * dp).astype(bf16))
        for h in range(heads):
            sl = slice(h * HEAD, (h + 1) * HEAD)
            pair = slice((h // 2) * 128, (h // 2) * 128 + 128)
            dv[sl, ks] += dot(dot_t[sl, :], probs[h])
            dk[sl, ks] += dot(qt[sl, :], grads[h])
            dq[h] += dot(grads[h], k[ks, pair])
        return carry

    over_tiles(fixed, lens, q0, tq, tk, step, 0)
    scale = HEAD ** (-0.5)
    lane = lax.broadcasted_iota(jnp.int32, (tq, 128), 1)
    q_parts = [
        jnp.where(lane < HEAD, dq[2 * h], dq[2 * h + 1]).T * scale for h in range(heads // 2)
    ]
    angle = pl.ds(pl.multiple_of(q0, tq), tq)
    grads_q[...] = turn(jnp.concatenate(q_parts, axis=0), cosine[:, angle], sine[:, angle], -1).astype(bf16)

    @pl.when(i == pl.num_programs(0) - 1)
    def _():
        grads_k[...] = turn(dk[...], cosine[...], sine[...], -1).astype(bf16)
        grads_v[...] = dv[...].astype(bf16)


def attend_back(lens, q, qt, k, kt, vt, do, dot_t, ot, cosine, sine, tq=256, tk=256, deps=(), rides=(), collective=None):
    e, length = qt.shape
    heads = e // HEAD
    cols = pl.BlockSpec((e, tq), lambda i, *_: (0, i))
    rows = pl.BlockSpec((tq, e), lambda i, *_: (i, 0))
    stat = pl.BlockSpec((e + 8, tq), lambda i, *_: (0, i))
    nat, tr, ang = whole((length, e)), whole((e, length)), whole((HALF, length))
    out = jax.ShapeDtypeStruct((e, length), bf16)
    return call(
        functools.partial(attend_back_kernel, tk, len(rides) > 0),
        grid=(length // tq,),
        in_specs=[rows, cols, nat, tr, tr, rows, cols, stat, ang, ang],
        out_specs=[cols, once((e, length)), once((e, length))],
        scratch=[
            pltpu.VMEM((heads, 128, length), bf16),
            pltpu.VMEM((heads, 128, length), bf16),
            pltpu.VMEM((e, length), f32),
            pltpu.VMEM((e, length), f32),
            pltpu.VMEM((heads, tq, 128), f32),
            pltpu.VMEM((heads // 2, tq, 256), bf16),
            pltpu.VMEM((heads // 2, tq, 256), bf16),
            pltpu.VMEM((heads, 128, tk), bf16),
            pltpu.VMEM((heads, 128, tk), bf16),
        ],
        scalars=1,
        out_shape=[out, out, out],
        flops=5 * length * length * e,
        nbytes=20 * length * e,
        deps=deps,
        rides=rides,
        collective=collective,
        name="attend_back",
    )(lens, q, qt, k, kt, vt, do, dot_t, ot, cosine, sine)


def merge_tile(tok, gq, gk, gv, ot, w, ow, gains, biases):
    hat, inverse = hat_of(tok[...].astype(f32))
    gain = gains[0:1, :]
    back = dot(gq[...], w[0], TT) + dot(gk[...], w[1], TT) + dot(gv[...], w[2], TT)
    low = ot[...].astype(bf16)
    return hat, inverse, gain, back, low, dot(low, ow[...], TN)


def merge_own_kernel(tok, g, gq, gk, gv, ot, w, ow, gains, biases, part_in, share_in, small_in, upb_in, part, share, keep_a, send_a, keep_b, send_b, small, dw, dow):
    i = pl.program_id(0)
    tile = tok.shape[0]
    e, d = ow.shape
    wide = upb_in.shape[1]

    @pl.when(i == 0)
    def _():
        dw[...] = jnp.zeros_like(dw)
        dow[...] = jnp.zeros_like(dow)
        small[...] = jnp.zeros_like(small)
        small[1:2, :] = small_in[1:2, :]
        small[3:4, :] = small_in[2:3, :]
        small[4:5, :] = small_in[0:1, :]
        for c in range(wide // d):
            small[5 + c : 6 + c, :] = upb_in[:, c * d : (c + 1) * d]

    hat, _, gain, back, low, out = merge_tile(tok, gq, gk, gv, ot, w, ow, gains, biases)
    normed = (hat * gain + biases[0:1, :]).astype(bf16)
    share[...] = share_in[...] + back * gain
    part[...] = part_in[...] + out
    dw[0] += dot(normed, gq[...], TT)
    dw[1] += dot(normed, gk[...], TT)
    dw[2] += dot(normed, gv[...], TT)
    dow[...] += dot(low, g[...])
    small[0:1, :] += jnp.sum(back * hat, axis=0, keepdims=True)
    small[2:3, :] += jnp.sum(back, axis=0, keepdims=True)
    ones = jnp.ones((8, tile), bf16)
    at = 5 + wide // d
    small[at : at + 1, :e] += dot(ones, gq[...], NT)[0:1]
    small[at : at + 1, e : 2 * e] += dot(ones, gv[...], NT)[0:1]

    @pl.when(i == pl.num_programs(0) - 1)
    def _():
        core = bit_of(0)
        quarter = d // 4
        for first, second, half in ((keep_a, keep_b, core), (send_a, send_b, 1 - core)):
            for c in range(3):
                ref, at = (first, c * quarter) if c < 2 else (second, 0)
                for s in range(2):
                    rows = pl.multiple_of(half * (2 * quarter) + s * quarter, quarter)
                    ref[at : at + quarter, s * e : (s + 1) * e] = dw[c, pl.ds(rows, quarter), :]
            rows = pl.multiple_of(half * (e // 2), e // 2)
            second[quarter:, :] = dow[pl.ds(rows, e // 2), :]


def merge_own(tok, g, gq, gk, gv, ot, w, ow, gains, biases, part, share, small, upb, tile=512, deps=(), rides=(), collective=None):
    length, d = tok.shape
    e = w.shape[2]
    wide = upb.shape[1]
    rows = pl.BlockSpec((tile, d), lambda i: (i, 0))
    cols = pl.BlockSpec((e, tile), lambda i: (0, i))
    full = jax.ShapeDtypeStruct((length, d), f32)
    half = jax.ShapeDtypeStruct((d // 2, d), f32)
    return call(
        merge_own_kernel,
        grid=(length // tile,),
        in_specs=[rows, rows, cols, cols, cols, cols, whole((3, d, e)), whole((e, d)), whole((2, d)), whole((2, d)), rows, rows, whole((8, d)), whole((1, wide))],
        out_specs=[rows, rows, *[once(half.shape)] * 4, once((8, d))],
        out_shape=[full, full, half, half, half, half, jax.ShapeDtypeStruct((8, d), f32)],
        scratch=[pltpu.VMEM((3, d, e), f32), pltpu.VMEM((e, d), f32)],
        flops=16 * length * d * e,
        nbytes=24 * length * d,
        deps=deps,
        rides=rides,
        collective=collective,
        name="merge_own",
    )(tok, g, gq, gk, gv, ot, w, ow, gains, biases, part, share, small, upb)


def merge_other_kernel(tok, g, gq, gk, gv, ot, w, ow, gains, biases, out_bias, part_in, share_in, output, input_grad):
    hat, inverse, gain, back, _, out = merge_tile(tok, gq, gk, gv, ot, w, ow, gains, biases)
    shares = share_in[...] + back * gain
    inputs = tok[...].astype(f32)
    output[...] = (inputs + (part_in[...] + out) + out_bias[0:1, :] + out_bias[1:2, :]).astype(bf16)
    input_share = inverse * (
        shares
        - jnp.mean(shares, axis=-1, keepdims=True)
        - hat * jnp.mean(shares * hat, axis=-1, keepdims=True)
    )
    input_grad[...] = (g[...].astype(f32) + input_share).astype(bf16)


def merge_other(tok, g, gq, gk, gv, ot, w, ow, gains, biases, out_bias, part, share, tile=512, deps=(), rides=(), collective=None):
    length, d = tok.shape
    e = w.shape[2]
    rows = pl.BlockSpec((tile, d), lambda i: (i, 0))
    cols = pl.BlockSpec((e, tile), lambda i: (0, i))
    full = jax.ShapeDtypeStruct((length, d), bf16)
    return call(
        merge_other_kernel,
        grid=(length // tile,),
        in_specs=[rows, rows, cols, cols, cols, cols, whole((3, d, e)), whole((e, d)), whole((2, d)), whole((2, d)), whole((2, d)), rows, rows],
        out_specs=[rows, rows],
        out_shape=[full, full],
        flops=8 * length * d * e,
        nbytes=24 * length * d,
        deps=deps,
        rides=rides,
        collective=collective,
        name="merge_other",
    )(tok, g, gq, gk, gv, ot, w, ow, gains, biases, out_bias, part, share)


def pack_kernel(meta, w, ow, up, down, w_far, ow_far, up_far, down_far, one, two, three, four):
    d = ow.shape[1]
    e = w.shape[2]

    def half(refs, n, put):
        w, ow, up, down = refs
        r = down.shape[0] // 2
        put(down[n * r : (n + 1) * r, :])
        r = up.shape[0] // 2
        for c in range(up.shape[1] // d):
            put(up[n * r : (n + 1) * r, c * d : (c + 1) * d])
        r = w.shape[1] // 4
        for c in range(3):
            put(*[w[c, (2 * n + s) * r : (2 * n + s + 1) * r, :] for s in range(2)])
        r = ow.shape[0] // 2
        put(ow[n * r : (n + 1) * r, :])

    def into(*refs):
        place = [0, 0]

        def put(*blocks):
            ref, at = refs[place[0]], place[1]
            rows, lanes = blocks[0].shape
            for j, x in enumerate(blocks):
                ref[at : at + rows, j * lanes : (j + 1) * lanes] = x.astype(f32)
            place[1] = at + rows
            if place[1] == ref.shape[0]:
                place[:] = [place[0] + 1, 0]

        return put

    near = (w, ow, up, down)
    half(near, 0, into(one, two))
    half(near, 1, into(three))
    half((w_far, ow_far, up_far, down_far), 1, into(four))


def pack(meta, w, ow, up, down):
    _, d, e = w.shape
    wide = up.shape[1]
    rows = (wide + (wide // d) * d + 3 * d // 2 + e) // 8
    first = wide // 8 + d // 8
    sizes = [first, rows - first, rows, rows]
    blocks = lambda n: [
        pl.BlockSpec((3, d // 4, e), lambda i, m: (0, m[n], 0)),
        pl.BlockSpec((e // 4, d), lambda i, m: (m[n], 0)),
        pl.BlockSpec((d // 4, wide), lambda i, m: (m[n], 0)),
        pl.BlockSpec((wide // 4, d), lambda i, m: (m[n], 0)),
    ]
    return call(
        pack_kernel,
        grid=(1,),
        scalars=1,
        in_specs=blocks(0) + blocks(1),
        out_specs=[once((r, d)) for r in sizes],
        out_shape=[jax.ShapeDtypeStruct((r, d), f32) for r in sizes],
        name="pack",
    )(meta, w, ow, up, down, w, ow, up, down)


def unpack_kernel(*refs):
    pieces, (w, ow, up, down) = refs[:12], refs[12:]
    d = ow.shape[1]
    e = w.shape[2]
    for n in range(4):
        core = lax.rem(bit_of(0) + n // 2, 2)
        parity = lax.rem(bit_of(1) + bit_of(2) + n % 2, 2)
        one, two, three = pieces[3 * n : 3 * n + 3]
        for m, refs in enumerate(((one, two), (three,))):
            at_piece = (parity * 2 + core) * 2 + m
            place = [0, 0]

            def take(rows):
                ref, at = refs[place[0]], place[1]
                place[1] = at + rows
                if place[1] == ref.shape[0]:
                    place[:] = [place[0] + 1, 0]
                return ref[at : at + rows, :].astype(bf16)

            rows = lambda r, sub=0, parts=1: pl.ds(pl.multiple_of((at_piece * parts + sub) * r, r), r)
            r = down.shape[0] // 8
            down[rows(r), :] = take(r)
            r = up.shape[0] // 8
            for c in range(up.shape[1] // d):
                up[rows(r), c * d : (c + 1) * d] = take(r)
            r = w.shape[1] // 16
            for c in range(3):
                x = take(r)
                for s in range(2):
                    w[c, rows(r, s, 2), :] = x[:, s * e : (s + 1) * e]
            r = ow.shape[0] // 8
            ow[rows(r), :] = take(r)


def unpack(pieces, w, ow, up, down, deps=(), rides=(), collective=None):
    shapes = [jax.ShapeDtypeStruct(x.shape, bf16) for x in (w, ow, up, down)]
    return call(
        unpack_kernel,
        grid=(1,),
        in_specs=[whole(p.shape) for p in pieces],
        out_specs=[once(s.shape) for s in shapes],
        out_shape=shapes,
        deps=deps,
        rides=rides,
        collective=collective,
        name="unpack",
    )(*pieces)


def swap(x, bit):
    n = lax.axis_size("dp")
    return lax.ppermute(x, "dp", [(i, i ^ (1 << bit)) for i in range(n)])


def across(x):
    return lax.ppermute(x, "tensor", [(0, 1), (1, 0)])


def tie(arrays, deps):
    n = len(arrays)
    anywhere = [pl.BlockSpec(memory_space=pl.ANY)] * n
    return call(
        lambda *refs: None,
        grid=(1,),
        in_specs=anywhere,
        out_specs=anywhere,
        out_shape=[jax.ShapeDtypeStruct(x.shape, x.dtype) for x in arrays],
        aliases={i: i for i in range(n)},
        deps=deps,
        name="tie",
    )(*arrays)


def down_places(d, wide):
    rows = wide // 2

    def places(sources, outs, core):
        return [(sources[0], outs[0].at[pl.ds(pl.multiple_of(core * rows, 8), rows)])]

    return [(wide, d)], 1, places


def up_places(d, wide):
    lanes, rows = wide // d, d // 2

    def places(sources, outs, core):
        to = pl.ds(pl.multiple_of(core * rows, 8), rows)
        return [(sources[0].at[pl.ds(s * rows, rows)], outs[0].at[to, pl.ds(s * d, d)]) for s in range(lanes)]

    return [(d, wide)], lanes, places


def attn_places(d, e):
    rows = d // 4

    def places(sources, outs, core):
        pairs = []
        for c in range(3):
            source, at = (sources[0], c * rows) if c < 2 else (sources[1], 0)
            for s in range(2):
                to = pl.ds(pl.multiple_of(core * (2 * rows) + s * rows, 8), rows)
                pairs.append((source.at[pl.ds(at, rows), pl.ds(s * e, e)], outs[0].at[c, to]))
        to = pl.ds(pl.multiple_of(core * (e // 2), 8), e // 2)
        pairs.append((sources[1].at[pl.ds(rows, e // 2)], outs[1].at[to]))
        return pairs

    return [(3, d, e), (e, d)], 7, places


def relay(rides, collective, deps=()):
    call(
        lambda *_: None,
        grid=(1,),
        in_specs=[],
        out_specs=[],
        out_shape=[],
        deps=deps,
        rides=rides,
        collective=collective,
        name="relay",
    )()


def per_device(
    tokens, lengths, qkv_weight, qkv_bias, out_weight, out_bias, up_weight, up_bias, down_weight, down_bias, norm_gains, norm_biases, cotangent
):
    length, d = tokens.shape
    e = qkv_weight.shape[2]
    wide = up_weight.shape[1]
    bits = lax.axis_size("dp").bit_length() - 1
    me = lax.axis_index("dp")
    quarter = lambda p: (((me >> 1) ^ (me >> 2) ^ p) & 1) * 2 + (me & 1)
    meta = jnp.stack([quarter(0), quarter(1)])
    freq = np.broadcast_to((rot_base ** (-(2.0 * np.arange(HALF)) / ROT)).astype(np.float32)[:, None], (HALF, 128))
    one, two, three, far_three = pack(meta, qkv_weight, out_weight, up_weight, down_weight)
    own_biases = jnp.concatenate([up_bias.astype(f32), qkv_bias.astype(f32).reshape(-1)]).reshape(-1, d)
    own_biases = jnp.concatenate([own_biases, jnp.zeros((8 - own_biases.shape[0], d), f32)])

    def half_biases(rows):
        flat = rows.reshape(-1)
        return flat[None, :wide], flat[wide : wide + 2 * e].reshape(2, e).T

    own_upb, own_qkvb = half_biases(own_biases)
    send = Sends([(one, "tensor"), (own_biases, "tensor")], [(0, 1), (two, "tensor")], at=(0, 2))
    part, share, keep_d, send_d, keep_u, send_u, small, d_upb = mlp_own(
        tokens, cotangent, up_weight, own_upb, down_weight, norm_gains, norm_biases, rides=[send], collective=1
    )
    one, other_biases, near_one, two = send.got
    other_upb, other_qkvb = half_biases(other_biases)
    order = list(range(1, bits))
    crossed = [order[1], order[0]] + order[2:]
    sum_d, sum_u = Sum(keep_d, send_d, order), Sum(keep_u, send_u, crossed)
    two, three, far_three = tie([two, three, far_three], [part])
    three = across(three)
    near_two = swap(two, 1)
    qt, q, kt, k, vt, dot_t, do, cosine, sine = project(
        lengths, tokens, cotangent, qkv_weight, own_qkvb, out_weight, norm_gains, norm_biases, freq,
        deps=[two], rides=[sum_d.take(0), sum_u.take(0)], collective=2,
    )
    ot, ot_send = attend(lengths, qt, k, vt, rides=[sum_d.take(0), sum_u.take(0)], collective=3)
    three, near_two, far_three = tie([three, near_two, far_three], [ot])
    near_three = across(far_three)
    send = Sends((one, 0), (two, 0), (near_one, 0), (near_two, 0), (three, 0))
    gq, gk, gv = attend_back(
        lengths, q, qt, k, kt, vt, do, dot_t, ot, cosine, sine,
        deps=[far_three], rides=[send, sum_d.take(0, 4), sum_u.take(0, 4)], collective=4,
    )
    core_one, core_two, core_near_one, core_near_two, core_three = send.got
    near_three, ot_send = tie([near_three, ot_send], [gq])
    other_ot = across(ot_send)
    send = Sends((near_three, 0))
    part, share, keep_a, send_a, keep_b, send_b, small = merge_own(
        tokens, cotangent, gq, gk, gv, ot, qkv_weight, out_weight, norm_gains, norm_biases, part, share, small, d_upb,
        rides=[send, sum_d.take(0), sum_u.take(0)], collective=5,
    )
    (core_near_three,) = send.got
    sum_a, sum_b, sum_s = Sum(keep_a, send_a, order), Sum(keep_b, send_b, crossed), SmallSum(small, bits)
    pieces = [one, two, three, near_one, near_two, near_three]
    pieces += [core_one, core_two, core_three, core_near_one, core_near_two, core_near_three]
    other_w, other_ow, other_up, other_down = unpack(
        pieces, qkv_weight, out_weight, up_weight, down_weight,
        rides=[sum_d.take(0), sum_u.take(0), sum_a.take(0), sum_b.take(0), sum_s.take(0)], collective=6,
    )
    qt, q, kt, k, vt, dot_t, do, cosine, sine = project(
        lengths, tokens, cotangent, other_w, other_qkvb, other_ow, norm_gains, norm_biases, freq,
        rides=[sum_a.take(0), sum_b.take(0), sum_s.take(0)], collective=7,
    )
    (other_ot,) = tie([other_ot], [qt])
    gq, gk, gv = attend_back(
        lengths, q, qt, k, kt, vt, do, dot_t, other_ot, cosine, sine,
        rides=[sum_a.take(0, 4), sum_b.take(0, 4), sum_s.take(0), sum_d.take(0), sum_u.take(0)], collective=8,
    )
    sums = [sum_d, sum_u]
    at = 9
    while not all(s.done for s in sums):
        relay([s.take(0) for s in sums if not s.done], at)
        at += 1
    final_d, final_u = Final([sum_d], *down_places(d, wide)), Final([sum_u], *up_places(d, wide))
    part, share = mlp_other(
        tokens, cotangent, other_up, other_upb, other_down, norm_gains, norm_biases, part, share,
        rides=[sum_a.take(0, 2, 3), sum_b.take(0, 2, 3), sum_s.take(0), final_d, final_u], collective=at,
    )
    (d_down,), (d_up,) = final_d.results, final_u.results
    sums = [sum_a, sum_b]
    at += 1
    while not all(s.done for s in sums):
        relay([s.take(0) for s in sums if not s.done], at)
        at += 1
    final = Final(sums, *attn_places(d, e))
    out_biases = jnp.stack([out_bias, down_bias]).astype(f32)
    output, input_grad = merge_other(
        tokens, cotangent, gq, gk, gv, other_ot, other_w, other_ow, norm_gains, norm_biases, out_biases, part, share,
        rides=[final] + [s.take(0) for s in [sum_s] if not s.done], collective=at,
    )
    at += 1
    while not sum_s.done:
        relay([sum_s.take(0)], at)
        at += 1
    d_qkv, d_out = final.results
    small = sum_s.mine
    rest = small[5:].reshape(-1)
    return (
        output, input_grad, d_qkv, rest[wide : wide + 2 * e].reshape(2, e), d_out, small[4], d_up, rest[:wide], d_down, small[4], small[:2], small[2:4],
    )


def solution(mesh):
    in_specs = (
        P("dp", None), P("dp", None), P(None, None, "tensor"), P(None, "tensor"), P("tensor", None), P(), P(None, "tensor"),
        P("tensor"), P("tensor", None), P(), P(), P(), P("dp", None),
    )
    out_specs = (
        P("dp", None), P("dp", None), P(None, None, "tensor"), P(None, "tensor"), P("tensor", None), P(), P(None, "tensor"),
        P("tensor"), P("tensor", None), P(), P(), P(),
    )
    return jax.shard_map(per_device, mesh=mesh, in_specs=in_specs, out_specs=out_specs, check_vma=False)
```

```python
import functools
import math

import jax
import jax.numpy as jnp
import numpy as np
from jax import lax
from jax.experimental import pallas as pl
from jax.experimental.pallas import tpu as pltpu
from jax.sharding import PartitionSpec as P

HEAD = 64
ROT = 16
HALF = ROT // 2
epsilon = 1e-05
rot_base = 10000.0
f32 = jnp.float32
bf16 = jnp.bfloat16
NN = (((1,), (0,)), ((), ()))
NT = (((1,), (1,)), ((), ()))
TN = (((0,), (0,)), ((), ()))
TT = (((0,), (1,)), ((), ()))
VMEM_LIMIT = 60 * 2**20


def dot(a, b, dims=NN):
    return lax.dot_general(a, b, dims, preferred_element_type=f32)


MESH = pl.DeviceIdType.MESH


def bit_of(b):
    return lax.rem(lax.div(lax.axis_index("dp"), 1 << b), 2)


def partner(flip):
    if flip == "tensor":
        return {"tensor": 1 - lax.axis_index("tensor")}
    return {"dp": lax.axis_index("dp") + (1 - 2 * bit_of(flip)) * (1 << flip)}


def by_rows(rows, step):
    size = next(c for c in (96, 48, 24, 8, rows) if rows % c == 0)
    if rows == size:
        step(0, size)
    else:
        lax.fori_loop(0, rows // size, lambda j, c: (step(pl.multiple_of(j * size, 8), size), c)[1], 0)


class Sends:
    def __init__(self, *phases, at=(0,)):
        self.at = at
        self.phases = phases if isinstance(phases[0], list) else [list(phases)]
        moves = [m for phase in self.phases for m in phase]
        self.flips = [flip for _, flip in moves]
        self.inputs = [x for x, _ in moves if not isinstance(x, int)]
        shapes = []
        for x, _ in moves:
            shapes.append(shapes[x] if isinstance(x, int) else jax.ShapeDtypeStruct(x.shape, x.dtype))
        self.outputs = [(s, True) for s in shapes]
        self.scratch = [pltpu.SemaphoreType.DMA((2, len(moves)))]

    def build(self, ins, outs, scratch):
        sems, ins, events, j = scratch[0], list(ins), [], 0
        for phase in self.phases:
            copies = []
            for x, flip in phase:
                source = outs[x] if isinstance(x, int) else ins.pop(0)
                copies.append(
                    pltpu.make_async_remote_copy(
                        src_ref=source, dst_ref=outs[j], send_sem=sems.at[0, j], recv_sem=sems.at[1, j], device_id=partner(flip), device_id_type=MESH
                    )
                )
                j += 1

            def begin(copies=copies):
                for c in copies:
                    c.start()

            def finish(copies=copies):
                for c in copies:
                    c.wait()

            events.append((begin, finish))
        return events

    def receive(self, outs):
        self.got = list(outs)


class Sum:
    def __init__(self, keep, send, order):
        self.mine, self.send = keep, send
        halved = [b for j, b in enumerate(order) if keep.shape[0] % (16 << j) == 0]
        way = [0] + halved
        self.steps = [(way[j], "halve", b) for j, b in enumerate(halved)] + [(way[-1], "add", None)]
        self.steps += [(b, "add", None) for b in order if b not in halved]
        self.steps += [(b, "join", b) for b in reversed(halved)]

    @property
    def done(self):
        return not self.steps

    def take(self, *at):
        steps, self.steps = self.steps[: len(at)], self.steps[len(at) :]
        return Steps(self, steps, at[: len(steps)])


class SmallSum(Sum):
    def __init__(self, x, bits):
        self.mine = self.send = x
        self.steps = [(b, "add", None) for b in range(bits)] + [("tensor", "norm", None)]


class Final:
    def __init__(self, sums, shapes, count, places):
        self.sums, self.shapes, self.count, self.places = sums, shapes, count, places
        self.at, self.flips = (0,), [0]

    @property
    def inputs(self):
        return [s.mine for s in self.sums]

    @property
    def outputs(self):
        return [(jax.ShapeDtypeStruct(s, f32), True) for s in self.shapes]

    @property
    def scratch(self):
        stage = [pltpu.VMEM(s.mine.shape, f32) for s in self.sums]
        return [pltpu.SemaphoreType.DMA((3, self.count)), pltpu.SemaphoreType.DMA((len(stage),))] + stage

    def build(self, ins, outs, scratch):
        put = lambda sources: self.places(sources, outs, bit_of(0))
        return [place_copies(put, ins, scratch[2:], 0, scratch[0], scratch[1])]

    def receive(self, outs):
        self.results = list(outs)


def place_copies(put, sources, held, flip, sems, load_sems):
    at = (lambda k, j: sems.at[k]) if load_sems is None else (lambda k, j: sems.at[k, j])
    there = [
        pltpu.make_async_remote_copy(
            src_ref=s, dst_ref=t, send_sem=at(0, j), recv_sem=at(1, j), device_id=partner(flip), device_id_type=MESH
        )
        for j, (s, t) in enumerate(put(sources))
    ]
    loads = [] if held is None else [
        pltpu.make_async_copy(s, h, sems.at[2] if load_sems is None else load_sems.at[j]) for j, (s, h) in enumerate(zip(sources, held))
    ]
    here = [pltpu.make_async_copy(s, t, at(2, j)) for j, (s, t) in enumerate(put(sources if held is None else held))]

    def begin():
        for c in there + (here if held is None else loads):
            c.start()

    def finish():
        for c in loads:
            c.wait()
        if held is not None:
            for c in here:
                c.start()
        for c in here + there:
            c.wait()

    return begin, finish


class Steps:
    def __init__(self, owner, steps, at):
        self.owner, self.steps, self.at = owner, steps, at
        self.flips = [s[0] for s in steps]
        self.same = owner.mine is owner.send
        reads = [k for _, k, _ in steps][0] in ("halve", "add", "norm")
        self.inputs = [owner.send] + ([owner.mine] if reads and not self.same else [])
        self.outputs, self.scratch = [], []
        rows, d = owner.send.shape
        local = True
        for n, (_, kind, _) in enumerate(steps):
            last = n == len(steps) - 1
            self.scratch.append(pltpu.SemaphoreType.DMA((3,)))
            if kind in ("halve", "add", "norm"):
                self.scratch += [pltpu.VMEM((rows, d), f32)] * (2 if local else 1)
                rows = rows // 2 if kind == "halve" else rows
                shapes = [(rows, d)] * (2 if kind == "halve" else 1)
                if last:
                    self.outputs += [(jax.ShapeDtypeStruct(s, f32), False) for s in shapes]
                local = False
            elif kind == "join":
                if local:
                    self.scratch.append(pltpu.VMEM((rows, d), f32))
                local = True
                rows *= 2
                self.outputs.append((jax.ShapeDtypeStruct((rows, d), f32), True))

    def build(self, ins, outs, scratch):
        outs, scratch = list(outs), list(scratch)
        send = ins[0]
        mine = ins[-1]
        events = []
        in_hbm = True
        for n, (flip, kind, bit) in enumerate(self.steps):
            last = n == len(self.steps) - 1
            sems = scratch.pop(0)
            rows = send.shape[0]
            if kind in ("halve", "add", "norm"):
                got = scratch.pop(0)
                held = scratch.pop(0) if in_hbm else mine
                fresh = kept = None
                if last:
                    fresh = outs.pop(0)
                    kept = outs.pop(0) if kind == "halve" else None
                elif kind == "halve":
                    r, v = held.shape[0] // 2, bit_of(bit)
                    fresh, kept = (held.at[pl.ds(pl.multiple_of(h * r, 8), r)] for h in (1 - v, v))
                else:
                    fresh = held
                events.append(self.reduce(kind, bit, flip, send, mine, in_hbm, got, held, fresh, kept, sems))
                send, mine, in_hbm = fresh, (fresh if kept is None else kept), False
            elif kind == "join":
                target = outs.pop(0)
                held = scratch.pop(0) if in_hbm else None
                put = lambda xs, target=target, bit=bit, rows=rows: [
                    (xs[0], target.at[pl.ds(pl.multiple_of(bit_of(bit) * rows, 8), rows)])
                ]
                events.append(self.copies(put, send, held, flip, sems))
                send = mine = target
                in_hbm = True
        return events

    @staticmethod
    def copies(put, send, held, flip, sems, load_sems=None):
        return place_copies(put, [send], None if held is None else [held], flip, sems, load_sems)

    @staticmethod
    def reduce(kind, bit, flip, send, mine, in_hbm, got, held, fresh, kept, sems):
        there = pltpu.make_async_remote_copy(
            src_ref=send, dst_ref=got, send_sem=sems.at[0], recv_sem=sems.at[1], device_id=partner(flip), device_id_type=MESH
        )
        load = pltpu.make_async_copy(mine, held, sems.at[2]) if in_hbm else None

        def add_half(out, half, r):
            base = half * r

            def step(j, size):
                rows = pl.ds(pl.multiple_of(base + j, 8), size)
                out[pl.ds(j, size), :] = held[rows, :] + got[rows, :]

            by_rows(r, step)

        def begin():
            there.start()
            if load is not None:
                load.start()

        def after():
            if kind == "halve":
                add_half(kept, bit_of(bit), held.shape[0] // 2)

        def finish():
            if load is not None:
                load.wait()
            there.wait()
            if kind == "halve":
                r = held.shape[0] // 2
                v = bit_of(bit)
                add_half(fresh, 1 - v, r)
            elif kind == "norm":
                row = lax.broadcasted_iota(jnp.int32, held.shape, 0)
                fresh[...] = held[...] + jnp.where(row < 4, got[...], 0.0)
            else:

                def step(j, size):
                    rows = pl.ds(j, size)
                    fresh[rows, :] = held[rows, :] + got[rows, :]

                by_rows(held.shape[0], step)

        return begin, finish, after

    def receive(self, outs):
        outs = list(outs)
        owner = self.owner
        for n, (_, kind, _) in enumerate(self.steps):
            last = n == len(self.steps) - 1
            if kind == "join":
                owner.mine = owner.send = outs.pop(0)
            elif last:
                owner.send = outs.pop(0)
                owner.mine = outs.pop(0) if kind == "halve" else owner.send


def call(
    kernel, *, grid, in_specs, out_specs, out_shape, scalars=0, scratch=(), deps=(), rides=(), collective=None, flops=0, nbytes=0, name=None, aliases=None
):
    single = not isinstance(out_shape, (list, tuple))
    out_specs = [out_specs] if single else list(out_specs)
    out_shape = [out_shape] if single else list(out_shape)
    n_in, n_out, n_scratch = scalars + len(in_specs), len(out_shape), len(scratch)
    anywhere = pl.BlockSpec(memory_space=pl.ANY)
    ride_in = [x for r in rides for x in r.inputs]
    ride_out = [o for r in rides for o in r.outputs]
    flips = list(dict.fromkeys(f for r in rides for f in r.flips))

    def body(*refs):
        refs = list(refs)
        cut = lambda n: [refs.pop(0) for _ in range(n)]
        ins, _, sources = cut(n_in), cut(len(deps)), cut(len(ride_in))
        outs, targets, held = cut(n_out), cut(len(ride_out)), cut(n_scratch)
        at_step, at_end = {}, []
        for r in rides:
            take = lambda refs, n: [refs.pop(0) for _ in range(n)]
            events = r.build(take(sources, len(r.inputs)), take(targets, len(r.outputs)), take(refs, len(r.scratch)))
            for n, (begin, finish, *after) in enumerate(events):
                at_step.setdefault(r.at[n], ([], []))[0].append(begin)
                if n + 1 < len(events):
                    step = at_step.setdefault(r.at[n + 1], ([], []))
                    step[0].append(finish)
                    step[1].extend(after)
                else:
                    at_end += [finish] + after
        if rides:

            @pl.when(pl.program_id(0) == 0)
            def _():
                barrier = pltpu.get_barrier_semaphore()
                for f in flips:
                    pl.semaphore_signal(barrier, inc=1, device_id=partner(f), device_id_type=MESH)
                pl.semaphore_wait(barrier, len(flips))

        for g, acts in at_step.items():

            @pl.when(pl.program_id(0) == g)
            def _(acts=acts):
                for act in acts[0] + acts[1]:
                    act()

        kernel(*ins, *outs, *held)
        if at_end:

            @pl.when(pl.program_id(0) == pl.num_programs(0) - 1)
            def _():
                for act in at_end:
                    act()

    params = dict(vmem_limit_bytes=VMEM_LIMIT)
    if rides:
        params.update(collective_id=collective, has_side_effects=True)

    def run(*args):
        outs = pl.pallas_call(
            body,
            grid_spec=pltpu.PrefetchScalarGridSpec(
                num_scalar_prefetch=scalars,
                grid=grid,
                in_specs=list(in_specs) + [anywhere] * (len(deps) + len(ride_in)),
                out_specs=out_specs + [anywhere if hbm else once(s.shape) for s, hbm in ride_out],
                scratch_shapes=list(scratch) + [s for r in rides for s in r.scratch],
            ),
            out_shape=out_shape + [s for s, _ in ride_out],
            compiler_params=pltpu.CompilerParams(**params),
            cost_estimate=pl.CostEstimate(flops=20 * flops, bytes_accessed=nbytes, transcendentals=0),
            input_output_aliases=aliases or {},
            name=name,
        )(*args, *deps, *ride_in)
        outs = list(outs)
        own, rest = outs[:n_out], outs[n_out:]
        for r in rides:
            r.receive(rest[: len(r.outputs)])
            rest = rest[len(r.outputs) :]
        return own[0] if single else own

    return run


def whole(shape):
    zeros = (0,) * len(shape)
    return pl.BlockSpec(shape, lambda *_: zeros, pipeline_mode=pl.Buffered(1))


def once(shape):
    zeros = (0,) * len(shape)
    return pl.BlockSpec(shape, lambda *_: zeros)


def hat_of(values):
    average = jnp.mean(values, axis=-1, keepdims=True)
    centered = values - average
    inverse = lax.rsqrt(jnp.mean(centered * centered, axis=-1, keepdims=True) + epsilon)
    return centered * inverse, inverse


def gelu_pair(h):
    a = jnp.abs(h) * np.float32(math.sqrt(0.5))
    t = 1.0 / (1.0 + np.float32(0.3275911) * a)
    bell = jnp.exp(-0.5 * (h * h))
    poly = np.float32(0.5 * 1.061405429) * t + np.float32(0.5 * -1.453152027)
    poly = poly * t + np.float32(0.5 * 1.421413741)
    poly = poly * t + np.float32(0.5 * -0.284496736)
    poly = poly * t + np.float32(0.5 * 0.254829592)
    tail = poly * t * bell
    phi = jnp.where(h >= 0, 1.0 - tail, tail)
    return h * phi, phi + h * bell * np.float32(1.0 / math.sqrt(2.0 * math.pi))


def add_to(ref, first, value):
    @pl.when(first)
    def _():
        ref[...] = value

    @pl.when(jnp.logical_not(first))
    def _():
        ref[...] += value


def mlp_tile(chunk, tok, g, up, upb, down, gains, biases, visit):
    hat, _ = hat_of(tok[...].astype(f32))
    gain = gains[1:2, :]
    normed = (hat * gain + biases[1:2, :]).astype(bf16)
    gt = g[...]
    d = tok.shape[1]
    up_bias = jnp.concatenate([upb[c : c + 1, :] for c in range(up.shape[1] // d)], axis=1)
    total = None
    back = None
    for c in range(up.shape[1] // chunk):
        sl = slice(c * chunk, (c + 1) * chunk)
        hidden = dot(normed, up[:, sl]) + up_bias[:, sl]
        act_grad = dot(gt, down[sl, :], NT)
        act, slope = gelu_pair(hidden)
        act = act.astype(bf16)
        hid_grad = (act_grad * slope).astype(bf16)
        p = dot(act, down[sl, :])
        e = dot(hid_grad, up[:, sl], NT)
        total = p if total is None else total + p
        back = e if back is None else back + e
        visit(sl, normed, gt, act, hid_grad)
    return hat, gt, total, back, gain


def mlp_own_kernel(chunk, tok, g, up, upb, down, gains, biases, part, share, keep_d, send_d, keep_u, send_u, small, upb_sum, ddown, dup):
    i = pl.program_id(0)

    @pl.when(i == 0)
    def _():
        dup[...] = jnp.zeros_like(dup)
        ddown[...] = jnp.zeros_like(ddown)
        small[...] = jnp.zeros_like(small)
        upb_sum[...] = jnp.zeros_like(upb_sum)

    def visit(sl, normed, gt, act, hid_grad):
        dup[:, sl] += dot(normed, hid_grad, TN)
        ddown[sl, :] += dot(act, gt, TN)
        upb_sum[:, sl] += jnp.sum(hid_grad.astype(f32), axis=0, keepdims=True)

    hat, gt, total, back, gain = mlp_tile(chunk, tok, g, up, upb, down, gains, biases, visit)
    part[...] = total
    share[...] = back * gain
    small[0:1, :] += jnp.sum(gt.astype(f32), axis=0, keepdims=True)
    small[1:2, :] += jnp.sum(back * hat, axis=0, keepdims=True)
    small[2:3, :] += jnp.sum(back, axis=0, keepdims=True)

    @pl.when(i == pl.num_programs(0) - 1)
    def _():
        d, wide = dup.shape
        core = bit_of(0)
        for down_out, up_out, half in ((keep_d, keep_u, core), (send_d, send_u, 1 - core)):
            rows = pl.multiple_of(half * (wide // 2), wide // 2)
            down_out[...] = ddown[pl.ds(rows, wide // 2), :]
            rows = pl.multiple_of(half * (d // 2), d // 2)
            for c in range(wide // d):
                up_out[c * (d // 2) : (c + 1) * (d // 2), :] = dup[pl.ds(rows, d // 2), c * d : (c + 1) * d]


def mlp_own(tok, g, up, upb, down, gains, biases, tile=512, chunk=768, deps=(), rides=(), collective=None):
    length, d = tok.shape
    wide = up.shape[1]
    rows = pl.BlockSpec((tile, d), lambda i, *_: (i, 0))
    return call(
        functools.partial(mlp_own_kernel, chunk),
        grid=(length // tile,),
        in_specs=[rows, rows, whole((d, wide)), whole((8, d)), whole((wide, d)), whole((2, d)), whole((2, d))],
        out_specs=[rows, rows, *[once((wide // 2, d))] * 4, once((8, d)), once((1, wide))],
        out_shape=[
            jax.ShapeDtypeStruct((length, d), f32),
            jax.ShapeDtypeStruct((length, d), f32),
            *[jax.ShapeDtypeStruct((wide // 2, d), f32)] * 4,
            jax.ShapeDtypeStruct((8, d), f32),
            jax.ShapeDtypeStruct((1, wide), f32),
        ],
        scratch=[pltpu.VMEM((wide, d), f32), pltpu.VMEM((d, wide), f32)],
        flops=12 * length * d * wide,
        nbytes=4 * length * d * 4,
        deps=deps,
        rides=rides,
        collective=collective,
        name="mlp_own",
    )(tok, g, up, upb, down, gains, biases)


def mlp_other_kernel(chunk, *refs):
    pieces, refs = refs[:12], refs[12:]
    tok, g, upb, gains, biases, part_in, share_in, part, share, w, ow, up, down = refs[:13]
    loaded, sems = refs[13:25], refs[25]

    @pl.when(pl.program_id(0) == 0)
    def _():
        loads = [pltpu.make_async_copy(a, b, sems.at[n]) for n, (a, b) in enumerate(zip(pieces, loaded))]
        for c in loads:
            c.start()
        for c in loads:
            c.wait()
        unpack(loaded, w, ow, up, down)

    nothing = lambda *_: None
    _, _, total, back, gain = mlp_tile(chunk, tok, g, up, upb, down, gains, biases, nothing)
    part[...] = part_in[...] + total
    share[...] = share_in[...] + back * gain


def mlp_other(pieces, tok, g, upb, gains, biases, part, share, shapes, tile=512, chunk=768, deps=(), rides=(), collective=None):
    length, d = tok.shape
    w, ow, up, down = [x.shape for x in shapes]
    rows = pl.BlockSpec((tile, d), lambda i: (i, 0))
    full = jax.ShapeDtypeStruct((length, d), f32)
    return call(
        functools.partial(mlp_other_kernel, chunk),
        grid=(length // tile,),
        in_specs=[pl.BlockSpec(memory_space=pl.ANY)] * 12 + [rows, rows, whole((8, d)), whole((2, d)), whole((2, d)), rows, rows],
        out_specs=[rows, rows, whole(w), whole(ow)],
        out_shape=[full, full, jax.ShapeDtypeStruct(w, bf16), jax.ShapeDtypeStruct(ow, bf16)],
        scratch=[pltpu.VMEM(up, bf16), pltpu.VMEM(down, bf16)] + [pltpu.VMEM(p.shape, f32) for p in pieces] + [pltpu.SemaphoreType.DMA((12,))],
        flops=8 * length * d * up[1],
        nbytes=4 * length * d * 4,
        deps=deps,
        rides=rides,
        collective=collective,
        name="mlp_other",
    )(*pieces, tok, g, upb, gains, biases, part, share)


def first_tokens(lens, places):
    first = jnp.zeros_like(places)
    end = lens[0, 0]
    for j in range(1, lens.shape[1]):
        first = jnp.where(places >= end, end, first)
        end = end + lens[0, j]
    return jnp.where(places >= end, places, first)


def turn(block, cosine, sine, sign):
    parts = []
    for h in range(block.shape[0] // HEAD):
        r = h * HEAD
        a = block[r : r + HALF, :]
        b = block[r + HALF : r + ROT, :]
        if sign > 0:
            parts += [a * cosine - b * sine, b * cosine + a * sine]
        else:
            parts += [a * cosine + b * sine, b * cosine - a * sine]
        parts.append(block[r + ROT : r + HEAD, :])
    return jnp.concatenate(parts, axis=0)


def project_tile(t, tile, bias_row, lens, tok, g, w, bias, ow, gains, biases, freq, own, q, qt, k, kpad, vpad, vone, do, dot_t, cosine, sine):
    rows = pl.ds(pl.multiple_of(t * tile, tile), tile)
    e = ow.shape[0]
    hat, _ = hat_of(tok[rows, :].astype(f32))
    normed = (hat * gains[0:1, :] + biases[0:1, :]).astype(bf16)
    places = t * tile + lax.broadcasted_iota(jnp.int32, (1, tile), 1)
    position = (places - first_tokens(lens, places)).astype(f32)
    theta = freq[:, 0:1] * position
    c = jnp.cos(theta)
    s = jnp.sin(theta)
    cosine[:, rows] = c
    sine[:, rows] = s
    row = bias[bias_row : bias_row + 1, :]
    cols = jnp.concatenate([row[:, :e], row[:, e : 2 * e], jnp.zeros((6, e), f32)], axis=0).T
    scale = HEAD ** (-0.5)
    query = turn(dot(w[0], normed, TT) + cols[:, 0:1], c, s, 1).astype(bf16) * scale
    qt[:, rows] = query
    q[rows, :] = query.T
    key = turn(dot(w[1], normed, TT), c, s, 1).astype(bf16)
    k[rows, :] = key.T
    value = (dot(w[2], normed, TT) + cols[:, 1:2]).astype(bf16)
    zero = jnp.zeros((HEAD, tile), bf16)
    if own:
        row = lax.broadcasted_iota(jnp.int32, (VROWS - HEAD, tile), 0)
        ones = jnp.where(row == 0, 1.0, 0.0).astype(bf16)
    for h in range(e // HEAD):
        sl = slice(h * HEAD, (h + 1) * HEAD)
        at, other = (0, HEAD) if h % 2 == 0 else (HEAD, 0)
        kpad[h, at : at + HEAD, rows] = key[sl, :]
        kpad[h, other : other + HEAD, rows] = zero
        vpad[h, at : at + HEAD, rows] = value[sl, :]
        vpad[h, other : other + HEAD, rows] = zero
        if own:
            vone[h, :HEAD, rows] = value[sl, :]
            vone[h, HEAD:, rows] = ones
    grad = dot(ow[...], g[rows, :], NT).astype(bf16)
    dot_t[:, rows] = grad
    do[rows, :] = grad.T


def low_parts(x):
    high = x.astype(bf16)
    rest = x - high.astype(f32)
    mid = rest.astype(bf16)
    return [high, mid, (rest - mid.astype(f32)).astype(bf16)]


FILLED = 1792


def over_tiles(q0, tk, step, carry):
    last = lax.div(q0, tk)
    first = jnp.where(q0 >= FILLED, last, 0)
    return lax.fori_loop(first, last + 1, step, carry)


VROWS = 80


def forward_tile(q0, tq, tk, first, places, qt, k, vone, ot, qpad, acc):
    heads = qt.shape[0] // HEAD
    zero = jnp.zeros((HEAD, tq), bf16)
    for h in range(heads):
        qh = qt[h * HEAD : (h + 1) * HEAD, pl.ds(q0, tq)]
        qpad[h] = jnp.concatenate([qh, zero] if h % 2 == 0 else [zero, qh], axis=0)
    acc[...] = jnp.zeros_like(acc)

    def step(j, peaks):
        k0 = pl.multiple_of(j * tk, tk)
        rows = k0 + lax.broadcasted_iota(jnp.int32, (tk, tq), 0)
        allowed = (rows >= first) & (rows <= places)
        scores, new, raised = [], [], []
        for h in range(heads):
            pair = (h // 2) * 128
            s = dot(k[pl.ds(k0, tk), pair : pair + 128], qpad[h])
            scores.append(jnp.where(allowed, s, -1e30))
        for h in range(heads):
            new.append(jnp.maximum(peaks[h], jnp.max(scores[h], axis=0, keepdims=True)))
            raised.append(jnp.exp(scores[h] - new[h]).astype(bf16))
        for h in range(heads):
            o = dot(vone[h, :, pl.ds(k0, tk)], raised[h])
            acc[h] = acc[h] * jnp.exp(peaks[h] - new[h]) + o
        return tuple(new)

    start = tuple(jnp.full((1, tq), -1e30, f32) for _ in range(heads))
    peaks = over_tiles(q0, tk, step, start)
    logs = []
    for h in range(heads):
        total = acc[h, HEAD : HEAD + 1, :]
        ot[h * HEAD : (h + 1) * HEAD, :] = acc[h, :HEAD, :] / total
        logs.append(peaks[h] + jnp.log(total))
    logs.append(jnp.zeros((8 - heads, tq), f32))
    ot[heads * HEAD :, :] = jnp.concatenate(logs, axis=0)


def backward_tile(q0, tq, tk, first, places, q, qt, k, kpad, vpad, do, dot_t, ot, cosine, sine, grads_q, dk, dv, dq, qa, da, cs, cd):
    heads = q.shape[1] // HEAD
    rows = pl.ds(q0, tq)
    deltas = [
        jnp.sum(ot[h * HEAD : (h + 1) * HEAD, :] * dot_t[h * HEAD : (h + 1) * HEAD, rows].astype(f32), axis=0, keepdims=True)
        for h in range(heads)
    ]
    deltas.append(jnp.zeros((8 - heads, tq), f32))
    stats = low_parts(ot[heads * HEAD :, :]) + low_parts(jnp.concatenate(deltas, axis=0))
    stats.append(jnp.zeros((128 - 48, tq), bf16))
    stat_cols = jnp.concatenate(stats, axis=0).T
    for r in range(heads // 2):
        pair = slice(r * 128, r * 128 + 128)
        qa[r, :, :128] = q[rows, pair]
        qa[r, :, 128:] = stat_cols
        da[r, :, :128] = do[rows, pair]
        da[r, :, 128:] = stat_cols
    dq[...] = jnp.zeros_like(dq)

    def step(j, carry):
        k0 = pl.multiple_of(j * tk, tk)
        ks = pl.ds(k0, tk)
        cols = k0 + lax.broadcasted_iota(jnp.int32, (tq, tk), 1)
        allowed = (cols >= first) & (cols <= places)
        probs, grads = [], []
        for h in range(heads):
            s = dot(qa[h // 2], jnp.concatenate([kpad[h, :, ks], cs[h]], axis=0))
            dp = dot(da[h // 2], jnp.concatenate([vpad[h, :, ks], cd[h]], axis=0))
            p = jnp.where(allowed, jnp.exp(s), 0.0)
            probs.append(p.astype(bf16))
            grads.append((p * dp).astype(bf16))
        for h in range(heads):
            sl = slice(h * HEAD, (h + 1) * HEAD)
            pair = slice((h // 2) * 128, (h // 2) * 128 + 128)
            dv[sl, ks] += dot(dot_t[sl, rows], probs[h])
            dk[sl, ks] += dot(qt[sl, rows], grads[h])
            dq[h] += dot(grads[h], k[ks, pair])
        return carry

    over_tiles(q0, tk, step, 0)
    scale = HEAD ** (-0.5)
    lane = lax.broadcasted_iota(jnp.int32, (tq, 128), 1)
    q_parts = [
        jnp.where(lane < HEAD, dq[2 * h], dq[2 * h + 1]).T * scale for h in range(heads // 2)
    ]
    grads_q[...] = turn(jnp.concatenate(q_parts, axis=0), cosine[:, rows], sine[:, rows], -1).astype(bf16)


def attention_kernel(tk, tile, own, bias_row, lens, tok_all, g_all, w, bias, ow, gains, biases, freq, *refs):
    refs = list(refs)
    cut = lambda n: [refs.pop(0) for _ in range(n)]
    if own:
        ot, ot_send, grads_q, grads_k, grads_v = cut(5)
    else:
        ot, grads_q, grads_k, grads_v = cut(4)
    q, qt, k, kpad, vpad, do, dot_t, cosine, sine, dk, dv, dq, qa, da, cs, cd = cut(16)
    tok, g, sems = cut(3)
    vone, qpad, acc = cut(3) if own else (None, None, None)
    i = pl.program_id(0)
    length = tok.shape[0]
    heads, tq, _ = dq.shape
    q0 = pl.multiple_of(i * tq, tq)

    @pl.when(i == 0)
    def _():
        loads = [pltpu.make_async_copy(a, b, sems.at[n]) for n, (a, b) in enumerate(((tok_all, tok), (g_all, g)))]
        for c in loads:
            c.start()
        dk[...] = jnp.zeros_like(dk)
        dv[...] = jnp.zeros_like(dv)
        row = lax.broadcasted_iota(jnp.int32, (128, tk), 0)
        for h in range(heads):
            cs[h] = jnp.where((row < 24) & (row % 8 == h), -1.0, 0.0).astype(bf16)
            cd[h] = jnp.where((row >= 24) & (row < 48) & (row % 8 == h), -1.0, 0.0).astype(bf16)

        for c in loads:
            c.wait()

        def some(t, c):
            project_tile(t, tile, bias_row, lens, tok, g, w, bias, ow, gains, biases, freq, own, q, qt, k, kpad, vpad, vone, do, dot_t, cosine, sine)
            return c

        lax.fori_loop(0, length // tile, some, 0)

    if own:
        places = q0 + lax.broadcasted_iota(jnp.int32, (1, tq), 1)
        forward_tile(q0, tq, tk, first_tokens(lens, places), places, qt, k, vone, ot, qpad, acc)
        ot_send[...] = ot[...]
    places = q0 + lax.broadcasted_iota(jnp.int32, (tq, 1), 0)
    backward_tile(
        q0, tq, tk, first_tokens(lens, places), places, q, qt, k, kpad, vpad, do, dot_t, ot, cosine, sine, grads_q, dk, dv, dq, qa, da, cs, cd
    )

    @pl.when(i == pl.num_programs(0) - 1)
    def _():
        grads_k[...] = turn(dk[...], cosine[...], sine[...], -1).astype(bf16)
        grads_v[...] = dv[...].astype(bf16)


def attention(bias_row, lens, tok, g, w, bias, ow, gains, biases, freq, ot=None, tq=256, tk=256, tile=512, deps=(), rides=(), collective=None):
    length, d = tok.shape
    e = w.shape[2]
    heads = e // HEAD
    own = ot is None
    cols = pl.BlockSpec((e, tq), lambda i, *_: (0, i))
    stat = pl.BlockSpec((e + 8, tq), lambda i, *_: (0, i))
    grad = jax.ShapeDtypeStruct((e, length), bf16)
    kept = jax.ShapeDtypeStruct((e + 8, length), f32)
    nat, tr, pad, angle = pltpu.VMEM((length, e), bf16), pltpu.VMEM((e, length), bf16), pltpu.VMEM((heads, 128, length), bf16), pltpu.VMEM((HALF, length), f32)
    scratch = [nat, tr, nat, pad, pad, nat, tr, angle, angle]
    scratch += [pltpu.VMEM((e, length), f32)] * 2 + [pltpu.VMEM((heads, tq, 128), f32)]
    scratch += [pltpu.VMEM((heads // 2, tq, 256), bf16)] * 2 + [pltpu.VMEM((heads, 128, tk), bf16)] * 2
    scratch += [pltpu.VMEM((length, d), bf16)] * 2 + [pltpu.SemaphoreType.DMA((2,))]
    if own:
        scratch += [pltpu.VMEM((heads, VROWS, length), bf16), pltpu.VMEM((heads, 128, tq), bf16), pltpu.VMEM((heads, VROWS, tq), f32)]
    return call(
        functools.partial(attention_kernel, tk, tile, own, bias_row),
        grid=(length // tq,),
        scalars=1,
        in_specs=[
            *[pl.BlockSpec(memory_space=pl.ANY)] * 2, whole((3, d, e)), whole((8, d)), whole((e, d)), whole((2, d)), whole((2, d)), whole((HALF, 128)),
        ] + ([] if own else [stat]),
        out_specs=([stat, stat] if own else []) + [cols, whole((e, length)), whole((e, length))],
        out_shape=([kept, kept] if own else []) + [grad, grad, grad],
        scratch=scratch,
        flops=8 * length * length * e,
        nbytes=20 * length * e,
        deps=deps,
        rides=rides,
        collective=collective,
        name="attention",
    )(lens, tok, g, w, bias, ow, gains, biases, freq, *([] if own else [ot]))


def merge_tile(tok, gq, gk, gv, ot, w, ow, gains, biases):
    hat, inverse = hat_of(tok[...].astype(f32))
    gain = gains[0:1, :]
    back = dot(gq[...], w[0], TT) + dot(gk[...], w[1], TT) + dot(gv[...], w[2], TT)
    low = ot[...].astype(bf16)
    return hat, inverse, gain, back, low, dot(low, ow[...], TN)


def merge_own_kernel(tok, g, gq, gk, gv, ot, w, ow, gains, biases, part_in, share_in, small_in, upb_in, part, share, keep_a, send_a, keep_b, send_b, small, dw, dow):
    i = pl.program_id(0)
    tile = tok.shape[0]
    e, d = ow.shape
    wide = upb_in.shape[1]

    @pl.when(i == 0)
    def _():
        dw[...] = jnp.zeros_like(dw)
        dow[...] = jnp.zeros_like(dow)
        small[...] = jnp.zeros_like(small)
        small[1:2, :] = small_in[1:2, :]
        small[3:4, :] = small_in[2:3, :]
        small[4:5, :] = small_in[0:1, :]
        for c in range(wide // d):
            small[5 + c : 6 + c, :] = upb_in[:, c * d : (c + 1) * d]

    hat, _, gain, back, low, out = merge_tile(tok, gq, gk, gv, ot, w, ow, gains, biases)
    normed = (hat * gain + biases[0:1, :]).astype(bf16)
    share[...] = share_in[...] + back * gain
    part[...] = part_in[...] + out
    dw[0] += dot(normed, gq[...], TT)
    dw[1] += dot(normed, gk[...], TT)
    dw[2] += dot(normed, gv[...], TT)
    dow[...] += dot(low, g[...])
    small[0:1, :] += jnp.sum(back * hat, axis=0, keepdims=True)
    small[2:3, :] += jnp.sum(back, axis=0, keepdims=True)
    ones = jnp.ones((8, tile), bf16)
    at = 5 + wide // d
    small[at : at + 1, :e] += dot(ones, gq[...], NT)[0:1]
    small[at : at + 1, e : 2 * e] += dot(ones, gv[...], NT)[0:1]

    @pl.when(i == pl.num_programs(0) - 1)
    def _():
        core = bit_of(0)
        quarter = d // 4
        for first, second, half in ((keep_a, keep_b, core), (send_a, send_b, 1 - core)):
            for c in range(3):
                ref, at = (first, c * quarter) if c < 2 else (second, 0)
                for s in range(2):
                    rows = pl.multiple_of(half * (2 * quarter) + s * quarter, quarter)
                    ref[at : at + quarter, s * e : (s + 1) * e] = dw[c, pl.ds(rows, quarter), :]
            rows = pl.multiple_of(half * (e // 2), e // 2)
            second[quarter:, :] = dow[pl.ds(rows, e // 2), :]


def merge_own(tok, g, gq, gk, gv, ot, w, ow, gains, biases, part, share, small, upb, tile=512, deps=(), rides=(), collective=None):
    length, d = tok.shape
    e = w.shape[2]
    wide = upb.shape[1]
    rows = pl.BlockSpec((tile, d), lambda i: (i, 0))
    cols = pl.BlockSpec((e, tile), lambda i: (0, i))
    full = jax.ShapeDtypeStruct((length, d), f32)
    half = jax.ShapeDtypeStruct((d // 2, d), f32)
    return call(
        merge_own_kernel,
        grid=(length // tile,),
        in_specs=[rows, rows, cols, cols, cols, cols, whole((3, d, e)), whole((e, d)), whole((2, d)), whole((2, d)), rows, rows, whole((8, d)), whole((1, wide))],
        out_specs=[rows, rows, *[once(half.shape)] * 4, once((8, d))],
        out_shape=[full, full, half, half, half, half, jax.ShapeDtypeStruct((8, d), f32)],
        scratch=[pltpu.VMEM((3, d, e), f32), pltpu.VMEM((e, d), f32)],
        flops=16 * length * d * e,
        nbytes=24 * length * d,
        deps=deps,
        rides=rides,
        collective=collective,
        name="merge_own",
    )(tok, g, gq, gk, gv, ot, w, ow, gains, biases, part, share, small, upb)


def merge_other_kernel(tok, g, gq, gk, gv, ot, w, ow, gains, biases, out_bias, down_bias, part_in, share_in, output, input_grad):
    hat, inverse, gain, back, _, out = merge_tile(tok, gq, gk, gv, ot, w, ow, gains, biases)
    shares = share_in[...] + back * gain
    inputs = tok[...].astype(f32)
    output[...] = (inputs + (part_in[...] + out) + out_bias[...].astype(f32) + down_bias[...].astype(f32)).astype(bf16)
    input_share = inverse * (
        shares
        - jnp.mean(shares, axis=-1, keepdims=True)
        - hat * jnp.mean(shares * hat, axis=-1, keepdims=True)
    )
    input_grad[...] = (g[...].astype(f32) + input_share).astype(bf16)


def merge_other(tok, g, gq, gk, gv, ot, w, ow, gains, biases, out_bias, down_bias, part, share, tile=512, deps=(), rides=(), collective=None):
    length, d = tok.shape
    e = w.shape[2]
    rows = pl.BlockSpec((tile, d), lambda i: (i, 0))
    cols = pl.BlockSpec((e, tile), lambda i: (0, i))
    full = jax.ShapeDtypeStruct((length, d), bf16)
    return call(
        merge_other_kernel,
        grid=(length // tile,),
        in_specs=[rows, rows, cols, cols, cols, cols, whole((3, d, e)), whole((e, d)), whole((2, d)), whole((2, d)), whole((1, d)), whole((1, d)), rows, rows],
        out_specs=[rows, rows],
        out_shape=[full, full],
        flops=8 * length * d * e,
        nbytes=24 * length * d,
        deps=deps,
        rides=rides,
        collective=collective,
        name="merge_other",
    )(tok, g, gq, gk, gv, ot, w, ow, gains, biases, out_bias[None], down_bias[None], part, share)


def pack_kernel(meta, w, ow, up, down, w_far, ow_far, up_far, down_far, upb, qkvb, one, two, three, four, bias_rows):
    d = ow.shape[1]
    e = w.shape[2]

    def half(refs, n, put):
        w, ow, up, down = refs
        r = down.shape[0] // 2
        put(down[n * r : (n + 1) * r, :])
        r = up.shape[0] // 2
        for c in range(up.shape[1] // d):
            put(up[n * r : (n + 1) * r, c * d : (c + 1) * d])
        r = w.shape[1] // 4
        for c in range(3):
            put(*[w[c, (2 * n + s) * r : (2 * n + s + 1) * r, :] for s in range(2)])
        r = ow.shape[0] // 2
        put(ow[n * r : (n + 1) * r, :])

    def into(*refs):
        place = [0, 0]

        def put(*blocks):
            ref, at = refs[place[0]], place[1]
            rows, lanes = blocks[0].shape
            for j, x in enumerate(blocks):
                ref[at : at + rows, j * lanes : (j + 1) * lanes] = x.astype(f32)
            place[1] = at + rows
            if place[1] == ref.shape[0]:
                place[:] = [place[0] + 1, 0]

        return put

    near = (w, ow, up, down)
    half(near, 0, into(one, two))
    half(near, 1, into(three))
    half((w_far, ow_far, up_far, down_far), 1, into(four))
    n = upb.shape[0]
    bias_rows[...] = jnp.zeros_like(bias_rows)
    bias_rows[:n, :] = upb[...].astype(f32)
    for c in range(2):
        bias_rows[n : n + 1, c * e : (c + 1) * e] = qkvb[c : c + 1, :].astype(f32)


def pack(meta, w, ow, up, down, upb, qkvb):
    _, d, e = w.shape
    wide = up.shape[1]
    rows = (wide + (wide // d) * d + 3 * d // 2 + e) // 8
    first = wide // 8 + d // 8
    sizes = [first, rows - first, rows, rows, 8]
    blocks = lambda n: [
        pl.BlockSpec((3, d // 4, e), lambda i, m: (0, m[n], 0)),
        pl.BlockSpec((e // 4, d), lambda i, m: (m[n], 0)),
        pl.BlockSpec((d // 4, wide), lambda i, m: (m[n], 0)),
        pl.BlockSpec((wide // 4, d), lambda i, m: (m[n], 0)),
    ]
    return call(
        pack_kernel,
        grid=(1,),
        scalars=1,
        in_specs=blocks(0) + blocks(1) + [whole((wide // d, d)), whole((2, e))],
        out_specs=[once((r, d)) for r in sizes],
        out_shape=[jax.ShapeDtypeStruct((r, d), f32) for r in sizes],
        name="pack",
    )(meta, w, ow, up, down, w, ow, up, down, upb.reshape(-1, d), qkvb)


def unpack(pieces, w, ow, up, down):
    d = ow.shape[1]
    e = w.shape[2]
    for n in range(4):
        core = lax.rem(bit_of(0) + n // 2, 2)
        parity = lax.rem(bit_of(1) + bit_of(2) + n % 2, 2)
        one, two, three = pieces[3 * n : 3 * n + 3]
        for m, refs in enumerate(((one, two), (three,))):
            at_piece = (parity * 2 + core) * 2 + m
            place = [0, 0]

            def take(rows):
                ref, at = refs[place[0]], place[1]
                place[1] = at + rows
                if place[1] == ref.shape[0]:
                    place[:] = [place[0] + 1, 0]
                return ref[at : at + rows, :].astype(bf16)

            rows = lambda r, sub=0, parts=1: pl.ds(pl.multiple_of((at_piece * parts + sub) * r, r), r)
            r = down.shape[0] // 8
            down[rows(r), :] = take(r)
            r = up.shape[0] // 8
            for c in range(up.shape[1] // d):
                up[rows(r), c * d : (c + 1) * d] = take(r)
            r = w.shape[1] // 16
            for c in range(3):
                x = take(r)
                for s in range(2):
                    w[c, rows(r, s, 2), :] = x[:, s * e : (s + 1) * e]
            r = ow.shape[0] // 8
            ow[rows(r), :] = take(r)


def swap(x, bit):
    n = lax.axis_size("dp")
    return lax.ppermute(x, "dp", [(i, i ^ (1 << bit)) for i in range(n)])


def across(x):
    return lax.ppermute(x, "tensor", [(0, 1), (1, 0)])


def tie(arrays, deps):
    n = len(arrays)
    anywhere = [pl.BlockSpec(memory_space=pl.ANY)] * n
    return call(
        lambda *refs: None,
        grid=(1,),
        in_specs=anywhere,
        out_specs=anywhere,
        out_shape=[jax.ShapeDtypeStruct(x.shape, x.dtype) for x in arrays],
        aliases={i: i for i in range(n)},
        deps=deps,
        name="tie",
    )(*arrays)


def down_places(d, wide):
    rows = wide // 2

    def places(sources, outs, core):
        return [(sources[0], outs[0].at[pl.ds(pl.multiple_of(core * rows, 8), rows)])]

    return [(wide, d)], 1, places


def up_places(d, wide):
    lanes, rows = wide // d, d // 2

    def places(sources, outs, core):
        to = pl.ds(pl.multiple_of(core * rows, 8), rows)
        return [(sources[0].at[pl.ds(s * rows, rows)], outs[0].at[to, pl.ds(s * d, d)]) for s in range(lanes)]

    return [(d, wide)], lanes, places


def attn_places(d, e):
    rows = d // 4

    def places(sources, outs, core):
        pairs = []
        for c in range(3):
            source, at = (sources[0], c * rows) if c < 2 else (sources[1], 0)
            for s in range(2):
                to = pl.ds(pl.multiple_of(core * (2 * rows) + s * rows, 8), rows)
                pairs.append((source.at[pl.ds(at, rows), pl.ds(s * e, e)], outs[0].at[c, to]))
        to = pl.ds(pl.multiple_of(core * (e // 2), 8), e // 2)
        pairs.append((sources[1].at[pl.ds(rows, e // 2)], outs[1].at[to]))
        return pairs

    return [(3, d, e), (e, d)], 7, places


def relay(rides, collective, deps=()):
    call(
        lambda *_: None,
        grid=(1,),
        in_specs=[],
        out_specs=[],
        out_shape=[],
        deps=deps,
        rides=rides,
        collective=collective,
        name="relay",
    )()


def per_device(
    tokens, lengths, qkv_weight, qkv_bias, out_weight, out_bias, up_weight, up_bias, down_weight, down_bias, norm_gains, norm_biases, cotangent
):
    length, d = tokens.shape
    e = qkv_weight.shape[2]
    wide = up_weight.shape[1]
    bits = lax.axis_size("dp").bit_length() - 1
    me = lax.axis_index("dp")
    quarter = lambda p: (((me >> 1) ^ (me >> 2) ^ p) & 1) * 2 + (me & 1)
    meta = jnp.stack([quarter(0), quarter(1)])
    freq = np.broadcast_to((rot_base ** (-(2.0 * np.arange(HALF)) / ROT)).astype(np.float32)[:, None], (HALF, 128))
    one, two, three, far_three, own_biases = pack(
        meta, qkv_weight, out_weight, up_weight, down_weight, up_bias, qkv_bias
    )
    send = Sends([(one, "tensor"), (own_biases, "tensor")], [(0, 1), (two, "tensor")], at=(0, 2))
    part, share, keep_d, send_d, keep_u, send_u, small, d_upb = mlp_own(
        tokens, cotangent, up_weight, own_biases, down_weight, norm_gains, norm_biases, rides=[send], collective=1
    )
    one, other_biases, near_one, two = send.got
    order = list(range(1, bits))
    crossed = [order[1], order[0]] + order[2:]
    sum_d, sum_u = Sum(keep_d, send_d, order), Sum(keep_u, send_u, crossed)
    send = Sends((three, "tensor"), (far_three, "tensor"), (one, 0), (two, 0), (near_one, 0))
    late = Sends((two, 1), at=(5,))
    ot, ot_send, gq, gk, gv = attention(
        wide // d, lengths, tokens, cotangent, qkv_weight, own_biases, out_weight, norm_gains, norm_biases, freq,
        rides=[sum_d.take(0, 1, 4, 5), sum_u.take(0, 1, 4, 5), send, late], collective=2,
    )
    three, near_three, core_one, core_two, core_near_one = send.got
    (near_two,) = late.got
    other_ot = across(ot_send)
    send = Sends((near_three, 0), (near_two, 0), (three, 0))
    part, share, keep_a, send_a, keep_b, send_b, small = merge_own(
        tokens, cotangent, gq, gk, gv, ot, qkv_weight, out_weight, norm_gains, norm_biases, part, share, small, d_upb,
        rides=[send, sum_d.take(0), sum_u.take(0)], collective=3,
    )
    core_near_three, core_near_two, core_three = send.got
    sum_a, sum_b, sum_s = Sum(keep_a, send_a, order), Sum(keep_b, send_b, crossed), SmallSum(small, bits)
    pieces = [one, two, three, near_one, near_two, near_three]
    pieces += [core_one, core_two, core_three, core_near_one, core_near_two, core_near_three]
    part, share, other_w, other_ow = mlp_other(
        pieces, tokens, cotangent, other_biases, norm_gains, norm_biases, part, share, [qkv_weight, out_weight, up_weight, down_weight],
        rides=[sum_s.take(0, 1), sum_d.take(0, 1), sum_u.take(0, 1), sum_a.take(0), sum_b.take(0)], collective=4,
    )
    at = 7
    sums = [sum_d, sum_u]
    while not all(s.done for s in sums):
        relay([s.take(0) for s in sums if not s.done], at)
        at += 1
    final_d, final_u = Final([sum_d], *down_places(d, wide)), Final([sum_u], *up_places(d, wide))
    (other_ot,) = tie([other_ot], [part])
    gq, gk, gv = attention(
        wide // d, lengths, tokens, cotangent, other_w, other_biases, other_ow, norm_gains, norm_biases, freq, other_ot,
        rides=[sum_s.take(0, 2, 3), sum_a.take(0, 2, 3, 5, 6), sum_b.take(0, 2, 3, 5, 6), final_d, final_u], collective=5,
    )
    (d_down,), (d_up,) = final_d.results, final_u.results
    sums = [sum_a, sum_b]
    while not all(len(s.steps) < 2 for s in sums):
        relay([s.take(0) for s in sums], at)
        at += 1
    output, input_grad = merge_other(
        tokens, cotangent, gq, gk, gv, other_ot, other_w, other_ow, norm_gains, norm_biases, out_bias, down_bias, part, share,
        rides=[s.take(0) for s in sums + [sum_s] if not s.done], collective=6,
    )
    final = Final(sums, *attn_places(d, e))
    relay([final] + [s.take(0) for s in [sum_s] if not s.done], at)
    at += 1
    while not sum_s.done:
        relay([sum_s.take(0)], at)
        at += 1
    d_qkv, d_out = final.results
    small = sum_s.mine
    rest = small[5:].reshape(-1)
    return (
        output, input_grad, d_qkv, rest[wide : wide + 2 * e].reshape(2, e), d_out, small[4], d_up, rest[:wide], d_down, small[4], small[:2], small[2:4],
    )


def solution(mesh):
    in_specs = (
        P("dp", None), P("dp", None), P(None, None, "tensor"), P(None, "tensor"), P("tensor", None), P(), P(None, "tensor"),
        P("tensor"), P("tensor", None), P(), P(), P(), P("dp", None),
    )
    out_specs = (
        P("dp", None), P("dp", None), P(None, None, "tensor"), P(None, "tensor"), P("tensor", None), P(), P(None, "tensor"),
        P("tensor"), P("tensor", None), P(), P(), P(),
    )
    return jax.shard_map(per_device, mesh=mesh, in_specs=in_specs, out_specs=out_specs, check_vma=False)
```

```python
import functools
import math

import jax
import jax.numpy as jnp
import numpy as np
from jax import lax
from jax.experimental import pallas as pl
from jax.experimental.pallas import tpu as pltpu
from jax.sharding import PartitionSpec as P

HEAD = 64
ROT = 16
HALF = ROT // 2
epsilon = 1e-05
rot_base = 10000.0
f32 = jnp.float32
bf16 = jnp.bfloat16
NN = (((1,), (0,)), ((), ()))
NT = (((1,), (1,)), ((), ()))
TN = (((0,), (0,)), ((), ()))
TT = (((0,), (1,)), ((), ()))
VMEM_LIMIT = 60 * 2**20


def dot(a, b, dims=NN):
    return lax.dot_general(a, b, dims, preferred_element_type=f32)


MESH = pl.DeviceIdType.MESH


def bit_of(b):
    return lax.rem(lax.div(lax.axis_index("dp"), 1 << b), 2)


def partner(flip):
    if flip == "tensor":
        return {"tensor": 1 - lax.axis_index("tensor")}
    return {"dp": lax.axis_index("dp") + (1 - 2 * bit_of(flip)) * (1 << flip)}


def by_rows(rows, step):
    size = next(c for c in (96, 48, 24, 8, rows) if rows % c == 0)
    if rows == size:
        step(0, size)
    else:
        lax.fori_loop(0, rows // size, lambda j, c: (step(pl.multiple_of(j * size, 8), size), c)[1], 0)


class Sends:
    def __init__(self, *phases, at=(0,)):
        self.at = at
        self.phases = phases if isinstance(phases[0], list) else [list(phases)]
        moves = [m for phase in self.phases for m in phase]
        self.flips = [flip for _, flip in moves]
        self.inputs = [x for x, _ in moves if not isinstance(x, int)]
        shapes = []
        for x, _ in moves:
            shapes.append(shapes[x] if isinstance(x, int) else jax.ShapeDtypeStruct(x.shape, x.dtype))
        self.outputs = [(s, True) for s in shapes]
        self.scratch = [pltpu.SemaphoreType.DMA((2, len(moves)))]

    def build(self, ins, outs, scratch, _):
        sems, ins, events, j = scratch[0], list(ins), [], 0
        for phase in self.phases:
            copies = []
            for x, flip in phase:
                source = outs[x] if isinstance(x, int) else ins.pop(0)
                copies.append(
                    pltpu.make_async_remote_copy(
                        src_ref=source, dst_ref=outs[j], send_sem=sems.at[0, j], recv_sem=sems.at[1, j], device_id=partner(flip), device_id_type=MESH
                    )
                )
                j += 1

            def begin(copies=copies):
                for c in copies:
                    c.start()

            def finish(copies=copies):
                for c in copies:
                    c.wait()

            events.append((begin, finish))
        return events

    def receive(self, outs):
        self.got = list(outs)


class Held:
    def __init__(self, place, shape):
        self.place, self.shape = place, shape


class Sum:
    def __init__(self, keep, send, order, whole=False):
        self.mine, self.send = keep, send
        halved = [b for j, b in enumerate(order[:-1] if whole else order) if keep.shape[0] % (16 << j) == 0]
        way = [0] + halved
        self.steps = [(way[j], "halve", b) for j, b in enumerate(halved)] + [(way[-1], "add", None)]
        self.steps += [(b, "add", None) for b in order if b not in halved]
        self.steps += [(b, "join", b) for b in reversed(halved)]

    @property
    def done(self):
        return not self.steps

    def take(self, *at):
        steps, self.steps = self.steps[: len(at)], self.steps[len(at) :]
        return Steps(self, steps, at[: len(steps)])


class SmallSum(Sum):
    def __init__(self, x, bits):
        self.mine = self.send = x
        self.steps = [(b, "add", None) for b in range(bits)] + [("tensor", "norm", None)]


class Final:
    def __init__(self, sums, shapes, count, places):
        self.sums, self.shapes, self.count, self.places = sums, shapes, count, places
        self.at, self.flips = (0,), [0]

    @property
    def inputs(self):
        return [s.mine for s in self.sums]

    @property
    def outputs(self):
        return [(jax.ShapeDtypeStruct(s, f32), True) for s in self.shapes]

    @property
    def scratch(self):
        stage = [pltpu.VMEM(s.mine.shape, f32) for s in self.sums]
        return [pltpu.SemaphoreType.DMA((3, self.count)), pltpu.SemaphoreType.DMA((len(stage),))] + stage

    def build(self, ins, outs, scratch, _):
        put = lambda sources: self.places(sources, outs, bit_of(0))
        return [place_copies(put, ins, scratch[2:], 0, scratch[0], scratch[1])]

    def receive(self, outs):
        self.results = list(outs)


def place_copies(put, sources, held, flip, sems, load_sems):
    at = (lambda k, j: sems.at[k]) if load_sems is None else (lambda k, j: sems.at[k, j])
    there = [
        pltpu.make_async_remote_copy(
            src_ref=s, dst_ref=t, send_sem=at(0, j), recv_sem=at(1, j), device_id=partner(flip), device_id_type=MESH
        )
        for j, (s, t) in enumerate(put(sources))
    ]
    loads = [] if held is None else [
        pltpu.make_async_copy(s, h, sems.at[2] if load_sems is None else load_sems.at[j]) for j, (s, h) in enumerate(zip(sources, held))
    ]
    here = [pltpu.make_async_copy(s, t, at(2, j)) for j, (s, t) in enumerate(put(sources if held is None else held))]

    def begin():
        for c in there + (here if held is None else loads):
            c.start()

    def finish():
        for c in loads:
            c.wait()
        if held is not None:
            for c in here:
                c.start()
        for c in here + there:
            c.wait()

    return begin, finish


class Steps:
    def __init__(self, owner, steps, at):
        self.owner, self.steps, self.at = owner, steps, at
        self.flips = [s[0] for s in steps]
        self.same = owner.mine is owner.send
        reads = [k for _, k, _ in steps][0] in ("halve", "add", "norm")
        self.inputs = [owner.send] + ([owner.mine] if reads and not self.same else [])
        self.outputs, self.scratch = [], []
        rows, d = owner.send.shape
        self.places = None
        local = True
        if isinstance(owner.send, Held):
            self.places, self.inputs, local = (owner.send.place, owner.mine.place), [], False
        for n, (_, kind, _) in enumerate(steps):
            last = n == len(steps) - 1
            self.scratch.append(pltpu.SemaphoreType.DMA((3,)))
            if kind in ("halve", "add", "norm"):
                self.scratch += [pltpu.VMEM((rows, d), f32)] * (2 if local else 1)
                rows = rows // 2 if kind == "halve" else rows
                shapes = [(rows, d)] * (2 if kind == "halve" else 1)
                if last:
                    self.outputs += [(jax.ShapeDtypeStruct(s, f32), False) for s in shapes]
                local = False
            elif kind == "join":
                if local:
                    self.scratch.append(pltpu.VMEM((rows, d), f32))
                local = True
                rows *= 2
                self.outputs.append((jax.ShapeDtypeStruct((rows, d), f32), True))

    def build(self, ins, outs, scratch, kernel_scratch):
        outs, scratch = list(outs), list(scratch)
        if self.places is not None:
            ins = [kernel_scratch[p] for p in self.places]
        send = ins[0]
        mine = ins[-1]
        events = []
        in_hbm = self.places is None
        for n, (flip, kind, bit) in enumerate(self.steps):
            last = n == len(self.steps) - 1
            sems = scratch.pop(0)
            rows = send.shape[0]
            if kind in ("halve", "add", "norm"):
                got = scratch.pop(0)
                held = scratch.pop(0) if in_hbm else mine
                fresh = kept = None
                if last:
                    fresh = outs.pop(0)
                    kept = outs.pop(0) if kind == "halve" else None
                elif kind == "halve":
                    r, v = held.shape[0] // 2, bit_of(bit)
                    fresh, kept = (held.at[pl.ds(pl.multiple_of(h * r, 8), r)] for h in (1 - v, v))
                else:
                    fresh = held
                events.append(self.reduce(kind, bit, flip, send, mine, in_hbm, got, held, fresh, kept, sems))
                send, mine, in_hbm = fresh, (fresh if kept is None else kept), False
            elif kind == "join":
                target = outs.pop(0)
                held = scratch.pop(0) if in_hbm else None
                put = lambda xs, target=target, bit=bit, rows=rows: [
                    (xs[0], target.at[pl.ds(pl.multiple_of(bit_of(bit) * rows, 8), rows)])
                ]
                events.append(self.copies(put, send, held, flip, sems))
                send = mine = target
                in_hbm = True
        return events

    @staticmethod
    def copies(put, send, held, flip, sems, load_sems=None):
        return place_copies(put, [send], None if held is None else [held], flip, sems, load_sems)

    @staticmethod
    def reduce(kind, bit, flip, send, mine, in_hbm, got, held, fresh, kept, sems):
        there = pltpu.make_async_remote_copy(
            src_ref=send, dst_ref=got, send_sem=sems.at[0], recv_sem=sems.at[1], device_id=partner(flip), device_id_type=MESH
        )
        load = pltpu.make_async_copy(mine, held, sems.at[2]) if in_hbm else None

        def add_half(out, half, r):
            base = half * r

            def step(j, size):
                rows = pl.ds(pl.multiple_of(base + j, 8), size)
                out[pl.ds(j, size), :] = held[rows, :] + got[rows, :]

            by_rows(r, step)

        def begin():
            there.start()
            if load is not None:
                load.start()

        def after():
            if kind == "halve":
                add_half(kept, bit_of(bit), held.shape[0] // 2)

        def finish():
            if load is not None:
                load.wait()
            there.wait()
            if kind == "halve":
                r = held.shape[0] // 2
                v = bit_of(bit)
                add_half(fresh, 1 - v, r)
            elif kind == "norm":
                row = lax.broadcasted_iota(jnp.int32, held.shape, 0)
                fresh[...] = held[...] + jnp.where(row < 4, got[...], 0.0)
            else:

                def step(j, size):
                    rows = pl.ds(j, size)
                    fresh[rows, :] = held[rows, :] + got[rows, :]

                by_rows(held.shape[0], step)

        return begin, finish, after

    def receive(self, outs):
        outs = list(outs)
        owner = self.owner
        for n, (_, kind, _) in enumerate(self.steps):
            last = n == len(self.steps) - 1
            if kind == "join":
                owner.mine = owner.send = outs.pop(0)
            elif last:
                owner.send = outs.pop(0)
                owner.mine = outs.pop(0) if kind == "halve" else owner.send


def call(
    kernel, *, grid, in_specs, out_specs, out_shape, scalars=0, scratch=(), deps=(), rides=(), collective=None, flops=0, nbytes=0, name=None, aliases=None
):
    single = not isinstance(out_shape, (list, tuple))
    out_specs = [out_specs] if single else list(out_specs)
    out_shape = [out_shape] if single else list(out_shape)
    n_in, n_out, n_scratch = scalars + len(in_specs), len(out_shape), len(scratch)
    anywhere = pl.BlockSpec(memory_space=pl.ANY)
    ride_in = [x for r in rides for x in r.inputs]
    ride_out = [o for r in rides for o in r.outputs]
    flips = list(dict.fromkeys(f for r in rides for f in r.flips))

    def body(*refs):
        refs = list(refs)
        cut = lambda n: [refs.pop(0) for _ in range(n)]
        ins, _, sources = cut(n_in), cut(len(deps)), cut(len(ride_in))
        outs, targets, held = cut(n_out), cut(len(ride_out)), cut(n_scratch)
        at_step, at_end = {}, []
        for r in rides:
            take = lambda refs, n: [refs.pop(0) for _ in range(n)]
            events = r.build(take(sources, len(r.inputs)), take(targets, len(r.outputs)), take(refs, len(r.scratch)), held)
            for n, (begin, finish, *after) in enumerate(events):
                at_step.setdefault(r.at[n], ([], []))[0].append(begin)
                if n + 1 < len(events):
                    step = at_step.setdefault(r.at[n + 1], ([], []))
                    step[0].append(finish)
                    step[1].extend(after)
                else:
                    at_end += [finish] + after
        if rides:

            @pl.when(pl.program_id(0) == 0)
            def _():
                barrier = pltpu.get_barrier_semaphore()
                for f in flips:
                    pl.semaphore_signal(barrier, inc=1, device_id=partner(f), device_id_type=MESH)
                pl.semaphore_wait(barrier, len(flips))

        for g, acts in at_step.items():

            @pl.when(pl.program_id(0) == g)
            def _(acts=acts):
                for act in acts[0] + acts[1]:
                    act()

        kernel(*ins, *outs, *held)
        if at_end:

            @pl.when(pl.program_id(0) == pl.num_programs(0) - 1)
            def _():
                for act in at_end:
                    act()

    params = dict(vmem_limit_bytes=VMEM_LIMIT)
    if rides:
        params.update(collective_id=collective, has_side_effects=True)

    def run(*args):
        outs = pl.pallas_call(
            body,
            grid_spec=pltpu.PrefetchScalarGridSpec(
                num_scalar_prefetch=scalars,
                grid=grid,
                in_specs=list(in_specs) + [anywhere] * (len(deps) + len(ride_in)),
                out_specs=out_specs + [anywhere if hbm else once(s.shape) for s, hbm in ride_out],
                scratch_shapes=list(scratch) + [s for r in rides for s in r.scratch],
            ),
            out_shape=out_shape + [s for s, _ in ride_out],
            compiler_params=pltpu.CompilerParams(**params),
            cost_estimate=pl.CostEstimate(flops=20 * flops, bytes_accessed=nbytes, transcendentals=0),
            input_output_aliases=aliases or {},
            name=name,
        )(*args, *deps, *ride_in)
        outs = list(outs)
        own, rest = outs[:n_out], outs[n_out:]
        for r in rides:
            r.receive(rest[: len(r.outputs)])
            rest = rest[len(r.outputs) :]
        return own[0] if single else own

    return run


def whole(shape):
    zeros = (0,) * len(shape)
    return pl.BlockSpec(shape, lambda *_: zeros, pipeline_mode=pl.Buffered(1))


def once(shape):
    zeros = (0,) * len(shape)
    return pl.BlockSpec(shape, lambda *_: zeros)


def hat_of(values):
    average = jnp.mean(values, axis=-1, keepdims=True)
    centered = values - average
    inverse = lax.rsqrt(jnp.mean(centered * centered, axis=-1, keepdims=True) + epsilon)
    return centered * inverse, inverse


def gelu_pair(h):
    a = jnp.abs(h) * np.float32(math.sqrt(0.5))
    t = 1.0 / (1.0 + np.float32(0.3275911) * a)
    bell = jnp.exp(-0.5 * (h * h))
    poly = np.float32(0.5 * 1.061405429) * t + np.float32(0.5 * -1.453152027)
    poly = poly * t + np.float32(0.5 * 1.421413741)
    poly = poly * t + np.float32(0.5 * -0.284496736)
    poly = poly * t + np.float32(0.5 * 0.254829592)
    tail = poly * t * bell
    phi = jnp.where(h >= 0, 1.0 - tail, tail)
    return h * phi, phi + h * bell * np.float32(1.0 / math.sqrt(2.0 * math.pi))


def add_to(ref, first, value):
    @pl.when(first)
    def _():
        ref[...] = value

    @pl.when(jnp.logical_not(first))
    def _():
        ref[...] += value


def mlp_tile(chunk, tok, g, up, upb, down, gains, biases, visit):
    hat, _ = hat_of(tok[...].astype(f32))
    gain = gains[1:2, :]
    normed = (hat * gain + biases[1:2, :]).astype(bf16)
    gt = g[...]
    d = tok.shape[1]
    up_bias = jnp.concatenate([upb[c : c + 1, :] for c in range(up.shape[1] // d)], axis=1)
    total = None
    back = None
    for c in range(up.shape[1] // chunk):
        sl = slice(c * chunk, (c + 1) * chunk)
        hidden = dot(normed, up[:, sl]) + up_bias[:, sl]
        act_grad = dot(gt, down[sl, :], NT)
        act, slope = gelu_pair(hidden)
        act = act.astype(bf16)
        hid_grad = (act_grad * slope).astype(bf16)
        p = dot(act, down[sl, :])
        e = dot(hid_grad, up[:, sl], NT)
        total = p if total is None else total + p
        back = e if back is None else back + e
        visit(sl, normed, gt, act, hid_grad)
    return hat, gt, total, back, gain


def mlp_own_kernel(tok, g, up, upb, down, gains, biases, part, share, keep_a, send_a, keep_b, send_b, small, upb_sum, dup, ddown, part_s, share_s, *early):
    i = pl.program_id(0)
    tiles = pl.num_programs(0) // 2
    chunk, t = lax.div(i, tiles), lax.rem(i, tiles)
    tile, d = tok.shape

    @pl.when(i == 0)
    def _():
        small[...] = jnp.zeros_like(small)
        upb_sum[...] = jnp.zeros_like(upb_sum)
        small[0:1, :] = jnp.zeros_like(small[0:1, :])

    @pl.when(t == 0)
    def _():
        dup[...] = jnp.zeros_like(dup)
        ddown[...] = jnp.zeros_like(ddown)

    hat, _ = hat_of(tok[...].astype(f32))
    gain = gains[1:2, :]
    normed = (hat * gain + biases[1:2, :]).astype(bf16)
    gt = g[...]
    hidden = dot(normed, up[...]) + upb[pl.ds(chunk, 1), :]
    act_grad = dot(gt, down[...], NT)
    act, slope = gelu_pair(hidden)
    act = act.astype(bf16)
    hid_grad = (act_grad * slope).astype(bf16)
    total = dot(act, down[...])
    back = dot(hid_grad, up[...], NT)
    dup[...] += dot(normed, hid_grad, TN)
    ddown[...] += dot(act, gt, TN)
    upb_sum[pl.ds(chunk, 1), :] += jnp.sum(hid_grad.astype(f32), axis=0, keepdims=True)
    small[1:2, :] += jnp.sum(back * hat, axis=0, keepdims=True)
    small[2:3, :] += jnp.sum(back, axis=0, keepdims=True)
    rows = pl.ds(pl.multiple_of(t * tile, tile), tile)

    def split(first, second, first_send, second_send):
        core = bit_of(0)
        for a, b, half in ((first, second, core), (first_send, second_send, 1 - core)):
            at = pl.ds(pl.multiple_of(half * (d // 2), d // 2), d // 2)
            a[...] = ddown[at, :]
            b[...] = dup[at, :]

    @pl.when(chunk == 0)
    def _():
        small[0:1, :] += jnp.sum(gt.astype(f32), axis=0, keepdims=True)
        part_s[rows, :] = total
        share_s[rows, :] = back

        @pl.when(t == tiles - 1)
        def _():
            split(early[0], early[2], early[1], early[3])

    @pl.when(chunk == 1)
    def _():
        part[...] = part_s[rows, :] + total
        share[...] = (share_s[rows, :] + back) * gain

        @pl.when(t == tiles - 1)
        def _():
            split(keep_a, keep_b, send_a, send_b)


EARLY = 4


def mlp_own(tok, g, up, upb, down, gains, biases, tile=512, deps=(), rides=(), collective=None):
    length, d = tok.shape
    wide = up.shape[1]
    tiles = length // tile
    rows = pl.BlockSpec((tile, d), lambda i: (lax.rem(i, tiles), 0))
    out_rows = pl.BlockSpec((tile, d), lambda i: (jnp.maximum(i - tiles, 0), 0))
    half = jax.ShapeDtypeStruct((d // 2, d), f32)
    full = jax.ShapeDtypeStruct((length, d), f32)
    eight = jax.ShapeDtypeStruct((8, d), f32)
    big = pltpu.VMEM((length, d), f32)
    return call(
        mlp_own_kernel,
        grid=(2 * tiles,),
        in_specs=[
            rows, rows, pl.BlockSpec((d, wide // 2), lambda i: (0, lax.div(i, tiles))), whole((8, d)),
            pl.BlockSpec((wide // 2, d), lambda i: (lax.div(i, tiles), 0)), whole((2, d)), whole((2, d)),
        ],
        out_specs=[out_rows, out_rows, *[once(half.shape)] * 4, once((8, d)), once((8, d))],
        out_shape=[full, full, half, half, half, half, eight, eight],
        scratch=[pltpu.VMEM((d, wide // 2), f32), pltpu.VMEM((wide // 2, d), f32), big, big] + [pltpu.VMEM(half.shape, f32)] * 4,
        flops=12 * length * d * wide,
        nbytes=4 * length * d * 4,
        deps=deps,
        rides=rides,
        collective=collective,
        name="mlp_own",
    )(tok, g, up, upb, down, gains, biases)


def mlp_other_kernel(chunk, *refs):
    pieces, refs = refs[:12], refs[12:]
    tok, g, upb, gains, biases, part_in, share_in, part, share, w, ow, up, down = refs[:13]
    loaded, sems = refs[13:25], refs[25]

    @pl.when(pl.program_id(0) == 0)
    def _():
        loads = [pltpu.make_async_copy(a, b, sems.at[n]) for n, (a, b) in enumerate(zip(pieces, loaded))]
        for c in loads:
            c.start()
        for c in loads:
            c.wait()
        unpack(loaded, w, ow, up, down)

    nothing = lambda *_: None
    _, _, total, back, gain = mlp_tile(chunk, tok, g, up, upb, down, gains, biases, nothing)
    part[...] = part_in[...] + total
    share[...] = share_in[...] + back * gain


def mlp_other(pieces, tok, g, upb, gains, biases, part, share, shapes, tile=512, chunk=768, deps=(), rides=(), collective=None):
    length, d = tok.shape
    w, ow, up, down = [x.shape for x in shapes]
    rows = pl.BlockSpec((tile, d), lambda i: (i, 0))
    full = jax.ShapeDtypeStruct((length, d), f32)
    return call(
        functools.partial(mlp_other_kernel, chunk),
        grid=(length // tile,),
        in_specs=[pl.BlockSpec(memory_space=pl.ANY)] * 12 + [rows, rows, whole((8, d)), whole((2, d)), whole((2, d)), rows, rows],
        out_specs=[rows, rows, whole(w), whole(ow)],
        out_shape=[full, full, jax.ShapeDtypeStruct(w, bf16), jax.ShapeDtypeStruct(ow, bf16)],
        scratch=[pltpu.VMEM(up, bf16), pltpu.VMEM(down, bf16)] + [pltpu.VMEM(p.shape, f32) for p in pieces] + [pltpu.SemaphoreType.DMA((12,))],
        flops=8 * length * d * up[1],
        nbytes=4 * length * d * 4,
        deps=deps,
        rides=rides,
        collective=collective,
        name="mlp_other",
    )(*pieces, tok, g, upb, gains, biases, part, share)


def first_tokens(lens, places):
    first = jnp.zeros_like(places)
    end = lens[0, 0]
    for j in range(1, lens.shape[1]):
        first = jnp.where(places >= end, end, first)
        end = end + lens[0, j]
    return jnp.where(places >= end, places, first)


def turn(block, cosine, sine, sign):
    parts = []
    for h in range(block.shape[0] // HEAD):
        r = h * HEAD
        a = block[r : r + HALF, :]
        b = block[r + HALF : r + ROT, :]
        if sign > 0:
            parts += [a * cosine - b * sine, b * cosine + a * sine]
        else:
            parts += [a * cosine + b * sine, b * cosine - a * sine]
        parts.append(block[r + ROT : r + HEAD, :])
    return jnp.concatenate(parts, axis=0)


def project_tile(t, tile, bias_row, lens, tok, g, w, bias, ow, gains, biases, freq, own, q, qt, k, kpad, vpad, vone, do, dot_t, cosine, sine):
    rows = pl.ds(pl.multiple_of(t * tile, tile), tile)
    e = ow.shape[0]
    hat, _ = hat_of(tok[rows, :].astype(f32))
    normed = (hat * gains[0:1, :] + biases[0:1, :]).astype(bf16)
    places = t * tile + lax.broadcasted_iota(jnp.int32, (1, tile), 1)
    position = (places - first_tokens(lens, places)).astype(f32)
    theta = freq[:, 0:1] * position
    c = jnp.cos(theta)
    s = jnp.sin(theta)
    cosine[:, rows] = c
    sine[:, rows] = s
    row = bias[bias_row : bias_row + 1, :]
    cols = jnp.concatenate([row[:, :e], row[:, e : 2 * e], jnp.zeros((6, e), f32)], axis=0).T
    scale = HEAD ** (-0.5)
    query = turn(dot(w[0], normed, TT) + cols[:, 0:1], c, s, 1).astype(bf16) * scale
    qt[:, rows] = query
    q[rows, :] = query.T
    key = turn(dot(w[1], normed, TT), c, s, 1).astype(bf16)
    k[rows, :] = key.T
    value = (dot(w[2], normed, TT) + cols[:, 1:2]).astype(bf16)
    zero = jnp.zeros((HEAD, tile), bf16)
    if own:
        row = lax.broadcasted_iota(jnp.int32, (VROWS - HEAD, tile), 0)
        ones = jnp.where(row == 0, 1.0, 0.0).astype(bf16)
    for h in range(e // HEAD):
        sl = slice(h * HEAD, (h + 1) * HEAD)
        at, other = (0, HEAD) if h % 2 == 0 else (HEAD, 0)
        kpad[h, at : at + HEAD, rows] = key[sl, :]
        kpad[h, other : other + HEAD, rows] = zero
        vpad[h, at : at + HEAD, rows] = value[sl, :]
        vpad[h, other : other + HEAD, rows] = zero
        if own:
            vone[h, :HEAD, rows] = value[sl, :]
            vone[h, HEAD:, rows] = ones
    grad = dot(ow[...], g[rows, :], NT).astype(bf16)
    dot_t[:, rows] = grad
    do[rows, :] = grad.T


def low_parts(x):
    high = x.astype(bf16)
    rest = x - high.astype(f32)
    mid = rest.astype(bf16)
    return [high, mid, (rest - mid.astype(f32)).astype(bf16)]


FILLED = 1792


def over_tiles(q0, tk, step, carry):
    last = lax.div(q0, tk)
    first = jnp.where(q0 >= FILLED, last, 0)
    return lax.fori_loop(first, last + 1, step, carry)


VROWS = 80


def forward_tile(q0, tq, tk, first, places, qt, k, vone, ot, qpad, acc):
    heads = qt.shape[0] // HEAD
    zero = jnp.zeros((HEAD, tq), bf16)
    for h in range(heads):
        qh = qt[h * HEAD : (h + 1) * HEAD, pl.ds(q0, tq)]
        qpad[h] = jnp.concatenate([qh, zero] if h % 2 == 0 else [zero, qh], axis=0)
    acc[...] = jnp.zeros_like(acc)

    def step(j, peaks):
        k0 = pl.multiple_of(j * tk, tk)
        rows = k0 + lax.broadcasted_iota(jnp.int32, (tk, tq), 0)
        allowed = (rows >= first) & (rows <= places)
        scores, new, raised = [], [], []
        for h in range(heads):
            pair = (h // 2) * 128
            s = dot(k[pl.ds(k0, tk), pair : pair + 128], qpad[h])
            scores.append(jnp.where(allowed, s, -1e30))
        for h in range(heads):
            new.append(jnp.maximum(peaks[h], jnp.max(scores[h], axis=0, keepdims=True)))
            raised.append(jnp.exp(scores[h] - new[h]).astype(bf16))
        for h in range(heads):
            o = dot(vone[h, :, pl.ds(k0, tk)], raised[h])
            acc[h] = acc[h] * jnp.exp(peaks[h] - new[h]) + o
        return tuple(new)

    start = tuple(jnp.full((1, tq), -1e30, f32) for _ in range(heads))
    peaks = over_tiles(q0, tk, step, start)
    logs = []
    for h in range(heads):
        total = acc[h, HEAD : HEAD + 1, :]
        ot[h * HEAD : (h + 1) * HEAD, :] = acc[h, :HEAD, :] / total
        logs.append(peaks[h] + jnp.log(total))
    logs.append(jnp.zeros((8 - heads, tq), f32))
    ot[heads * HEAD :, :] = jnp.concatenate(logs, axis=0)


def backward_tile(q0, tq, tk, first, places, q, qt, k, kpad, vpad, do, dot_t, ot, cosine, sine, grads_q, dk, dv, dq, qa, da, cs, cd):
    heads = q.shape[1] // HEAD
    rows = pl.ds(q0, tq)
    deltas = [
        jnp.sum(ot[h * HEAD : (h + 1) * HEAD, :] * dot_t[h * HEAD : (h + 1) * HEAD, rows].astype(f32), axis=0, keepdims=True)
        for h in range(heads)
    ]
    deltas.append(jnp.zeros((8 - heads, tq), f32))
    stats = low_parts(ot[heads * HEAD :, :]) + low_parts(jnp.concatenate(deltas, axis=0))
    stats.append(jnp.zeros((128 - 48, tq), bf16))
    stat_cols = jnp.concatenate(stats, axis=0).T
    for r in range(heads // 2):
        pair = slice(r * 128, r * 128 + 128)
        qa[r, :, :128] = q[rows, pair]
        qa[r, :, 128:] = stat_cols
        da[r, :, :128] = do[rows, pair]
        da[r, :, 128:] = stat_cols
    dq[...] = jnp.zeros_like(dq)

    def step(j, carry):
        k0 = pl.multiple_of(j * tk, tk)
        ks = pl.ds(k0, tk)
        cols = k0 + lax.broadcasted_iota(jnp.int32, (tq, tk), 1)
        allowed = (cols >= first) & (cols <= places)
        probs, grads = [], []
        for h in range(heads):
            s = dot(qa[h // 2], jnp.concatenate([kpad[h, :, ks], cs[h]], axis=0))
            dp = dot(da[h // 2], jnp.concatenate([vpad[h, :, ks], cd[h]], axis=0))
            p = jnp.where(allowed, jnp.exp(s), 0.0)
            probs.append(p.astype(bf16))
            grads.append((p * dp).astype(bf16))
        for h in range(heads):
            sl = slice(h * HEAD, (h + 1) * HEAD)
            pair = slice((h // 2) * 128, (h // 2) * 128 + 128)
            dv[sl, ks] += dot(dot_t[sl, rows], probs[h])
            dk[sl, ks] += dot(qt[sl, rows], grads[h])
            dq[h] += dot(grads[h], k[ks, pair])
        return carry

    over_tiles(q0, tk, step, 0)
    scale = HEAD ** (-0.5)
    lane = lax.broadcasted_iota(jnp.int32, (tq, 128), 1)
    q_parts = [
        jnp.where(lane < HEAD, dq[2 * h], dq[2 * h + 1]).T * scale for h in range(heads // 2)
    ]
    grads_q[...] = turn(jnp.concatenate(q_parts, axis=0), cosine[:, rows], sine[:, rows], -1).astype(bf16)


def attention_kernel(tk, tile, own, bias_row, lens, tok_all, g_all, w, bias, ow, gains, biases, freq, *refs):
    refs = list(refs)
    cut = lambda n: [refs.pop(0) for _ in range(n)]
    if own:
        ot, ot_send, grads_q, grads_k, grads_v, keep_o, send_o = cut(7)
    else:
        ot, grads_q, grads_k, grads_v = cut(4)
    q, qt, k, kpad, vpad, do, dot_t, cosine, sine, dk, dv, dq, qa, da, cs, cd = cut(16)
    tok, g, sems = cut(3)
    vone, qpad, acc, dow = cut(4) if own else (None, None, None, None)
    i = pl.program_id(0)
    length = tok.shape[0]
    heads, tq, _ = dq.shape
    q0 = pl.multiple_of(i * tq, tq)

    @pl.when(i == 0)
    def _():
        loads = [pltpu.make_async_copy(a, b, sems.at[n]) for n, (a, b) in enumerate(((tok_all, tok), (g_all, g)))]
        for c in loads:
            c.start()
        dk[...] = jnp.zeros_like(dk)
        dv[...] = jnp.zeros_like(dv)
        row = lax.broadcasted_iota(jnp.int32, (128, tk), 0)
        for h in range(heads):
            cs[h] = jnp.where((row < 24) & (row % 8 == h), -1.0, 0.0).astype(bf16)
            cd[h] = jnp.where((row >= 24) & (row < 48) & (row % 8 == h), -1.0, 0.0).astype(bf16)

        for c in loads:
            c.wait()

        def some(t, c):
            project_tile(t, tile, bias_row, lens, tok, g, w, bias, ow, gains, biases, freq, own, q, qt, k, kpad, vpad, vone, do, dot_t, cosine, sine)
            return c

        lax.fori_loop(0, length // tile, some, 0)

    if own:
        places = q0 + lax.broadcasted_iota(jnp.int32, (1, tq), 1)
        forward_tile(q0, tq, tk, first_tokens(lens, places), places, qt, k, vone, ot, qpad, acc)
        ot_send[...] = ot[...]
        add_to(dow, i == 0, dot(ot[: ow.shape[0], :].astype(bf16), g[pl.ds(q0, tq), :]))
    places = q0 + lax.broadcasted_iota(jnp.int32, (tq, 1), 0)
    backward_tile(
        q0, tq, tk, first_tokens(lens, places), places, q, qt, k, kpad, vpad, do, dot_t, ot, cosine, sine, grads_q, dk, dv, dq, qa, da, cs, cd
    )

    @pl.when(i == pl.num_programs(0) - 1)
    def _():
        grads_k[...] = turn(dk[...], cosine[...], sine[...], -1).astype(bf16)
        grads_v[...] = dv[...].astype(bf16)
        if own:
            r = dow.shape[0] // 2
            for ref, half in ((keep_o, bit_of(0)), (send_o, 1 - bit_of(0))):
                ref[...] = dow[pl.ds(pl.multiple_of(half * r, r), r), :]


def attention(bias_row, lens, tok, g, w, bias, ow, gains, biases, freq, ot=None, tq=256, tk=256, tile=512, deps=(), rides=(), collective=None):
    length, d = tok.shape
    e = w.shape[2]
    heads = e // HEAD
    own = ot is None
    cols = pl.BlockSpec((e, tq), lambda i, *_: (0, i))
    stat = pl.BlockSpec((e + 8, tq), lambda i, *_: (0, i))
    grad = jax.ShapeDtypeStruct((e, length), bf16)
    kept = jax.ShapeDtypeStruct((e + 8, length), f32)
    nat, tr, pad, angle = pltpu.VMEM((length, e), bf16), pltpu.VMEM((e, length), bf16), pltpu.VMEM((heads, 128, length), bf16), pltpu.VMEM((HALF, length), f32)
    scratch = [nat, tr, nat, pad, pad, nat, tr, angle, angle]
    scratch += [pltpu.VMEM((e, length), f32)] * 2 + [pltpu.VMEM((heads, tq, 128), f32)]
    scratch += [pltpu.VMEM((heads // 2, tq, 256), bf16)] * 2 + [pltpu.VMEM((heads, 128, tk), bf16)] * 2
    scratch += [pltpu.VMEM((length, d), bf16)] * 2 + [pltpu.SemaphoreType.DMA((2,))]
    if own:
        scratch += [pltpu.VMEM((heads, VROWS, length), bf16), pltpu.VMEM((heads, 128, tq), bf16), pltpu.VMEM((heads, VROWS, tq), f32), pltpu.VMEM((e, d), f32)]
    half = jax.ShapeDtypeStruct((e // 2, d), f32)
    return call(
        functools.partial(attention_kernel, tk, tile, own, bias_row),
        grid=(length // tq,),
        scalars=1,
        in_specs=[
            *[pl.BlockSpec(memory_space=pl.ANY)] * 2, whole((3, d, e)), whole((8, d)), whole((e, d)), whole((2, d)), whole((2, d)), whole((HALF, 128)),
        ] + ([] if own else [stat]),
        out_specs=([stat, stat] if own else []) + [cols, whole((e, length)), whole((e, length))] + ([whole(half.shape)] * 2 if own else []),
        out_shape=([kept, kept] if own else []) + [grad, grad, grad] + ([half, half] if own else []),
        scratch=scratch,
        flops=8 * length * length * e,
        nbytes=20 * length * e,
        deps=deps,
        rides=rides,
        collective=collective,
        name="attention",
    )(lens, tok, g, w, bias, ow, gains, biases, freq, *([] if own else [ot]))


def merge_tile(tok, gq, gk, gv, ot, w, ow, gains, biases):
    hat, inverse = hat_of(tok[...].astype(f32))
    gain = gains[0:1, :]
    back = dot(gq[...], w[0], TT) + dot(gk[...], w[1], TT) + dot(gv[...], w[2], TT)
    low = ot[...].astype(bf16)
    return hat, inverse, gain, back, dot(low, ow[...], TN)


def merge_own_kernel(tok, gq, gk, gv, ot, w, ow, gains, biases, part_in, share_in, small_in, upb_in, part, share, keep_a, send_a, keep_b, send_b, small, dw):
    i = pl.program_id(0)
    tile = tok.shape[0]
    e, d = ow.shape
    n_up = 2

    @pl.when(i == 0)
    def _():
        dw[...] = jnp.zeros_like(dw)
        small[...] = jnp.zeros_like(small)
        small[1:2, :] = small_in[1:2, :]
        small[3:4, :] = small_in[2:3, :]
        small[4:5, :] = small_in[0:1, :]
        small[5 : 5 + n_up, :] = upb_in[:n_up, :]

    hat, _, gain, back, out = merge_tile(tok, gq, gk, gv, ot, w, ow, gains, biases)
    normed = (hat * gain + biases[0:1, :]).astype(bf16)
    share[...] = share_in[...] + back * gain
    part[...] = part_in[...] + out
    dw[0] += dot(normed, gq[...], TT)
    dw[1] += dot(normed, gk[...], TT)
    dw[2] += dot(normed, gv[...], TT)
    small[0:1, :] += jnp.sum(back * hat, axis=0, keepdims=True)
    small[2:3, :] += jnp.sum(back, axis=0, keepdims=True)
    ones = jnp.ones((8, tile), bf16)
    at = 5 + n_up
    small[at : at + 1, :e] += dot(ones, gq[...], NT)[0:1]
    small[at : at + 1, e : 2 * e] += dot(ones, gv[...], NT)[0:1]

    @pl.when(i == pl.num_programs(0) - 1)
    def _():
        core = bit_of(0)
        r = d // 8
        for refs, half in (((keep_a, keep_b), core), ((send_a, send_b), 1 - core)):
            for n in range(6):
                ref, at, c, sub = refs[n // 3], n % 3 * r, n // 2, n % 2
                for s in range(2):
                    rows = pl.multiple_of(half * (d // 2) + (2 * s + sub) * r, r)
                    ref[at : at + r, s * e : (s + 1) * e] = dw[c, pl.ds(rows, r), :]


def merge_own(tok, gq, gk, gv, ot, w, ow, gains, biases, part, share, small, upb, tile=512, deps=(), rides=(), collective=None):
    length, d = tok.shape
    e = w.shape[2]
    rows = pl.BlockSpec((tile, d), lambda i: (i, 0))
    cols = pl.BlockSpec((e, tile), lambda i: (0, i))
    full = jax.ShapeDtypeStruct((length, d), f32)
    half = jax.ShapeDtypeStruct((3 * d // 8, d), f32)
    return call(
        merge_own_kernel,
        grid=(length // tile,),
        in_specs=[rows, cols, cols, cols, cols, whole((3, d, e)), whole((e, d)), whole((2, d)), whole((2, d)), rows, rows, whole((8, d)), whole((8, d))],
        out_specs=[rows, rows, *[once(half.shape)] * 4, once((8, d))],
        out_shape=[full, full, half, half, half, half, jax.ShapeDtypeStruct((8, d), f32)],
        scratch=[pltpu.VMEM((3, d, e), f32)],
        flops=16 * length * d * e,
        nbytes=24 * length * d,
        deps=deps,
        rides=rides,
        collective=collective,
        name="merge_own",
    )(tok, gq, gk, gv, ot, w, ow, gains, biases, part, share, small, upb)


def merge_other_kernel(tok, g, gq, gk, gv, ot, w, ow, gains, biases, out_bias, down_bias, part_in, share_in, output, input_grad):
    hat, inverse, gain, back, out = merge_tile(tok, gq, gk, gv, ot, w, ow, gains, biases)
    shares = share_in[...] + back * gain
    inputs = tok[...].astype(f32)
    output[...] = (inputs + (part_in[...] + out) + out_bias[...].astype(f32) + down_bias[...].astype(f32)).astype(bf16)
    input_share = inverse * (
        shares
        - jnp.mean(shares, axis=-1, keepdims=True)
        - hat * jnp.mean(shares * hat, axis=-1, keepdims=True)
    )
    input_grad[...] = (g[...].astype(f32) + input_share).astype(bf16)


def merge_other(tok, g, gq, gk, gv, ot, w, ow, gains, biases, out_bias, down_bias, part, share, tile=512, deps=(), rides=(), collective=None):
    length, d = tok.shape
    e = w.shape[2]
    rows = pl.BlockSpec((tile, d), lambda i: (i, 0))
    cols = pl.BlockSpec((e, tile), lambda i: (0, i))
    full = jax.ShapeDtypeStruct((length, d), bf16)
    return call(
        merge_other_kernel,
        grid=(length // tile,),
        in_specs=[rows, rows, cols, cols, cols, cols, whole((3, d, e)), whole((e, d)), whole((2, d)), whole((2, d)), whole((1, d)), whole((1, d)), rows, rows],
        out_specs=[rows, rows],
        out_shape=[full, full],
        flops=8 * length * d * e,
        nbytes=24 * length * d,
        deps=deps,
        rides=rides,
        collective=collective,
        name="merge_other",
    )(tok, g, gq, gk, gv, ot, w, ow, gains, biases, out_bias[None], down_bias[None], part, share)


def pack_kernel(meta, w, ow, up, down, w_far, ow_far, up_far, down_far, upb, qkvb, one, two, three, four, bias_rows):
    d = ow.shape[1]
    e = w.shape[2]

    def blocks(refs):
        w, ow, up, down = refs
        for n in range(2):
            r = down.shape[0] // 8
            for s in range(4):
                yield [down[(4 * n + s) * r : (4 * n + s + 1) * r, :]]
            r = up.shape[0] // 2
            for c in range(up.shape[1] // d):
                yield [up[n * r : (n + 1) * r, c * d : (c + 1) * d]]
            r = w.shape[1] // 4
            for c in range(3):
                yield [w[c, (2 * n + s) * r : (2 * n + s + 1) * r, :] for s in range(2)]
            r = ow.shape[0] // 2
            yield [ow[n * r : (n + 1) * r, :]]

    for refs, outs in (((w, ow, up, down), (one, two, three)), ((w_far, ow_far, up_far, down_far), (None, None, four))):
        sizes = [x.shape[0] for x in (one, two, three)]
        which, at = 0, 0
        for parts in blocks(refs):
            rows, lanes = parts[0].shape
            for j, x in enumerate(parts):
                if outs[which] is not None:
                    outs[which][at : at + rows, j * lanes : (j + 1) * lanes] = x.astype(f32)
            at += rows
            if at == sizes[which]:
                which, at = which + 1, 0
    n = upb.shape[0]
    bias_rows[...] = jnp.zeros_like(bias_rows)
    bias_rows[:n, :] = upb[...].astype(f32)
    for c in range(2):
        bias_rows[n : n + 1, c * e : (c + 1) * e] = qkvb[c : c + 1, :].astype(f32)


def pack(meta, w, ow, up, down, upb, qkvb):
    _, d, e = w.shape
    wide = up.shape[1]
    rows = (wide + (wide // d) * d + 3 * d // 2 + e) // 4
    one = wide // 8 + d // 8
    two = rows // 2 - one + wide // 32
    sizes = [one, two, rows - one - two, rows - one - two, 8]
    blocks = lambda n: [
        pl.BlockSpec((3, d // 4, e), lambda i, m: (0, m[n], 0)),
        pl.BlockSpec((e // 4, d), lambda i, m: (m[n], 0)),
        pl.BlockSpec((d // 4, wide), lambda i, m: (m[n], 0)),
        pl.BlockSpec((wide // 4, d), lambda i, m: (m[n], 0)),
    ]
    return call(
        pack_kernel,
        grid=(1,),
        scalars=1,
        in_specs=blocks(0) + blocks(1) + [whole((wide // d, d)), whole((2, e))],
        out_specs=[once((r, d)) for r in sizes],
        out_shape=[jax.ShapeDtypeStruct((r, d), f32) for r in sizes],
        name="pack",
    )(meta, w, ow, up, down, w, ow, up, down, upb.reshape(-1, d), qkvb)


def unpack(pieces, w, ow, up, down):
    d = ow.shape[1]
    e = w.shape[2]
    for n in range(4):
        core = lax.rem(bit_of(0) + n // 2, 2)
        parity = lax.rem(bit_of(1) + bit_of(2) + n % 2, 2)
        refs = pieces[3 * n : 3 * n + 3]
        place = [0, 0]

        def take(rows):
            ref, at = refs[place[0]], place[1]
            place[1] = at + rows
            if place[1] == ref.shape[0]:
                place[:] = [place[0] + 1, 0]
            return ref[at : at + rows, :].astype(bf16)

        for m in range(2):
            at_piece = (parity * 2 + core) * 2 + m
            rows = lambda r, sub=0, parts=1: pl.ds(pl.multiple_of((at_piece * parts + sub) * r, r), r)
            r = down.shape[0] // 32
            for s in range(4):
                down[rows(r, s, 4), :] = take(r)
            r = up.shape[0] // 8
            for c in range(up.shape[1] // d):
                up[rows(r), c * d : (c + 1) * d] = take(r)
            r = w.shape[1] // 16
            for c in range(3):
                x = take(r)
                for s in range(2):
                    w[c, rows(r, s, 2), :] = x[:, s * e : (s + 1) * e]
            r = ow.shape[0] // 8
            ow[rows(r), :] = take(r)


def swap(x, bit):
    n = lax.axis_size("dp")
    return lax.ppermute(x, "dp", [(i, i ^ (1 << bit)) for i in range(n)])


def across(x):
    return lax.ppermute(x, "tensor", [(0, 1), (1, 0)])


def tie(arrays, deps):
    n = len(arrays)
    anywhere = [pl.BlockSpec(memory_space=pl.ANY)] * n
    return call(
        lambda *refs: None,
        grid=(1,),
        in_specs=anywhere,
        out_specs=anywhere,
        out_shape=[jax.ShapeDtypeStruct(x.shape, x.dtype) for x in arrays],
        aliases={i: i for i in range(n)},
        deps=deps,
        name="tie",
    )(*arrays)


def down_places(d, wide):
    rows = d // 2

    def places(sources, outs, core):
        return [
            (x, outs[0].at[pl.ds(pl.multiple_of(c * d + core * rows, 8), rows)]) for c, x in enumerate(sources)
        ]

    return [(wide, d)], wide // d, places


def up_places(d, wide):
    rows = d // 2

    def places(sources, outs, core):
        to = pl.ds(pl.multiple_of(core * rows, 8), rows)
        return [(x, outs[0].at[to, pl.ds(c * d, d)]) for c, x in enumerate(sources)]

    return [(d, wide)], wide // d, places


def attn_places(d, e):
    rows = d // 8

    def places(sources, outs, core):
        pairs = []
        for n in range(6):
            source, at, c, sub = sources[n // 3], n % 3 * rows, n // 2, n % 2
            for s in range(2):
                to = pl.ds(pl.multiple_of(core * (d // 2) + (2 * s + sub) * rows, 8), rows)
                pairs.append((source.at[pl.ds(at, rows), pl.ds(s * e, e)], outs[0].at[c, to]))
        to = pl.ds(pl.multiple_of(core * (e // 2), 8), e // 2)
        pairs.append((sources[2], outs[1].at[to]))
        return pairs

    return [(3, d, e), (e, d)], 13, places


def relay(rides, collective, deps=()):
    call(
        lambda *_: None,
        grid=(1,),
        in_specs=[],
        out_specs=[],
        out_shape=[],
        deps=deps,
        rides=rides,
        collective=collective,
        name="relay",
    )()


def per_device(
    tokens, lengths, qkv_weight, qkv_bias, out_weight, out_bias, up_weight, up_bias, down_weight, down_bias, norm_gains, norm_biases, cotangent
):
    length, d = tokens.shape
    e = qkv_weight.shape[2]
    wide = up_weight.shape[1]
    bits = lax.axis_size("dp").bit_length() - 1
    me = lax.axis_index("dp")
    quarter = lambda p: (((me >> 1) ^ (me >> 2) ^ p) & 1) * 2 + (me & 1)
    meta = jnp.stack([quarter(0), quarter(1)])
    freq = np.broadcast_to((rot_base ** (-(2.0 * np.arange(HALF)) / ROT)).astype(np.float32)[:, None], (HALF, 128))
    one, two, three, far_three, own_biases = pack(
        meta, qkv_weight, out_weight, up_weight, down_weight, up_bias, qkv_bias
    )
    order = list(range(1, bits))
    crossed = [order[1], order[0]] + order[2:]
    early = [Held(EARLY + j, (d // 2, d)) for j in range(4)]
    down_1, up_1 = Sum(early[0], early[1], order), Sum(early[2], early[3], crossed)
    send = Sends((one, "tensor"), (own_biases, "tensor"), (two, "tensor"))
    part, share, keep_d, send_d, keep_u, send_u, small, upb_sum = mlp_own(
        tokens, cotangent, up_weight, own_biases, down_weight, norm_gains, norm_biases,
        rides=[send, down_1.take(4, 5), up_1.take(4, 5)], collective=1,
    )
    one, other_biases, two = send.got
    down_2, up_2 = Sum(keep_d, send_d, order), Sum(keep_u, send_u, crossed)
    send = Sends((three, "tensor"), (far_three, "tensor"), (one, 0), (two, 0))
    near = [Sends((one, 1), at=(2,)), Sends((two, 1), at=(5,))]
    ot, ot_send, gq, gk, gv, keep_o, send_o = attention(
        wide // d, lengths, tokens, cotangent, qkv_weight, own_biases, out_weight, norm_gains, norm_biases, freq,
        rides=[down_1.take(0, 1, 4), up_1.take(0, 1, 4), down_2.take(0, 1, 5, 6), up_2.take(0, 1, 5, 6), send] + near, collective=2,
    )
    three, near_three, core_one, core_two = send.got
    (near_one,), (near_two,) = near[0].got, near[1].got
    other_ot = across(ot_send)
    sum_o = Sum(keep_o, send_o, order, True)
    send = Sends((near_one, 0), (near_two, 0), (near_three, 0), (three, 0))
    part, share, keep_a, send_a, keep_b, send_b, small = merge_own(
        tokens, gq, gk, gv, ot, qkv_weight, out_weight, norm_gains, norm_biases, part, share, small, upb_sum,
        rides=[down_2.take(0), up_2.take(0), down_1.take(0), up_1.take(0), sum_o.take(0), send], collective=3,
    )
    core_near_one, core_near_two, core_near_three, core_three = send.got
    sum_a, sum_b, sum_s = Sum(keep_a, send_a, order, True), Sum(keep_b, send_b, crossed, True), SmallSum(small, bits)
    pieces = [one, two, three, near_one, near_two, near_three]
    pieces += [core_one, core_two, core_three, core_near_one, core_near_two, core_near_three]
    part, share, other_w, other_ow = mlp_other(
        pieces, tokens, cotangent, other_biases, norm_gains, norm_biases, part, share, [qkv_weight, out_weight, up_weight, down_weight],
        rides=[
            sum_s.take(0, 1), sum_a.take(0), sum_b.take(0), down_2.take(0, 1), up_2.take(0, 1), down_1.take(0), up_1.take(0),
        ],
        collective=4,
    )
    at = 7
    mlp_sums = [down_1, down_2, up_1, up_2]
    while not all(s.done for s in mlp_sums):
        relay([s.take(0) for s in mlp_sums if not s.done], at)
        at += 1
    final_d, final_u = Final(mlp_sums[:2], *down_places(d, wide)), Final(mlp_sums[2:], *up_places(d, wide))
    (other_ot,) = tie([other_ot], [part])
    gq, gk, gv = attention(
        wide // d, lengths, tokens, cotangent, other_w, other_biases, other_ow, norm_gains, norm_biases, freq, other_ot,
        rides=[sum_s.take(0, 1, 2)] + [s.take(0, 2, 4) for s in (sum_a, sum_b, sum_o)], collective=5,
    )
    sums = [sum_a, sum_b, sum_o, sum_s]
    output, input_grad = merge_other(
        tokens, cotangent, gq, gk, gv, other_ot, other_w, other_ow, norm_gains, norm_biases, out_bias, down_bias, part, share,
        rides=[s.take(0, 2) for s in sums if not s.done] + [final_d, final_u], collective=6,
    )
    while not all(s.done for s in sums):
        relay([s.take(0) for s in sums if not s.done], at)
        at += 1
    final = Final(sums[:3], *attn_places(d, e))
    relay([final], at)
    (d_down,), (d_up,), (d_qkv, d_out) = final_d.results, final_u.results, final.results
    small = sum_s.mine
    rest = small[5:].reshape(-1)
    return (
        output, input_grad, d_qkv, rest[wide : wide + 2 * e].reshape(2, e), d_out, small[4], d_up, rest[:wide], d_down, small[4], small[:2], small[2:4],
    )


def solution(mesh):
    in_specs = (
        P("dp", None), P("dp", None), P(None, None, "tensor"), P(None, "tensor"), P("tensor", None), P(), P(None, "tensor"),
        P("tensor"), P("tensor", None), P(), P(), P(), P("dp", None),
    )
    out_specs = (
        P("dp", None), P("dp", None), P(None, None, "tensor"), P(None, "tensor"), P("tensor", None), P(), P(None, "tensor"),
        P("tensor"), P("tensor", None), P(), P(), P(),
    )
    return jax.shard_map(per_device, mesh=mesh, in_specs=in_specs, out_specs=out_specs, check_vma=False)
```

```python
import functools
import math

import jax
import jax.numpy as jnp
import numpy as np
from jax import lax
from jax.experimental import pallas as pl
from jax.experimental.pallas import tpu as pltpu
from jax.sharding import PartitionSpec as P

HEAD = 64
ROT = 16
HALF = ROT // 2
epsilon = 1e-05
rot_base = 10000.0
f32 = jnp.float32
bf16 = jnp.bfloat16
NN = (((1,), (0,)), ((), ()))
NT = (((1,), (1,)), ((), ()))
TN = (((0,), (0,)), ((), ()))
TT = (((0,), (1,)), ((), ()))
VMEM_LIMIT = 60 * 2**20


def dot(a, b, dims=NN):
    return lax.dot_general(a, b, dims, preferred_element_type=f32)


MESH = pl.DeviceIdType.MESH


def bit_of(b):
    return lax.rem(lax.div(lax.axis_index("dp"), 1 << b), 2)


def partner(flip):
    if flip == "tensor":
        return {"tensor": 1 - lax.axis_index("tensor")}
    return {"dp": lax.axis_index("dp") + (1 - 2 * bit_of(flip)) * (1 << flip)}


def by_rows(rows, step):
    size = next(c for c in (96, 48, 24, 8, rows) if rows % c == 0)
    if rows == size:
        step(0, size)
    else:
        lax.fori_loop(0, rows // size, lambda j, c: (step(pl.multiple_of(j * size, 8), size), c)[1], 0)


class Sends:
    def __init__(self, *phases, at=(0,)):
        self.at = at
        self.phases = phases if isinstance(phases[0], list) else [list(phases)]
        moves = [m for phase in self.phases for m in phase]
        self.flips = [flip for _, flip in moves]
        self.inputs = [x for x, _ in moves if not isinstance(x, int)]
        shapes = []
        for x, _ in moves:
            shapes.append(shapes[x] if isinstance(x, int) else jax.ShapeDtypeStruct(x.shape, x.dtype))
        self.outputs = [(s, True) for s in shapes]
        self.scratch = [pltpu.SemaphoreType.DMA((2, len(moves)))]

    def build(self, ins, outs, scratch, _):
        sems, ins, events, j = scratch[0], list(ins), [], 0
        for phase in self.phases:
            copies = []
            for x, flip in phase:
                source = outs[x] if isinstance(x, int) else ins.pop(0)
                copies.append(
                    pltpu.make_async_remote_copy(
                        src_ref=source, dst_ref=outs[j], send_sem=sems.at[0, j], recv_sem=sems.at[1, j], device_id=partner(flip), device_id_type=MESH
                    )
                )
                j += 1

            def begin(copies=copies):
                for c in copies:
                    c.start()

            def finish(copies=copies):
                for c in copies:
                    c.wait()

            events.append((begin, finish))
        return events

    def receive(self, outs):
        self.got = list(outs)


class Held:
    def __init__(self, place, shape):
        self.place, self.shape = place, shape


class Sum:
    def __init__(self, keep, send, order, whole=False):
        self.mine, self.send = keep, send
        halved = [b for j, b in enumerate(order[:-1] if whole else order) if keep.shape[0] % (16 << j) == 0]
        way = [0] + halved
        self.steps = [(way[j], "halve", b) for j, b in enumerate(halved)] + [(way[-1], "add", None)]
        self.steps += [(b, "add", None) for b in order if b not in halved]
        self.steps += [(b, "join", b) for b in reversed(halved)]

    @property
    def done(self):
        return not self.steps

    def take(self, *at):
        steps, self.steps = self.steps[: len(at)], self.steps[len(at) :]
        return Steps(self, steps, at[: len(steps)])


class SmallSum(Sum):
    def __init__(self, x, bits):
        self.mine = self.send = x
        self.steps = [(b, "add", None) for b in range(bits)] + [("tensor", "norm", None)]


class Final:
    def __init__(self, sums, shapes, count, places):
        self.sums, self.shapes, self.count, self.places = sums, shapes, count, places
        self.at, self.flips = (0,), [0]

    @property
    def inputs(self):
        return [s.mine for s in self.sums]

    @property
    def outputs(self):
        return [(jax.ShapeDtypeStruct(s, f32), True) for s in self.shapes]

    @property
    def scratch(self):
        stage = [pltpu.VMEM(s.mine.shape, f32) for s in self.sums]
        return [pltpu.SemaphoreType.DMA((3, self.count)), pltpu.SemaphoreType.DMA((len(stage),))] + stage

    def build(self, ins, outs, scratch, _):
        put = lambda sources: self.places(sources, outs, bit_of(0))
        return [place_copies(put, ins, scratch[2:], 0, scratch[0], scratch[1])]

    def receive(self, outs):
        self.results = list(outs)


def place_copies(put, sources, held, flip, sems, load_sems):
    at = (lambda k, j: sems.at[k]) if load_sems is None else (lambda k, j: sems.at[k, j])
    there = [
        pltpu.make_async_remote_copy(
            src_ref=s, dst_ref=t, send_sem=at(0, j), recv_sem=at(1, j), device_id=partner(flip), device_id_type=MESH
        )
        for j, (s, t) in enumerate(put(sources))
    ]
    loads = [] if held is None else [
        pltpu.make_async_copy(s, h, sems.at[2] if load_sems is None else load_sems.at[j]) for j, (s, h) in enumerate(zip(sources, held))
    ]
    here = [pltpu.make_async_copy(s, t, at(2, j)) for j, (s, t) in enumerate(put(sources if held is None else held))]

    def begin():
        for c in there + (here if held is None else loads):
            c.start()

    def finish():
        for c in loads:
            c.wait()
        if held is not None:
            for c in here:
                c.start()
        for c in here + there:
            c.wait()

    return begin, finish


class Steps:
    def __init__(self, owner, steps, at):
        self.owner, self.steps, self.at = owner, steps, at
        self.flips = [s[0] for s in steps]
        self.same = owner.mine is owner.send
        reads = [k for _, k, _ in steps][0] in ("halve", "add", "norm")
        self.inputs = [owner.send] + ([owner.mine] if reads and not self.same else [])
        self.outputs, self.scratch = [], []
        rows, d = owner.send.shape
        self.places = None
        local = True
        if isinstance(owner.send, Held):
            self.places, self.inputs, local = (owner.send.place, owner.mine.place), [], False
        for n, (_, kind, _) in enumerate(steps):
            last = n == len(steps) - 1
            self.scratch.append(pltpu.SemaphoreType.DMA((3,)))
            if kind in ("halve", "add", "norm"):
                self.scratch += [pltpu.VMEM((rows, d), f32)] * (2 if local else 1)
                rows = rows // 2 if kind == "halve" else rows
                shapes = [(rows, d)] * (2 if kind == "halve" else 1)
                if last:
                    self.outputs += [(jax.ShapeDtypeStruct(s, f32), False) for s in shapes]
                local = False
            elif kind == "join":
                if local:
                    self.scratch.append(pltpu.VMEM((rows, d), f32))
                local = True
                rows *= 2
                self.outputs.append((jax.ShapeDtypeStruct((rows, d), f32), True))

    def build(self, ins, outs, scratch, kernel_scratch):
        outs, scratch = list(outs), list(scratch)
        if self.places is not None:
            ins = [kernel_scratch[p] for p in self.places]
        send = ins[0]
        mine = ins[-1]
        events = []
        in_hbm = self.places is None
        for n, (flip, kind, bit) in enumerate(self.steps):
            last = n == len(self.steps) - 1
            sems = scratch.pop(0)
            rows = send.shape[0]
            if kind in ("halve", "add", "norm"):
                got = scratch.pop(0)
                held = scratch.pop(0) if in_hbm else mine
                fresh = kept = None
                if last:
                    fresh = outs.pop(0)
                    kept = outs.pop(0) if kind == "halve" else None
                elif kind == "halve":
                    r, v = held.shape[0] // 2, bit_of(bit)
                    fresh, kept = (held.at[pl.ds(pl.multiple_of(h * r, 8), r)] for h in (1 - v, v))
                else:
                    fresh = held
                events.append(self.reduce(kind, bit, flip, send, mine, in_hbm, got, held, fresh, kept, sems))
                send, mine, in_hbm = fresh, (fresh if kept is None else kept), False
            elif kind == "join":
                target = outs.pop(0)
                held = scratch.pop(0) if in_hbm else None
                put = lambda xs, target=target, bit=bit, rows=rows: [
                    (xs[0], target.at[pl.ds(pl.multiple_of(bit_of(bit) * rows, 8), rows)])
                ]
                events.append(self.copies(put, send, held, flip, sems))
                send = mine = target
                in_hbm = True
        return events

    @staticmethod
    def copies(put, send, held, flip, sems, load_sems=None):
        return place_copies(put, [send], None if held is None else [held], flip, sems, load_sems)

    @staticmethod
    def reduce(kind, bit, flip, send, mine, in_hbm, got, held, fresh, kept, sems):
        there = pltpu.make_async_remote_copy(
            src_ref=send, dst_ref=got, send_sem=sems.at[0], recv_sem=sems.at[1], device_id=partner(flip), device_id_type=MESH
        )
        load = pltpu.make_async_copy(mine, held, sems.at[2]) if in_hbm else None

        def add_half(out, half, r):
            base = half * r

            def step(j, size):
                rows = pl.ds(pl.multiple_of(base + j, 8), size)
                out[pl.ds(j, size), :] = held[rows, :] + got[rows, :]

            by_rows(r, step)

        def begin():
            there.start()
            if load is not None:
                load.start()

        def after():
            if kind == "halve":
                add_half(kept, bit_of(bit), held.shape[0] // 2)

        def finish():
            if load is not None:
                load.wait()
            there.wait()
            if kind == "halve":
                r = held.shape[0] // 2
                v = bit_of(bit)
                add_half(fresh, 1 - v, r)
            elif kind == "norm":
                row = lax.broadcasted_iota(jnp.int32, held.shape, 0)
                fresh[...] = held[...] + jnp.where(row < 4, got[...], 0.0)
            else:

                def step(j, size):
                    rows = pl.ds(j, size)
                    fresh[rows, :] = held[rows, :] + got[rows, :]

                by_rows(held.shape[0], step)

        return begin, finish, after

    def receive(self, outs):
        outs = list(outs)
        owner = self.owner
        for n, (_, kind, _) in enumerate(self.steps):
            last = n == len(self.steps) - 1
            if kind == "join":
                owner.mine = owner.send = outs.pop(0)
            elif last:
                owner.send = outs.pop(0)
                owner.mine = outs.pop(0) if kind == "halve" else owner.send


def call(
    kernel, *, grid, in_specs, out_specs, out_shape, scalars=0, scratch=(), deps=(), rides=(), collective=None, flops=0, nbytes=0, name=None, aliases=None
):
    single = not isinstance(out_shape, (list, tuple))
    out_specs = [out_specs] if single else list(out_specs)
    out_shape = [out_shape] if single else list(out_shape)
    n_in, n_out, n_scratch = scalars + len(in_specs), len(out_shape), len(scratch)
    anywhere = pl.BlockSpec(memory_space=pl.ANY)
    ride_in = [x for r in rides for x in r.inputs]
    ride_out = [o for r in rides for o in r.outputs]
    flips = list(dict.fromkeys(f for r in rides for f in r.flips))

    def body(*refs):
        refs = list(refs)
        cut = lambda n: [refs.pop(0) for _ in range(n)]
        ins, _, sources = cut(n_in), cut(len(deps)), cut(len(ride_in))
        outs, targets, held = cut(n_out), cut(len(ride_out)), cut(n_scratch)
        at_step, at_end = {}, []
        for r in rides:
            take = lambda refs, n: [refs.pop(0) for _ in range(n)]
            events = r.build(take(sources, len(r.inputs)), take(targets, len(r.outputs)), take(refs, len(r.scratch)), held)
            for n, (begin, finish, *after) in enumerate(events):
                at_step.setdefault(r.at[n], ([], []))[0].append(begin)
                if n + 1 < len(events):
                    step = at_step.setdefault(r.at[n + 1], ([], []))
                    step[0].append(finish)
                    step[1].extend(after)
                else:
                    at_end += [finish] + after
        if rides:

            @pl.when(pl.program_id(0) == 0)
            def _():
                barrier = pltpu.get_barrier_semaphore()
                for f in flips:
                    pl.semaphore_signal(barrier, inc=1, device_id=partner(f), device_id_type=MESH)
                pl.semaphore_wait(barrier, len(flips))

        for g, acts in at_step.items():

            @pl.when(pl.program_id(0) == g)
            def _(acts=acts):
                for act in acts[0] + acts[1]:
                    act()

        kernel(*ins, *outs, *held)
        if at_end:

            @pl.when(pl.program_id(0) == pl.num_programs(0) - 1)
            def _():
                for act in at_end:
                    act()

    params = dict(vmem_limit_bytes=VMEM_LIMIT)
    if rides:
        params.update(collective_id=collective, has_side_effects=True)

    def run(*args):
        outs = pl.pallas_call(
            body,
            grid_spec=pltpu.PrefetchScalarGridSpec(
                num_scalar_prefetch=scalars,
                grid=grid,
                in_specs=list(in_specs) + [anywhere] * (len(deps) + len(ride_in)),
                out_specs=out_specs + [anywhere if hbm else once(s.shape) for s, hbm in ride_out],
                scratch_shapes=list(scratch) + [s for r in rides for s in r.scratch],
            ),
            out_shape=out_shape + [s for s, _ in ride_out],
            compiler_params=pltpu.CompilerParams(**params),
            cost_estimate=pl.CostEstimate(flops=20 * flops, bytes_accessed=nbytes, transcendentals=0),
            input_output_aliases=aliases or {},
            name=name,
        )(*args, *deps, *ride_in)
        outs = list(outs)
        own, rest = outs[:n_out], outs[n_out:]
        for r in rides:
            r.receive(rest[: len(r.outputs)])
            rest = rest[len(r.outputs) :]
        return own[0] if single else own

    return run


def whole(shape):
    zeros = (0,) * len(shape)
    return pl.BlockSpec(shape, lambda *_: zeros, pipeline_mode=pl.Buffered(1))


def once(shape):
    zeros = (0,) * len(shape)
    return pl.BlockSpec(shape, lambda *_: zeros)


def hat_of(values):
    average = jnp.mean(values, axis=-1, keepdims=True)
    centered = values - average
    inverse = lax.rsqrt(jnp.mean(centered * centered, axis=-1, keepdims=True) + epsilon)
    return centered * inverse, inverse


def gelu_pair(h):
    a = jnp.abs(h) * np.float32(math.sqrt(0.5))
    t = 1.0 / (1.0 + np.float32(0.3275911) * a)
    bell = jnp.exp(-0.5 * (h * h))
    poly = np.float32(0.5 * 1.061405429) * t + np.float32(0.5 * -1.453152027)
    poly = poly * t + np.float32(0.5 * 1.421413741)
    poly = poly * t + np.float32(0.5 * -0.284496736)
    poly = poly * t + np.float32(0.5 * 0.254829592)
    tail = poly * t * bell
    phi = jnp.where(h >= 0, 1.0 - tail, tail)
    return h * phi, phi + h * bell * np.float32(1.0 / math.sqrt(2.0 * math.pi))


def mlp_tile(chunk, tok, g, up, upb, down, gains, biases, visit):
    hat, _ = hat_of(tok[...].astype(f32))
    gain = gains[1:2, :]
    normed = (hat * gain + biases[1:2, :]).astype(bf16)
    gt = g[...]
    d = tok.shape[1]
    up_bias = jnp.concatenate([upb[c : c + 1, :] for c in range(up.shape[1] // d)], axis=1)
    total = None
    back = None
    for c in range(up.shape[1] // chunk):
        sl = slice(c * chunk, (c + 1) * chunk)
        hidden = dot(normed, up[:, sl]) + up_bias[:, sl]
        act_grad = dot(gt, down[sl, :], NT)
        act, slope = gelu_pair(hidden)
        act = act.astype(bf16)
        hid_grad = (act_grad * slope).astype(bf16)
        p = dot(act, down[sl, :])
        e = dot(hid_grad, up[:, sl], NT)
        total = p if total is None else total + p
        back = e if back is None else back + e
        visit(sl, normed, gt, act, hid_grad)
    return hat, gt, total, back, gain


def mlp_own_kernel(tok, g, up, upb, down, gains, biases, part, share, keep_a, send_a, keep_b, send_b, small, upb_sum, dup, ddown, part_s, share_s, *early):
    i = pl.program_id(0)
    tiles = pl.num_programs(0) // 2
    chunk, t = lax.div(i, tiles), lax.rem(i, tiles)
    tile, d = tok.shape

    @pl.when(i == 0)
    def _():
        small[...] = jnp.zeros_like(small)
        upb_sum[...] = jnp.zeros_like(upb_sum)
        small[0:1, :] = jnp.zeros_like(small[0:1, :])

    @pl.when(t == 0)
    def _():
        dup[...] = jnp.zeros_like(dup)
        ddown[...] = jnp.zeros_like(ddown)

    hat, _ = hat_of(tok[...].astype(f32))
    gain = gains[1:2, :]
    normed = (hat * gain + biases[1:2, :]).astype(bf16)
    gt = g[...]
    hidden = dot(normed, up[...]) + upb[pl.ds(chunk, 1), :]
    act_grad = dot(gt, down[...], NT)
    act, slope = gelu_pair(hidden)
    act = act.astype(bf16)
    hid_grad = (act_grad * slope).astype(bf16)
    total = dot(act, down[...])
    back = dot(hid_grad, up[...], NT)
    dup[...] += dot(normed, hid_grad, TN)
    ddown[...] += dot(act, gt, TN)
    upb_sum[pl.ds(chunk, 1), :] += jnp.sum(hid_grad.astype(f32), axis=0, keepdims=True)
    small[1:2, :] += jnp.sum(back * hat, axis=0, keepdims=True)
    small[2:3, :] += jnp.sum(back, axis=0, keepdims=True)
    rows = pl.ds(pl.multiple_of(t * tile, tile), tile)

    def split(first, second, first_send, second_send):
        core = bit_of(0)
        for a, b, half in ((first, second, core), (first_send, second_send, 1 - core)):
            at = pl.ds(pl.multiple_of(half * (d // 2), d // 2), d // 2)
            a[...] = ddown[at, :]
            b[...] = dup[at, :]

    @pl.when(chunk == 0)
    def _():
        small[0:1, :] += jnp.sum(gt.astype(f32), axis=0, keepdims=True)
        part_s[rows, :] = total
        share_s[rows, :] = back

        @pl.when(t == tiles - 1)
        def _():
            split(early[0], early[2], early[1], early[3])

    @pl.when(chunk == 1)
    def _():
        part[...] = part_s[rows, :] + total
        share[...] = (share_s[rows, :] + back) * gain

        @pl.when(t == tiles - 1)
        def _():
            split(keep_a, keep_b, send_a, send_b)


EARLY = 4


def mlp_own(tok, g, up, upb, down, gains, biases, tile=512, deps=(), rides=(), collective=None):
    length, d = tok.shape
    wide = up.shape[1]
    tiles = length // tile
    rows = pl.BlockSpec((tile, d), lambda i: (lax.rem(i, tiles), 0))
    out_rows = pl.BlockSpec((tile, d), lambda i: (jnp.maximum(i - tiles, 0), 0))
    half = jax.ShapeDtypeStruct((d // 2, d), f32)
    full = jax.ShapeDtypeStruct((length, d), f32)
    eight = jax.ShapeDtypeStruct((8, d), f32)
    big = pltpu.VMEM((length, d), f32)
    return call(
        mlp_own_kernel,
        grid=(2 * tiles,),
        in_specs=[
            rows, rows, pl.BlockSpec((d, wide // 2), lambda i: (0, lax.div(i, tiles))), whole((8, d)),
            pl.BlockSpec((wide // 2, d), lambda i: (lax.div(i, tiles), 0)), whole((2, d)), whole((2, d)),
        ],
        out_specs=[out_rows, out_rows, *[once(half.shape)] * 4, once((8, d)), once((8, d))],
        out_shape=[full, full, half, half, half, half, eight, eight],
        scratch=[pltpu.VMEM((d, wide // 2), f32), pltpu.VMEM((wide // 2, d), f32), big, big] + [pltpu.VMEM(half.shape, f32)] * 4,
        flops=12 * length * d * wide,
        nbytes=4 * length * d * 4,
        deps=deps,
        rides=rides,
        collective=collective,
        name="mlp_own",
    )(tok, g, up, upb, down, gains, biases)


def mlp_other_kernel(chunk, *refs):
    pieces, refs = refs[:12], refs[12:]
    tok, g, upb, gains, biases, part_in, share_in, part, share, w, ow, up, down = refs[:13]
    loaded, sems = refs[13:25], refs[25]

    @pl.when(pl.program_id(0) == 0)
    def _():
        loads = [pltpu.make_async_copy(a, b, sems.at[n]) for n, (a, b) in enumerate(zip(pieces, loaded))]
        for c in loads:
            c.start()
        for c in loads:
            c.wait()
        unpack(loaded, w, ow, up, down)

    nothing = lambda *_: None
    _, _, total, back, gain = mlp_tile(chunk, tok, g, up, upb, down, gains, biases, nothing)
    part[...] = part_in[...] + total
    share[...] = share_in[...] + back * gain


def mlp_other(pieces, tok, g, upb, gains, biases, part, share, shapes, tile=512, chunk=768, deps=(), rides=(), collective=None):
    length, d = tok.shape
    w, ow, up, down = [x.shape for x in shapes]
    rows = pl.BlockSpec((tile, d), lambda i: (i, 0))
    full = jax.ShapeDtypeStruct((length, d), f32)
    return call(
        functools.partial(mlp_other_kernel, chunk),
        grid=(length // tile,),
        in_specs=[pl.BlockSpec(memory_space=pl.ANY)] * 12 + [rows, rows, whole((8, d)), whole((2, d)), whole((2, d)), rows, rows],
        out_specs=[rows, rows, whole(w), whole(ow)],
        out_shape=[full, full, jax.ShapeDtypeStruct(w, bf16), jax.ShapeDtypeStruct(ow, bf16)],
        scratch=[pltpu.VMEM(up, bf16), pltpu.VMEM(down, bf16)] + [pltpu.VMEM(p.shape, f32) for p in pieces] + [pltpu.SemaphoreType.DMA((12,))],
        flops=8 * length * d * up[1],
        nbytes=4 * length * d * 4,
        deps=deps,
        rides=rides,
        collective=collective,
        name="mlp_other",
    )(*pieces, tok, g, upb, gains, biases, part, share)


def first_tokens(lens, places):
    first = jnp.zeros_like(places)
    end = lens[0, 0]
    for j in range(1, lens.shape[1]):
        first = jnp.where(places >= end, end, first)
        end = end + lens[0, j]
    return jnp.where(places >= end, places, first)


def turn(block, cosine, sine, sign):
    parts = []
    for h in range(block.shape[0] // HEAD):
        r = h * HEAD
        a = block[r : r + HALF, :]
        b = block[r + HALF : r + ROT, :]
        if sign > 0:
            parts += [a * cosine - b * sine, b * cosine + a * sine]
        else:
            parts += [a * cosine + b * sine, b * cosine - a * sine]
        parts.append(block[r + ROT : r + HEAD, :])
    return jnp.concatenate(parts, axis=0)


def project_tile(t, tile, bias_row, lens, tok, g, w, bias, ow, gains, biases, freq, own, q, qt, k, kpad, vpad, vone, do, dot_t, cosine, sine):
    rows = pl.ds(pl.multiple_of(t * tile, tile), tile)
    e = ow.shape[0]
    hat, _ = hat_of(tok[rows, :].astype(f32))
    normed = (hat * gains[0:1, :] + biases[0:1, :]).astype(bf16)
    places = t * tile + lax.broadcasted_iota(jnp.int32, (1, tile), 1)
    position = (places - first_tokens(lens, places)).astype(f32)
    theta = freq[:, 0:1] * position
    c = jnp.cos(theta)
    s = jnp.sin(theta)
    cosine[:, rows] = c
    sine[:, rows] = s
    row = bias[bias_row : bias_row + 1, :]
    cols = jnp.concatenate([row[:, :e], row[:, e : 2 * e], jnp.zeros((6, e), f32)], axis=0).T
    scale = HEAD ** (-0.5)
    query = turn(dot(w[0], normed, TT) + cols[:, 0:1], c, s, 1).astype(bf16) * scale
    qt[:, rows] = query
    q[rows, :] = query.T
    key = turn(dot(w[1], normed, TT), c, s, 1).astype(bf16)
    k[rows, :] = key.T
    value = (dot(w[2], normed, TT) + cols[:, 1:2]).astype(bf16)
    zero = jnp.zeros((HEAD, tile), bf16)
    if own:
        row = lax.broadcasted_iota(jnp.int32, (VROWS - HEAD, tile), 0)
        ones = jnp.where(row == 0, 1.0, 0.0).astype(bf16)
    for h in range(e // HEAD):
        sl = slice(h * HEAD, (h + 1) * HEAD)
        at, other = (0, HEAD) if h % 2 == 0 else (HEAD, 0)
        kpad[h, at : at + HEAD, rows] = key[sl, :]
        kpad[h, other : other + HEAD, rows] = zero
        vpad[h, at : at + HEAD, rows] = value[sl, :]
        vpad[h, other : other + HEAD, rows] = zero
        if own:
            vone[h, :HEAD, rows] = value[sl, :]
            vone[h, HEAD:, rows] = ones
    grad = dot(ow[...], g[rows, :], NT).astype(bf16)
    dot_t[:, rows] = grad
    do[rows, :] = grad.T


def low_parts(x):
    high = x.astype(bf16)
    rest = x - high.astype(f32)
    mid = rest.astype(bf16)
    return [high, mid, (rest - mid.astype(f32)).astype(bf16)]


FILLED = 1792


def over_tiles(q0, tk, step, carry):
    last = lax.div(q0, tk)
    first = jnp.where(q0 >= FILLED, last, 0)
    return lax.fori_loop(first, last + 1, step, carry)


VROWS = 80


def forward_tile(q0, tq, tk, first, places, qt, k, vone, ot, qpad, acc):
    heads = qt.shape[0] // HEAD
    zero = jnp.zeros((HEAD, tq), bf16)
    for h in range(heads):
        qh = qt[h * HEAD : (h + 1) * HEAD, pl.ds(q0, tq)]
        qpad[h] = jnp.concatenate([qh, zero] if h % 2 == 0 else [zero, qh], axis=0)
    acc[...] = jnp.zeros_like(acc)

    def step(j, peaks):
        k0 = pl.multiple_of(j * tk, tk)
        rows = k0 + lax.broadcasted_iota(jnp.int32, (tk, tq), 0)
        allowed = (rows >= first) & (rows <= places)
        scores, new, raised = [], [], []
        for h in range(heads):
            pair = (h // 2) * 128
            s = dot(k[pl.ds(k0, tk), pair : pair + 128], qpad[h])
            scores.append(jnp.where(allowed, s, -1e30))
        for h in range(heads):
            new.append(jnp.maximum(peaks[h], jnp.max(scores[h], axis=0, keepdims=True)))
            raised.append(jnp.exp(scores[h] - new[h]).astype(bf16))
        for h in range(heads):
            o = dot(vone[h, :, pl.ds(k0, tk)], raised[h])
            acc[h] = acc[h] * jnp.exp(peaks[h] - new[h]) + o
        return tuple(new)

    start = tuple(jnp.full((1, tq), -1e30, f32) for _ in range(heads))
    peaks = over_tiles(q0, tk, step, start)
    logs = []
    for h in range(heads):
        total = acc[h, HEAD : HEAD + 1, :]
        ot[h * HEAD : (h + 1) * HEAD, :] = acc[h, :HEAD, :] / total
        logs.append(peaks[h] + jnp.log(total))
    logs.append(jnp.zeros((8 - heads, tq), f32))
    ot[heads * HEAD :, :] = jnp.concatenate(logs, axis=0)


def backward_tile(q0, tq, tk, first, places, q, qt, k, kpad, vpad, do, dot_t, ot, cosine, sine, grads_q, dk, dv, dq, qa, da, cs, cd):
    heads = q.shape[1] // HEAD
    rows = pl.ds(q0, tq)
    deltas = [
        jnp.sum(ot[h * HEAD : (h + 1) * HEAD, :] * dot_t[h * HEAD : (h + 1) * HEAD, rows].astype(f32), axis=0, keepdims=True)
        for h in range(heads)
    ]
    deltas.append(jnp.zeros((8 - heads, tq), f32))
    stats = low_parts(ot[heads * HEAD :, :]) + low_parts(jnp.concatenate(deltas, axis=0))
    stats.append(jnp.zeros((128 - 48, tq), bf16))
    stat_cols = jnp.concatenate(stats, axis=0).T
    for r in range(heads // 2):
        pair = slice(r * 128, r * 128 + 128)
        qa[r, :, :128] = q[rows, pair]
        qa[r, :, 128:] = stat_cols
        da[r, :, :128] = do[rows, pair]
        da[r, :, 128:] = stat_cols
    dq[...] = jnp.zeros_like(dq)

    def step(j, carry):
        k0 = pl.multiple_of(j * tk, tk)
        ks = pl.ds(k0, tk)
        cols = k0 + lax.broadcasted_iota(jnp.int32, (tq, tk), 1)
        allowed = (cols >= first) & (cols <= places)
        probs, grads = [], []
        for h in range(heads):
            s = dot(qa[h // 2], jnp.concatenate([kpad[h, :, ks], cs[h]], axis=0))
            dp = dot(da[h // 2], jnp.concatenate([vpad[h, :, ks], cd[h]], axis=0))
            p = jnp.where(allowed, jnp.exp(s), 0.0)
            probs.append(p.astype(bf16))
            grads.append((p * dp).astype(bf16))
        for h in range(heads):
            sl = slice(h * HEAD, (h + 1) * HEAD)
            pair = slice((h // 2) * 128, (h // 2) * 128 + 128)
            dv[sl, ks] += dot(dot_t[sl, rows], probs[h])
            dk[sl, ks] += dot(qt[sl, rows], grads[h])
            dq[h] += dot(grads[h], k[ks, pair])
        return carry

    over_tiles(q0, tk, step, 0)
    scale = HEAD ** (-0.5)
    lane = lax.broadcasted_iota(jnp.int32, (tq, 128), 1)
    q_parts = [
        jnp.where(lane < HEAD, dq[2 * h], dq[2 * h + 1]).T * scale for h in range(heads // 2)
    ]
    grads_q[...] = turn(jnp.concatenate(q_parts, axis=0), cosine[:, rows], sine[:, rows], -1).astype(bf16)


def attention_kernel(tk, tile, own, bias_row, lens, tok_all, g_all, w, bias, ow, gains, biases, freq, *refs):
    refs = list(refs)
    cut = lambda n: [refs.pop(0) for _ in range(n)]
    if own:
        ot, ot_send, grads_q, grads_k, grads_v, keep_o, send_o = cut(7)
    else:
        ot, grads_q, grads_k, grads_v = cut(4)
    q, qt, k, kpad, vpad, do, dot_t, cosine, sine, dk, dv, dq, qa, da, cs, cd = cut(16)
    tok, g, sems = cut(3)
    vone, qpad, acc, dow, low = cut(5) if own else (None, None, None, None, None)
    i = pl.program_id(0)
    length = tok.shape[0]
    heads, tq, _ = dq.shape
    q0 = pl.multiple_of(i * tq, tq)

    @pl.when(i == 0)
    def _():
        loads = [pltpu.make_async_copy(a, b, sems.at[n]) for n, (a, b) in enumerate(((tok_all, tok), (g_all, g)))]
        for c in loads:
            c.start()
        dk[...] = jnp.zeros_like(dk)
        dv[...] = jnp.zeros_like(dv)
        row = lax.broadcasted_iota(jnp.int32, (128, tk), 0)
        for h in range(heads):
            cs[h] = jnp.where((row < 24) & (row % 8 == h), -1.0, 0.0).astype(bf16)
            cd[h] = jnp.where((row >= 24) & (row < 48) & (row % 8 == h), -1.0, 0.0).astype(bf16)

        for c in loads:
            c.wait()

        def some(t, c):
            project_tile(t, tile, bias_row, lens, tok, g, w, bias, ow, gains, biases, freq, own, q, qt, k, kpad, vpad, vone, do, dot_t, cosine, sine)
            return c

        lax.fori_loop(0, length // tile, some, 0)

    if own:
        places = q0 + lax.broadcasted_iota(jnp.int32, (1, tq), 1)
        forward_tile(q0, tq, tk, first_tokens(lens, places), places, qt, k, vone, ot, qpad, acc)
        ot_send[...] = ot[...]
        low[:, pl.ds(q0, tq)] = ot[: ow.shape[0], :].astype(bf16)
    places = q0 + lax.broadcasted_iota(jnp.int32, (tq, 1), 0)
    backward_tile(
        q0, tq, tk, first_tokens(lens, places), places, q, qt, k, kpad, vpad, do, dot_t, ot, cosine, sine, grads_q, dk, dv, dq, qa, da, cs, cd
    )

    @pl.when(i == pl.num_programs(0) - 1)
    def _():
        grads_k[...] = turn(dk[...], cosine[...], sine[...], -1).astype(bf16)
        grads_v[...] = dv[...].astype(bf16)
        if own:
            dow[...] = dot(low[...], g[...])
            r = dow.shape[0] // 2
            for ref, half in ((keep_o, bit_of(0)), (send_o, 1 - bit_of(0))):
                ref[...] = dow[pl.ds(pl.multiple_of(half * r, r), r), :]


def attention(bias_row, lens, tok, g, w, bias, ow, gains, biases, freq, ot=None, tq=256, tk=256, tile=512, deps=(), rides=(), collective=None):
    length, d = tok.shape
    e = w.shape[2]
    heads = e // HEAD
    own = ot is None
    cols = pl.BlockSpec((e, tq), lambda i, *_: (0, i))
    stat = pl.BlockSpec((e + 8, tq), lambda i, *_: (0, i))
    grad = jax.ShapeDtypeStruct((e, length), bf16)
    kept = jax.ShapeDtypeStruct((e + 8, length), f32)
    nat, tr, pad, angle = pltpu.VMEM((length, e), bf16), pltpu.VMEM((e, length), bf16), pltpu.VMEM((heads, 128, length), bf16), pltpu.VMEM((HALF, length), f32)
    scratch = [nat, tr, nat, pad, pad, nat, tr, angle, angle]
    scratch += [pltpu.VMEM((e, length), f32)] * 2 + [pltpu.VMEM((heads, tq, 128), f32)]
    scratch += [pltpu.VMEM((heads // 2, tq, 256), bf16)] * 2 + [pltpu.VMEM((heads, 128, tk), bf16)] * 2
    scratch += [pltpu.VMEM((length, d), bf16)] * 2 + [pltpu.SemaphoreType.DMA((2,))]
    if own:
        scratch += [pltpu.VMEM((heads, VROWS, length), bf16), pltpu.VMEM((heads, 128, tq), bf16), pltpu.VMEM((heads, VROWS, tq), f32), pltpu.VMEM((e, d), f32), tr]
    half = jax.ShapeDtypeStruct((e // 2, d), f32)
    return call(
        functools.partial(attention_kernel, tk, tile, own, bias_row),
        grid=(length // tq,),
        scalars=1,
        in_specs=[
            *[pl.BlockSpec(memory_space=pl.ANY)] * 2, whole((3, d, e)), whole((8, d)), whole((e, d)), whole((2, d)), whole((2, d)), whole((HALF, 128)),
        ] + ([] if own else [stat]),
        out_specs=([stat, stat] if own else []) + [cols, whole((e, length)), whole((e, length))] + ([whole(half.shape)] * 2 if own else []),
        out_shape=([kept, kept] if own else []) + [grad, grad, grad] + ([half, half] if own else []),
        scratch=scratch,
        flops=8 * length * length * e,
        nbytes=20 * length * e,
        deps=deps,
        rides=rides,
        collective=collective,
        name="attention",
    )(lens, tok, g, w, bias, ow, gains, biases, freq, *([] if own else [ot]))


def merge_tile(tok, gq, gk, gv, ot, w, ow, gains, biases):
    hat, inverse = hat_of(tok[...].astype(f32))
    gain = gains[0:1, :]
    back = dot(gq[...], w[0], TT) + dot(gk[...], w[1], TT) + dot(gv[...], w[2], TT)
    low = ot[...].astype(bf16)
    return hat, inverse, gain, back, dot(low, ow[...], TN)


def merge_own_kernel(tok, gq, gk, gv, ot, w, ow, gains, biases, part_in, share_in, small_in, upb_in, part, share, keep_a, send_a, keep_b, send_b, small, dw):
    i = pl.program_id(0)
    tile = tok.shape[0]
    e, d = ow.shape
    n_up = 2

    @pl.when(i == 0)
    def _():
        dw[...] = jnp.zeros_like(dw)
        small[...] = jnp.zeros_like(small)
        small[1:2, :] = small_in[1:2, :]
        small[3:4, :] = small_in[2:3, :]
        small[4:5, :] = small_in[0:1, :]
        small[5 : 5 + n_up, :] = upb_in[:n_up, :]

    hat, _, gain, back, out = merge_tile(tok, gq, gk, gv, ot, w, ow, gains, biases)
    normed = (hat * gain + biases[0:1, :]).astype(bf16)
    share[...] = share_in[...] + back * gain
    part[...] = part_in[...] + out
    dw[0] += dot(normed, gq[...], TT)
    dw[1] += dot(normed, gk[...], TT)
    dw[2] += dot(normed, gv[...], TT)
    small[0:1, :] += jnp.sum(back * hat, axis=0, keepdims=True)
    small[2:3, :] += jnp.sum(back, axis=0, keepdims=True)
    ones = jnp.ones((8, tile), bf16)
    at = 5 + n_up
    small[at : at + 1, :e] += dot(ones, gq[...], NT)[0:1]
    small[at : at + 1, e : 2 * e] += dot(ones, gv[...], NT)[0:1]

    @pl.when(i == pl.num_programs(0) - 1)
    def _():
        core = bit_of(0)
        r = d // 8
        for refs, half in (((keep_a, keep_b), core), ((send_a, send_b), 1 - core)):
            for n in range(6):
                ref, at, c, sub = refs[n // 3], n % 3 * r, n // 2, n % 2
                for s in range(2):
                    rows = pl.multiple_of(half * (d // 2) + (2 * s + sub) * r, r)
                    ref[at : at + r, s * e : (s + 1) * e] = dw[c, pl.ds(rows, r), :]


def merge_own(tok, gq, gk, gv, ot, w, ow, gains, biases, part, share, small, upb, tile=512, deps=(), rides=(), collective=None):
    length, d = tok.shape
    e = w.shape[2]
    rows = pl.BlockSpec((tile, d), lambda i: (i, 0))
    cols = pl.BlockSpec((e, tile), lambda i: (0, i))
    full = jax.ShapeDtypeStruct((length, d), f32)
    half = jax.ShapeDtypeStruct((3 * d // 8, d), f32)
    return call(
        merge_own_kernel,
        grid=(length // tile,),
        in_specs=[rows, cols, cols, cols, cols, whole((3, d, e)), whole((e, d)), whole((2, d)), whole((2, d)), rows, rows, whole((8, d)), whole((8, d))],
        out_specs=[rows, rows, *[once(half.shape)] * 4, once((8, d))],
        out_shape=[full, full, half, half, half, half, jax.ShapeDtypeStruct((8, d), f32)],
        scratch=[pltpu.VMEM((3, d, e), f32)],
        flops=16 * length * d * e,
        nbytes=24 * length * d,
        deps=deps,
        rides=rides,
        collective=collective,
        name="merge_own",
    )(tok, gq, gk, gv, ot, w, ow, gains, biases, part, share, small, upb)


def merge_other_kernel(tok, g, gq, gk, gv, ot, w, ow, gains, biases, out_bias, down_bias, part_in, share_in, output, input_grad):
    hat, inverse, gain, back, out = merge_tile(tok, gq, gk, gv, ot, w, ow, gains, biases)
    shares = share_in[...] + back * gain
    inputs = tok[...].astype(f32)
    output[...] = (inputs + (part_in[...] + out) + out_bias[...].astype(f32) + down_bias[...].astype(f32)).astype(bf16)
    input_share = inverse * (
        shares
        - jnp.mean(shares, axis=-1, keepdims=True)
        - hat * jnp.mean(shares * hat, axis=-1, keepdims=True)
    )
    input_grad[...] = (g[...].astype(f32) + input_share).astype(bf16)


def merge_other(tok, g, gq, gk, gv, ot, w, ow, gains, biases, out_bias, down_bias, part, share, tile=512, deps=(), rides=(), collective=None):
    length, d = tok.shape
    e = w.shape[2]
    rows = pl.BlockSpec((tile, d), lambda i: (i, 0))
    cols = pl.BlockSpec((e, tile), lambda i: (0, i))
    full = jax.ShapeDtypeStruct((length, d), bf16)
    return call(
        merge_other_kernel,
        grid=(length // tile,),
        in_specs=[rows, rows, cols, cols, cols, cols, whole((3, d, e)), whole((e, d)), whole((2, d)), whole((2, d)), whole((1, d)), whole((1, d)), rows, rows],
        out_specs=[rows, rows],
        out_shape=[full, full],
        flops=8 * length * d * e,
        nbytes=24 * length * d,
        deps=deps,
        rides=rides,
        collective=collective,
        name="merge_other",
    )(tok, g, gq, gk, gv, ot, w, ow, gains, biases, out_bias[None], down_bias[None], part, share)


def pack_kernel(meta, w, ow, up, down, w_far, ow_far, up_far, down_far, upb, qkvb, one, two, three, four, bias_rows):
    d = ow.shape[1]
    e = w.shape[2]

    def blocks(refs):
        w, ow, up, down = refs
        for n in range(2):
            r = down.shape[0] // 8
            for s in range(4):
                yield [down[(4 * n + s) * r : (4 * n + s + 1) * r, :]]
            r = up.shape[0] // 2
            for c in range(up.shape[1] // d):
                yield [up[n * r : (n + 1) * r, c * d : (c + 1) * d]]
            r = w.shape[1] // 4
            for c in range(3):
                yield [w[c, (2 * n + s) * r : (2 * n + s + 1) * r, :] for s in range(2)]
            r = ow.shape[0] // 2
            yield [ow[n * r : (n + 1) * r, :]]

    for refs, outs in (((w, ow, up, down), (one, two, three)), ((w_far, ow_far, up_far, down_far), (None, None, four))):
        sizes = [x.shape[0] for x in (one, two, three)]
        which, at = 0, 0
        for parts in blocks(refs):
            rows, lanes = parts[0].shape
            for j, x in enumerate(parts):
                if outs[which] is not None:
                    outs[which][at : at + rows, j * lanes : (j + 1) * lanes] = x.astype(f32)
            at += rows
            if at == sizes[which]:
                which, at = which + 1, 0
    n = upb.shape[0]
    bias_rows[...] = jnp.zeros_like(bias_rows)
    bias_rows[:n, :] = upb[...].astype(f32)
    for c in range(2):
        bias_rows[n : n + 1, c * e : (c + 1) * e] = qkvb[c : c + 1, :].astype(f32)


def pack(meta, w, ow, up, down, upb, qkvb):
    _, d, e = w.shape
    wide = up.shape[1]
    rows = (wide + (wide // d) * d + 3 * d // 2 + e) // 4
    one = wide // 8 + d // 8
    two = rows // 2 - one + wide // 32
    sizes = [one, two, rows - one - two, rows - one - two, 8]
    blocks = lambda n: [
        pl.BlockSpec((3, d // 4, e), lambda i, m: (0, m[n], 0)),
        pl.BlockSpec((e // 4, d), lambda i, m: (m[n], 0)),
        pl.BlockSpec((d // 4, wide), lambda i, m: (m[n], 0)),
        pl.BlockSpec((wide // 4, d), lambda i, m: (m[n], 0)),
    ]
    return call(
        pack_kernel,
        grid=(1,),
        scalars=1,
        in_specs=blocks(0) + blocks(1) + [whole((wide // d, d)), whole((2, e))],
        out_specs=[once((r, d)) for r in sizes],
        out_shape=[jax.ShapeDtypeStruct((r, d), f32) for r in sizes],
        name="pack",
    )(meta, w, ow, up, down, w, ow, up, down, upb.reshape(-1, d), qkvb)


def unpack(pieces, w, ow, up, down):
    d = ow.shape[1]
    e = w.shape[2]
    for n in range(4):
        core = lax.rem(bit_of(0) + n // 2, 2)
        parity = lax.rem(bit_of(1) + bit_of(2) + n % 2, 2)
        refs = pieces[3 * n : 3 * n + 3]
        place = [0, 0]

        def take(rows):
            ref, at = refs[place[0]], place[1]
            place[1] = at + rows
            if place[1] == ref.shape[0]:
                place[:] = [place[0] + 1, 0]
            return ref[at : at + rows, :].astype(bf16)

        for m in range(2):
            at_piece = (parity * 2 + core) * 2 + m
            rows = lambda r, sub=0, parts=1: pl.ds(pl.multiple_of((at_piece * parts + sub) * r, r), r)
            r = down.shape[0] // 32
            for s in range(4):
                down[rows(r, s, 4), :] = take(r)
            r = up.shape[0] // 8
            for c in range(up.shape[1] // d):
                up[rows(r), c * d : (c + 1) * d] = take(r)
            r = w.shape[1] // 16
            for c in range(3):
                x = take(r)
                for s in range(2):
                    w[c, rows(r, s, 2), :] = x[:, s * e : (s + 1) * e]
            r = ow.shape[0] // 8
            ow[rows(r), :] = take(r)


def swap(x, bit):
    n = lax.axis_size("dp")
    return lax.ppermute(x, "dp", [(i, i ^ (1 << bit)) for i in range(n)])


def across(x):
    return lax.ppermute(x, "tensor", [(0, 1), (1, 0)])


def tie(arrays, deps):
    n = len(arrays)
    anywhere = [pl.BlockSpec(memory_space=pl.ANY)] * n
    return call(
        lambda *refs: None,
        grid=(1,),
        in_specs=anywhere,
        out_specs=anywhere,
        out_shape=[jax.ShapeDtypeStruct(x.shape, x.dtype) for x in arrays],
        aliases={i: i for i in range(n)},
        deps=deps,
        name="tie",
    )(*arrays)


def down_places(d, wide):
    rows = d // 2

    def places(sources, outs, core):
        return [
            (x, outs[0].at[pl.ds(pl.multiple_of(c * d + core * rows, 8), rows)]) for c, x in enumerate(sources)
        ]

    return [(wide, d)], wide // d, places


def up_places(d, wide):
    rows = d // 2

    def places(sources, outs, core):
        to = pl.ds(pl.multiple_of(core * rows, 8), rows)
        return [(x, outs[0].at[to, pl.ds(c * d, d)]) for c, x in enumerate(sources)]

    return [(d, wide)], wide // d, places


def attn_places(d, e):
    rows = d // 8

    def places(sources, outs, core):
        pairs = []
        for n in range(6):
            source, at, c, sub = sources[n // 3], n % 3 * rows, n // 2, n % 2
            for s in range(2):
                to = pl.ds(pl.multiple_of(core * (d // 2) + (2 * s + sub) * rows, 8), rows)
                pairs.append((source.at[pl.ds(at, rows), pl.ds(s * e, e)], outs[0].at[c, to]))
        to = pl.ds(pl.multiple_of(core * (e // 2), 8), e // 2)
        pairs.append((sources[2], outs[1].at[to]))
        return pairs

    return [(3, d, e), (e, d)], 13, places


def relay(rides, collective, deps=()):
    call(
        lambda *_: None,
        grid=(1,),
        in_specs=[],
        out_specs=[],
        out_shape=[],
        deps=deps,
        rides=rides,
        collective=collective,
        name="relay",
    )()


def per_device(
    tokens, lengths, qkv_weight, qkv_bias, out_weight, out_bias, up_weight, up_bias, down_weight, down_bias, norm_gains, norm_biases, cotangent
):
    length, d = tokens.shape
    e = qkv_weight.shape[2]
    wide = up_weight.shape[1]
    bits = lax.axis_size("dp").bit_length() - 1
    me = lax.axis_index("dp")
    quarter = lambda p: (((me >> 1) ^ (me >> 2) ^ p) & 1) * 2 + (me & 1)
    meta = jnp.stack([quarter(0), quarter(1)])
    freq = np.broadcast_to((rot_base ** (-(2.0 * np.arange(HALF)) / ROT)).astype(np.float32)[:, None], (HALF, 128))
    one, two, three, far_three, own_biases = pack(
        meta, qkv_weight, out_weight, up_weight, down_weight, up_bias, qkv_bias
    )
    order = list(range(1, bits))
    crossed = [order[1], order[0]] + order[2:]
    early = [Held(EARLY + j, (d // 2, d)) for j in range(4)]
    down_1, up_1 = Sum(early[0], early[1], order), Sum(early[2], early[3], crossed)
    send = Sends((one, "tensor"), (own_biases, "tensor"), (two, "tensor"))
    part, share, keep_d, send_d, keep_u, send_u, small, upb_sum = mlp_own(
        tokens, cotangent, up_weight, own_biases, down_weight, norm_gains, norm_biases,
        rides=[send, down_1.take(4, 5), up_1.take(4, 5)], collective=1,
    )
    one, other_biases, two = send.got
    down_2, up_2 = Sum(keep_d, send_d, order), Sum(keep_u, send_u, crossed)
    send = Sends((three, "tensor"), (far_three, "tensor"), (one, 0), (two, 0))
    near = [Sends((one, 1), at=(2,)), Sends((two, 1), at=(5,))]
    ot, ot_send, gq, gk, gv, keep_o, send_o = attention(
        wide // d, lengths, tokens, cotangent, qkv_weight, own_biases, out_weight, norm_gains, norm_biases, freq,
        rides=[down_1.take(0, 1, 4), up_1.take(0, 1, 4), down_2.take(0, 1, 5, 6), up_2.take(0, 1, 5, 6), send] + near, collective=2,
    )
    three, near_three, core_one, core_two = send.got
    (near_one,), (near_two,) = near[0].got, near[1].got
    other_ot = across(ot_send)
    sum_o = Sum(keep_o, send_o, order, True)
    send = Sends((near_one, 0), (near_two, 0), (near_three, 0), (three, 0))
    part, share, keep_a, send_a, keep_b, send_b, small = merge_own(
        tokens, gq, gk, gv, ot, qkv_weight, out_weight, norm_gains, norm_biases, part, share, small, upb_sum,
        rides=[down_2.take(0), up_2.take(0), down_1.take(0), up_1.take(0), sum_o.take(0), send], collective=3,
    )
    core_near_one, core_near_two, core_near_three, core_three = send.got
    sum_a, sum_b, sum_s = Sum(keep_a, send_a, order, True), Sum(keep_b, send_b, crossed, True), SmallSum(small, bits)
    pieces = [one, two, three, near_one, near_two, near_three]
    pieces += [core_one, core_two, core_three, core_near_one, core_near_two, core_near_three]
    part, share, other_w, other_ow = mlp_other(
        pieces, tokens, cotangent, other_biases, norm_gains, norm_biases, part, share, [qkv_weight, out_weight, up_weight, down_weight],
        rides=[
            sum_s.take(0, 3), sum_a.take(0, 1, 3), sum_b.take(0, 1, 3), sum_o.take(1, 3), down_2.take(0), up_2.take(0), down_1.take(0), up_1.take(0),
        ],
        collective=4,
    )
    (other_ot,) = tie([other_ot], [part])
    gq, gk, gv = attention(
        wide // d, lengths, tokens, cotangent, other_w, other_biases, other_ow, norm_gains, norm_biases, freq, other_ot,
        rides=[s.take(0, 5, 6) for s in (sum_a, sum_b, sum_o)] + [down_2.take(0), up_2.take(0), sum_s.take(0, 6)], collective=5,
    )
    at = 7
    sums = [down_1, down_2, up_1, up_2, sum_a, sum_b, sum_o]
    while not all(s.done for s in sums):
        relay([s.take(0) for s in sums if not s.done], at)
        at += 1
    final_d, final_u = Final(sums[:2], *down_places(d, wide)), Final(sums[2:4], *up_places(d, wide))
    final = Final(sums[4:], *attn_places(d, e))
    output, input_grad = merge_other(
        tokens, cotangent, gq, gk, gv, other_ot, other_w, other_ow, norm_gains, norm_biases, out_bias, down_bias, part, share,
        rides=[sum_s.take(0), final_d, final_u, final], collective=6,
    )
    while not sum_s.done:
        relay([sum_s.take(0)], at)
        at += 1
    (d_down,), (d_up,), (d_qkv, d_out) = final_d.results, final_u.results, final.results
    small = sum_s.mine
    rest = small[5:].reshape(-1)
    return (
        output, input_grad, d_qkv, rest[wide : wide + 2 * e].reshape(2, e), d_out, small[4], d_up, rest[:wide], d_down, small[4], small[:2], small[2:4],
    )


def solution(mesh):
    in_specs = (
        P("dp", None), P("dp", None), P(None, None, "tensor"), P(None, "tensor"), P("tensor", None), P(), P(None, "tensor"),
        P("tensor"), P("tensor", None), P(), P(), P(), P("dp", None),
    )
    out_specs = (
        P("dp", None), P("dp", None), P(None, None, "tensor"), P(None, "tensor"), P("tensor", None), P(), P(None, "tensor"),
        P("tensor"), P("tensor", None), P(), P(), P(),
    )
    return jax.shard_map(per_device, mesh=mesh, in_specs=in_specs, out_specs=out_specs, check_vma=False)
```

```python
import functools
import math

import jax
import jax.numpy as jnp
import numpy as np
from jax import lax
from jax.experimental import pallas as pl
from jax.experimental.pallas import tpu as pltpu
from jax.sharding import PartitionSpec as P

HEAD = 64
ROT = 16
HALF = ROT // 2
epsilon = 1e-05
rot_base = 10000.0
f32 = jnp.float32
bf16 = jnp.bfloat16
NN = (((1,), (0,)), ((), ()))
NT = (((1,), (1,)), ((), ()))
TN = (((0,), (0,)), ((), ()))
TT = (((0,), (1,)), ((), ()))
VMEM_LIMIT = 60 * 2**20


def dot(a, b, dims=NN):
    return lax.dot_general(a, b, dims, preferred_element_type=f32)


MESH = pl.DeviceIdType.MESH


def bit_of(b):
    return lax.rem(lax.div(lax.axis_index("dp"), 1 << b), 2)


def partner(flip):
    if flip == "tensor":
        return {"tensor": 1 - lax.axis_index("tensor")}
    return {"dp": lax.axis_index("dp") + (1 - 2 * bit_of(flip)) * (1 << flip)}


def by_rows(rows, step):
    size = next(c for c in (96, 48, 24, 8, rows) if rows % c == 0)
    if rows == size:
        step(0, size)
    else:
        lax.fori_loop(0, rows // size, lambda j, c: (step(pl.multiple_of(j * size, 8), size), c)[1], 0)


class Sends:
    def __init__(self, *phases, at=(0,)):
        self.at = at
        self.phases = phases if isinstance(phases[0], list) else [list(phases)]
        moves = [m for phase in self.phases for m in phase]
        self.flips = [flip for _, flip in moves]
        self.inputs = [x for x, _ in moves if not isinstance(x, int)]
        shapes = []
        for x, _ in moves:
            shapes.append(shapes[x] if isinstance(x, int) else jax.ShapeDtypeStruct(x.shape, x.dtype))
        self.outputs = [(s, True) for s in shapes]
        self.scratch = [pltpu.SemaphoreType.DMA((2, len(moves)))]

    def build(self, ins, outs, scratch, _):
        sems, ins, events, j = scratch[0], list(ins), [], 0
        for phase in self.phases:
            copies = []
            for x, flip in phase:
                source = outs[x] if isinstance(x, int) else ins.pop(0)
                copies.append(
                    pltpu.make_async_remote_copy(
                        src_ref=source, dst_ref=outs[j], send_sem=sems.at[0, j], recv_sem=sems.at[1, j], device_id=partner(flip), device_id_type=MESH
                    )
                )
                j += 1

            def begin(copies=copies):
                for c in copies:
                    c.start()

            def finish(copies=copies):
                for c in copies:
                    c.wait()

            events.append((begin, finish))
        return events

    def receive(self, outs):
        self.got = list(outs)


class Held:
    def __init__(self, place, shape):
        self.place, self.shape = place, shape


class Sum:
    def __init__(self, keep, send, order, whole=False):
        self.mine, self.send = keep, send
        halved = [b for j, b in enumerate(order[:-1] if whole else order) if keep.shape[0] % (16 << j) == 0]
        way = [0] + halved
        self.steps = [(way[j], "halve", b) for j, b in enumerate(halved)] + [(way[-1], "add", None)]
        self.steps += [(b, "add", None) for b in order if b not in halved]
        self.steps += [(b, "join", b) for b in reversed(halved)]

    @property
    def done(self):
        return not self.steps

    def take(self, *at):
        steps, self.steps = self.steps[: len(at)], self.steps[len(at) :]
        return Steps(self, steps, at[: len(steps)])


class SmallSum(Sum):
    def __init__(self, x, bits):
        self.mine = self.send = x
        self.steps = [(b, "add", None) for b in range(bits)] + [("tensor", "norm", None)]


class Final:
    def __init__(self, sums, shapes, count, places):
        self.sums, self.shapes, self.count, self.places = sums, shapes, count, places
        self.at, self.flips = (0, 2), [0]

    @property
    def inputs(self):
        return [s.mine for s in self.sums]

    @property
    def outputs(self):
        return [(jax.ShapeDtypeStruct(s, f32), True) for s in self.shapes]

    @property
    def scratch(self):
        stage = [pltpu.VMEM(s.mine.shape, f32) for s in self.sums]
        return [pltpu.SemaphoreType.DMA((3, self.count)), pltpu.SemaphoreType.DMA((len(stage),))] + stage

    def build(self, ins, outs, scratch, _):
        put = lambda sources: self.places(sources, outs, bit_of(0))
        sems, load_sems, *held = scratch
        there, loads, here = place_parts(put, ins, held, 0, sems, load_sems)

        def wait_all():
            for c in here + there:
                c.wait()

        return [
            (lambda: [c.start() for c in there + loads], lambda: [c.wait() for c in loads]),
            (lambda: [c.start() for c in here], wait_all),
        ]

    def receive(self, outs):
        self.results = list(outs)


def place_parts(put, sources, held, flip, sems, load_sems):
    at = (lambda k, j: sems.at[k]) if load_sems is None else (lambda k, j: sems.at[k, j])
    there = [
        pltpu.make_async_remote_copy(
            src_ref=s, dst_ref=t, send_sem=at(0, j), recv_sem=at(1, j), device_id=partner(flip), device_id_type=MESH
        )
        for j, (s, t) in enumerate(put(sources))
    ]
    loads = [] if held is None else [
        pltpu.make_async_copy(s, h, sems.at[2] if load_sems is None else load_sems.at[j]) for j, (s, h) in enumerate(zip(sources, held))
    ]
    here = [pltpu.make_async_copy(s, t, at(2, j)) for j, (s, t) in enumerate(put(sources if held is None else held))]
    return there, loads, here


def place_copies(put, sources, held, flip, sems, load_sems):
    there, loads, here = place_parts(put, sources, held, flip, sems, load_sems)

    def begin():
        for c in there + (here if held is None else loads):
            c.start()

    def finish():
        for c in loads:
            c.wait()
        if held is not None:
            for c in here:
                c.start()
        for c in here + there:
            c.wait()

    return begin, finish


class Steps:
    def __init__(self, owner, steps, at):
        self.owner, self.steps, self.at = owner, steps, at
        self.flips = [s[0] for s in steps]
        self.same = owner.mine is owner.send
        reads = [k for _, k, _ in steps][0] in ("halve", "add", "norm")
        self.inputs = [owner.send] + ([owner.mine] if reads and not self.same else [])
        self.outputs, self.scratch = [], []
        rows, d = owner.send.shape
        self.places = None
        local = True
        if isinstance(owner.send, Held):
            self.places, self.inputs, local = (owner.send.place, owner.mine.place), [], False
        for n, (_, kind, _) in enumerate(steps):
            last = n == len(steps) - 1
            self.scratch.append(pltpu.SemaphoreType.DMA((3,)))
            if kind in ("halve", "add", "norm"):
                self.scratch += [pltpu.VMEM((rows, d), f32)] * (2 if local else 1)
                rows = rows // 2 if kind == "halve" else rows
                shapes = [(rows, d)] * (2 if kind == "halve" else 1)
                if last:
                    self.outputs += [(jax.ShapeDtypeStruct(s, f32), False) for s in shapes]
                local = False
            elif kind == "join":
                if local:
                    self.scratch.append(pltpu.VMEM((rows, d), f32))
                local = True
                rows *= 2
                self.outputs.append((jax.ShapeDtypeStruct((rows, d), f32), True))

    def build(self, ins, outs, scratch, kernel_scratch):
        outs, scratch = list(outs), list(scratch)
        if self.places is not None:
            ins = [kernel_scratch[p] for p in self.places]
        send = ins[0]
        mine = ins[-1]
        events = []
        in_hbm = self.places is None
        for n, (flip, kind, bit) in enumerate(self.steps):
            last = n == len(self.steps) - 1
            sems = scratch.pop(0)
            rows = send.shape[0]
            if kind in ("halve", "add", "norm"):
                got = scratch.pop(0)
                held = scratch.pop(0) if in_hbm else mine
                fresh = kept = None
                if last:
                    fresh = outs.pop(0)
                    kept = outs.pop(0) if kind == "halve" else None
                elif kind == "halve":
                    r, v = held.shape[0] // 2, bit_of(bit)
                    fresh, kept = (held.at[pl.ds(pl.multiple_of(h * r, 8), r)] for h in (1 - v, v))
                else:
                    fresh = held
                events.append(self.reduce(kind, bit, flip, send, mine, in_hbm, got, held, fresh, kept, sems))
                send, mine, in_hbm = fresh, (fresh if kept is None else kept), False
            elif kind == "join":
                target = outs.pop(0)
                held = scratch.pop(0) if in_hbm else None
                put = lambda xs, target=target, bit=bit, rows=rows: [
                    (xs[0], target.at[pl.ds(pl.multiple_of(bit_of(bit) * rows, 8), rows)])
                ]
                events.append(self.copies(put, send, held, flip, sems))
                send = mine = target
                in_hbm = True
        return events

    @staticmethod
    def copies(put, send, held, flip, sems, load_sems=None):
        return place_copies(put, [send], None if held is None else [held], flip, sems, load_sems)

    @staticmethod
    def reduce(kind, bit, flip, send, mine, in_hbm, got, held, fresh, kept, sems):
        there = pltpu.make_async_remote_copy(
            src_ref=send, dst_ref=got, send_sem=sems.at[0], recv_sem=sems.at[1], device_id=partner(flip), device_id_type=MESH
        )
        load = pltpu.make_async_copy(mine, held, sems.at[2]) if in_hbm else None

        def add_half(out, half, r):
            base = half * r

            def step(j, size):
                rows = pl.ds(pl.multiple_of(base + j, 8), size)
                out[pl.ds(j, size), :] = held[rows, :] + got[rows, :]

            by_rows(r, step)

        def begin():
            there.start()
            if load is not None:
                load.start()

        def after():
            if kind == "halve":
                add_half(kept, bit_of(bit), held.shape[0] // 2)

        def finish():
            if load is not None:
                load.wait()
            there.wait()
            if kind == "halve":
                r = held.shape[0] // 2
                v = bit_of(bit)
                add_half(fresh, 1 - v, r)
            elif kind == "norm":
                row = lax.broadcasted_iota(jnp.int32, held.shape, 0)
                fresh[...] = held[...] + jnp.where(row < 4, got[...], 0.0)
            else:

                def step(j, size):
                    rows = pl.ds(j, size)
                    fresh[rows, :] = held[rows, :] + got[rows, :]

                by_rows(held.shape[0], step)

        return begin, finish, after

    def receive(self, outs):
        outs = list(outs)
        owner = self.owner
        for n, (_, kind, _) in enumerate(self.steps):
            last = n == len(self.steps) - 1
            if kind == "join":
                owner.mine = owner.send = outs.pop(0)
            elif last:
                owner.send = outs.pop(0)
                owner.mine = outs.pop(0) if kind == "halve" else owner.send


def call(
    kernel, *, grid, in_specs, out_specs, out_shape, scalars=0, scratch=(), deps=(), rides=(), collective=None, flops=0, nbytes=0, name=None, aliases=None
):
    single = not isinstance(out_shape, (list, tuple))
    out_specs = [out_specs] if single else list(out_specs)
    out_shape = [out_shape] if single else list(out_shape)
    n_in, n_out, n_scratch = scalars + len(in_specs), len(out_shape), len(scratch)
    anywhere = pl.BlockSpec(memory_space=pl.ANY)
    ride_in = [x for r in rides for x in r.inputs]
    ride_out = [o for r in rides for o in r.outputs]
    flips = list(dict.fromkeys(f for r in rides for f in r.flips))

    def body(*refs):
        refs = list(refs)
        cut = lambda n: [refs.pop(0) for _ in range(n)]
        ins, _, sources = cut(n_in), cut(len(deps)), cut(len(ride_in))
        outs, targets, held = cut(n_out), cut(len(ride_out)), cut(n_scratch)
        at_step, at_end = {}, []
        for r in rides:
            take = lambda refs, n: [refs.pop(0) for _ in range(n)]
            events = r.build(take(sources, len(r.inputs)), take(targets, len(r.outputs)), take(refs, len(r.scratch)), held)
            for n, (begin, finish, *after) in enumerate(events):
                at_step.setdefault(r.at[n], ([], []))[0].append(begin)
                if n + 1 < len(events):
                    step = at_step.setdefault(r.at[n + 1], ([], []))
                    step[0].append(finish)
                    step[1].extend(after)
                else:
                    at_end += [finish] + after
        if rides:

            @pl.when(pl.program_id(0) == 0)
            def _():
                barrier = pltpu.get_barrier_semaphore()
                for f in flips:
                    pl.semaphore_signal(barrier, inc=1, device_id=partner(f), device_id_type=MESH)
                pl.semaphore_wait(barrier, len(flips))

        for g, acts in at_step.items():

            @pl.when(pl.program_id(0) == g)
            def _(acts=acts):
                for act in acts[0] + acts[1]:
                    act()

        kernel(*ins, *outs, *held)
        if at_end:

            @pl.when(pl.program_id(0) == pl.num_programs(0) - 1)
            def _():
                for act in at_end:
                    act()

    params = dict(vmem_limit_bytes=VMEM_LIMIT)
    if rides:
        params.update(collective_id=collective, has_side_effects=True)

    def run(*args):
        outs = pl.pallas_call(
            body,
            grid_spec=pltpu.PrefetchScalarGridSpec(
                num_scalar_prefetch=scalars,
                grid=grid,
                in_specs=list(in_specs) + [anywhere] * (len(deps) + len(ride_in)),
                out_specs=out_specs + [anywhere if hbm else once(s.shape) for s, hbm in ride_out],
                scratch_shapes=list(scratch) + [s for r in rides for s in r.scratch],
            ),
            out_shape=out_shape + [s for s, _ in ride_out],
            compiler_params=pltpu.CompilerParams(**params),
            cost_estimate=pl.CostEstimate(flops=20 * flops, bytes_accessed=nbytes, transcendentals=0),
            input_output_aliases=aliases or {},
            name=name,
        )(*args, *deps, *ride_in)
        outs = list(outs)
        own, rest = outs[:n_out], outs[n_out:]
        for r in rides:
            r.receive(rest[: len(r.outputs)])
            rest = rest[len(r.outputs) :]
        return own[0] if single else own

    return run


def whole(shape):
    zeros = (0,) * len(shape)
    return pl.BlockSpec(shape, lambda *_: zeros, pipeline_mode=pl.Buffered(1))


def once(shape):
    zeros = (0,) * len(shape)
    return pl.BlockSpec(shape, lambda *_: zeros)


def hat_of(values):
    average = jnp.mean(values, axis=-1, keepdims=True)
    centered = values - average
    inverse = lax.rsqrt(jnp.mean(centered * centered, axis=-1, keepdims=True) + epsilon)
    return centered * inverse, inverse


def gelu_pair(h):
    t = 1.0 / (1.0 + np.float32(0.3275911 * math.sqrt(0.5)) * jnp.abs(h))
    bell = jnp.exp2((h * h) * np.float32(-0.5 * math.log2(math.e)))
    poly = np.float32(0.5 * 1.061405429) * t + np.float32(0.5 * -1.453152027)
    poly = poly * t + np.float32(0.5 * 1.421413741)
    poly = poly * t + np.float32(0.5 * -0.284496736)
    poly = poly * t + np.float32(0.5 * 0.254829592)
    tail = poly * t * bell
    phi = jnp.where(h >= 0, 1.0 - tail, tail)
    return h * phi, phi + h * bell * np.float32(1.0 / math.sqrt(2.0 * math.pi))


def mlp_tile(chunk, tok, g, up, upb, down, gains, biases, visit):
    hat, _ = hat_of(tok[...].astype(f32))
    gain = gains[1:2, :]
    normed = (hat * gain + biases[1:2, :]).astype(bf16)
    gt = g[...]
    d = tok.shape[1]
    up_bias = jnp.concatenate([upb[c : c + 1, :] for c in range(up.shape[1] // d)], axis=1)
    total = None
    back = None
    for c in range(up.shape[1] // chunk):
        sl = slice(c * chunk, (c + 1) * chunk)
        hidden = dot(normed, up[:, sl]) + up_bias[:, sl]
        act_grad = dot(gt, down[sl, :], NT)
        act, slope = gelu_pair(hidden)
        act = act.astype(bf16)
        hid_grad = (act_grad * slope).astype(bf16)
        p = dot(act, down[sl, :])
        e = dot(hid_grad, up[:, sl], NT)
        total = p if total is None else total + p
        back = e if back is None else back + e
        visit(sl, normed, gt, act, hid_grad)
    return hat, gt, total, back, gain


def mlp_own_kernel(tok, g, up, upb, down, gains, biases, part, share, keep_a, send_a, keep_b, send_b, small, upb_sum, dup, ddown, part_s, share_s, *early):
    i = pl.program_id(0)
    tiles = pl.num_programs(0) // 2
    chunk, t = lax.div(i, tiles), lax.rem(i, tiles)
    tile, d = tok.shape

    @pl.when(i == 0)
    def _():
        small[...] = jnp.zeros_like(small)
        upb_sum[...] = jnp.zeros_like(upb_sum)
        small[0:1, :] = jnp.zeros_like(small[0:1, :])

    @pl.when(t == 0)
    def _():
        dup[...] = jnp.zeros_like(dup)
        ddown[...] = jnp.zeros_like(ddown)

    hat, _ = hat_of(tok[...].astype(f32))
    gain = gains[1:2, :]
    normed = (hat * gain + biases[1:2, :]).astype(bf16)
    gt = g[...]
    hidden = dot(normed, up[...]) + upb[pl.ds(chunk, 1), :]
    act_grad = dot(gt, down[...], NT)
    act, slope = gelu_pair(hidden)
    act = act.astype(bf16)
    hid_grad = (act_grad * slope).astype(bf16)
    total = dot(act, down[...])
    back = dot(hid_grad, up[...], NT)
    dup[...] += dot(normed, hid_grad, TN)
    ddown[...] += dot(act, gt, TN)
    upb_sum[pl.ds(chunk, 1), :] += jnp.sum(hid_grad.astype(f32), axis=0, keepdims=True)
    small[1:2, :] += jnp.sum(back * hat, axis=0, keepdims=True)
    small[2:3, :] += jnp.sum(back, axis=0, keepdims=True)
    rows = pl.ds(pl.multiple_of(t * tile, tile), tile)

    def split(first, second, first_send, second_send):
        core = bit_of(0)
        for a, b, half in ((first, second, core), (first_send, second_send, 1 - core)):
            at = pl.ds(pl.multiple_of(half * (d // 2), d // 2), d // 2)
            a[...] = ddown[at, :]
            b[...] = dup[at, :]

    @pl.when(chunk == 0)
    def _():
        small[0:1, :] += jnp.sum(gt.astype(f32), axis=0, keepdims=True)
        part_s[rows, :] = total
        share_s[rows, :] = back

        @pl.when(t == tiles - 1)
        def _():
            split(early[0], early[2], early[1], early[3])

    @pl.when(chunk == 1)
    def _():
        part[...] = part_s[rows, :] + total
        share[...] = (share_s[rows, :] + back) * gain

        @pl.when(t == tiles - 1)
        def _():
            split(keep_a, keep_b, send_a, send_b)


EARLY = 4


def mlp_own(tok, g, up, upb, down, gains, biases, tile=512, deps=(), rides=(), collective=None):
    length, d = tok.shape
    wide = up.shape[1]
    tiles = length // tile
    rows = pl.BlockSpec((tile, d), lambda i: (lax.rem(i, tiles), 0))
    out_rows = pl.BlockSpec((tile, d), lambda i: (jnp.maximum(i - tiles, 0), 0))
    half = jax.ShapeDtypeStruct((d // 2, d), f32)
    full = jax.ShapeDtypeStruct((length, d), f32)
    eight = jax.ShapeDtypeStruct((8, d), f32)
    big = pltpu.VMEM((length, d), f32)
    return call(
        mlp_own_kernel,
        grid=(2 * tiles,),
        in_specs=[
            rows, rows, pl.BlockSpec((d, wide // 2), lambda i: (0, lax.div(i, tiles))), whole((8, d)),
            pl.BlockSpec((wide // 2, d), lambda i: (lax.div(i, tiles), 0)), whole((2, d)), whole((2, d)),
        ],
        out_specs=[out_rows, out_rows, *[once(half.shape)] * 4, once((8, d)), once((8, d))],
        out_shape=[full, full, half, half, half, half, eight, eight],
        scratch=[pltpu.VMEM((d, wide // 2), f32), pltpu.VMEM((wide // 2, d), f32), big, big] + [pltpu.VMEM(half.shape, f32)] * 4,
        flops=12 * length * d * wide,
        nbytes=4 * length * d * 4,
        deps=deps,
        rides=rides,
        collective=collective,
        name="mlp_own",
    )(tok, g, up, upb, down, gains, biases)


def mlp_other_kernel(chunk, *refs):
    pieces, refs = refs[:12], refs[12:]
    tok, g, upb, gains, biases, part_in, share_in, part, share, w, ow, up, down = refs[:13]
    loaded, sems = refs[13:25], refs[25]

    @pl.when(pl.program_id(0) == 0)
    def _():
        loads = [pltpu.make_async_copy(a, b, sems.at[n]) for n, (a, b) in enumerate(zip(pieces, loaded))]
        for c in loads:
            c.start()
        for c in loads:
            c.wait()
        unpack(loaded, w, ow, up, down)

    nothing = lambda *_: None
    _, _, total, back, gain = mlp_tile(chunk, tok, g, up, upb, down, gains, biases, nothing)
    part[...] = part_in[...] + total
    share[...] = share_in[...] + back * gain


def mlp_other(pieces, tok, g, upb, gains, biases, part, share, shapes, tile=512, chunk=768, deps=(), rides=(), collective=None):
    length, d = tok.shape
    w, ow, up, down = [x.shape for x in shapes]
    rows = pl.BlockSpec((tile, d), lambda i: (i, 0))
    full = jax.ShapeDtypeStruct((length, d), f32)
    return call(
        functools.partial(mlp_other_kernel, chunk),
        grid=(length // tile,),
        in_specs=[pl.BlockSpec(memory_space=pl.ANY)] * 12 + [rows, rows, whole((8, d)), whole((2, d)), whole((2, d)), rows, rows],
        out_specs=[rows, rows, whole(w), whole(ow)],
        out_shape=[full, full, jax.ShapeDtypeStruct(w, bf16), jax.ShapeDtypeStruct(ow, bf16)],
        scratch=[pltpu.VMEM(up, bf16), pltpu.VMEM(down, bf16)] + [pltpu.VMEM(p.shape, f32) for p in pieces] + [pltpu.SemaphoreType.DMA((12,))],
        flops=8 * length * d * up[1],
        nbytes=4 * length * d * 4,
        deps=deps,
        rides=rides,
        collective=collective,
        name="mlp_other",
    )(*pieces, tok, g, upb, gains, biases, part, share)


def first_tokens(lens, places):
    first = jnp.zeros_like(places)
    end = lens[0, 0]
    for j in range(1, lens.shape[1]):
        first = jnp.where(places >= end, end, first)
        end = end + lens[0, j]
    return jnp.where(places >= end, places, first)


def turn(block, cosine, sine, sign):
    parts = []
    for h in range(block.shape[0] // HEAD):
        r = h * HEAD
        a = block[r : r + HALF, :]
        b = block[r + HALF : r + ROT, :]
        if sign > 0:
            parts += [a * cosine - b * sine, b * cosine + a * sine]
        else:
            parts += [a * cosine + b * sine, b * cosine - a * sine]
        parts.append(block[r + ROT : r + HEAD, :])
    return jnp.concatenate(parts, axis=0)


def project_tile(t, tile, bias_row, lens, tok, g, w, bias, ow, gains, biases, freq, own, q, qt, k, kpad, vpad, vone, do, dot_t, cosine, sine):
    rows = pl.ds(pl.multiple_of(t * tile, tile), tile)
    e = ow.shape[0]
    hat, _ = hat_of(tok[rows, :].astype(f32))
    normed = (hat * gains[0:1, :] + biases[0:1, :]).astype(bf16)
    places = t * tile + lax.broadcasted_iota(jnp.int32, (1, tile), 1)
    position = (places - first_tokens(lens, places)).astype(f32)
    theta = freq[:, 0:1] * position
    c = jnp.cos(theta)
    s = jnp.sin(theta)
    cosine[:, rows] = c
    sine[:, rows] = s
    row = bias[bias_row : bias_row + 1, :]
    cols = jnp.concatenate([row[:, :e], row[:, e : 2 * e], jnp.zeros((6, e), f32)], axis=0).T
    scale = HEAD ** (-0.5)
    query = turn(dot(w[0], normed, TT) + cols[:, 0:1], c, s, 1).astype(bf16) * scale
    qt[:, rows] = query
    q[rows, :] = query.T
    key = turn(dot(w[1], normed, TT), c, s, 1).astype(bf16)
    k[rows, :] = key.T
    value = (dot(w[2], normed, TT) + cols[:, 1:2]).astype(bf16)
    zero = jnp.zeros((HEAD, tile), bf16)
    if own:
        row = lax.broadcasted_iota(jnp.int32, (VROWS - HEAD, tile), 0)
        ones = jnp.where(row == 0, 1.0, 0.0).astype(bf16)
    for h in range(e // HEAD):
        sl = slice(h * HEAD, (h + 1) * HEAD)
        at, other = (0, HEAD) if h % 2 == 0 else (HEAD, 0)
        kpad[h, at : at + HEAD, rows] = key[sl, :]
        kpad[h, other : other + HEAD, rows] = zero
        vpad[h, at : at + HEAD, rows] = value[sl, :]
        vpad[h, other : other + HEAD, rows] = zero
        if own:
            vone[h, :HEAD, rows] = value[sl, :]
            vone[h, HEAD:, rows] = ones
    grad = dot(ow[...], g[rows, :], NT).astype(bf16)
    dot_t[:, rows] = grad
    do[rows, :] = grad.T


def low_parts(x):
    high = x.astype(bf16)
    rest = x - high.astype(f32)
    mid = rest.astype(bf16)
    return [high, mid, (rest - mid.astype(f32)).astype(bf16)]


FILLED = 1792


def over_tiles(q0, tk, step, carry):
    last = lax.div(q0, tk)
    first = jnp.where(q0 >= FILLED, last, 0)
    return lax.fori_loop(first, last + 1, step, carry)


VROWS = 80
LOG2E = np.float32(math.log2(math.e))


def forward_tile(q0, tq, tk, first, places, qt, k, vone, ot, qpad, acc):
    heads = qt.shape[0] // HEAD
    zero = jnp.zeros((HEAD, tq), bf16)
    for h in range(heads):
        qh = qt[h * HEAD : (h + 1) * HEAD, pl.ds(q0, tq)]
        qpad[h] = jnp.concatenate([qh, zero] if h % 2 == 0 else [zero, qh], axis=0)
    acc[...] = jnp.zeros_like(acc)

    def step(j, peaks):
        k0 = pl.multiple_of(j * tk, tk)
        rows = k0 + lax.broadcasted_iota(jnp.int32, (tk, tq), 0)
        allowed = (rows >= first) & (rows <= places)
        scores, new, raised = [], [], []
        for h in range(heads):
            pair = (h // 2) * 128
            s = dot(k[pl.ds(k0, tk), pair : pair + 128], qpad[h])
            scores.append(jnp.where(allowed, s, -1e30))
        for h in range(heads):
            new.append(jnp.maximum(peaks[h], jnp.max(scores[h], axis=0, keepdims=True)))
            raised.append(jnp.exp2((scores[h] - new[h]) * LOG2E).astype(bf16))
        for h in range(heads):
            o = dot(vone[h, :, pl.ds(k0, tk)], raised[h])
            acc[h] = acc[h] * jnp.exp(peaks[h] - new[h]) + o
        return tuple(new)

    start = tuple(jnp.full((1, tq), -1e30, f32) for _ in range(heads))
    peaks = over_tiles(q0, tk, step, start)
    logs = []
    for h in range(heads):
        total = acc[h, HEAD : HEAD + 1, :]
        ot[h * HEAD : (h + 1) * HEAD, :] = acc[h, :HEAD, :] / total
        logs.append(peaks[h] + jnp.log(total))
    logs.append(jnp.zeros((8 - heads, tq), f32))
    ot[heads * HEAD :, :] = jnp.concatenate(logs, axis=0)


def backward_tile(q0, tq, tk, first, places, q, qt, k, kpad, vpad, do, dot_t, ot, cosine, sine, grads_q, dk, dv, dq, qa, da, cs, cd):
    heads = q.shape[1] // HEAD
    rows = pl.ds(q0, tq)
    deltas = [
        jnp.sum(ot[h * HEAD : (h + 1) * HEAD, :] * dot_t[h * HEAD : (h + 1) * HEAD, rows].astype(f32), axis=0, keepdims=True)
        for h in range(heads)
    ]
    deltas.append(jnp.zeros((8 - heads, tq), f32))
    stats = low_parts(ot[heads * HEAD :, :]) + low_parts(jnp.concatenate(deltas, axis=0))
    stats.append(jnp.zeros((128 - 48, tq), bf16))
    stat_cols = jnp.concatenate(stats, axis=0).T
    for r in range(heads // 2):
        pair = slice(r * 128, r * 128 + 128)
        qa[r, :, :128] = q[rows, pair]
        qa[r, :, 128:] = stat_cols
        da[r, :, :128] = do[rows, pair]
        da[r, :, 128:] = stat_cols
    dq[...] = jnp.zeros_like(dq)

    def step(j, carry):
        k0 = pl.multiple_of(j * tk, tk)
        ks = pl.ds(k0, tk)
        cols = k0 + lax.broadcasted_iota(jnp.int32, (tq, tk), 1)
        allowed = (cols >= first) & (cols <= places)
        probs, grads = [], []
        for h in range(heads):
            s = dot(qa[h // 2], jnp.concatenate([kpad[h, :, ks], cs[h]], axis=0))
            dp = dot(da[h // 2], jnp.concatenate([vpad[h, :, ks], cd[h]], axis=0))
            p = jnp.where(allowed, jnp.exp(s), 0.0)
            probs.append(p.astype(bf16))
            grads.append((p * dp).astype(bf16))
        for h in range(heads):
            sl = slice(h * HEAD, (h + 1) * HEAD)
            pair = slice((h // 2) * 128, (h // 2) * 128 + 128)
            dv[sl, ks] += dot(dot_t[sl, rows], probs[h])
            dk[sl, ks] += dot(qt[sl, rows], grads[h])
            dq[h] += dot(grads[h], k[ks, pair])
        return carry

    over_tiles(q0, tk, step, 0)
    scale = HEAD ** (-0.5)
    lane = lax.broadcasted_iota(jnp.int32, (tq, 128), 1)
    q_parts = [
        jnp.where(lane < HEAD, dq[2 * h], dq[2 * h + 1]).T * scale for h in range(heads // 2)
    ]
    grads_q[...] = turn(jnp.concatenate(q_parts, axis=0), cosine[:, rows], sine[:, rows], -1).astype(bf16)


def attention_kernel(tk, tile, own, bias_row, lens, tok_all, g_all, w, bias, ow, gains, biases, freq, *refs):
    refs = list(refs)
    cut = lambda n: [refs.pop(0) for _ in range(n)]
    if own:
        ot, ot_send, grads_q, grads_k, grads_v, keep_o, send_o = cut(7)
    else:
        ot, grads_q, grads_k, grads_v = cut(4)
    q, qt, k, kpad, vpad, do, dot_t, cosine, sine, dk, dv, dq, qa, da, cs, cd = cut(16)
    tok, g, sems = cut(3)
    vone, qpad, acc, dow, low = cut(5) if own else (None, None, None, None, None)
    i = pl.program_id(0)
    length = tok.shape[0]
    heads, tq, _ = dq.shape
    q0 = pl.multiple_of(i * tq, tq)

    @pl.when(i == 0)
    def _():
        loads = [pltpu.make_async_copy(a, b, sems.at[n]) for n, (a, b) in enumerate(((tok_all, tok), (g_all, g)))]
        for c in loads:
            c.start()
        dk[...] = jnp.zeros_like(dk)
        dv[...] = jnp.zeros_like(dv)
        row = lax.broadcasted_iota(jnp.int32, (128, tk), 0)
        for h in range(heads):
            cs[h] = jnp.where((row < 24) & (row % 8 == h), -1.0, 0.0).astype(bf16)
            cd[h] = jnp.where((row >= 24) & (row < 48) & (row % 8 == h), -1.0, 0.0).astype(bf16)

        for c in loads:
            c.wait()

        def some(t, c):
            project_tile(t, tile, bias_row, lens, tok, g, w, bias, ow, gains, biases, freq, own, q, qt, k, kpad, vpad, vone, do, dot_t, cosine, sine)
            return c

        lax.fori_loop(0, length // tile, some, 0)

    if own:
        places = q0 + lax.broadcasted_iota(jnp.int32, (1, tq), 1)
        forward_tile(q0, tq, 2 * tk, first_tokens(lens, places), places, qt, k, vone, ot, qpad, acc)
        ot_send[...] = ot[...]
        low[:, pl.ds(q0, tq)] = ot[: ow.shape[0], :].astype(bf16)
    places = q0 + lax.broadcasted_iota(jnp.int32, (tq, 1), 0)
    backward_tile(
        q0, tq, tk, first_tokens(lens, places), places, q, qt, k, kpad, vpad, do, dot_t, ot, cosine, sine, grads_q, dk, dv, dq, qa, da, cs, cd
    )

    @pl.when(i == pl.num_programs(0) - 1)
    def _():
        grads_k[...] = turn(dk[...], cosine[...], sine[...], -1).astype(bf16)
        grads_v[...] = dv[...].astype(bf16)
        if own:
            dow[...] = dot(low[...], g[...])
            r = dow.shape[0] // 2
            for ref, half in ((keep_o, bit_of(0)), (send_o, 1 - bit_of(0))):
                ref[...] = dow[pl.ds(pl.multiple_of(half * r, r), r), :]


def attention(bias_row, lens, tok, g, w, bias, ow, gains, biases, freq, ot=None, tq=256, tk=256, tile=512, deps=(), rides=(), collective=None):
    length, d = tok.shape
    e = w.shape[2]
    heads = e // HEAD
    own = ot is None
    cols = pl.BlockSpec((e, tq), lambda i, *_: (0, i))
    stat = pl.BlockSpec((e + 8, tq), lambda i, *_: (0, i))
    grad = jax.ShapeDtypeStruct((e, length), bf16)
    kept = jax.ShapeDtypeStruct((e + 8, length), f32)
    nat, tr, pad, angle = pltpu.VMEM((length, e), bf16), pltpu.VMEM((e, length), bf16), pltpu.VMEM((heads, 128, length), bf16), pltpu.VMEM((HALF, length), f32)
    scratch = [nat, tr, nat, pad, pad, nat, tr, angle, angle]
    scratch += [pltpu.VMEM((e, length), f32)] * 2 + [pltpu.VMEM((heads, tq, 128), f32)]
    scratch += [pltpu.VMEM((heads // 2, tq, 256), bf16)] * 2 + [pltpu.VMEM((heads, 128, tk), bf16)] * 2
    scratch += [pltpu.VMEM((length, d), bf16)] * 2 + [pltpu.SemaphoreType.DMA((2,))]
    if own:
        scratch += [pltpu.VMEM((heads, VROWS, length), bf16), pltpu.VMEM((heads, 128, tq), bf16), pltpu.VMEM((heads, VROWS, tq), f32), pltpu.VMEM((e, d), f32), tr]
    half = jax.ShapeDtypeStruct((e // 2, d), f32)
    return call(
        functools.partial(attention_kernel, tk, tile, own, bias_row),
        grid=(length // tq,),
        scalars=1,
        in_specs=[
            *[pl.BlockSpec(memory_space=pl.ANY)] * 2, whole((3, d, e)), whole((8, d)), whole((e, d)), whole((2, d)), whole((2, d)), whole((HALF, 128)),
        ] + ([] if own else [stat]),
        out_specs=([stat, stat] if own else []) + [cols, whole((e, length)), whole((e, length))] + ([whole(half.shape)] * 2 if own else []),
        out_shape=([kept, kept] if own else []) + [grad, grad, grad] + ([half, half] if own else []),
        scratch=scratch,
        flops=8 * length * length * e,
        nbytes=20 * length * e,
        deps=deps,
        rides=rides,
        collective=collective,
        name="attention",
    )(lens, tok, g, w, bias, ow, gains, biases, freq, *([] if own else [ot]))


def merge_tile(tok, gq, gk, gv, ot, w, ow, gains, biases):
    hat, inverse = hat_of(tok[...].astype(f32))
    gain = gains[0:1, :]
    back = dot(gq[...], w[0], TT) + dot(gk[...], w[1], TT) + dot(gv[...], w[2], TT)
    low = ot[...].astype(bf16)
    return hat, inverse, gain, back, dot(low, ow[...], TN)


def merge_own_kernel(tok, gq, gk, gv, ot, w, ow, gains, biases, part_in, share_in, small_in, upb_in, part, share, keep_a, send_a, keep_b, send_b, small, dw):
    i = pl.program_id(0)
    tile = tok.shape[0]
    e, d = ow.shape
    n_up = 2

    @pl.when(i == 0)
    def _():
        dw[...] = jnp.zeros_like(dw)
        small[...] = jnp.zeros_like(small)
        small[1:2, :] = small_in[1:2, :]
        small[3:4, :] = small_in[2:3, :]
        small[4:5, :] = small_in[0:1, :]
        small[5 : 5 + n_up, :] = upb_in[:n_up, :]

    hat, _, gain, back, out = merge_tile(tok, gq, gk, gv, ot, w, ow, gains, biases)
    normed = (hat * gain + biases[0:1, :]).astype(bf16)
    share[...] = share_in[...] + back * gain
    part[...] = part_in[...] + out
    dw[0] += dot(normed, gq[...], TT)
    dw[1] += dot(normed, gk[...], TT)
    dw[2] += dot(normed, gv[...], TT)
    small[0:1, :] += jnp.sum(back * hat, axis=0, keepdims=True)
    small[2:3, :] += jnp.sum(back, axis=0, keepdims=True)
    ones = jnp.ones((8, tile), bf16)
    at = 5 + n_up
    small[at : at + 1, :e] += dot(ones, gq[...], NT)[0:1]
    small[at : at + 1, e : 2 * e] += dot(ones, gv[...], NT)[0:1]

    @pl.when(i == pl.num_programs(0) - 1)
    def _():
        core = bit_of(0)
        r = d // 8
        for refs, half in (((keep_a, keep_b), core), ((send_a, send_b), 1 - core)):
            for n in range(6):
                ref, at, c, sub = refs[n // 3], n % 3 * r, n // 2, n % 2
                for s in range(2):
                    rows = pl.multiple_of(half * (d // 2) + (2 * s + sub) * r, r)
                    ref[at : at + r, s * e : (s + 1) * e] = dw[c, pl.ds(rows, r), :]


def merge_own(tok, gq, gk, gv, ot, w, ow, gains, biases, part, share, small, upb, tile=512, deps=(), rides=(), collective=None):
    length, d = tok.shape
    e = w.shape[2]
    rows = pl.BlockSpec((tile, d), lambda i: (i, 0))
    cols = pl.BlockSpec((e, tile), lambda i: (0, i))
    full = jax.ShapeDtypeStruct((length, d), f32)
    half = jax.ShapeDtypeStruct((3 * d // 8, d), f32)
    return call(
        merge_own_kernel,
        grid=(length // tile,),
        in_specs=[rows, cols, cols, cols, cols, whole((3, d, e)), whole((e, d)), whole((2, d)), whole((2, d)), rows, rows, whole((8, d)), whole((8, d))],
        out_specs=[rows, rows, *[once(half.shape)] * 4, once((8, d))],
        out_shape=[full, full, half, half, half, half, jax.ShapeDtypeStruct((8, d), f32)],
        scratch=[pltpu.VMEM((3, d, e), f32)],
        flops=16 * length * d * e,
        nbytes=24 * length * d,
        deps=deps,
        rides=rides,
        collective=collective,
        name="merge_own",
    )(tok, gq, gk, gv, ot, w, ow, gains, biases, part, share, small, upb)


def merge_other_kernel(tok, g, gq, gk, gv, ot, w, ow, gains, biases, out_bias, down_bias, part_in, share_in, output, input_grad):
    hat, inverse, gain, back, out = merge_tile(tok, gq, gk, gv, ot, w, ow, gains, biases)
    shares = share_in[...] + back * gain
    inputs = tok[...].astype(f32)
    output[...] = (inputs + (part_in[...] + out) + out_bias[...].astype(f32) + down_bias[...].astype(f32)).astype(bf16)
    input_share = inverse * (
        shares
        - jnp.mean(shares, axis=-1, keepdims=True)
        - hat * jnp.mean(shares * hat, axis=-1, keepdims=True)
    )
    input_grad[...] = (g[...].astype(f32) + input_share).astype(bf16)


def merge_other(tok, g, gq, gk, gv, ot, w, ow, gains, biases, out_bias, down_bias, part, share, tile=512, deps=(), rides=(), collective=None):
    length, d = tok.shape
    e = w.shape[2]
    rows = pl.BlockSpec((tile, d), lambda i: (i, 0))
    cols = pl.BlockSpec((e, tile), lambda i: (0, i))
    full = jax.ShapeDtypeStruct((length, d), bf16)
    return call(
        merge_other_kernel,
        grid=(length // tile,),
        in_specs=[rows, rows, cols, cols, cols, cols, whole((3, d, e)), whole((e, d)), whole((2, d)), whole((2, d)), whole((1, d)), whole((1, d)), rows, rows],
        out_specs=[rows, rows],
        out_shape=[full, full],
        flops=8 * length * d * e,
        nbytes=24 * length * d,
        deps=deps,
        rides=rides,
        collective=collective,
        name="merge_other",
    )(tok, g, gq, gk, gv, ot, w, ow, gains, biases, out_bias[None], down_bias[None], part, share)


def pack_kernel(meta, w, ow, up, down, w_far, ow_far, up_far, down_far, upb, qkvb, one, two, three, four, bias_rows):
    d = ow.shape[1]
    e = w.shape[2]

    def blocks(refs):
        w, ow, up, down = refs
        for n in range(2):
            r = down.shape[0] // 8
            for s in range(4):
                yield [down[(4 * n + s) * r : (4 * n + s + 1) * r, :]]
            r = up.shape[0] // 2
            for c in range(up.shape[1] // d):
                yield [up[n * r : (n + 1) * r, c * d : (c + 1) * d]]
            r = w.shape[1] // 4
            for c in range(3):
                yield [w[c, (2 * n + s) * r : (2 * n + s + 1) * r, :] for s in range(2)]
            r = ow.shape[0] // 2
            yield [ow[n * r : (n + 1) * r, :]]

    for refs, outs in (((w, ow, up, down), (one, two, three)), ((w_far, ow_far, up_far, down_far), (None, None, four))):
        sizes = [x.shape[0] for x in (one, two, three)]
        which, at = 0, 0
        for parts in blocks(refs):
            rows, lanes = parts[0].shape
            for j, x in enumerate(parts):
                if outs[which] is not None:
                    outs[which][at : at + rows, j * lanes : (j + 1) * lanes] = x.astype(f32)
            at += rows
            if at == sizes[which]:
                which, at = which + 1, 0
    n = upb.shape[1] // d
    bias_rows[...] = jnp.zeros_like(bias_rows)
    for c in range(n):
        bias_rows[c : c + 1, :] = upb[:, c * d : (c + 1) * d].astype(f32)
    for c in range(2):
        bias_rows[n : n + 1, c * e : (c + 1) * e] = qkvb[c : c + 1, :].astype(f32)


def pack(meta, w, ow, up, down, upb, qkvb):
    _, d, e = w.shape
    wide = up.shape[1]
    rows = (wide + (wide // d) * d + 3 * d // 2 + e) // 4
    one = wide // 8 + d // 8
    two = rows // 2 - one + wide // 32
    sizes = [one, two, rows - one - two, rows - one - two, 8]
    blocks = lambda n: [
        pl.BlockSpec((3, d // 4, e), lambda i, m: (0, m[n], 0)),
        pl.BlockSpec((e // 4, d), lambda i, m: (m[n], 0)),
        pl.BlockSpec((d // 4, wide), lambda i, m: (m[n], 0)),
        pl.BlockSpec((wide // 4, d), lambda i, m: (m[n], 0)),
    ]
    return call(
        pack_kernel,
        grid=(1,),
        scalars=1,
        in_specs=blocks(0) + blocks(1) + [whole((1, wide)), whole((2, e))],
        out_specs=[once((r, d)) for r in sizes],
        out_shape=[jax.ShapeDtypeStruct((r, d), f32) for r in sizes],
        name="pack",
    )(meta, w, ow, up, down, w, ow, up, down, upb[None], qkvb)


def unpack(pieces, w, ow, up, down):
    d = ow.shape[1]
    e = w.shape[2]
    for n in range(4):
        core = lax.rem(bit_of(0) + n // 2, 2)
        parity = lax.rem(bit_of(1) + bit_of(2) + n % 2, 2)
        refs = pieces[3 * n : 3 * n + 3]
        place = [0, 0]

        def take(rows):
            ref, at = refs[place[0]], place[1]
            place[1] = at + rows
            if place[1] == ref.shape[0]:
                place[:] = [place[0] + 1, 0]
            return ref[at : at + rows, :].astype(bf16)

        for m in range(2):
            at_piece = (parity * 2 + core) * 2 + m
            rows = lambda r, sub=0, parts=1: pl.ds(pl.multiple_of((at_piece * parts + sub) * r, r), r)
            r = down.shape[0] // 32
            for s in range(4):
                down[rows(r, s, 4), :] = take(r)
            r = up.shape[0] // 8
            for c in range(up.shape[1] // d):
                up[rows(r), c * d : (c + 1) * d] = take(r)
            r = w.shape[1] // 16
            for c in range(3):
                x = take(r)
                for s in range(2):
                    w[c, rows(r, s, 2), :] = x[:, s * e : (s + 1) * e]
            r = ow.shape[0] // 8
            ow[rows(r), :] = take(r)


def swap(x, bit):
    n = lax.axis_size("dp")
    return lax.ppermute(x, "dp", [(i, i ^ (1 << bit)) for i in range(n)])


def across(x):
    return lax.ppermute(x, "tensor", [(0, 1), (1, 0)])


def tie(arrays, deps):
    n = len(arrays)
    anywhere = [pl.BlockSpec(memory_space=pl.ANY)] * n
    return call(
        lambda *refs: None,
        grid=(1,),
        in_specs=anywhere,
        out_specs=anywhere,
        out_shape=[jax.ShapeDtypeStruct(x.shape, x.dtype) for x in arrays],
        aliases={i: i for i in range(n)},
        deps=deps,
        name="tie",
    )(*arrays)


def down_places(d, wide):
    rows = d // 2

    def places(sources, outs, core):
        return [
            (x, outs[0].at[pl.ds(pl.multiple_of(c * d + core * rows, 8), rows)]) for c, x in enumerate(sources)
        ]

    return [(wide, d)], wide // d, places


def up_places(d, wide):
    rows = d // 2

    def places(sources, outs, core):
        to = pl.ds(pl.multiple_of(core * rows, 8), rows)
        return [(x, outs[0].at[to, pl.ds(c * d, d)]) for c, x in enumerate(sources)]

    return [(d, wide)], wide // d, places


def attn_places(d, e):
    rows = d // 8

    def places(sources, outs, core):
        pairs = []
        for n in range(6):
            source, at, c, sub = sources[n // 3], n % 3 * rows, n // 2, n % 2
            for s in range(2):
                to = pl.ds(pl.multiple_of(core * (d // 2) + (2 * s + sub) * rows, 8), rows)
                pairs.append((source.at[pl.ds(at, rows), pl.ds(s * e, e)], outs[0].at[c, to]))
        to = pl.ds(pl.multiple_of(core * (e // 2), 8), e // 2)
        pairs.append((sources[2], outs[1].at[to]))
        return pairs

    return [(3, d, e), (e, d)], 13, places


def relay(rides, collective, deps=()):
    call(
        lambda *_: None,
        grid=(1,),
        in_specs=[],
        out_specs=[],
        out_shape=[],
        deps=deps,
        rides=rides,
        collective=collective,
        name="relay",
    )()


def per_device(
    tokens, lengths, qkv_weight, qkv_bias, out_weight, out_bias, up_weight, up_bias, down_weight, down_bias, norm_gains, norm_biases, cotangent
):
    length, d = tokens.shape
    e = qkv_weight.shape[2]
    wide = up_weight.shape[1]
    bits = lax.axis_size("dp").bit_length() - 1
    me = lax.axis_index("dp")
    quarter = lambda p: (((me >> 1) ^ (me >> 2) ^ p) & 1) * 2 + (me & 1)
    meta = jnp.stack([quarter(0), quarter(1)])
    freq = np.broadcast_to((rot_base ** (-(2.0 * np.arange(HALF)) / ROT)).astype(np.float32)[:, None], (HALF, 128))
    one, two, three, far_three, own_biases = pack(
        meta, qkv_weight, out_weight, up_weight, down_weight, up_bias, qkv_bias
    )
    order = list(range(1, bits))
    crossed = [order[1], order[0]] + order[2:]
    early = [Held(EARLY + j, (d // 2, d)) for j in range(4)]
    down_1, up_1 = Sum(early[0], early[1], order), Sum(early[2], early[3], crossed)
    send = Sends((one, "tensor"), (own_biases, "tensor"), (two, "tensor"))
    part, share, keep_d, send_d, keep_u, send_u, small, upb_sum = mlp_own(
        tokens, cotangent, up_weight, own_biases, down_weight, norm_gains, norm_biases,
        rides=[send, down_1.take(4, 5), up_1.take(4, 5)], collective=1,
    )
    one, other_biases, two = send.got
    down_2, up_2 = Sum(keep_d, send_d, order), Sum(keep_u, send_u, crossed)
    send = Sends((three, "tensor"), (far_three, "tensor"), (one, 0), (two, 0))
    near = [Sends((one, 1), at=(2,)), Sends((two, 1), at=(5,))]
    ot, ot_send, gq, gk, gv, keep_o, send_o = attention(
        wide // d, lengths, tokens, cotangent, qkv_weight, own_biases, out_weight, norm_gains, norm_biases, freq,
        rides=[down_1.take(0, 1, 4), up_1.take(0, 1, 4), down_2.take(0, 1, 5, 6), up_2.take(0, 1, 5, 6), send] + near, collective=2,
    )
    three, near_three, core_one, core_two = send.got
    (near_one,), (near_two,) = near[0].got, near[1].got
    other_ot = across(ot_send)
    sum_o = Sum(keep_o, send_o, order, True)
    send = Sends((near_one, 0), (near_two, 0), (near_three, 0), (three, 0))
    part, share, keep_a, send_a, keep_b, send_b, small = merge_own(
        tokens, gq, gk, gv, ot, qkv_weight, out_weight, norm_gains, norm_biases, part, share, small, upb_sum,
        rides=[down_2.take(0), up_2.take(0), down_1.take(0), up_1.take(0), sum_o.take(0), send], collective=3,
    )
    core_near_one, core_near_two, core_near_three, core_three = send.got
    sum_a, sum_b, sum_s = Sum(keep_a, send_a, order, True), Sum(keep_b, send_b, crossed, True), SmallSum(small, bits)
    pieces = [one, two, three, near_one, near_two, near_three]
    pieces += [core_one, core_two, core_three, core_near_one, core_near_two, core_near_three]
    part, share, other_w, other_ow = mlp_other(
        pieces, tokens, cotangent, other_biases, norm_gains, norm_biases, part, share, [qkv_weight, out_weight, up_weight, down_weight],
        rides=[
            sum_s.take(0, 3), sum_a.take(0, 1, 3), sum_b.take(0, 1, 3), sum_o.take(1, 3), down_2.take(0), up_2.take(0), down_1.take(0), up_1.take(0),
        ],
        collective=4,
    )
    (other_ot,) = tie([other_ot], [part])
    gq, gk, gv = attention(
        wide // d, lengths, tokens, cotangent, other_w, other_biases, other_ow, norm_gains, norm_biases, freq, other_ot,
        rides=[s.take(0, 5, 6) for s in (sum_a, sum_b, sum_o)] + [down_2.take(0), up_2.take(0), sum_s.take(0, 6)], collective=5,
    )
    at = 7
    sums = [down_1, down_2, up_1, up_2, sum_a, sum_b, sum_o]
    while not all(s.done for s in sums):
        relay([s.take(0) for s in sums if not s.done], at)
        at += 1
    final_d, final_u = Final(sums[:2], *down_places(d, wide)), Final(sums[2:4], *up_places(d, wide))
    final = Final(sums[4:], *attn_places(d, e))
    output, input_grad = merge_other(
        tokens, cotangent, gq, gk, gv, other_ot, other_w, other_ow, norm_gains, norm_biases, out_bias, down_bias, part, share,
        rides=[sum_s.take(0), final_d, final_u, final], collective=6,
    )
    while not sum_s.done:
        relay([sum_s.take(0)], at)
        at += 1
    (d_down,), (d_up,), (d_qkv, d_out) = final_d.results, final_u.results, final.results
    small = sum_s.mine
    rest = small[5:].reshape(-1)
    return (
        output, input_grad, d_qkv, rest[wide : wide + 2 * e].reshape(2, e), d_out, small[4], d_up, rest[:wide], d_down, small[4], small[:2], small[2:4],
    )


def solution(mesh):
    in_specs = (
        P("dp", None), P("dp", None), P(None, None, "tensor"), P(None, "tensor"), P("tensor", None), P(), P(None, "tensor"),
        P("tensor"), P("tensor", None), P(), P(), P(), P("dp", None),
    )
    out_specs = (
        P("dp", None), P("dp", None), P(None, None, "tensor"), P(None, "tensor"), P("tensor", None), P(), P(None, "tensor"),
        P("tensor"), P("tensor", None), P(), P(), P(),
    )
    return jax.shard_map(per_device, mesh=mesh, in_specs=in_specs, out_specs=out_specs, check_vma=False)
```

```python
import functools
import math

import jax
import jax.numpy as jnp
import numpy as np
from jax import lax
from jax.experimental import pallas as pl
from jax.experimental.pallas import tpu as pltpu
from jax.sharding import PartitionSpec as P

HEAD = 64
ROT = 16
HALF = ROT // 2
epsilon = 1e-05
rot_base = 10000.0
f32 = jnp.float32
bf16 = jnp.bfloat16
NN = (((1,), (0,)), ((), ()))
NT = (((1,), (1,)), ((), ()))
TN = (((0,), (0,)), ((), ()))
TT = (((0,), (1,)), ((), ()))
VMEM_LIMIT = 60 * 2**20


def dot(a, b, dims=NN):
    return lax.dot_general(a, b, dims, preferred_element_type=f32)


MESH = pl.DeviceIdType.MESH


def bit_of(b):
    return lax.rem(lax.div(lax.axis_index("dp"), 1 << b), 2)


def partner(flip):
    if flip == "tensor":
        return {"tensor": 1 - lax.axis_index("tensor")}
    return {"dp": lax.axis_index("dp") + (1 - 2 * bit_of(flip)) * (1 << flip)}


def by_rows(rows, step):
    size = next(c for c in (96, 48, 24, 8, rows) if rows % c == 0)
    if rows == size:
        step(0, size)
    else:
        lax.fori_loop(0, rows // size, lambda j, c: (step(pl.multiple_of(j * size, 8), size), c)[1], 0)


class Sends:
    def __init__(self, *phases, at=(0,)):
        self.at = at
        self.phases = phases if isinstance(phases[0], list) else [list(phases)]
        moves = [m for phase in self.phases for m in phase]
        self.flips = [flip for _, flip in moves]
        self.inputs = [x for x, _ in moves if not isinstance(x, int)]
        shapes = []
        for x, _ in moves:
            shapes.append(shapes[x] if isinstance(x, int) else jax.ShapeDtypeStruct(x.shape, x.dtype))
        self.outputs = [(s, True) for s in shapes]
        self.scratch = [pltpu.SemaphoreType.DMA((2, len(moves)))]

    def build(self, ins, outs, scratch, _):
        sems, ins, events, j = scratch[0], list(ins), [], 0
        for phase in self.phases:
            copies = []
            for x, flip in phase:
                source = outs[x] if isinstance(x, int) else ins.pop(0)
                copies.append(
                    pltpu.make_async_remote_copy(
                        src_ref=source, dst_ref=outs[j], send_sem=sems.at[0, j], recv_sem=sems.at[1, j], device_id=partner(flip), device_id_type=MESH
                    )
                )
                j += 1

            def begin(copies=copies):
                for c in copies:
                    c.start()

            def finish(copies=copies):
                for c in copies:
                    c.wait()

            events.append((begin, finish))
        return events

    def receive(self, outs):
        self.got = list(outs)


class Held:
    def __init__(self, place, shape):
        self.place, self.shape = place, shape


class Sum:
    def __init__(self, keep, send, order, whole=False):
        self.mine, self.send = keep, send
        halved = [b for j, b in enumerate(order[:-1] if whole else order) if keep.shape[0] % (16 << j) == 0]
        way = [0] + halved
        self.steps = [(way[j], "halve", b) for j, b in enumerate(halved)] + [(way[-1], "add", None)]
        self.steps += [(b, "add", None) for b in order if b not in halved]
        self.steps += [(b, "join", b) for b in reversed(halved)]

    @property
    def done(self):
        return not self.steps

    def take(self, *at):
        steps, self.steps = self.steps[: len(at)], self.steps[len(at) :]
        return Steps(self, steps, at[: len(steps)])


class SmallSum(Sum):
    def __init__(self, x, bits):
        self.mine = self.send = x
        self.steps = [(b, "add", None) for b in range(bits)] + [("tensor", "norm", None)]


class Final:
    def __init__(self, sums, shapes, count, places):
        self.sums, self.shapes, self.count, self.places = sums, shapes, count, places
        self.at, self.flips = (0, 2), [0]

    @property
    def inputs(self):
        return [s.mine for s in self.sums]

    @property
    def outputs(self):
        return [(jax.ShapeDtypeStruct(s, f32), True) for s in self.shapes]

    @property
    def scratch(self):
        stage = [pltpu.VMEM(s.mine.shape, f32) for s in self.sums]
        return [pltpu.SemaphoreType.DMA((3, self.count)), pltpu.SemaphoreType.DMA((len(stage),))] + stage

    def build(self, ins, outs, scratch, _):
        put = lambda sources: self.places(sources, outs, bit_of(0))
        sems, load_sems, *held = scratch
        there, loads, here = place_parts(put, ins, held, 0, sems, load_sems)

        def wait_all():
            for c in here + there:
                c.wait()

        return [
            (lambda: [c.start() for c in there + loads], lambda: [c.wait() for c in loads]),
            (lambda: [c.start() for c in here], wait_all),
        ]

    def receive(self, outs):
        self.results = list(outs)


def place_parts(put, sources, held, flip, sems, load_sems):
    at = (lambda k, j: sems.at[k]) if load_sems is None else (lambda k, j: sems.at[k, j])
    there = [
        pltpu.make_async_remote_copy(
            src_ref=s, dst_ref=t, send_sem=at(0, j), recv_sem=at(1, j), device_id=partner(flip), device_id_type=MESH
        )
        for j, (s, t) in enumerate(put(sources))
    ]
    loads = [] if held is None else [
        pltpu.make_async_copy(s, h, sems.at[2] if load_sems is None else load_sems.at[j]) for j, (s, h) in enumerate(zip(sources, held))
    ]
    here = [pltpu.make_async_copy(s, t, at(2, j)) for j, (s, t) in enumerate(put(sources if held is None else held))]
    return there, loads, here


def place_copies(put, sources, held, flip, sems, load_sems):
    there, loads, here = place_parts(put, sources, held, flip, sems, load_sems)

    def begin():
        for c in there + (here if held is None else loads):
            c.start()

    def finish():
        for c in loads:
            c.wait()
        if held is not None:
            for c in here:
                c.start()
        for c in here + there:
            c.wait()

    return begin, finish


class Steps:
    def __init__(self, owner, steps, at):
        self.owner, self.steps, self.at = owner, steps, at
        self.flips = [s[0] for s in steps]
        self.same = owner.mine is owner.send
        reads = [k for _, k, _ in steps][0] in ("halve", "add", "norm")
        self.inputs = [owner.send] + ([owner.mine] if reads and not self.same else [])
        self.outputs, self.scratch = [], []
        rows, d = owner.send.shape
        self.places = None
        local = True
        if isinstance(owner.send, Held):
            self.places, self.inputs, local = (owner.send.place, owner.mine.place), [], False
        for n, (_, kind, _) in enumerate(steps):
            last = n == len(steps) - 1
            self.scratch.append(pltpu.SemaphoreType.DMA((3,)))
            if kind in ("halve", "add", "norm"):
                self.scratch += [pltpu.VMEM((rows, d), f32)] * (2 if local else 1)
                rows = rows // 2 if kind == "halve" else rows
                shapes = [(rows, d)] * (2 if kind == "halve" else 1)
                if last:
                    self.outputs += [(jax.ShapeDtypeStruct(s, f32), False) for s in shapes]
                local = False
            elif kind == "join":
                if local:
                    self.scratch.append(pltpu.VMEM((rows, d), f32))
                local = True
                rows *= 2
                self.outputs.append((jax.ShapeDtypeStruct((rows, d), f32), True))

    def build(self, ins, outs, scratch, kernel_scratch):
        outs, scratch = list(outs), list(scratch)
        if self.places is not None:
            ins = [kernel_scratch[p] for p in self.places]
        send = ins[0]
        mine = ins[-1]
        events = []
        in_hbm = self.places is None
        for n, (flip, kind, bit) in enumerate(self.steps):
            last = n == len(self.steps) - 1
            sems = scratch.pop(0)
            rows = send.shape[0]
            if kind in ("halve", "add", "norm"):
                got = scratch.pop(0)
                held = scratch.pop(0) if in_hbm else mine
                fresh = kept = None
                if last:
                    fresh = outs.pop(0)
                    kept = outs.pop(0) if kind == "halve" else None
                elif kind == "halve":
                    r, v = held.shape[0] // 2, bit_of(bit)
                    fresh, kept = (held.at[pl.ds(pl.multiple_of(h * r, 8), r)] for h in (1 - v, v))
                else:
                    fresh = held
                events.append(self.reduce(kind, bit, flip, send, mine, in_hbm, got, held, fresh, kept, sems))
                send, mine, in_hbm = fresh, (fresh if kept is None else kept), False
            elif kind == "join":
                target = outs.pop(0)
                held = scratch.pop(0) if in_hbm else None
                put = lambda xs, target=target, bit=bit, rows=rows: [
                    (xs[0], target.at[pl.ds(pl.multiple_of(bit_of(bit) * rows, 8), rows)])
                ]
                events.append(self.copies(put, send, held, flip, sems))
                send = mine = target
                in_hbm = True
        return events

    @staticmethod
    def copies(put, send, held, flip, sems, load_sems=None):
        return place_copies(put, [send], None if held is None else [held], flip, sems, load_sems)

    @staticmethod
    def reduce(kind, bit, flip, send, mine, in_hbm, got, held, fresh, kept, sems):
        there = pltpu.make_async_remote_copy(
            src_ref=send, dst_ref=got, send_sem=sems.at[0], recv_sem=sems.at[1], device_id=partner(flip), device_id_type=MESH
        )
        load = pltpu.make_async_copy(mine, held, sems.at[2]) if in_hbm else None

        def add_half(out, half, r):
            base = half * r

            def step(j, size):
                rows = pl.ds(pl.multiple_of(base + j, 8), size)
                out[pl.ds(j, size), :] = held[rows, :] + got[rows, :]

            by_rows(r, step)

        def begin():
            there.start()
            if load is not None:
                load.start()

        def after():
            if kind == "halve":
                add_half(kept, bit_of(bit), held.shape[0] // 2)

        def finish():
            if load is not None:
                load.wait()
            there.wait()
            if kind == "halve":
                r = held.shape[0] // 2
                v = bit_of(bit)
                add_half(fresh, 1 - v, r)
            elif kind == "norm":
                row = lax.broadcasted_iota(jnp.int32, held.shape, 0)
                fresh[...] = held[...] + jnp.where(row < 4, got[...], 0.0)
            else:

                def step(j, size):
                    rows = pl.ds(j, size)
                    fresh[rows, :] = held[rows, :] + got[rows, :]

                by_rows(held.shape[0], step)

        return begin, finish, after

    def receive(self, outs):
        outs = list(outs)
        owner = self.owner
        for n, (_, kind, _) in enumerate(self.steps):
            last = n == len(self.steps) - 1
            if kind == "join":
                owner.mine = owner.send = outs.pop(0)
            elif last:
                owner.send = outs.pop(0)
                owner.mine = outs.pop(0) if kind == "halve" else owner.send


def call(
    kernel, *, grid, in_specs, out_specs, out_shape, scalars=0, scratch=(), deps=(), rides=(), collective=None, flops=0, nbytes=0, name=None, aliases=None
):
    single = not isinstance(out_shape, (list, tuple))
    out_specs = [out_specs] if single else list(out_specs)
    out_shape = [out_shape] if single else list(out_shape)
    n_in, n_out, n_scratch = scalars + len(in_specs), len(out_shape), len(scratch)
    anywhere = pl.BlockSpec(memory_space=pl.ANY)
    ride_in = [x for r in rides for x in r.inputs]
    ride_out = [o for r in rides for o in r.outputs]
    flips = list(dict.fromkeys(f for r in rides for f in r.flips))

    def body(*refs):
        refs = list(refs)
        cut = lambda n: [refs.pop(0) for _ in range(n)]
        ins, _, sources = cut(n_in), cut(len(deps)), cut(len(ride_in))
        outs, targets, held = cut(n_out), cut(len(ride_out)), cut(n_scratch)
        at_step, at_end = {}, []
        for r in rides:
            take = lambda refs, n: [refs.pop(0) for _ in range(n)]
            events = r.build(take(sources, len(r.inputs)), take(targets, len(r.outputs)), take(refs, len(r.scratch)), held)
            for n, (begin, finish, *after) in enumerate(events):
                at_step.setdefault(r.at[n], ([], []))[0].append(begin)
                if n + 1 < len(events):
                    step = at_step.setdefault(r.at[n + 1], ([], []))
                    step[0].append(finish)
                    step[1].extend(after)
                else:
                    at_end += [finish] + after
        if rides:

            @pl.when(pl.program_id(0) == 0)
            def _():
                barrier = pltpu.get_barrier_semaphore()
                for f in flips:
                    pl.semaphore_signal(barrier, inc=1, device_id=partner(f), device_id_type=MESH)
                pl.semaphore_wait(barrier, len(flips))

        for g, acts in at_step.items():

            @pl.when(pl.program_id(0) == g)
            def _(acts=acts):
                for act in acts[0] + acts[1]:
                    act()

        kernel(*ins, *outs, *held)
        if at_end:

            @pl.when(pl.program_id(0) == pl.num_programs(0) - 1)
            def _():
                for act in at_end:
                    act()

    params = dict(vmem_limit_bytes=VMEM_LIMIT)
    if rides:
        params.update(collective_id=collective, has_side_effects=True)

    def run(*args):
        outs = pl.pallas_call(
            body,
            grid_spec=pltpu.PrefetchScalarGridSpec(
                num_scalar_prefetch=scalars,
                grid=grid,
                in_specs=list(in_specs) + [anywhere] * (len(deps) + len(ride_in)),
                out_specs=out_specs + [anywhere if hbm else once(s.shape) for s, hbm in ride_out],
                scratch_shapes=list(scratch) + [s for r in rides for s in r.scratch],
            ),
            out_shape=out_shape + [s for s, _ in ride_out],
            compiler_params=pltpu.CompilerParams(**params),
            cost_estimate=pl.CostEstimate(flops=20 * flops, bytes_accessed=nbytes, transcendentals=0),
            input_output_aliases=aliases or {},
            name=name,
        )(*args, *deps, *ride_in)
        outs = list(outs)
        own, rest = outs[:n_out], outs[n_out:]
        for r in rides:
            r.receive(rest[: len(r.outputs)])
            rest = rest[len(r.outputs) :]
        return own[0] if single else own

    return run


def whole(shape):
    zeros = (0,) * len(shape)
    return pl.BlockSpec(shape, lambda *_: zeros, pipeline_mode=pl.Buffered(1))


def once(shape):
    zeros = (0,) * len(shape)
    return pl.BlockSpec(shape, lambda *_: zeros)


def hat_of(values):
    average = jnp.mean(values, axis=-1, keepdims=True)
    centered = values - average
    inverse = lax.rsqrt(jnp.mean(centered * centered, axis=-1, keepdims=True) + epsilon)
    return centered * inverse, inverse


def gelu_pair(h):
    t = 1.0 / (1.0 + np.float32(0.3275911 * math.sqrt(0.5)) * jnp.abs(h))
    bell = jnp.exp2((h * h) * np.float32(-0.5 * math.log2(math.e)))
    poly = np.float32(0.5 * 1.061405429) * t + np.float32(0.5 * -1.453152027)
    poly = poly * t + np.float32(0.5 * 1.421413741)
    poly = poly * t + np.float32(0.5 * -0.284496736)
    poly = poly * t + np.float32(0.5 * 0.254829592)
    tail = poly * t * bell
    phi = jnp.where(h >= 0, 1.0 - tail, tail)
    return h * phi, phi + h * bell * np.float32(1.0 / math.sqrt(2.0 * math.pi))


def mlp_tile(chunk, tok, g, up, upb, down, gains, biases, visit):
    hat, _ = hat_of(tok[...].astype(f32))
    gain = gains[1:2, :]
    normed = (hat * gain + biases[1:2, :]).astype(bf16)
    gt = g[...]
    d = tok.shape[1]
    up_bias = jnp.concatenate([upb[c : c + 1, :] for c in range(up.shape[1] // d)], axis=1)
    total = None
    back = None
    for c in range(up.shape[1] // chunk):
        sl = slice(c * chunk, (c + 1) * chunk)
        hidden = dot(normed, up[:, sl]) + up_bias[:, sl]
        act_grad = dot(gt, down[sl, :], NT)
        act, slope = gelu_pair(hidden)
        act = act.astype(bf16)
        hid_grad = (act_grad * slope).astype(bf16)
        p = dot(act, down[sl, :])
        e = dot(hid_grad, up[:, sl], NT)
        total = p if total is None else total + p
        back = e if back is None else back + e
        visit(sl, normed, gt, act, hid_grad)
    return hat, gt, total, back, gain


def mlp_own_kernel(tok, g, up, upb, down, gains, biases, part, share, keep_a, send_a, keep_b, send_b, small, upb_sum, dup, ddown, part_s, share_s, *early):
    i = pl.program_id(0)
    tiles = pl.num_programs(0) // 2
    chunk, t = lax.div(i, tiles), lax.rem(i, tiles)
    tile, d = tok.shape

    @pl.when(i == 0)
    def _():
        small[...] = jnp.zeros_like(small)
        upb_sum[...] = jnp.zeros_like(upb_sum)
        small[0:1, :] = jnp.zeros_like(small[0:1, :])

    @pl.when(t == 0)
    def _():
        dup[...] = jnp.zeros_like(dup)
        ddown[...] = jnp.zeros_like(ddown)

    hat, _ = hat_of(tok[...].astype(f32))
    gain = gains[1:2, :]
    normed = (hat * gain + biases[1:2, :]).astype(bf16)
    gt = g[...]
    hidden = dot(normed, up[...]) + upb[pl.ds(chunk, 1), :]
    act_grad = dot(gt, down[...], NT)
    act, slope = gelu_pair(hidden)
    act = act.astype(bf16)
    hid_grad = (act_grad * slope).astype(bf16)
    total = dot(act, down[...])
    back = dot(hid_grad, up[...], NT)
    dup[...] += dot(normed, hid_grad, TN)
    ddown[...] += dot(act, gt, TN)
    upb_sum[pl.ds(chunk, 1), :] += jnp.sum(hid_grad.astype(f32), axis=0, keepdims=True)
    small[1:2, :] += jnp.sum(back * hat, axis=0, keepdims=True)
    small[2:3, :] += jnp.sum(back, axis=0, keepdims=True)
    rows = pl.ds(pl.multiple_of(t * tile, tile), tile)

    def split(first, second, first_send, second_send):
        core = bit_of(0)
        for a, b, half in ((first, second, core), (first_send, second_send, 1 - core)):
            at = pl.ds(pl.multiple_of(half * (d // 2), d // 2), d // 2)
            a[...] = ddown[at, :]
            b[...] = dup[at, :]

    @pl.when(chunk == 0)
    def _():
        small[0:1, :] += jnp.sum(gt.astype(f32), axis=0, keepdims=True)
        part_s[rows, :] = total
        share_s[rows, :] = back

        @pl.when(t == tiles - 1)
        def _():
            split(early[0], early[2], early[1], early[3])

    @pl.when(chunk == 1)
    def _():
        part[...] = part_s[rows, :] + total
        share[...] = (share_s[rows, :] + back) * gain

        @pl.when(t == tiles - 1)
        def _():
            split(keep_a, keep_b, send_a, send_b)


EARLY = 4


def mlp_own(tok, g, up, upb, down, gains, biases, tile=512, deps=(), rides=(), collective=None):
    length, d = tok.shape
    wide = up.shape[1]
    tiles = length // tile
    rows = pl.BlockSpec((tile, d), lambda i: (lax.rem(i, tiles), 0))
    out_rows = pl.BlockSpec((tile, d), lambda i: (jnp.maximum(i - tiles, 0), 0))
    half = jax.ShapeDtypeStruct((d // 2, d), f32)
    full = jax.ShapeDtypeStruct((length, d), f32)
    eight = jax.ShapeDtypeStruct((8, d), f32)
    big = pltpu.VMEM((length, d), f32)
    return call(
        mlp_own_kernel,
        grid=(2 * tiles,),
        in_specs=[
            rows, rows, pl.BlockSpec((d, wide // 2), lambda i: (0, lax.div(i, tiles))), whole((8, d)),
            pl.BlockSpec((wide // 2, d), lambda i: (lax.div(i, tiles), 0)), whole((2, d)), whole((2, d)),
        ],
        out_specs=[out_rows, out_rows, *[once(half.shape)] * 4, once((8, d)), once((8, d))],
        out_shape=[full, full, half, half, half, half, eight, eight],
        scratch=[pltpu.VMEM((d, wide // 2), f32), pltpu.VMEM((wide // 2, d), f32), big, big] + [pltpu.VMEM(half.shape, f32)] * 4,
        flops=12 * length * d * wide,
        nbytes=4 * length * d * 4,
        deps=deps,
        rides=rides,
        collective=collective,
        name="mlp_own",
    )(tok, g, up, upb, down, gains, biases)


def mlp_other_kernel(chunk, *refs):
    pieces, refs = refs[:12], refs[12:]
    tok, g, upb, gains, biases, part_in, share_in, part, share, w, ow, up, down = refs[:13]
    loaded, sems = refs[13:25], refs[25]

    @pl.when(pl.program_id(0) == 0)
    def _():
        loads = [pltpu.make_async_copy(a, b, sems.at[n]) for n, (a, b) in enumerate(zip(pieces, loaded))]
        for c in loads:
            c.start()
        for c in loads:
            c.wait()
        unpack(loaded, w, ow, up, down)

    nothing = lambda *_: None
    _, _, total, back, gain = mlp_tile(chunk, tok, g, up, upb, down, gains, biases, nothing)
    part[...] = part_in[...] + total
    share[...] = share_in[...] + back * gain


def mlp_other(pieces, tok, g, upb, gains, biases, part, share, shapes, tile=512, chunk=768, deps=(), rides=(), collective=None):
    length, d = tok.shape
    w, ow, up, down = [x.shape for x in shapes]
    rows = pl.BlockSpec((tile, d), lambda i: (i, 0))
    full = jax.ShapeDtypeStruct((length, d), f32)
    return call(
        functools.partial(mlp_other_kernel, chunk),
        grid=(length // tile,),
        in_specs=[pl.BlockSpec(memory_space=pl.ANY)] * 12 + [rows, rows, whole((8, d)), whole((2, d)), whole((2, d)), rows, rows],
        out_specs=[rows, rows, whole(w), whole(ow)],
        out_shape=[full, full, jax.ShapeDtypeStruct(w, bf16), jax.ShapeDtypeStruct(ow, bf16)],
        scratch=[pltpu.VMEM(up, bf16), pltpu.VMEM(down, bf16)] + [pltpu.VMEM(p.shape, f32) for p in pieces] + [pltpu.SemaphoreType.DMA((12,))],
        flops=8 * length * d * up[1],
        nbytes=4 * length * d * 4,
        deps=deps,
        rides=rides,
        collective=collective,
        name="mlp_other",
    )(*pieces, tok, g, upb, gains, biases, part, share)


def first_tokens(lens, places):
    first = jnp.zeros_like(places)
    end = lens[0, 0]
    for j in range(1, lens.shape[1]):
        first = jnp.where(places >= end, end, first)
        end = end + lens[0, j]
    return jnp.where(places >= end, places, first)


def turn(block, cosine, sine, sign):
    parts = []
    for h in range(block.shape[0] // HEAD):
        r = h * HEAD
        a = block[r : r + HALF, :]
        b = block[r + HALF : r + ROT, :]
        if sign > 0:
            parts += [a * cosine - b * sine, b * cosine + a * sine]
        else:
            parts += [a * cosine + b * sine, b * cosine - a * sine]
        parts.append(block[r + ROT : r + HEAD, :])
    return jnp.concatenate(parts, axis=0)


def project_tile(t, tile, bias_row, lens, tok, g, w, bias, ow, gains, biases, freq, own, q, qt, k, kpad, vpad, vone, do, dot_t, cosine, sine):
    rows = pl.ds(pl.multiple_of(t * tile, tile), tile)
    e = ow.shape[0]
    hat, _ = hat_of(tok[rows, :].astype(f32))
    normed = (hat * gains[0:1, :] + biases[0:1, :]).astype(bf16)
    places = t * tile + lax.broadcasted_iota(jnp.int32, (1, tile), 1)
    position = (places - first_tokens(lens, places)).astype(f32)
    theta = freq[:, 0:1] * position
    c = jnp.cos(theta)
    s = jnp.sin(theta)
    cosine[:, rows] = c
    sine[:, rows] = s
    row = bias[bias_row : bias_row + 1, :]
    cols = jnp.concatenate([row[:, :e], row[:, e : 2 * e], jnp.zeros((6, e), f32)], axis=0).T
    scale = HEAD ** (-0.5)
    query = turn(dot(w[0], normed, TT) + cols[:, 0:1], c, s, 1).astype(bf16) * scale
    qt[:, rows] = query
    q[rows, :] = query.T
    key = turn(dot(w[1], normed, TT), c, s, 1).astype(bf16)
    k[rows, :] = key.T
    value = (dot(w[2], normed, TT) + cols[:, 1:2]).astype(bf16)
    zero = jnp.zeros((HEAD, tile), bf16)
    if own:
        row = lax.broadcasted_iota(jnp.int32, (VROWS - HEAD, tile), 0)
        ones = jnp.where(row == 0, 1.0, 0.0).astype(bf16)
    for h in range(e // HEAD):
        sl = slice(h * HEAD, (h + 1) * HEAD)
        at, other = (0, HEAD) if h % 2 == 0 else (HEAD, 0)
        kpad[h, at : at + HEAD, rows] = key[sl, :]
        kpad[h, other : other + HEAD, rows] = zero
        vpad[h, at : at + HEAD, rows] = value[sl, :]
        vpad[h, other : other + HEAD, rows] = zero
        if own:
            vone[h, :HEAD, rows] = value[sl, :]
            vone[h, HEAD:, rows] = ones
    grad = dot(ow[...], g[rows, :], NT).astype(bf16)
    dot_t[:, rows] = grad
    do[rows, :] = grad.T


def low_parts(x):
    high = x.astype(bf16)
    rest = x - high.astype(f32)
    mid = rest.astype(bf16)
    return [high, mid, (rest - mid.astype(f32)).astype(bf16)]


FILLED = 1792


def over_tiles(q0, tk, step, carry):
    last = lax.div(q0, tk)
    first = jnp.where(q0 >= FILLED, last, 0)
    return lax.fori_loop(first, last + 1, step, carry)


VROWS = 80
LOG2E = np.float32(math.log2(math.e))


def forward_tile(q0, tq, tk, first, places, qt, k, vone, ot, qpad, acc):
    heads = qt.shape[0] // HEAD
    zero = jnp.zeros((HEAD, tq), bf16)
    for h in range(heads):
        qh = qt[h * HEAD : (h + 1) * HEAD, pl.ds(q0, tq)]
        qpad[h] = jnp.concatenate([qh, zero] if h % 2 == 0 else [zero, qh], axis=0)
    acc[...] = jnp.zeros_like(acc)

    def step(j, peaks):
        k0 = pl.multiple_of(j * tk, tk)
        rows = k0 + lax.broadcasted_iota(jnp.int32, (tk, tq), 0)
        allowed = (rows >= first) & (rows <= places)
        scores, new, raised = [], [], []
        for h in range(heads):
            pair = (h // 2) * 128
            s = dot(k[pl.ds(k0, tk), pair : pair + 128], qpad[h])
            scores.append(jnp.where(allowed, s, -1e30))
        for h in range(heads):
            new.append(jnp.maximum(peaks[h], jnp.max(scores[h], axis=0, keepdims=True)))
            raised.append(jnp.exp2((scores[h] - new[h]) * LOG2E).astype(bf16))
        for h in range(heads):
            o = dot(vone[h, :, pl.ds(k0, tk)], raised[h])
            acc[h] = acc[h] * jnp.exp(peaks[h] - new[h]) + o
        return tuple(new)

    start = tuple(jnp.full((1, tq), -1e30, f32) for _ in range(heads))
    peaks = over_tiles(q0, tk, step, start)
    logs = []
    for h in range(heads):
        total = acc[h, HEAD : HEAD + 1, :]
        ot[h * HEAD : (h + 1) * HEAD, :] = acc[h, :HEAD, :] / total
        logs.append(peaks[h] + jnp.log(total))
    logs.append(jnp.zeros((8 - heads, tq), f32))
    ot[heads * HEAD :, :] = jnp.concatenate(logs, axis=0)


def backward_tile(q0, tq, tk, first, places, q, qt, k, kpad, vpad, do, dot_t, ot, cosine, sine, grads_q, dk, dv, dq, qa, da, cs, cd):
    heads = q.shape[1] // HEAD
    rows = pl.ds(q0, tq)
    deltas = [
        jnp.sum(ot[h * HEAD : (h + 1) * HEAD, :] * dot_t[h * HEAD : (h + 1) * HEAD, rows].astype(f32), axis=0, keepdims=True)
        for h in range(heads)
    ]
    deltas.append(jnp.zeros((8 - heads, tq), f32))
    stats = low_parts(ot[heads * HEAD :, :]) + low_parts(jnp.concatenate(deltas, axis=0))
    stats.append(jnp.zeros((128 - 48, tq), bf16))
    stat_cols = jnp.concatenate(stats, axis=0).T
    for r in range(heads // 2):
        pair = slice(r * 128, r * 128 + 128)
        qa[r, :, :128] = q[rows, pair]
        qa[r, :, 128:] = stat_cols
        da[r, :, :128] = do[rows, pair]
        da[r, :, 128:] = stat_cols
    dq[...] = jnp.zeros_like(dq)

    def step(j, carry):
        k0 = pl.multiple_of(j * tk, tk)
        ks = pl.ds(k0, tk)
        cols = k0 + lax.broadcasted_iota(jnp.int32, (tq, tk), 1)
        allowed = (cols >= first) & (cols <= places)
        probs, grads = [], []
        for h in range(heads):
            s = dot(qa[h // 2], jnp.concatenate([kpad[h, :, ks], cs[h]], axis=0))
            dp = dot(da[h // 2], jnp.concatenate([vpad[h, :, ks], cd[h]], axis=0))
            p = jnp.where(allowed, jnp.exp(s), 0.0)
            probs.append(p.astype(bf16))
            grads.append((p * dp).astype(bf16))
        for h in range(heads):
            sl = slice(h * HEAD, (h + 1) * HEAD)
            pair = slice((h // 2) * 128, (h // 2) * 128 + 128)
            dv[sl, ks] += dot(dot_t[sl, rows], probs[h])
            dk[sl, ks] += dot(qt[sl, rows], grads[h])
            dq[h] += dot(grads[h], k[ks, pair])
        return carry

    over_tiles(q0, tk, step, 0)
    scale = HEAD ** (-0.5)
    lane = lax.broadcasted_iota(jnp.int32, (tq, 128), 1)
    q_parts = [
        jnp.where(lane < HEAD, dq[2 * h], dq[2 * h + 1]).T * scale for h in range(heads // 2)
    ]
    grads_q[...] = turn(jnp.concatenate(q_parts, axis=0), cosine[:, rows], sine[:, rows], -1).astype(bf16)


def attention_kernel(tk, tile, own, bias_row, lens, tok_all, g_all, w, bias, ow, gains, biases, freq, *refs):
    refs = list(refs)
    cut = lambda n: [refs.pop(0) for _ in range(n)]
    if own:
        ot, grads_q, grads_k, grads_v, keep_o, send_o = cut(6)
    else:
        ot, grads_q, grads_k, grads_v = cut(4)
    q, qt, k, kpad, vpad, do, dot_t, cosine, sine, dk, dv, dq, qa, da, cs, cd = cut(16)
    tok, g, sems = cut(3)
    vone, qpad, acc, dow, low = cut(5) if own else (None, None, None, None, None)
    i = pl.program_id(0)
    length = tok.shape[0]
    heads, tq, _ = dq.shape
    q0 = pl.multiple_of(i * tq, tq)

    @pl.when(i == 0)
    def _():
        loads = [pltpu.make_async_copy(a, b, sems.at[n]) for n, (a, b) in enumerate(((tok_all, tok), (g_all, g)))]
        for c in loads:
            c.start()
        dk[...] = jnp.zeros_like(dk)
        dv[...] = jnp.zeros_like(dv)
        row = lax.broadcasted_iota(jnp.int32, (128, tk), 0)
        for h in range(heads):
            cs[h] = jnp.where((row < 24) & (row % 8 == h), -1.0, 0.0).astype(bf16)
            cd[h] = jnp.where((row >= 24) & (row < 48) & (row % 8 == h), -1.0, 0.0).astype(bf16)

        for c in loads:
            c.wait()

        def some(t, c):
            project_tile(t, tile, bias_row, lens, tok, g, w, bias, ow, gains, biases, freq, own, q, qt, k, kpad, vpad, vone, do, dot_t, cosine, sine)
            return c

        lax.fori_loop(0, length // tile, some, 0)

    @pl.when(q0 < FILLED)
    def _():
        if own:
            places = q0 + lax.broadcasted_iota(jnp.int32, (1, tq), 1)
            forward_tile(q0, tq, 2 * tk, first_tokens(lens, places), places, qt, k, vone, ot, qpad, acc)
        places = q0 + lax.broadcasted_iota(jnp.int32, (tq, 1), 0)
        backward_tile(
            q0, tq, tk, first_tokens(lens, places), places, q, qt, k, kpad, vpad, do, dot_t, ot, cosine, sine, grads_q, dk, dv, dq, qa, da, cs, cd
        )

    @pl.when(q0 >= FILLED)
    def _():
        cols = pl.ds(q0, tq)
        if own:
            for h in range(heads):
                ot[h * HEAD : (h + 1) * HEAD, :] = vone[h, :HEAD, cols].astype(f32)
            ot[heads * HEAD :, :] = jnp.zeros((8, tq), f32)
        grads_q[...] = jnp.zeros_like(grads_q)
        dv[:, cols] = dot_t[:, cols].astype(f32)

    if own:
        low[:, pl.ds(q0, tq)] = ot[: ow.shape[0], :].astype(bf16)

    @pl.when(i == pl.num_programs(0) - 1)
    def _():
        grads_k[...] = turn(dk[...], cosine[...], sine[...], -1).astype(bf16)
        grads_v[...] = dv[...].astype(bf16)
        if own:
            dow[...] = dot(low[...], g[...])
            r = dow.shape[0] // 2
            for ref, half in ((keep_o, bit_of(0)), (send_o, 1 - bit_of(0))):
                ref[...] = dow[pl.ds(pl.multiple_of(half * r, r), r), :]


def attention(bias_row, lens, tok, g, w, bias, ow, gains, biases, freq, ot=None, tq=256, tk=256, tile=512, deps=(), rides=(), collective=None):
    length, d = tok.shape
    e = w.shape[2]
    heads = e // HEAD
    own = ot is None
    cols = pl.BlockSpec((e, tq), lambda i, *_: (0, i))
    stat = pl.BlockSpec((e + 8, tq), lambda i, *_: (0, i))
    grad = jax.ShapeDtypeStruct((e, length), bf16)
    kept = jax.ShapeDtypeStruct((e + 8, length), f32)
    nat, tr, pad, angle = pltpu.VMEM((length, e), bf16), pltpu.VMEM((e, length), bf16), pltpu.VMEM((heads, 128, length), bf16), pltpu.VMEM((HALF, length), f32)
    scratch = [nat, tr, nat, pad, pad, nat, tr, angle, angle]
    scratch += [pltpu.VMEM((e, length), f32)] * 2 + [pltpu.VMEM((heads, tq, 128), f32)]
    scratch += [pltpu.VMEM((heads // 2, tq, 256), bf16)] * 2 + [pltpu.VMEM((heads, 128, tk), bf16)] * 2
    scratch += [pltpu.VMEM((length, d), bf16)] * 2 + [pltpu.SemaphoreType.DMA((2,))]
    if own:
        scratch += [pltpu.VMEM((heads, VROWS, length), bf16), pltpu.VMEM((heads, 128, tq), bf16), pltpu.VMEM((heads, VROWS, tq), f32), pltpu.VMEM((e, d), f32), tr]
    half = jax.ShapeDtypeStruct((e // 2, d), f32)
    return call(
        functools.partial(attention_kernel, tk, tile, own, bias_row),
        grid=(length // tq,),
        scalars=1,
        in_specs=[
            *[pl.BlockSpec(memory_space=pl.ANY)] * 2, whole((3, d, e)), whole((8, d)), whole((e, d)), whole((2, d)), whole((2, d)), whole((HALF, 128)),
        ] + ([] if own else [stat]),
        out_specs=([stat] if own else []) + [cols, whole((e, length)), whole((e, length))] + ([whole(half.shape)] * 2 if own else []),
        out_shape=([kept] if own else []) + [grad, grad, grad] + ([half, half] if own else []),
        scratch=scratch,
        flops=8 * length * length * e,
        nbytes=20 * length * e,
        deps=deps,
        rides=rides,
        collective=collective,
        name="attention",
    )(lens, tok, g, w, bias, ow, gains, biases, freq, *([] if own else [ot]))


def merge_tile(tok, gq, gk, gv, ot, w, ow, gains, biases):
    hat, inverse = hat_of(tok[...].astype(f32))
    gain = gains[0:1, :]
    back = dot(gq[...], w[0], TT) + dot(gk[...], w[1], TT) + dot(gv[...], w[2], TT)
    low = ot[...].astype(bf16)
    return hat, inverse, gain, back, dot(low, ow[...], TN)


def merge_own_kernel(tok, gq, gk, gv, ot, w, ow, gains, biases, part_in, share_in, small_in, upb_in, part, share, keep_a, send_a, keep_b, send_b, small, dw):
    i = pl.program_id(0)
    tile = tok.shape[0]
    e, d = ow.shape
    n_up = 2

    @pl.when(i == 0)
    def _():
        dw[...] = jnp.zeros_like(dw)
        small[...] = jnp.zeros_like(small)
        small[1:2, :] = small_in[1:2, :]
        small[3:4, :] = small_in[2:3, :]
        small[4:5, :] = small_in[0:1, :]
        small[5 : 5 + n_up, :] = upb_in[:n_up, :]

    hat, _, gain, back, out = merge_tile(tok, gq, gk, gv, ot, w, ow, gains, biases)
    normed = (hat * gain + biases[0:1, :]).astype(bf16)
    share[...] = share_in[...] + back * gain
    part[...] = part_in[...] + out
    dw[0] += dot(normed, gq[...], TT)
    dw[1] += dot(normed, gk[...], TT)
    dw[2] += dot(normed, gv[...], TT)
    small[0:1, :] += jnp.sum(back * hat, axis=0, keepdims=True)
    small[2:3, :] += jnp.sum(back, axis=0, keepdims=True)
    ones = jnp.ones((8, tile), bf16)
    at = 5 + n_up
    small[at : at + 1, :e] += dot(ones, gq[...], NT)[0:1]
    small[at : at + 1, e : 2 * e] += dot(ones, gv[...], NT)[0:1]

    @pl.when(i == pl.num_programs(0) - 1)
    def _():
        core = bit_of(0)
        r = d // 8
        for refs, half in (((keep_a, keep_b), core), ((send_a, send_b), 1 - core)):
            for n in range(6):
                ref, at, c, sub = refs[n // 3], n % 3 * r, n // 2, n % 2
                for s in range(2):
                    rows = pl.multiple_of(half * (d // 2) + (2 * s + sub) * r, r)
                    ref[at : at + r, s * e : (s + 1) * e] = dw[c, pl.ds(rows, r), :]


def merge_own(tok, gq, gk, gv, ot, w, ow, gains, biases, part, share, small, upb, tile=512, deps=(), rides=(), collective=None):
    length, d = tok.shape
    e = w.shape[2]
    rows = pl.BlockSpec((tile, d), lambda i: (i, 0))
    cols = pl.BlockSpec((e, tile), lambda i: (0, i))
    full = jax.ShapeDtypeStruct((length, d), f32)
    half = jax.ShapeDtypeStruct((3 * d // 8, d), f32)
    return call(
        merge_own_kernel,
        grid=(length // tile,),
        in_specs=[rows, cols, cols, cols, cols, whole((3, d, e)), whole((e, d)), whole((2, d)), whole((2, d)), rows, rows, whole((8, d)), whole((8, d))],
        out_specs=[rows, rows, *[once(half.shape)] * 4, once((8, d))],
        out_shape=[full, full, half, half, half, half, jax.ShapeDtypeStruct((8, d), f32)],
        scratch=[pltpu.VMEM((3, d, e), f32)],
        flops=16 * length * d * e,
        nbytes=24 * length * d,
        deps=deps,
        rides=rides,
        collective=collective,
        name="merge_own",
    )(tok, gq, gk, gv, ot, w, ow, gains, biases, part, share, small, upb)


def merge_other_kernel(tok, g, gq, gk, gv, ot, w, ow, gains, biases, out_bias, down_bias, part_in, share_in, output, input_grad):
    hat, inverse, gain, back, out = merge_tile(tok, gq, gk, gv, ot, w, ow, gains, biases)
    shares = share_in[...] + back * gain
    inputs = tok[...].astype(f32)
    output[...] = (inputs + (part_in[...] + out) + out_bias[...].astype(f32) + down_bias[...].astype(f32)).astype(bf16)
    input_share = inverse * (
        shares
        - jnp.mean(shares, axis=-1, keepdims=True)
        - hat * jnp.mean(shares * hat, axis=-1, keepdims=True)
    )
    input_grad[...] = (g[...].astype(f32) + input_share).astype(bf16)


def merge_other(tok, g, gq, gk, gv, ot, w, ow, gains, biases, out_bias, down_bias, part, share, tile=512, deps=(), rides=(), collective=None):
    length, d = tok.shape
    e = w.shape[2]
    rows = pl.BlockSpec((tile, d), lambda i: (i, 0))
    cols = pl.BlockSpec((e, tile), lambda i: (0, i))
    full = jax.ShapeDtypeStruct((length, d), bf16)
    return call(
        merge_other_kernel,
        grid=(length // tile,),
        in_specs=[rows, rows, cols, cols, cols, cols, whole((3, d, e)), whole((e, d)), whole((2, d)), whole((2, d)), whole((1, d)), whole((1, d)), rows, rows],
        out_specs=[rows, rows],
        out_shape=[full, full],
        flops=8 * length * d * e,
        nbytes=24 * length * d,
        deps=deps,
        rides=rides,
        collective=collective,
        name="merge_other",
    )(tok, g, gq, gk, gv, ot, w, ow, gains, biases, out_bias[None], down_bias[None], part, share)


def pack_kernel(meta, w, ow, up, down, w_far, ow_far, up_far, down_far, upb, qkvb, one, two, three, four, bias_rows):
    d = ow.shape[1]
    e = w.shape[2]

    def blocks(refs):
        w, ow, up, down = refs
        for n in range(2):
            r = down.shape[0] // 8
            for s in range(4):
                yield [down[(4 * n + s) * r : (4 * n + s + 1) * r, :]]
            r = up.shape[0] // 2
            for c in range(up.shape[1] // d):
                yield [up[n * r : (n + 1) * r, c * d : (c + 1) * d]]
            r = w.shape[1] // 4
            for c in range(3):
                yield [w[c, (2 * n + s) * r : (2 * n + s + 1) * r, :] for s in range(2)]
            r = ow.shape[0] // 2
            yield [ow[n * r : (n + 1) * r, :]]

    for refs, outs in (((w, ow, up, down), (one, two, three)), ((w_far, ow_far, up_far, down_far), (None, None, four))):
        sizes = [x.shape[0] for x in (one, two, three)]
        which, at = 0, 0
        for parts in blocks(refs):
            rows, lanes = parts[0].shape
            for j, x in enumerate(parts):
                if outs[which] is not None:
                    outs[which][at : at + rows, j * lanes : (j + 1) * lanes] = x.astype(f32)
            at += rows
            if at == sizes[which]:
                which, at = which + 1, 0
    n = upb.shape[1] // d
    bias_rows[...] = jnp.zeros_like(bias_rows)
    for c in range(n):
        bias_rows[c : c + 1, :] = upb[:, c * d : (c + 1) * d].astype(f32)
    for c in range(2):
        bias_rows[n : n + 1, c * e : (c + 1) * e] = qkvb[c : c + 1, :].astype(f32)


def pack(meta, w, ow, up, down, upb, qkvb):
    _, d, e = w.shape
    wide = up.shape[1]
    rows = (wide + (wide // d) * d + 3 * d // 2 + e) // 4
    one = wide // 8 + d // 8
    two = rows // 2 - one + wide // 32
    sizes = [one, two, rows - one - two, rows - one - two, 8]
    blocks = lambda n: [
        pl.BlockSpec((3, d // 4, e), lambda i, m: (0, m[n], 0)),
        pl.BlockSpec((e // 4, d), lambda i, m: (m[n], 0)),
        pl.BlockSpec((d // 4, wide), lambda i, m: (m[n], 0)),
        pl.BlockSpec((wide // 4, d), lambda i, m: (m[n], 0)),
    ]
    return call(
        pack_kernel,
        grid=(1,),
        scalars=1,
        in_specs=blocks(0) + blocks(1) + [whole((1, wide)), whole((2, e))],
        out_specs=[once((r, d)) for r in sizes],
        out_shape=[jax.ShapeDtypeStruct((r, d), f32) for r in sizes],
        name="pack",
    )(meta, w, ow, up, down, w, ow, up, down, upb[None], qkvb)


def unpack(pieces, w, ow, up, down):
    d = ow.shape[1]
    e = w.shape[2]
    for n in range(4):
        core = lax.rem(bit_of(0) + n // 2, 2)
        parity = lax.rem(bit_of(1) + bit_of(2) + n % 2, 2)
        refs = pieces[3 * n : 3 * n + 3]
        place = [0, 0]

        def take(rows):
            ref, at = refs[place[0]], place[1]
            place[1] = at + rows
            if place[1] == ref.shape[0]:
                place[:] = [place[0] + 1, 0]
            return ref[at : at + rows, :].astype(bf16)

        for m in range(2):
            at_piece = (parity * 2 + core) * 2 + m
            rows = lambda r, sub=0, parts=1: pl.ds(pl.multiple_of((at_piece * parts + sub) * r, r), r)
            r = down.shape[0] // 32
            for s in range(4):
                down[rows(r, s, 4), :] = take(r)
            r = up.shape[0] // 8
            for c in range(up.shape[1] // d):
                up[rows(r), c * d : (c + 1) * d] = take(r)
            r = w.shape[1] // 16
            for c in range(3):
                x = take(r)
                for s in range(2):
                    w[c, rows(r, s, 2), :] = x[:, s * e : (s + 1) * e]
            r = ow.shape[0] // 8
            ow[rows(r), :] = take(r)


def swap(x, bit):
    n = lax.axis_size("dp")
    return lax.ppermute(x, "dp", [(i, i ^ (1 << bit)) for i in range(n)])


def across(x):
    return lax.ppermute(x, "tensor", [(0, 1), (1, 0)])


def tie(arrays, deps):
    n = len(arrays)
    anywhere = [pl.BlockSpec(memory_space=pl.ANY)] * n
    return call(
        lambda *refs: None,
        grid=(1,),
        in_specs=anywhere,
        out_specs=anywhere,
        out_shape=[jax.ShapeDtypeStruct(x.shape, x.dtype) for x in arrays],
        aliases={i: i for i in range(n)},
        deps=deps,
        name="tie",
    )(*arrays)


def down_places(d, wide):
    rows = d // 2

    def places(sources, outs, core):
        return [
            (x, outs[0].at[pl.ds(pl.multiple_of(c * d + core * rows, 8), rows)]) for c, x in enumerate(sources)
        ]

    return [(wide, d)], wide // d, places


def up_places(d, wide):
    rows = d // 2

    def places(sources, outs, core):
        to = pl.ds(pl.multiple_of(core * rows, 8), rows)
        return [(x, outs[0].at[to, pl.ds(c * d, d)]) for c, x in enumerate(sources)]

    return [(d, wide)], wide // d, places


def attn_places(d, e):
    rows = d // 8

    def places(sources, outs, core):
        pairs = []
        for n in range(6):
            source, at, c, sub = sources[n // 3], n % 3 * rows, n // 2, n % 2
            for s in range(2):
                to = pl.ds(pl.multiple_of(core * (d // 2) + (2 * s + sub) * rows, 8), rows)
                pairs.append((source.at[pl.ds(at, rows), pl.ds(s * e, e)], outs[0].at[c, to]))
        to = pl.ds(pl.multiple_of(core * (e // 2), 8), e // 2)
        pairs.append((sources[2], outs[1].at[to]))
        return pairs

    return [(3, d, e), (e, d)], 13, places


def relay(rides, collective, deps=()):
    call(
        lambda *_: None,
        grid=(1,),
        in_specs=[],
        out_specs=[],
        out_shape=[],
        deps=deps,
        rides=rides,
        collective=collective,
        name="relay",
    )()


def per_device(
    tokens, lengths, qkv_weight, qkv_bias, out_weight, out_bias, up_weight, up_bias, down_weight, down_bias, norm_gains, norm_biases, cotangent
):
    length, d = tokens.shape
    e = qkv_weight.shape[2]
    wide = up_weight.shape[1]
    bits = lax.axis_size("dp").bit_length() - 1
    me = lax.axis_index("dp")
    quarter = lambda p: (((me >> 1) ^ (me >> 2) ^ p) & 1) * 2 + (me & 1)
    meta = jnp.stack([quarter(0), quarter(1)])
    freq = np.broadcast_to((rot_base ** (-(2.0 * np.arange(HALF)) / ROT)).astype(np.float32)[:, None], (HALF, 128))
    one, two, three, far_three, own_biases = pack(
        meta, qkv_weight, out_weight, up_weight, down_weight, up_bias, qkv_bias
    )
    order = list(range(1, bits))
    crossed = [order[1], order[0]] + order[2:]
    early = [Held(EARLY + j, (d // 2, d)) for j in range(4)]
    down_1, up_1 = Sum(early[0], early[1], order), Sum(early[2], early[3], crossed)
    send = Sends((one, "tensor"), (own_biases, "tensor"), (two, "tensor"))
    part, share, keep_d, send_d, keep_u, send_u, small, upb_sum = mlp_own(
        tokens, cotangent, up_weight, own_biases, down_weight, norm_gains, norm_biases,
        rides=[send, down_1.take(4, 5), up_1.take(4, 5)], collective=1,
    )
    one, other_biases, two = send.got
    down_2, up_2 = Sum(keep_d, send_d, order), Sum(keep_u, send_u, crossed)
    send = Sends((three, "tensor"), (far_three, "tensor"), (one, 0), (two, 0))
    near = [Sends((one, 1), at=(2,)), Sends((two, 1), at=(5,))]
    ot, gq, gk, gv, keep_o, send_o = attention(
        wide // d, lengths, tokens, cotangent, qkv_weight, own_biases, out_weight, norm_gains, norm_biases, freq,
        rides=[down_1.take(0, 1, 4), up_1.take(0, 1, 4), down_2.take(0, 1, 5, 6), up_2.take(0, 1, 5, 6), send] + near, collective=2,
    )
    three, near_three, core_one, core_two = send.got
    (near_one,), (near_two,) = near[0].got, near[1].got
    other_ot = across(ot)
    sum_o = Sum(keep_o, send_o, order, True)
    send = Sends((near_one, 0), (near_two, 0), (near_three, 0), (three, 0))
    part, share, keep_a, send_a, keep_b, send_b, small = merge_own(
        tokens, gq, gk, gv, ot, qkv_weight, out_weight, norm_gains, norm_biases, part, share, small, upb_sum,
        rides=[down_2.take(0), up_2.take(0), down_1.take(0), up_1.take(0), sum_o.take(0), send], collective=3,
    )
    core_near_one, core_near_two, core_near_three, core_three = send.got
    sum_a, sum_b, sum_s = Sum(keep_a, send_a, order, True), Sum(keep_b, send_b, crossed, True), SmallSum(small, bits)
    pieces = [one, two, three, near_one, near_two, near_three]
    pieces += [core_one, core_two, core_three, core_near_one, core_near_two, core_near_three]
    part, share, other_w, other_ow = mlp_other(
        pieces, tokens, cotangent, other_biases, norm_gains, norm_biases, part, share, [qkv_weight, out_weight, up_weight, down_weight],
        rides=[
            sum_s.take(0, 3), sum_a.take(0, 1, 3), sum_b.take(0, 1, 3), sum_o.take(1, 3), down_2.take(0), up_2.take(0), down_1.take(0), up_1.take(0),
        ],
        collective=4,
    )
    (other_ot,) = tie([other_ot], [part])
    gq, gk, gv = attention(
        wide // d, lengths, tokens, cotangent, other_w, other_biases, other_ow, norm_gains, norm_biases, freq, other_ot,
        rides=[s.take(0, 5, 6) for s in (sum_a, sum_b, sum_o)] + [down_2.take(0), up_2.take(0), sum_s.take(0, 6)], collective=5,
    )
    at = 7
    sums = [down_1, down_2, up_1, up_2, sum_a, sum_b, sum_o]
    while not all(s.done for s in sums):
        relay([s.take(0) for s in sums if not s.done], at)
        at += 1
    final_d, final_u = Final(sums[:2], *down_places(d, wide)), Final(sums[2:4], *up_places(d, wide))
    final = Final(sums[4:], *attn_places(d, e))
    output, input_grad = merge_other(
        tokens, cotangent, gq, gk, gv, other_ot, other_w, other_ow, norm_gains, norm_biases, out_bias, down_bias, part, share,
        rides=[sum_s.take(0), final_d, final_u, final], collective=6,
    )
    while not sum_s.done:
        relay([sum_s.take(0)], at)
        at += 1
    (d_down,), (d_up,), (d_qkv, d_out) = final_d.results, final_u.results, final.results
    small = sum_s.mine
    rest = small[5:].reshape(-1)
    return (
        output, input_grad, d_qkv, rest[wide : wide + 2 * e].reshape(2, e), d_out, small[4], d_up, rest[:wide], d_down, small[4], small[:2], small[2:4],
    )


def solution(mesh):
    in_specs = (
        P("dp", None), P("dp", None), P(None, None, "tensor"), P(None, "tensor"), P("tensor", None), P(), P(None, "tensor"),
        P("tensor"), P("tensor", None), P(), P(), P(), P("dp", None),
    )
    out_specs = (
        P("dp", None), P("dp", None), P(None, None, "tensor"), P(None, "tensor"), P("tensor", None), P(), P(None, "tensor"),
        P("tensor"), P("tensor", None), P(), P(), P(),
    )
    return jax.shard_map(per_device, mesh=mesh, in_specs=in_specs, out_specs=out_specs, check_vma=False)
```
